32 devices in a mesh: dom: 32 (over z, y, x, core).
Axes of the slice: x: 2, y: 2, z: 4, core: 2. Of those that a mesh axis runs over, the one named last changes fastest.
Arguments:
- rhs_field: float32 [64, 4096], P(None, 'dom'), may hold values from -6 to 6
- initial_guess: float32 [64, 4096], P(None, 'dom'), may hold values from -6 to 6
- start_vector: float32 [64, 4096], P(None, 'dom'), may hold values from -90 to 90
- coefficient: float32 [4096], P('dom'), may hold values from 1 to 10
- refine_level: int32 [4096], P('dom'), may hold values from 0 to 2
- block_inverse: bfloat16 [64, 64, 4096], P(None, None, 'dom'), may hold values from -0.015 to 1, as said below
- side_elem: int32 [29760], P('dom'), may hold values from 0 to 127, as said below
- side_dir: int32 [29760], P('dom'), may hold values from 0 to 5, as said below
- side_case: int32 [29760], P('dom'), may hold values from 0 to 4, as said below
- side_kind: int32 [29760], P('dom'), may hold values from 0 to 1, as said below
- partner: int32 [29760], P('dom'), may hold values from 0 to 1625, as said below
- send_list: int32 [256, 96], P('dom'), may hold values from 0 to 930, as said below
Outputs:
- smoothed: float32 [64, 4096], P(None, 'dom')
- eigen_bound: float32 [], replicated
The draws below stay inside these ranges and needn't reach their ends.
Inputs may be any that keep to these rules, and one draw needn't show every extreme that they name: `block_inverse`: each element's block is symmetric and positive definite. `side_elem`: an index among the 128 elements of the side's device. `side_dir`: 2 a is the face at the upper end of dimension a, 2 a + 1 the one at the lower end; partners lie on opposite faces of one dimension. `side_case`: 0 to 3 mark one quarter of a coarse face whose partner is the whole face of a finer element (case 4). `side_kind`: 1 marks a boundary side, whose partner entry is the side itself. `partner`: a device-local index; interior partners are mutual. `send_list`: row 8 d + p lists device d's sides for the device peer_offset[p] places higher; live entries are the first 96, 48, 24 or 24 of a row for offsets of size 1, 2, 3, 4; 930 marks an empty slot.
All inputs are finite; a program needn't handle non-finite values.
Results may differ from the reference program's by a relative error of at most 0.0003.
Values sent between devices are 32-bit elements; how exact they have to be, the bound alone decides.
No kernel may reach another device: no remote copies, remote signals or barrier semaphores. Data moves between devices by JAX's collectives and lax.ppermute only.
A program may use at most 64 MiB of HBM per device.

```python
import math
import jax
import jax.numpy as jnp
import numpy as np
from jax import lax

ELEM_DEV = 128
DOFS = 64
POWER = 4
CHEB = 2
CROSS1 = 16
CROSS2 = 8
CROSS3 = 4
CROSS4 = 4
SIDE_DEV = 930
SLOT = 96
ELEMENTS = 4096
N_DOM = 32


draw_offsets = (1, -1, 2, -2, 3, -3, 4, -4)


def layout_template():
    crossing = [CROSS1, CROSS2, CROSS3, CROSS4]
    local_count = ELEM_DEV - 2 * sum(crossing)

    def group_size(group_offset):
        if group_offset == 0:
            return local_count
        return crossing[abs(group_offset) - 1]
    group_order = [0, 1, -1, 2, -2, 3, -3, 4, -4]
    face_rows = []
    place_rows = []
    case_rows = []
    group_rows = []
    peer_rows = []
    loose_rows = []
    member_rows = []
    plus_flag = []
    plus_rows = {}
    minus_rows = {}

    def append_row(face_index, place_index, case_index, group_offset, peer_offset, loose, member, is_plus):
        face_rows.append(face_index)
        place_rows.append(place_index)
        case_rows.append(case_index)
        group_rows.append(group_offset)
        peer_rows.append(peer_offset)
        loose_rows.append(loose)
        member_rows.append(member)
        plus_flag.append(is_plus)
    for dimension in range(3):
        place_start = 0
        for group_offset in group_order:
            amount = group_size(group_offset)
            hanging = (amount + 4) // 8
            for block in range(amount // 4):
                first_place = place_start + 4 * block
                if block < hanging:
                    for quarter in range(4):
                        plus_rows[dimension, group_offset, 4 * block + quarter] = len(face_rows)
                        append_row(2 * dimension, first_place, quarter, group_offset, group_offset, 0, 4 * block + quarter, 1)
                    for member in range(1, 4):
                        append_row(2 * dimension, first_place + member, 4, group_offset, group_offset, 1, -1, 1)
                else:
                    for member in range(4):
                        plus_rows[dimension, group_offset, 4 * block + member] = len(face_rows)
                        append_row(2 * dimension, first_place + member, 4, group_offset, group_offset, 0, 4 * block + member, 1)
            place_start += amount
        place_start = 0
        for group_offset in group_order:
            amount = group_size(group_offset)
            for member in range(amount):
                minus_rows[dimension, group_offset, member] = len(face_rows)
                append_row(2 * dimension + 1, place_start + member, 4, group_offset, -group_offset, 0, member, 0)
            place_start += amount
    peer_place = {}
    for place_index in range(8):
        peer_place[draw_offsets[place_index]] = place_index
    partner_rows = []
    for row_index in range(len(face_rows)):
        dimension = face_rows[row_index] // 2
        group_offset = group_rows[row_index]
        member = member_rows[row_index]
        amount = group_size(group_offset)
        if loose_rows[row_index] == 1:
            partner_rows.append(row_index)
        elif group_offset == 0:
            if plus_flag[row_index] == 1:
                partner_rows.append(minus_rows[dimension, 0, member])
            else:
                partner_rows.append(plus_rows[dimension, 0, member])
        elif plus_flag[row_index] == 1:
            partner_rows.append(SIDE_DEV + peer_place[-group_offset] * SLOT + dimension * 2 * amount + amount + member)
        else:
            partner_rows.append(SIDE_DEV + peer_place[group_offset] * SLOT + dimension * 2 * amount + member)
    send_rows = np.full((8, SLOT), SIDE_DEV, dtype=np.int64)
    for place_index in range(8):
        group_offset = draw_offsets[place_index]
        amount = group_size(group_offset)
        for dimension in range(3):
            for member in range(amount):
                send_rows[place_index, dimension * 2 * amount + member] = plus_rows[dimension, group_offset, member]
                send_rows[place_index, dimension * 2 * amount + amount + member] = minus_rows[dimension, -group_offset, member]
    return (np.array(face_rows), np.array(place_rows), np.array(case_rows), np.array(group_rows), np.array(peer_rows), np.array(loose_rows), np.array(partner_rows), send_rows)


def mesh_arrays(key):
    face_rows, place_rows, case_rows, group_rows, peer_rows, loose_rows, partner_rows, send_rows = layout_template()
    devices = ELEMENTS // ELEM_DEV
    order_keys = jax.random.split(jax.random.fold_in(key, 401), devices * 6)
    orders = jax.vmap(lambda one_key: jax.random.permutation(one_key, ELEM_DEV))(order_keys).reshape(devices, 6, ELEM_DEV).astype(jnp.int32)
    row_keys = jax.random.split(jax.random.fold_in(key, 402), devices)
    new_place = jax.vmap(lambda one_key: jax.random.permutation(one_key, SIDE_DEV))(row_keys).astype(jnp.int32)
    element = orders[:, face_rows, place_rows]
    device_index = jnp.arange(devices, dtype=jnp.int32)[:, None]
    peer_device = device_index + jnp.asarray(peer_rows, jnp.int32)[None, :]
    outside = ((peer_device < 0) | (peer_device >= devices)) & (jnp.asarray(group_rows, jnp.int32)[None, :] != 0)
    kind = jnp.where(outside | (jnp.asarray(loose_rows, jnp.int32)[None, :] == 1), 1, 0).astype(jnp.int32)
    partner_table = jnp.asarray(partner_rows, jnp.int32)[None, :]
    partner_local = new_place[:, np.minimum(partner_rows, SIDE_DEV - 1)]
    partner_value = jnp.where(kind == 1, new_place, jnp.where(partner_table < SIDE_DEV, partner_local, partner_table))
    shape_full = (devices, SIDE_DEV)

    def place_values(values):
        return jnp.zeros(shape_full, jnp.int32).at[device_index, new_place].set(jnp.broadcast_to(values, shape_full).astype(jnp.int32)).reshape(devices * SIDE_DEV)
    send_table = jnp.asarray(send_rows, jnp.int32)[None, :, :]
    send_mapped = jnp.where(send_table < SIDE_DEV, new_place[:, np.minimum(send_rows, SIDE_DEV - 1)], SIDE_DEV).astype(jnp.int32)
    return (place_values(element), place_values(jnp.asarray(face_rows, jnp.int32)[None, :]), place_values(jnp.asarray(case_rows, jnp.int32)[None, :]), place_values(kind), place_values(partner_value), send_mapped.reshape(devices * 8, SLOT))


def element_fields(key):
    level_key = jax.random.fold_in(key, 301)
    kappa_key = jax.random.fold_in(key, 302)
    levels = jax.random.randint(level_key, (ELEMENTS,), 0, 3).astype(jnp.int32)
    kappa = jnp.exp(jax.random.uniform(kappa_key, (ELEMENTS,), jnp.float32) * math.log(10.0))
    return (levels, kappa)


def draw_side_elem(key, part):
    layout = mesh_arrays(key)
    return layout[0]


def draw_side_dir(key, part):
    layout = mesh_arrays(key)
    return layout[1]


def draw_side_case(key, part):
    layout = mesh_arrays(key)
    return layout[2]


def draw_side_kind(key, part):
    layout = mesh_arrays(key)
    return layout[3]


def draw_partner(key, part):
    layout = mesh_arrays(key)
    return layout[4]


def draw_send_list(key, part):
    layout = mesh_arrays(key)
    return layout[5]


def draw_refine_level(key, part):
    levels, kappa = element_fields(key)
    return levels


def draw_coefficient(key, part):
    levels, kappa = element_fields(key)
    return kappa


def draw_block_inverse(key, part):
    levels, kappa = element_fields(key)
    key = jax.random.fold_in(key, 29)
    scale = jnp.power(jnp.float32(2.0), levels.astype(jnp.float32)) / (4.0 * kappa)
    spread = jax.random.uniform(key, (64, 64, ELEMENTS), jnp.float32, -0.015, 0.015)
    spread = 0.5 * (spread + jnp.swapaxes(spread, 0, 1))
    diagonal = (jnp.arange(64)[:, None] == jnp.arange(64)[None, :]).astype(jnp.float32)[:, :, None]
    return (scale[None, None, :] * (diagonal + spread * (1.0 - diagonal))).astype(jnp.bfloat16)


def draw_start_vector(key, part):
    key = jax.random.fold_in(key, 30)
    keys = jax.random.split(key, 3)
    row_scale = jnp.exp(jax.random.uniform(keys[0], (64, 1), jnp.float32) * math.log(10.0))
    col_scale = jnp.exp(jax.random.uniform(keys[1], (1, ELEMENTS), jnp.float32) * math.log(10.0))
    base = jnp.clip(jax.random.normal(keys[2], (64, ELEMENTS), jnp.float32), -4.0, 4.0)
    along = jnp.arange(ELEMENTS, dtype=jnp.float32)[None, :] / ELEMENTS
    values = base * row_scale * col_scale * (1.0 + along)
    return 0.05 * values


def steps_of(rng, extent, cuts, low, largest):
    def one(axis_at, blocks):
        steps = jax.random.uniform(jax.random.fold_in(jax.random.fold_in(rng, 6), axis_at), (blocks,), jnp.float32, low / len(cuts), largest / len(cuts))
        return jnp.repeat(jnp.exp(steps), extent[axis_at] // blocks).reshape((-1,) + (1,) * (len(extent) - axis_at - 1))

    factor_of = one(*cuts[0])
    for cut in cuts[1:]:
        factor_of = factor_of * one(*cut)
    return factor_of


def centred(own_key, extent, width, bound, cuts=(), kind=jnp.bfloat16):
    gain = steps_of(own_key, extent, cuts, -0.22, 0.18) if cuts else 1.0
    values = jax.random.normal(own_key, extent, jnp.float32) * width * gain
    return jnp.minimum(jnp.maximum(values, -bound), bound).astype(kind)


def setup_inputs(seed: int = 0) -> dict:
    arg_keys = jax.random.split(jax.random.key(seed), 13)
    rhs_field = centred(arg_keys[0], (DOFS, ELEMENTS), 1.0, 6.0, ((1, 32),), jnp.float32)
    initial_guess = centred(arg_keys[1], (DOFS, ELEMENTS), 1.0, 6.0, ((1, 32),), jnp.float32)
    start_vector = draw_start_vector(jax.random.fold_in(arg_keys[12], 71), 0)
    coefficient = draw_coefficient(jax.random.fold_in(arg_keys[12], 71), 0)
    refine_level = draw_refine_level(jax.random.fold_in(arg_keys[12], 71), 0)
    block_inverse = draw_block_inverse(jax.random.fold_in(arg_keys[12], 71), 0)
    side_elem = draw_side_elem(jax.random.fold_in(arg_keys[12], 71), 0)
    side_dir = draw_side_dir(jax.random.fold_in(arg_keys[12], 71), 0)
    side_case = draw_side_case(jax.random.fold_in(arg_keys[12], 71), 0)
    side_kind = draw_side_kind(jax.random.fold_in(arg_keys[12], 71), 0)
    partner = draw_partner(jax.random.fold_in(arg_keys[12], 71), 0)
    send_list = draw_send_list(jax.random.fold_in(arg_keys[12], 71), 0)
    return dict(rhs_field=rhs_field, initial_guess=initial_guess, start_vector=start_vector, coefficient=coefficient, refine_level=refine_level, block_inverse=block_inverse, side_elem=side_elem, side_dir=side_dir, side_case=side_case, side_kind=side_kind, partner=partner, send_list=send_list)


penalty_factor = 32.0
highest = lax.Precision.HIGHEST
peer_offsets = (1, -1, 2, -2, 3, -3, 4, -4)

def lagrange_tables():
    root_five = 1.0 / math.sqrt(5.0)
    gll_nodes = np.array([0.0, 0.5 - 0.5 * root_five, 0.5 + 0.5 * root_five, 1.0])
    weights = np.array([1.0, 5.0, 5.0, 1.0]) / 12.0
    factor = np.array([np.prod([gll_nodes[row_node] - gll_nodes[other_node] for other_node in range(4) if other_node != row_node]) for row_node in range(4)])
    derivative = np.zeros((4, 4))
    for row_node in range(4):
        for col_node in range(4):
            if row_node != col_node:
                derivative[row_node, col_node] = factor[row_node] / (factor[col_node] * (gll_nodes[row_node] - gll_nodes[col_node]))
        derivative[row_node, row_node] = -np.sum(derivative[row_node])
    halves = []
    for half_index in range(2):
        points = 0.5 * (gll_nodes + half_index)
        half_table = np.ones((4, 4))
        for col_node in range(4):
            for other_node in range(4):
                if other_node != col_node:
                    half_table[:, col_node] *= (points - gll_nodes[other_node]) / (gll_nodes[col_node] - gll_nodes[other_node])
        halves.append(half_table)
    return (weights, derivative, halves)

def basis_tables():
    weights, derivative, halves = lagrange_tables()
    mass_matrix = np.eye(4) * weights[None, :]
    stiff_line = derivative.T @ mass_matrix @ derivative
    stiffness = np.kron(np.kron(stiff_line, mass_matrix), mass_matrix) + np.kron(np.kron(mass_matrix, stiff_line), mass_matrix) + np.kron(np.kron(mass_matrix, mass_matrix), stiff_line)
    trace_ops = np.zeros((32, 6, 64))
    for dimension in range(3):
        others = [other_dim for other_dim in range(3) if other_dim != dimension]
        for lower_end in range(2):
            face_index = 2 * dimension + lower_end
            fixed_node = 0 if lower_end else 3
            orientation = -1.0 if lower_end else 1.0
            for first_node in range(4):
                for second_node in range(4):
                    face_node = first_node * 4 + second_node
                    for along_node in range(4):
                        position = [0, 0, 0]
                        position[others[0]] = first_node
                        position[others[1]] = second_node
                        position[dimension] = along_node
                        nodal = position[0] * 16 + position[1] * 4 + position[2]
                        if along_node == fixed_node:
                            trace_ops[face_node, face_index, nodal] = 1.0
                        trace_ops[16 + face_node, face_index, nodal] = orientation * derivative[fixed_node, along_node]
    interp = np.zeros((5, 16, 16))
    for quarter in range(4):
        interp[quarter] = np.kron(halves[quarter // 2], halves[quarter % 2])
    interp[4] = np.eye(16)
    face_weight = np.kron(weights, weights)
    return (stiffness, trace_ops.reshape(192, 64), interp.reshape(80, 16), np.transpose(interp, (0, 2, 1)).reshape(80, 16), face_weight)

def jnp_tables():
    return tuple((jnp.asarray(table_item, jnp.float32) for table_item in basis_tables()))

def element_scales(coefficient, refine_level):
    elem_size = jnp.power(jnp.float32(0.5), refine_level.astype(jnp.float32))
    return (elem_size, coefficient * elem_size, coefficient / elem_size)

def apply_case(values, side_case, stack):
    side_count = values.shape[1]
    paired = jnp.concatenate([values[:16], values[16:]], axis=1)
    quarters = jnp.dot(stack[:64], paired, precision=highest).reshape(4, 16, 2 * side_count)
    choose = (side_case[None, :] == jnp.arange(4, dtype=jnp.int32)[:, None]).astype(jnp.float32)
    choose = jnp.concatenate([choose, choose], axis=1)
    chosen = lax.optimization_barrier(jnp.sum(quarters * choose[:, None, :], axis=0))
    hanging = side_case < 4
    hanging = jnp.concatenate([hanging, hanging], axis=0)[None, :]
    mixed = jnp.where(hanging, chosen, paired)
    return jnp.concatenate([mixed[:, :side_count], mixed[:, side_count:]], axis=0)

def mortar_traces(values_field, coefficient, refine_level, side_elem, side_dir, side_case, tables):
    stiffness, trace_ops, interp, interp_t, face_weight = tables
    elem_count = values_field.shape[1]
    elem_size, volume_scale, normal_scale = element_scales(coefficient, refine_level)
    face_values = jnp.dot(trace_ops, values_field, precision=highest)
    face_values = jnp.concatenate([face_values[:96], face_values[96:] * normal_scale[None, :]], axis=0)
    face_values = face_values.reshape(32, 6 * elem_count)
    columns = side_dir * elem_count + side_elem
    picked = jnp.take(face_values, columns, axis=1)
    mortar = apply_case(picked, side_case, interp)
    side_size = jnp.take(elem_size, side_elem) * jnp.where(side_case < 4, jnp.float32(0.5), jnp.float32(1.0))
    side_scalars = jnp.stack([jnp.take(coefficient, side_elem), side_size])
    return (mortar, side_scalars)

def apply_operator_local(values_field, coefficient, refine_level, mortar, side_scalars, outer_values, outer_scalars, side_elem, side_dir, side_case, side_kind, tables):
    stiffness, trace_ops, interp, interp_t, face_weight = tables
    elem_count = values_field.shape[1]
    elem_size, volume_scale, normal_scale = element_scales(coefficient, refine_level)
    boundary = (side_kind == 1).astype(jnp.float32)[None, :]
    trace_jump = mortar[:16] - (1.0 - boundary) * outer_values[:16]
    average = 0.5 * (mortar[16:] - outer_values[16:]) + boundary * 0.5 * (mortar[16:] + outer_values[16:])
    mortar_size = jnp.minimum(side_scalars[1], outer_scalars[1])
    penalty = penalty_factor * (side_scalars[0] + outer_scalars[0]) / (2.0 * mortar_size)
    weighted = face_weight[:, None] * (mortar_size * mortar_size)[None, :]
    value_flux = weighted * (penalty[None, :] * trace_jump - average)
    slope_flux = -weighted * trace_jump * (0.5 + 0.5 * boundary)
    face_flux = apply_case(jnp.concatenate([value_flux, slope_flux], axis=0), side_case, interp_t)
    columns = side_dir * elem_count + side_elem
    gathered = jnp.zeros((32, 6 * elem_count), jnp.float32).at[:, columns].add(face_flux)
    gathered = gathered.reshape(192, elem_count)
    gathered = jnp.concatenate([gathered[:96], gathered[96:] * normal_scale[None, :]], axis=0)
    surface = jnp.dot(trace_ops.T, gathered, precision=highest)
    volume = jnp.dot(stiffness, values_field, precision=highest) * volume_scale[None, :]
    return volume + surface

def block_solve(inverse, residual):
    return lax.optimization_barrier(jnp.sum(inverse.astype(jnp.float32) * residual[None, :, :], axis=1))

def shift_devices(blocks, offset):
    zero_block = jnp.zeros_like(blocks[:abs(offset)])
    if offset > 0:
        return jnp.concatenate([zero_block, blocks[:-offset]], axis=0)
    return jnp.concatenate([blocks[-offset:], zero_block], axis=0)

def reference(rhs_field, initial_guess, start_vector, coefficient, refine_level, block_inverse, side_elem, side_dir, side_case, side_kind, partner, send_list):
    tables = jnp_tables()

    def split_devices(values_field):
        return values_field.reshape(64, N_DOM, ELEM_DEV).transpose(1, 0, 2)

    def join_devices(blocks):
        return blocks.transpose(1, 0, 2).reshape(64, N_DOM * ELEM_DEV)
    coef_dev = coefficient.reshape(N_DOM, ELEM_DEV)
    level_dev = refine_level.reshape(N_DOM, ELEM_DEV)
    elem_dev = side_elem.reshape(N_DOM, SIDE_DEV)
    dir_dev = side_dir.reshape(N_DOM, SIDE_DEV)
    case_dev = side_case.reshape(N_DOM, SIDE_DEV)
    kind_dev = side_kind.reshape(N_DOM, SIDE_DEV)
    partner_dev = partner.reshape(N_DOM, SIDE_DEV)
    send_dev = send_list.reshape(N_DOM, 8, SLOT)

    def take_columns(source, indices):
        return jnp.take(source, indices, axis=1)

    def operate(values_field):
        blocks = split_devices(values_field)
        mortar, side_scalars = jax.vmap(lambda field_block, coef_block, level_block, elem_block, dir_block, case_block: mortar_traces(field_block, coef_block, level_block, elem_block, dir_block, case_block, tables))(blocks, coef_dev, level_dev, elem_dev, dir_dev, case_dev)
        padded_values = jnp.concatenate([mortar, jnp.zeros((N_DOM, 32, 1), jnp.float32)], axis=2)
        padded_scalars = jnp.concatenate([side_scalars, jnp.zeros((N_DOM, 2, 1), jnp.float32)], axis=2)
        value_parts = [mortar]
        scalar_parts = [side_scalars]
        for peer_place in range(8):
            offset = peer_offsets[peer_place]
            sent_values = jax.vmap(take_columns)(padded_values, send_dev[:, peer_place])
            sent_scalars = jax.vmap(take_columns)(padded_scalars, send_dev[:, peer_place])
            value_parts.append(shift_devices(sent_values, offset))
            scalar_parts.append(shift_devices(sent_scalars, offset))
        table_values = jnp.concatenate(value_parts, axis=2)
        table_scalars = jnp.concatenate(scalar_parts, axis=2)
        outer_values = jax.vmap(take_columns)(table_values, partner_dev)
        outer_scalars = jax.vmap(take_columns)(table_scalars, partner_dev)
        result = jax.vmap(lambda field_block, coef_block, level_block, mortar_block, scalar_block, outer_block, outer_scalar_block, elem_block, dir_block, case_block, kind_block: apply_operator_local(field_block, coef_block, level_block, mortar_block, scalar_block, outer_block, outer_scalar_block, elem_block, dir_block, case_block, kind_block, tables))(blocks, coef_dev, level_dev, mortar, side_scalars, outer_values, outer_scalars, elem_dev, dir_dev, case_dev, kind_dev)
        return join_devices(result)

    def precondition(residual):

        def one_block(block_index):
            first_column = block_index * ELEM_DEV
            inverse_block = lax.dynamic_slice_in_dim(block_inverse, first_column, ELEM_DEV, 2)
            residual_block = lax.dynamic_slice_in_dim(residual, first_column, ELEM_DEV, 1)
            return block_solve(inverse_block, residual_block)
        return join_devices(lax.map(one_block, jnp.arange(N_DOM, dtype=jnp.int32)))
    previous = start_vector
    current = start_vector
    for iteration in range(POWER):
        previous = current
        current = precondition(operate(current))
    eigen_bound = jnp.sqrt(jnp.sum(current * current) / jnp.sum(previous * previous))
    upper_bound = 1.2 * eigen_bound
    lower_bound = upper_bound / 15.0
    center = 0.5 * (upper_bound + lower_bound)
    half_width = 0.5 * (upper_bound - lower_bound)
    spread_ratio = center / half_width
    damping = 1.0 / spread_ratio
    solution = initial_guess
    residual = precondition(rhs_field - operate(solution))
    update = residual / center
    for iteration in range(CHEB - 1):
        solution = solution + update
        residual = precondition(rhs_field - operate(solution))
        damping_next = 1.0 / (2.0 * spread_ratio - damping)
        update = damping_next * damping * update + 2.0 * damping_next / half_width * residual
        damping = damping_next
    solution = solution + update
    return (solution, eigen_bound)
```

```python
import functools
import math

import jax
import jax.numpy as jnp
import numpy as np
from jax import lax
from jax.experimental import pallas as pl
from jax.experimental.pallas import tpu as pltpu
from jax.sharding import PartitionSpec as P

f32 = jnp.float32
bf16 = jnp.bfloat16
i32 = jnp.int32
peer_offsets = (1, -1, 2, -2, 3, -3, 4, -4)
live_width = {1: 96, 2: 48, 3: 24, 4: 24}
lanes = 128
side_pad = 1024


def lagrange_tables():
    root_five = 1.0 / math.sqrt(5.0)
    nodes = np.array([0.0, 0.5 - 0.5 * root_five, 0.5 + 0.5 * root_five, 1.0])
    weights = np.array([1.0, 5.0, 5.0, 1.0]) / 12.0
    factor = np.array(
        [np.prod([nodes[i] - nodes[j] for j in range(4) if j != i]) for i in range(4)]
    )
    derivative = np.zeros((4, 4))
    for i in range(4):
        for j in range(4):
            if i != j:
                derivative[i, j] = factor[i] / (factor[j] * (nodes[i] - nodes[j]))
        derivative[i, i] = -np.sum(derivative[i])
    halves = []
    for half in range(2):
        points = 0.5 * (nodes + half)
        table = np.ones((4, 4))
        for j in range(4):
            for other in range(4):
                if other != j:
                    table[:, j] *= (points - nodes[other]) / (nodes[j] - nodes[other])
        halves.append(table)
    return weights, derivative, halves


def basis_tables():
    weights, derivative, halves = lagrange_tables()
    mass = np.diag(weights)
    line = derivative.T @ mass @ derivative
    stiffness = (
        np.kron(np.kron(line, mass), mass)
        + np.kron(np.kron(mass, line), mass)
        + np.kron(np.kron(mass, mass), line)
    )
    trace = np.zeros((6, 32, 64))
    for dim in range(3):
        others = [d for d in range(3) if d != dim]
        for lower in range(2):
            face = 2 * dim + lower
            fixed = 0 if lower else 3
            sign = -1.0 if lower else 1.0
            for first in range(4):
                for second in range(4):
                    node = first * 4 + second
                    for along in range(4):
                        place = [0, 0, 0]
                        place[others[0]] = first
                        place[others[1]] = second
                        place[dim] = along
                        nodal = place[0] * 16 + place[1] * 4 + place[2]
                        if along == fixed:
                            trace[face, node, nodal] = 1.0
                        trace[face, 16 + node, nodal] = sign * derivative[fixed, along]
    quarter = [np.kron(halves[q // 2], halves[q % 2]) for q in range(4)]
    both = np.eye(2)
    interp = np.concatenate([np.kron(both, q) for q in quarter], axis=0)
    interp_t = np.concatenate([np.kron(both, q.T) for q in quarter], axis=0)
    face_weight = np.kron(weights, weights)
    return stiffness, trace.reshape(192, 64), interp, interp_t, face_weight


def stacked(table):
    table = np.asarray(table, np.float32)
    high = table.astype(jnp.bfloat16)
    low = (table - high.astype(np.float32)).astype(jnp.bfloat16)
    return np.concatenate([high, high, low], axis=1)


def const_tables():
    stiffness, trace, interp, interp_t, face_weight = basis_tables()
    lift = np.concatenate([stacked(trace.T), stacked(stiffness)], axis=1)
    weight = np.broadcast_to(np.concatenate([face_weight, face_weight])[:, None], (32, lanes))
    return (
        stacked(trace),
        stacked(interp),
        stacked(interp_t),
        lift,
        np.asarray(weight, np.float32),
    )


def two(x):
    high = x.astype(bf16)
    return high, (x - high.astype(f32)).astype(bf16)


def three(x):
    high = x.astype(bf16)
    rest = x - high.astype(f32)
    mid = rest.astype(bf16)
    return high, mid, (rest - mid.astype(f32)).astype(bf16)


def dot(a, b):
    return jnp.dot(a, b, preferred_element_type=f32)


def dot_t(a, b):
    return lax.dot_general(a, b, (((1,), (1,)), ((), ())), preferred_element_type=f32)


def cat(parts, axis):
    return parts[0] if len(parts) == 1 else jnp.concatenate(parts, axis=axis)


def table_dot(table, x):
    high, low = two(x)
    return dot(table, jnp.concatenate([high, low, high], axis=0))


def apply_case(table, x, case):
    quarters = table_dot(table, x)
    out = x
    for c in range(4):
        out = jnp.where(case == c, quarters[32 * c : 32 * c + 32], out)
    return out


def fields_case(table, x, case, nf):
    wide = cat([x[32 * k : 32 * k + 32] for k in range(nf)], 1)
    out = apply_case(table, wide, cat([case] * nf, 1))
    n = x.shape[1]
    return cat([out[:, n * k : n * k + n] for k in range(nf)], 0)


def one_hot(index_row, rows, first=0):
    place = lax.broadcasted_iota(i32, (rows, index_row.shape[1]), 0) + first
    return jnp.where(place == index_row, 1.0, 0.0).astype(bf16)


def element_rows(coef_ref, level_ref):
    coef = coef_ref[...]
    level = level_ref[...]
    size = jnp.where(level == 0, 1.0, jnp.where(level == 1, 0.5, 0.25)).astype(f32)
    inverse = jnp.where(level == 0, 1.0, jnp.where(level == 1, 2.0, 4.0)).astype(f32)
    return coef, size, coef * size, coef * inverse


def face_stack(trace_ref, u, normal_scale, nf):
    faces = table_dot(trace_ref[...], cat(u, 1))
    row = lax.broadcasted_iota(i32, (32, lanes), 0)
    scale = jnp.where(row < 16, 1.0, jnp.broadcast_to(normal_scale, (32, lanes)))
    fields = []
    for k in range(nf):
        part = faces[:, lanes * k : lanes * k + lanes]
        fields.append(
            jnp.concatenate([part[32 * f : 32 * f + 32] * scale for f in range(6)], axis=1)
        )
    high, low = two(cat(fields, 0))
    return jnp.concatenate([high, low], axis=0)


def gather_message(stack, hot, interp, case, nf):
    got = dot(stack, hot)
    h = 32 * nf
    out = fields_case(interp, got[:h] + got[h : 2 * h], case, nf)
    if stack.shape[0] == 2 * h:
        return out
    coef = got[2 * h : 2 * h + 1] + got[2 * h + 1 : 2 * h + 2] + got[2 * h + 2 : 2 * h + 3]
    size = got[2 * h + 3 : 2 * h + 4] * jnp.where((case >= 0) & (case < 4), 0.5, 1.0)
    row = lax.broadcasted_iota(i32, (8, out.shape[1]), 0)
    scalars = jnp.where(row == 0, coef, jnp.where(row == 1, size, 0.0))
    return jnp.concatenate([out, scalars], axis=0)


def where_am_i(chips):
    me = lax.axis_index("dom")
    chip = me // 2
    core = me - 2 * chip
    quad = lax.rem(chip, 4)
    odd = lax.rem(chip, 2)
    v_step = jnp.where(quad < 2, -1, 1)
    v_there = (chip + 2 * v_step >= 0) & (chip + 2 * v_step < chips)
    return chip, core, odd, -v_step, v_step, v_there


def row_of(offset):
    size = jnp.abs(offset)
    return 2 * (size - 1) + jnp.where(offset < 0, 1, 0)


def narrow(offset):
    return jnp.abs(offset) == 3


def send_setup_kernel(
    chips, start_ref, guess_ref, coef_ref, level_ref, side_ref, list_ref, trace_ref, interp_ref,
    hot_ref, case_ref, stack_ref, u_ref, v_ref, rolled_ref, slot_ref,
):
    chip, core, odd, u_step, v_step, v_there = where_am_i(chips)
    listed = jnp.concatenate([list_ref[...], jnp.full((8, 32), -1, i32)], axis=1)
    for place, shift in enumerate((0, 24, 48, 96)):
        rolled_ref[8 * place : 8 * place + 8] = (
            pltpu.roll(listed, shift, 1) if shift else listed
        )
    lane = lax.broadcasted_iota(i32, (1, lanes), 1)
    none = jnp.full((1, lanes), -1, i32)

    def part(place, row, low, high, valid):
        values = rolled_ref[pl.ds(8 * place + row, 1), :]
        keep = (lane >= low) & (lane < high) & valid
        return jnp.where(keep, values, none)

    always = core >= 0
    for tile, (step, there, place) in enumerate(((u_step, always, 0), (v_step, v_there, 1))):
        onward = there & (((odd == 1) & (step == 1)) | ((odd == 0) & (step == -1)))
        cross = 2 * step + 1 - 2 * core
        wide = part(1, row_of(cross), 24, 120, onward & (~narrow(cross)))
        slim = part(3, row_of(cross), 96, 120, onward & narrow(cross))
        slot_ref[0:1, 256 * tile : 256 * tile + 128] = jnp.maximum(wide, slim)
        over = there & (step == 2 * core - 1)
        direct = part(place, row_of(4 * step), 24 * place, 24 * place + 24, there)
        second = part(2, row_of(2 * step), 48, 96, onward)
        third = part(3, row_of(3 * step), 96, 120, over)
        slot_ref[0:1, 256 * tile + 128 : 256 * tile + 256] = jnp.maximum(
            jnp.maximum(direct, second), third
        )
    near = jnp.where(odd == 1, -1, 1)
    cross = 2 * near + 1 - 2 * core
    slot_ref[0:1, 512:640] = part(0, row_of(1 - 2 * core), 0, 96, always)
    slot_ref[0:1, 640:768] = part(0, row_of(2 * near), 0, 48, always)
    slot_ref[0:1, 768:896] = jnp.maximum(
        part(0, row_of(cross), 0, 96, ~narrow(cross)), part(0, row_of(cross), 0, 24, narrow(cross))
    )

    elem, direction, case = side_ref[0:1], side_ref[1:2], side_ref[2:3]
    live = lax.broadcasted_iota(i32, (1, side_pad), 1) < 930
    rows = [jnp.where(live, r, 0).astype(f32) for r in (elem, direction, case)]
    rows.append(jnp.where(live, 1.0, 0.0))
    row = lax.broadcasted_iota(i32, (16, side_pad), 0)
    attributes = jnp.zeros((16, side_pad), f32)
    for k, r in enumerate(rows):
        attributes = jnp.where(row == k, r, attributes)
    found = dot(attributes.astype(bf16), one_hot(slot_ref[0:1, :], side_pad))
    valid = found[3:4] > 0.5
    column = jnp.where(valid, (found[1:2] * 128.0 + found[0:1]).astype(i32), -1)
    slot_case = jnp.where(valid, found[2:3].astype(i32), -1)
    case_ref[0:1, :] = slot_case
    for f in range(6):
        hot_ref[lanes * f : lanes * f + lanes] = one_hot(column, lanes, lanes * f)

    coef, size, volume_scale, normal_scale = element_rows(coef_ref, level_ref)
    stack = face_stack(trace_ref, [start_ref[...], guess_ref[...]], normal_scale, 2)
    high, mid, low = (jnp.broadcast_to(x.astype(f32), (16, lanes)) for x in three(coef))
    row = lax.broadcasted_iota(i32, (16, lanes), 0)
    scalars = jnp.where(
        row == 0,
        high,
        jnp.where(row == 1, mid, jnp.where(row == 2, low, jnp.where(row == 3, size, 0.0))),
    ).astype(bf16)
    stack = jnp.concatenate([stack, jnp.concatenate([scalars] * 6, axis=1)], axis=0)
    stack_ref[...] = stack
    sent = gather_message(stack, hot_ref[:, 0:512], interp_ref[...], slot_case[:, 0:512], 2)
    u_ref[...] = sent[:, 0:256]
    v_ref[...] = sent[:, 256:512]


def own_kernel(nf, stack_ref, hot_ref, case_ref, interp_ref, own_ref):
    own_ref[...] = gather_message(
        stack_ref[...], hot_ref[:, 512:896], interp_ref[...], case_ref[0:1, 512:896], nf
    )


def relay_kernel(own_ref, u_ref, v_ref, one_ref, two_ref, three_ref):
    lane = lax.broadcasted_iota(i32, (1, lanes), 1)
    passed = u_ref[:, 128:256] + v_ref[:, 128:256]
    one_ref[...] = own_ref[:, 0:128] + jnp.where(lane >= 96, passed, 0.0)
    two_ref[...] = own_ref[:, 128:256] + jnp.where((lane >= 48) & (lane < 96), passed, 0.0)
    three_ref[...] = own_ref[:, 256:384] + (u_ref[:, 0:128] + v_ref[:, 0:128])


def setup_kernel(
    chips, coef_ref, level_ref, side_ref,
    own_hot_ref, partner_hot_ref, arrival_hot_ref, target_hot_ref, info_ref, arrived_case_ref,
):
    chip, core, odd, u_step, v_step, v_there = where_am_i(chips)
    elem, direction, case = side_ref[0:1], side_ref[1:2], side_ref[2:3]
    kind, partner = side_ref[3:4], side_ref[4:5]
    live = lax.broadcasted_iota(i32, (1, side_pad), 1) < 930
    column = jnp.where(live, direction * lanes + elem, -1)
    for f in range(6):
        own_hot_ref[lanes * f : lanes * f + lanes] = one_hot(column, lanes, lanes * f)

    coef, size, volume_scale, normal_scale = element_rows(coef_ref, level_ref)
    row = lax.broadcasted_iota(i32, (16, lanes), 0)
    scalars = jnp.zeros((16, lanes), f32)
    for k, r in enumerate([x.astype(f32) for x in three(coef)] + [size]):
        scalars = jnp.where(row == k, r, scalars)
    mine = dot(scalars.astype(bf16), one_hot(jnp.where(live, elem, -1), lanes))
    hanging = (case >= 0) & (case < 4)
    own_coef = mine[0:1] + mine[1:2] + mine[2:3]
    own_size = mine[3:4] * jnp.where(hanging, 0.5, 1.0)

    rows = [jnp.where(live, r, 0).astype(f32) for r in (elem, direction, case)]
    rows.append(jnp.where(live, 1.0, 0.0))
    rows += [mine[0:1], mine[1:2], mine[2:3], own_size]
    row = lax.broadcasted_iota(i32, (16, side_pad), 0)
    attributes = jnp.zeros((16, side_pad), f32)
    for k, r in enumerate(rows):
        attributes = jnp.where(row == k, r, attributes)
    attributes = attributes.astype(bf16)
    other = dot(attributes, one_hot(partner, side_pad))
    valid = other[3:4] > 0.5
    other_column = jnp.where(valid, (other[1:2] * 128.0 + other[0:1]).astype(i32), -1)
    for f in range(6):
        partner_hot_ref[lanes * f : lanes * f + lanes] = one_hot(other_column, lanes, lanes * f)
    boundary = jnp.where(kind == 1, 1.0, 0.0)
    info = [
        own_coef, own_size, other[4:5] + other[5:6] + other[6:7], other[7:8],
        case.astype(f32), other[2:3], boundary, boundary,
    ]
    row = lax.broadcasted_iota(i32, (8, side_pad), 0)
    table = jnp.zeros((8, side_pad), f32)
    for k, r in enumerate(info):
        table = jnp.where(row == k, r, table)
    info_ref[...] = table

    sought = jnp.where(live & (kind == 0), partner, -7)
    place = lax.broadcasted_iota(i32, (lanes, side_pad), 0)
    near = jnp.where(odd == 1, 1, -1)
    back = 1 - 2 * core
    own_cross = 2 * near - back
    far_cross = -2 * near - back
    split = jnp.where(narrow(own_cross), 24, 96)
    segments = (
        ((0, 96, row_of(-back)), (96, 120, row_of(3 * back))),
        ((0, 48, row_of(2 * near)), (48, 96, row_of(-2 * near))),
        ((0, split, row_of(own_cross)), (split, 120, row_of(far_cross))),
        ((0, 24, row_of(-4 * u_step)), (24, 48, row_of(-4 * v_step))),
    )
    for tile, parts in enumerate(segments):
        slot = jnp.full((lanes, side_pad), -5, i32)
        for low, high, peer in parts:
            slot = jnp.where((place >= low) & (place < high), 930 + 96 * peer + place - low, slot)
        arrival_hot_ref[lanes * tile : lanes * tile + lanes] = jnp.where(
            slot == sought, 1.0, 0.0
        ).astype(bf16)
    target = dot_t(attributes, arrival_hot_ref[...])
    valid = target[3:4] > 0.5
    target_column = jnp.where(valid, (target[1:2] * 128.0 + target[0:1]).astype(i32), -1)
    arrived_case_ref[0:1, :] = jnp.where(valid, target[2:3].astype(i32), -1)
    for f in range(6):
        target_hot_ref[lanes * f : lanes * f + lanes] = one_hot(target_column, lanes, lanes * f)


def sides_kernel(nf, stack_ref, own_hot_ref, partner_hot_ref, info_ref, interp_ref, own_ref, other_ref):
    h = 32 * nf
    stack = stack_ref[0 : 2 * h]
    table = interp_ref[...]
    got = dot(stack, own_hot_ref[...])
    own_ref[...] = fields_case(table, got[:h] + got[h:], info_ref[4:5].astype(i32), nf)
    got = dot(stack, partner_hot_ref[...])
    other_ref[...] = fields_case(table, got[:h] + got[h:], info_ref[5:6].astype(i32), nf)


def coef_kernel(one_ref, two_ref, three_ref, u_ref, v_ref, info_ref, arrival_hot_ref, side_coef_ref, arrived_coef_ref):
    scalars = jnp.concatenate(
        [one_ref[64:72], two_ref[64:72], three_ref[64:72], u_ref[64:72, 128:256] + v_ref[64:72, 128:256]],
        axis=1,
    )
    row = lax.broadcasted_iota(i32, (16, 512), 0)
    rows = jnp.zeros((16, 512), f32)
    for k, r in enumerate([x.astype(f32) for x in three(scalars[0:1])] + [scalars[1:2]]):
        rows = jnp.where(row == k, r, rows)
    hot = arrival_hot_ref[...]
    far = dot(rows.astype(bf16), hot)
    other_coef = info_ref[2:3] + far[0:1] + far[1:2] + far[2:3]
    other_size = info_ref[3:4] + far[3:4]
    edge = info_ref[6:7]
    least = jnp.minimum(info_ref[1:2], other_size)
    jump = 16.0 * (info_ref[0:1] + other_coef) * least
    area = least * least
    coefs = [jump, jump * (1.0 - edge), area * (0.5 + 0.5 * edge), area * (0.5 - 0.5 * edge)]
    row = lax.broadcasted_iota(i32, (8, side_pad), 0)
    table = jnp.zeros((8, side_pad), f32)
    for k, r in enumerate(coefs):
        table = jnp.where(row == k, r, table)
    side_coef_ref[...] = table
    row = lax.broadcasted_iota(i32, (16, side_pad), 0)
    rows = jnp.zeros((16, side_pad), f32)
    for k, r in enumerate([x.astype(f32) for x in three(coefs[1]) + three(coefs[3])]):
        rows = jnp.where(row == k, r, rows)
    got = dot_t(rows.astype(bf16), hot)
    row = lax.broadcasted_iota(i32, (8, 512), 0)
    arrived_coef_ref[...] = jnp.where(
        row == 0,
        got[0:1] + got[1:2] + got[2:3],
        jnp.where(row == 1, got[3:4] + got[4:5] + got[5:6], 0.0),
    )


def scatter(x, hot, nf):
    high, low = two(x)
    got = dot_t(jnp.concatenate([high, low], axis=0), hot)
    return got[: 32 * nf] + got[32 * nf :]


def flux_kernel(nf, own_ref, other_ref, coef_ref, info_ref, weight_ref, interp_ref, own_hot_ref, sum_ref):
    jump, jump_out, area, area_out = (coef_ref[k : k + 1] for k in range(4))
    weight = weight_ref[0:16, 0:1]
    flux = []
    for k in range(nf):
        value, slope = own_ref[32 * k : 32 * k + 16], own_ref[32 * k + 16 : 32 * k + 32]
        outer, outer_slope = other_ref[32 * k : 32 * k + 16], other_ref[32 * k + 16 : 32 * k + 32]
        flux.append(
            weight * (jump * value - jump_out * outer - area * slope + area_out * outer_slope)
        )
        flux.append(weight * (area_out * outer - area * value))
    flux = fields_case(interp_ref[...], jnp.concatenate(flux, axis=0), info_ref[4:5].astype(i32), nf)
    sum_ref[...] = scatter(flux, own_hot_ref[...], nf)


def halo_flux(nf, arrivals, coef_ref, case_ref, weight_ref, interp_ref, hot_ref):
    one_ref, two_ref, three_ref, u_ref, v_ref = arrivals
    h = 32 * nf
    got = jnp.concatenate(
        [one_ref[0:h], two_ref[0:h], three_ref[0:h], u_ref[0:h, 128:256] + v_ref[0:h, 128:256]], axis=1
    )
    jump, area = coef_ref[0:1], coef_ref[1:2]
    weight = weight_ref[0:16, 0:1]
    flux = []
    for k in range(nf):
        outer, outer_slope = got[32 * k : 32 * k + 16], got[32 * k + 16 : 32 * k + 32]
        flux.append(weight * (area * outer_slope - jump * outer))
        flux.append(weight * (area * outer))
    flux = fields_case(interp_ref[...], jnp.concatenate(flux, axis=0), case_ref[0:1], nf)
    return scatter(flux, hot_ref[...], nf)


def solve_blocks(inverse_ref, hold_ref, nf):
    sums = [jnp.zeros((64, lanes), f32) for _ in range(nf)]
    for col in range(64):
        block = inverse_ref[col].astype(f32)
        for k in range(nf):
            sums[k] = sums[k] + block * hold_ref[64 * k + col : 64 * k + col + 1, :]
    return sums


def update_kernel(
    nf, nf_next, residual,
    one_ref, two_ref, three_ref, u_in_ref, v_in_ref, local_ref, arrived_coef_ref, arrived_case_ref,
    target_hot_ref, weight_ref, interp_t_ref, lift_ref, field_ref, coef_ref, level_ref, inverse_ref,
    *rest,
):
    if residual:
        rhs_ref, *rest = rest
    if nf_next:
        trace_ref, interp_ref, hot_ref, case_ref, new_ref, stack_ref, u_ref, v_ref, hold_ref = rest
    else:
        new_ref, part_ref, hold_ref = rest
    arrivals = (one_ref, two_ref, three_ref, u_in_ref, v_in_ref)
    total = local_ref[...] + halo_flux(
        nf, arrivals, arrived_coef_ref, arrived_case_ref, weight_ref, interp_t_ref, target_hot_ref
    )
    coef, size, volume_scale, normal_scale = element_rows(coef_ref, level_ref)
    row = lax.broadcasted_iota(i32, (32, lanes), 0)
    scale = jnp.where(row < 16, 1.0, jnp.broadcast_to(normal_scale, (32, lanes)))
    operands = []
    for k in range(nf):
        mine = total[32 * k : 32 * k + 32]
        faces = jnp.concatenate(
            [mine[:, lanes * f : lanes * f + lanes] * scale for f in range(6)], axis=0
        )
        high, low = two(faces)
        field_high, field_low = two(field_ref[64 * k : 64 * k + 64] * volume_scale)
        operands.append(
            jnp.concatenate([high, low, high, field_high, field_low, field_high], axis=0)
        )
    image = dot(lift_ref[...], cat(operands, 1))
    for k in range(nf):
        part = image[:, lanes * k : lanes * k + lanes]
        if residual and k == 1:
            part = rhs_ref[...] - part
        hold_ref[64 * k : 64 * k + 64, :] = part
    new = solve_blocks(inverse_ref, hold_ref, nf)
    for k in range(nf):
        new_ref[64 * k : 64 * k + 64, :] = new[k]
    if nf_next:
        stack = face_stack(trace_ref, new[:nf_next], normal_scale, nf_next)
        stack_ref[...] = stack
        sent = gather_message(stack, hot_ref[:, 0:512], interp_ref[...], case_ref[0:1, 0:512], nf_next)
        u_ref[...] = sent[:, 0:256]
        v_ref[...] = sent[:, 256:512]
    else:
        before, after = field_ref[...], new[0]
        before = jnp.sum(jnp.sum(before * before, axis=1, keepdims=True), axis=0, keepdims=True)
        after = jnp.sum(jnp.sum(after * after, axis=1, keepdims=True), axis=0, keepdims=True)
        lane = lax.broadcasted_iota(i32, part_ref.shape, 1)
        part_ref[...] = jnp.where(lane == 0, before, jnp.where(lane == 1, after, 0.0))


def finish_kernel(part_ref, guess_ref, first_ref, second_ref, out_ref, bound_ref):
    total = jnp.sum(part_ref[...], axis=0, keepdims=True)
    bound = jnp.sqrt(total[:, 1:2] / total[:, 0:1])
    upper = 1.2 * bound
    lower = upper / 15.0
    center = 0.5 * (upper + lower)
    half = 0.5 * (upper - lower)
    ratio = center / half
    damping = 1.0 / ratio
    damping_next = 1.0 / (2.0 * ratio - damping)
    first = first_ref[64:128] / center
    second = first_ref[64:128] - second_ref[64:128] / center
    out_ref[...] = (
        guess_ref[...] + first + (damping_next * damping * first + 2.0 * damping_next / half * second)
    )
    bound_ref[...] = jnp.broadcast_to(bound, (1, lanes))


def in_vmem(x):
    return pltpu.with_memory_space_constraint(x, pltpu.VMEM)


def run(body, outs, ins, name, scratch=(), flops=1 << 24):
    spec = pl.BlockSpec(memory_space=pltpu.VMEM)
    return pl.pallas_call(
        body,
        out_shape=[pltpu.VMEM(shape, dtype) for shape, dtype in outs],
        in_specs=[spec] * len(ins),
        out_specs=[spec] * len(outs),
        scratch_shapes=list(scratch),
        compiler_params=pltpu.CompilerParams(vmem_limit_bytes=24 << 20),
        cost_estimate=pl.CostEstimate(flops=flops, bytes_accessed=1 << 20, transcendentals=0),
        name=name,
    )(*(in_vmem(x) for x in ins))


def local(
    rhs_field, initial_guess, start_vector, coefficient, refine_level, block_inverse,
    side_elem, side_dir, side_case, side_kind, partner, send_list,
):
    devices = lax.axis_size("dom")
    chips = devices // 2
    trace, interp, interp_t, lift, weight = (jnp.asarray(t) for t in const_tables())
    sides = jnp.stack([side_elem, side_dir, side_case, side_kind, partner])
    sides = jnp.pad(sides, ((0, 3), (0, side_pad - sides.shape[1])), constant_values=-1)
    coef = coefficient.reshape(1, lanes)
    level = refine_level.reshape(1, lanes)

    def swap(x, mask):
        return lax.ppermute(x, "dom", [(i, i ^ mask) for i in range(devices)])

    def swap_far(x):
        to = {}
        for c in range(chips):
            other = c + 2 if c % 4 >= 2 else c - 2
            to[c] = other if 0 <= other < chips else c ^ 1
        return lax.ppermute(
            x, "dom", [(2 * c + k, 2 * to[c] + k) for c in range(chips) for k in range(2)]
        )

    def exchange(u_out, v_out, stack, nf):
        rows = u_out.shape[0]
        u_in, v_in = swap(u_out, 4), swap_far(v_out)
        (own,) = run(
            functools.partial(own_kernel, nf), [((rows, 384), f32)], [stack, hot, case, interp], "own"
        )
        one, two_, three_ = run(
            relay_kernel, [((rows, lanes), f32)] * 3, [own, u_in, v_in], "relay"
        )
        return swap(one, 1), swap(two_, 2), swap(three_, 3), u_in, v_in

    hot, case, stack, u_out, v_out = run(
        functools.partial(send_setup_kernel, chips),
        [((768, 896), bf16), ((8, 896), i32), ((144, 768), bf16), ((72, 256), f32), ((72, 256), f32)],
        [start_vector, initial_guess, coef, level, sides, send_list, trace, interp],
        "send_setup",
        scratch=[pltpu.VMEM((32, lanes), i32), pltpu.VMEM((8, 896), i32)],
    )
    own_hot, partner_hot, arrival_hot, target_hot, info, arrived_case = run(
        functools.partial(setup_kernel, chips),
        [((768, side_pad), bf16), ((768, side_pad), bf16), ((512, side_pad), bf16), ((768, 512), bf16),
         ((8, side_pad), f32), ((8, 512), i32)],
        [coef, level, sides],
        "setup",
    )
    fields = jnp.concatenate([start_vector, initial_guess], axis=0)
    history = []
    side_coef = None
    for turn, nf in enumerate((2, 2, 1, 1)):
        arrivals = exchange(u_out, v_out, stack, nf)
        own_sides, other_sides = run(
            functools.partial(sides_kernel, nf),
            [((32 * nf, side_pad), f32)] * 2,
            [stack, own_hot, partner_hot, info, interp],
            "sides",
        )
        if turn == 0:
            side_coef, arrived_coef = run(
                coef_kernel,
                [((8, side_pad), f32), ((8, 512), f32)],
                [*arrivals, info, arrival_hot],
                "coef",
            )
        (sums,) = run(
            functools.partial(flux_kernel, nf),
            [((32 * nf, 768), f32)],
            [own_sides, other_sides, side_coef, info, weight, interp_t, own_hot],
            "flux",
        )
        ins = [
            *arrivals, sums, arrived_coef, arrived_case, target_hot, weight, interp_t, lift,
            fields, coef, level, block_inverse,
        ]
        if turn == 0:
            ins.append(rhs_field)
        nf_next = (2, 1, 1, 0)[turn]
        outs = [((64 * nf, lanes), f32)]
        if nf_next:
            ins += [trace, interp, hot, case]
            outs += [((64 * nf_next, 768), bf16)] + [((32 * nf_next, 256), f32)] * 2
        else:
            outs += [((devices, lanes), f32)]
        made = run(
            functools.partial(update_kernel, nf, nf_next, turn == 0),
            outs, ins, "update",
            scratch=[pltpu.VMEM((64 * nf, lanes), f32)],
        )
        if nf_next:
            fields, stack, u_out, v_out = made
            history.append(fields)
            if nf_next < nf:
                fields = fields[:64]
        else:
            fields, parts = made
    parts = lax.all_to_all(parts.reshape(devices, 1, lanes), "dom", 0, 0).reshape(devices, lanes)
    smoothed, bound = run(
        finish_kernel,
        [((64, lanes), f32), ((1, lanes), f32)],
        [parts, initial_guess, history[0], history[1]],
        "finish",
    )
    return smoothed, bound[0, 0]


def solution(mesh):
    placed = (
        P(None, "dom"), P(None, "dom"), P(None, "dom"), P("dom"), P("dom"), P(None, None, "dom"),
        P("dom"), P("dom"), P("dom"), P("dom"), P("dom"), P("dom", None),
    )
    return jax.shard_map(
        local, mesh=mesh, in_specs=placed, out_specs=(P(None, "dom"), P()), check_vma=False
    )
```

```python
import functools
import math

import jax
import jax.numpy as jnp
import numpy as np
from jax import lax
from jax.experimental import pallas as pl
from jax.experimental.pallas import tpu as pltpu
from jax.sharding import PartitionSpec as P

f32 = jnp.float32
bf16 = jnp.bfloat16
i32 = jnp.int32
peer_offsets = (1, -1, 2, -2, 3, -3, 4, -4)
live_width = {1: 96, 2: 48, 3: 24, 4: 24}
lanes = 128
side_pad = 1024


def lagrange_tables():
    root_five = 1.0 / math.sqrt(5.0)
    nodes = np.array([0.0, 0.5 - 0.5 * root_five, 0.5 + 0.5 * root_five, 1.0])
    weights = np.array([1.0, 5.0, 5.0, 1.0]) / 12.0
    factor = np.array(
        [np.prod([nodes[i] - nodes[j] for j in range(4) if j != i]) for i in range(4)]
    )
    derivative = np.zeros((4, 4))
    for i in range(4):
        for j in range(4):
            if i != j:
                derivative[i, j] = factor[i] / (factor[j] * (nodes[i] - nodes[j]))
        derivative[i, i] = -np.sum(derivative[i])
    halves = []
    for half in range(2):
        points = 0.5 * (nodes + half)
        table = np.ones((4, 4))
        for j in range(4):
            for other in range(4):
                if other != j:
                    table[:, j] *= (points - nodes[other]) / (nodes[j] - nodes[other])
        halves.append(table)
    return weights, derivative, halves


def basis_tables():
    weights, derivative, halves = lagrange_tables()
    mass = np.diag(weights)
    line = derivative.T @ mass @ derivative
    stiffness = (
        np.kron(np.kron(line, mass), mass)
        + np.kron(np.kron(mass, line), mass)
        + np.kron(np.kron(mass, mass), line)
    )
    trace = np.zeros((6, 32, 64))
    for dim in range(3):
        others = [d for d in range(3) if d != dim]
        for lower in range(2):
            face = 2 * dim + lower
            fixed = 0 if lower else 3
            sign = -1.0 if lower else 1.0
            for first in range(4):
                for second in range(4):
                    node = first * 4 + second
                    for along in range(4):
                        place = [0, 0, 0]
                        place[others[0]] = first
                        place[others[1]] = second
                        place[dim] = along
                        nodal = place[0] * 16 + place[1] * 4 + place[2]
                        if along == fixed:
                            trace[face, node, nodal] = 1.0
                        trace[face, 16 + node, nodal] = sign * derivative[fixed, along]
    quarter = [np.kron(halves[q // 2], halves[q % 2]) for q in range(4)]
    both = np.eye(2)
    interp = np.concatenate([np.kron(both, q) for q in quarter], axis=0)
    interp_t = np.concatenate([np.kron(both, q.T) for q in quarter], axis=0)
    face_weight = np.kron(weights, weights)
    return stiffness, trace.reshape(192, 64), interp, interp_t, face_weight


def stacked(table):
    table = np.asarray(table, np.float32)
    high = table.astype(jnp.bfloat16)
    low = (table - high.astype(np.float32)).astype(jnp.bfloat16)
    return np.concatenate([high, high, low], axis=1)


def const_tables():
    stiffness, trace, interp, interp_t, face_weight = basis_tables()
    lift = np.concatenate([stacked(trace.T), stacked(stiffness)], axis=1)
    weight = np.broadcast_to(np.concatenate([face_weight, face_weight])[:, None], (32, lanes))
    return (
        stacked(trace),
        stacked(interp),
        stacked(interp_t),
        lift,
        np.asarray(weight, np.float32),
    )


def two(x):
    high = x.astype(bf16)
    return high, (x - high.astype(f32)).astype(bf16)


def three(x):
    high = x.astype(bf16)
    rest = x - high.astype(f32)
    mid = rest.astype(bf16)
    return high, mid, (rest - mid.astype(f32)).astype(bf16)


def dot(a, b):
    return jnp.dot(a, b, preferred_element_type=f32)


def dot_t(a, b):
    return lax.dot_general(a, b, (((1,), (1,)), ((), ())), preferred_element_type=f32)


def cat(parts, axis):
    return parts[0] if len(parts) == 1 else jnp.concatenate(parts, axis=axis)


def table_dot(table, x):
    high, low = two(x)
    return dot(table, jnp.concatenate([high, low, high], axis=0))


def apply_case(table, x, case):
    quarters = table_dot(table, x)
    out = x
    for c in range(4):
        out = jnp.where(case == c, quarters[32 * c : 32 * c + 32], out)
    return out


def fields_case(table, x, case, nf):
    wide = cat([x[32 * k : 32 * k + 32] for k in range(nf)], 1)
    out = apply_case(table, wide, cat([case] * nf, 1))
    n = x.shape[1]
    return cat([out[:, n * k : n * k + n] for k in range(nf)], 0)


def rows_of(rows, count, width):
    place = lax.broadcasted_iota(i32, (count, width), 0)
    table = jnp.zeros((count, width), f32)
    for k, r in enumerate(rows):
        table = jnp.where(place == k, r, table)
    return table


def one_hot(index_row, rows, first=0):
    place = lax.broadcasted_iota(i32, (rows, index_row.shape[1]), 0) + first
    return jnp.where(place == index_row, 1.0, 0.0).astype(bf16)


def element_rows(coef_ref, level_ref):
    coef = coef_ref[...]
    level = level_ref[...]
    size = jnp.where(level == 0, 1.0, jnp.where(level == 1, 0.5, 0.25)).astype(f32)
    inverse = jnp.where(level == 0, 1.0, jnp.where(level == 1, 2.0, 4.0)).astype(f32)
    return coef, size, coef * size, coef * inverse


def face_stack(trace_ref, u, normal_scale, nf):
    faces = table_dot(trace_ref[...], cat(u, 1))
    row = lax.broadcasted_iota(i32, (32, lanes), 0)
    scale = jnp.where(row < 16, 1.0, jnp.broadcast_to(normal_scale, (32, lanes)))
    fields = []
    for k in range(nf):
        part = faces[:, lanes * k : lanes * k + lanes]
        fields.append(
            jnp.concatenate([part[32 * f : 32 * f + 32] * scale for f in range(6)], axis=1)
        )
    high, low = two(cat(fields, 0))
    return jnp.concatenate([high, low], axis=0)


def gather_message(stack, hot, interp, case, nf):
    got = dot(stack, hot)
    h = 32 * nf
    out = fields_case(interp, got[:h] + got[h : 2 * h], case, nf)
    if stack.shape[0] == 2 * h:
        return out
    coef = got[2 * h : 2 * h + 1] + got[2 * h + 1 : 2 * h + 2] + got[2 * h + 2 : 2 * h + 3]
    size = got[2 * h + 3 : 2 * h + 4] * jnp.where((case >= 0) & (case < 4), 0.5, 1.0)
    row = lax.broadcasted_iota(i32, (8, out.shape[1]), 0)
    scalars = jnp.where(row == 0, coef, jnp.where(row == 1, size, 0.0))
    return jnp.concatenate([out, scalars], axis=0)


def where_am_i(chips):
    me = lax.axis_index("dom")
    chip = me // 2
    core = me - 2 * chip
    near = jnp.where(lax.rem(chip, 2) == 1, -1, 1)
    u_step = jnp.where(lax.rem(chip, 4) < 2, 2, -2)
    w_there = (chip - near >= 0) & (chip - near < chips)
    v_there = (chip - u_step >= 0) & (chip - u_step < chips)
    return core, near, u_step, w_there, v_there


def mixed_lanes():
    lane = lax.broadcasted_iota(i32, (1, lanes), 1)
    u_lanes = (lane < 24) | ((lane >= 48) & (lane < 72))
    v_lanes = ((lane >= 24) & (lane < 48)) | ((lane >= 72) & (lane < 96))
    return lane, u_lanes, v_lanes


def fill_messages(sent, nf, w_ref, v_ref, u_ref, x_ref):
    lane, u_lanes, v_lanes = mixed_lanes()
    h = 32 * nf
    x_ref[0:h] = sent[0:h, 0:128]
    w_ref[0:h] = sent[0:h, 128:256]
    for k in range(nf):
        mixed = sent[32 * k : 32 * k + 32, 256:384]
        top, bottom = mixed[0:16], mixed[16:32]
        u_ref[16 * k : 16 * k + 16] = jnp.where(u_lanes, top, pltpu.roll(bottom, 24, 1))
        v_ref[16 * k : 16 * k + 16] = jnp.where(v_lanes, top, pltpu.roll(bottom, 104, 1))
        extra = mixed[0:8]
        for g in range(1, 4):
            moved = pltpu.roll(mixed[8 * g : 8 * g + 8], 128 - 32 * g, 1)
            extra = jnp.where((lane >= 96 - 32 * g) & (lane < 128 - 32 * g), moved, extra)
        x_ref[h + 8 * k : h + 8 * k + 8] = extra
        w_ref[h + 8 * k : h + 8 * k + 8] = extra
    if sent.shape[0] > h:
        third = [sent[h : h + 1, 256:384], sent[h + 1 : h + 2, 256:384]]
        for ref, low in ((x_ref, 0), (w_ref, 128)):
            main = [sent[h : h + 1, low : low + 128], sent[h + 1 : h + 2, low : low + 128]]
            ref[40 * nf : 40 * nf + 8] = rows_of(main + third, 8, lanes)
        for ref in (u_ref, v_ref):
            ref[16 * nf : 16 * nf + 8] = rows_of(third + third, 8, lanes)


def received(nf, w_ref, v_ref, u_ref, x_ref):
    lane, u_lanes, v_lanes = mixed_lanes()
    h = 32 * nf
    mixed = []
    for k in range(nf):
        u, v = u_ref[16 * k : 16 * k + 16], v_ref[16 * k : 16 * k + 16]
        x, w = x_ref[h + 8 * k : h + 8 * k + 8], w_ref[h + 8 * k : h + 8 * k + 8]
        far = jnp.concatenate(
            [jnp.where(u_lanes, u, v), jnp.where(u_lanes, pltpu.roll(u, 104, 1), pltpu.roll(v, 24, 1))],
            axis=0,
        )
        extra = jnp.where(lane < 112, x, w)
        rolled = [extra]
        for g in range(1, 4):
            rolled.append(
                jnp.where(lane < 112, pltpu.roll(x, 32 * g, 1), pltpu.roll(w, 32 * g, 1))
            )
        mixed.append(jnp.where(lane < 96, far, jnp.concatenate(rolled, axis=0)))
    main, after = x_ref[0:h], w_ref[0:h]
    if x_ref.shape[0] > 40 * nf:
        low = 40 * nf
        third = []
        for row in (2, 3):
            far = jnp.where(
                u_lanes, u_ref[16 * nf + row : 16 * nf + row + 1], v_ref[16 * nf + row : 16 * nf + row + 1]
            )
            extra = jnp.where(
                lane < 112, x_ref[low + row : low + row + 1], w_ref[low + row : low + row + 1]
            )
            third.append(jnp.where(lane < 96, far, extra))
        mixed.append(rows_of(third, 8, lanes))
        main = jnp.concatenate([main, x_ref[low : low + 8]], axis=0)
        after = jnp.concatenate([after, w_ref[low : low + 8]], axis=0)
    return main, after, cat(mixed, 0)


def row_of(offset):
    size = jnp.abs(offset)
    return 2 * (size - 1) + jnp.where(offset < 0, 1, 0)


def narrow(offset):
    return jnp.abs(offset) == 3


def slot_attributes(side_ref, slots):
    live = lax.broadcasted_iota(i32, (1, side_pad), 1) < 930
    rows = [jnp.where(live, side_ref[k : k + 1], 0).astype(f32) for k in range(3)]
    rows.append(jnp.where(live, 1.0, 0.0))
    found = dot(rows_of(rows, 16, side_pad).astype(bf16), one_hot(slots, side_pad))
    valid = found[3:4] > 0.5
    column = jnp.where(valid, (found[1:2] * 128.0 + found[0:1]).astype(i32), -1)
    return column, jnp.where(valid, found[2:3].astype(i32), -1)


def fill_one_hot(hot_ref, column):
    for f in range(6):
        hot_ref[lanes * f : lanes * f + lanes] = one_hot(column, lanes, lanes * f)


def listed_part(rolled_ref, place, offset, low, high, valid):
    lane = lax.broadcasted_iota(i32, (1, lanes), 1)
    values = rolled_ref[pl.ds(8 * place + jnp.minimum(row_of(offset), 7), 1), :]
    return jnp.where((lane >= low) & (lane < high) & valid, values, -1)


def send_setup_kernel(chips, *refs):
    sources, refs = refs[:12], refs[12:]
    hot_ref, case_ref, stack_ref, side_ref, rolled_ref = refs[:5]
    messages, landed = refs[5:9], (*refs[14:22], *refs[9:13])
    slot_ref, arrived = refs[13], refs[22]
    copies = [
        pltpu.make_async_copy(source, target, arrived.at[k])
        for k, (source, target) in enumerate(zip(sources, landed))
    ]
    for copy in copies:
        copy.start()
    elem_ref, dir_ref, sidecase_ref, kind_ref, partner_ref, list_ref = landed[:6]
    start_ref, guess_ref, coef_ref, level_ref, trace_ref, interp_ref = landed[6:]
    for copy in copies:
        copy.wait()
    side_ref[...] = jnp.full((8, side_pad), -1, i32)
    sides = elem_ref.shape[1]
    for k, ref in enumerate((elem_ref, dir_ref, sidecase_ref, kind_ref, partner_ref)):
        side_ref[k : k + 1, 0:sides] = ref[...]
    core, near, u_step, w_there, v_there = where_am_i(chips)
    listed = jnp.concatenate([list_ref[...], jnp.full((8, 32), -1, i32)], axis=1)
    shifts = (0, 24, 48, 72, 96, 64, 80)
    for place, shift in enumerate(shifts):
        rolled_ref[8 * place : 8 * place + 8] = (
            pltpu.roll(listed, shift, 1) if shift else listed
        )

    def part(shift, offset, low, high, valid):
        return listed_part(rolled_ref, shifts.index(shift), offset, low, high, valid)

    always = core >= 0
    flip = 1 - 2 * core
    mixed = []
    for tile, (step, there, extra) in enumerate(((near, always, 64), (-near, w_there, 80))):
        cross = 2 * step + flip
        direct = part(0, cross, 0, jnp.where(narrow(cross), 24, 96), there)
        passed = part(96, 2 * step, 96, 128, there)
        slot_ref[0:1, 128 * tile : 128 * tile + 128] = jnp.maximum(direct, passed)
        mixed.append(part(extra, 2 * step, extra + 32, extra + 48, there))
    for step, there, low in ((u_step, always, 0), (-u_step, v_there, 24)):
        cross = 2 * step + flip
        mixed.append(part(low, cross, low, low + 24, there & narrow(cross)))
        mixed.append(part(low + 48, 2 * step, low + 48, low + 72, there))
    slot_ref[0:1, 256:384] = functools.reduce(jnp.maximum, mixed)
    column, slot_case = slot_attributes(side_ref, slot_ref[0:1, :])
    case_ref[0:1, :] = slot_case
    fill_one_hot(hot_ref, column)

    coef, size, volume_scale, normal_scale = element_rows(coef_ref, level_ref)
    stack = face_stack(trace_ref, [start_ref[...], guess_ref[...]], normal_scale, 2)
    scalars = rows_of([x.astype(f32) for x in three(coef)] + [size], 16, lanes).astype(bf16)
    stack = jnp.concatenate([stack, jnp.concatenate([scalars] * 6, axis=1)], axis=0)
    stack_ref[...] = stack
    sent = gather_message(stack, hot_ref[...], interp_ref[...], slot_case, 2)
    fill_messages(sent, 2, *messages)


def own_setup_kernel(chips, side_ref, rolled_ref, hot_ref, case_ref):
    core = where_am_i(chips)[0]
    slots = listed_part(rolled_ref, 0, 1 - 2 * core, 0, 96, core >= 0)
    column, slot_case = slot_attributes(side_ref, slots)
    case_ref[0:1, :] = slot_case
    fill_one_hot(hot_ref, column)


def own_kernel(nf, stack_ref, hot_ref, case_ref, interp_ref, own_ref):
    own_ref[...] = gather_message(
        stack_ref[...], hot_ref[...], interp_ref[...], case_ref[0:1], nf
    )


def own_sides_kernel(
    nf, stack_ref, hot_ref, case_ref, interp_ref, own_hot_ref, partner_hot_ref, far_hot_ref, info_ref,
    arrival_ref, own_ref, mine_ref, other_ref, target_ref,
):
    own_kernel(nf, stack_ref, hot_ref, case_ref, interp_ref, own_ref)
    sides_kernel(
        nf, stack_ref, interp_ref, own_hot_ref, partner_hot_ref, far_hot_ref, info_ref, arrival_ref,
        mine_ref, other_ref, target_ref,
    )


def relay_kernel(nf, w_ref, v_ref, u_ref, x_ref, own_ref, *rest):
    out_ref = rest[-1]
    lane = lax.broadcasted_iota(i32, (1, lanes), 1)
    main, after, mixed = received(nf, w_ref, v_ref, u_ref, x_ref)
    out_ref[:, 0:128] = jnp.where(lane < 96, own_ref[...], main)
    out_ref[:, 128:256] = jnp.where(lane < 32, pltpu.roll(after, 32, 1), mixed)


def setup_kernel(
    chips, coef_ref, level_ref, side_ref,
    info_ref, own_hot_ref, partner_hot_ref, far_hot_ref, arrival_ref, arrival_hot_ref,
):
    core, near, u_step, w_there, v_there = where_am_i(chips)
    elem, direction, case = side_ref[0:1], side_ref[1:2], side_ref[2:3]
    kind, partner = side_ref[3:4], side_ref[4:5]
    live = lax.broadcasted_iota(i32, (1, side_pad), 1) < 930
    own_column = jnp.where(live, direction * lanes + elem, -1)

    coef, size, volume_scale, normal_scale = element_rows(coef_ref, level_ref)
    scalars = rows_of([x.astype(f32) for x in three(coef)] + [size], 16, lanes)
    mine = dot(scalars.astype(bf16), one_hot(jnp.where(live, elem, -1), lanes))
    hanging = (case >= 0) & (case < 4)
    own_coef = mine[0:1] + mine[1:2] + mine[2:3]
    own_size = mine[3:4] * jnp.where(hanging, 0.5, 1.0)

    rows = [jnp.where(live, r, 0).astype(f32) for r in (elem, direction, case)]
    rows.append(jnp.where(live, 1.0, 0.0))
    rows += [mine[0:1], mine[1:2], mine[2:3], own_size]
    attributes = rows_of(rows, 16, side_pad).astype(bf16)
    other = dot(attributes, one_hot(jnp.where(partner < 930, partner, -1), side_pad))
    valid = other[3:4] > 0.5
    fill_one_hot(
        partner_hot_ref, jnp.where(valid, (other[1:2] * 128.0 + other[0:1]).astype(i32), -1)
    )
    edge = jnp.where(kind == 1, 1.0, 0.0)
    least = jnp.where(valid, jnp.minimum(own_size, other[7:8]), 0.0)
    jump = 16.0 * (own_coef + other[4:5] + other[5:6] + other[6:7]) * least
    area = least * least
    info_ref[:, 0:side_pad] = rows_of(
        [jump, jump * (1.0 - edge), area * (0.5 + 0.5 * edge), area * (0.5 - 0.5 * edge),
         case.astype(f32), other[2:3]],
        8, side_pad,
    )

    sought = jnp.where(live & (kind == 0), partner, -7)
    place = lax.broadcasted_iota(i32, (lanes, side_pad), 0)
    flip = 1 - 2 * core
    pair, after = 2 * near + flip, flip - 2 * near
    segments = (
        ((0, jnp.where(narrow(pair), 24, 96), -pair, 0), (96, 120, -(2 * u_step + flip), 0)),
        ((0, jnp.where(narrow(after), 24, 96), -after, 0), (96, 120, -(flip - 2 * u_step), 0)),
        ((0, 96, -flip, 0), (96, 128, -2 * near, 0)),
        ((0, 32, 2 * near, 0), (48, 72, -2 * u_step, 0), (72, 96, 2 * u_step, 0),
         (96, 112, -2 * near, 32), (112, 128, 2 * near, 32)),
    )
    for tile, parts in enumerate(segments):
        slot = jnp.full((lanes, side_pad), -5, i32)
        for low, high, offset, begin in parts:
            entry = 930 + 96 * row_of(offset) + begin - low
            slot = jnp.where((place >= low) & (place < high), entry + place, slot)
        arrival_hot_ref[lanes * tile : lanes * tile + lanes] = jnp.where(
            slot == sought, 1.0, 0.0
        ).astype(bf16)
    target = dot_t(attributes, arrival_hot_ref[...])
    valid = target[3:4] > 0.5
    target_column = jnp.where(valid, (target[1:2] * 128.0 + target[0:1]).astype(i32), -1)
    fill_one_hot(own_hot_ref, jnp.concatenate([own_column, target_column[:, 0:256]], axis=1))
    fill_one_hot(far_hot_ref, target_column[:, 256:512])
    info_ref[:, side_pad:] = rows_of(
        [jnp.zeros((1, 256), f32)] * 4 + [jnp.where(valid, target[2:3], -1.0)[:, 0:256]], 8, 256
    )
    arrival_ref[...] = rows_of(
        [jnp.where(valid, target[2:3], -1.0), target[4:5] + target[5:6] + target[6:7], target[7:8]],
        8, 512,
    )


def sides_kernel(
    nf, stack_ref, interp_ref, own_hot_ref, partner_hot_ref, far_hot_ref, info_ref, arrival_ref,
    mine_ref, other_ref, target_ref,
):
    h = 32 * nf
    stack = stack_ref[0 : 2 * h]
    table = interp_ref[...]
    for hot_ref, case, out_ref in (
        (own_hot_ref, info_ref[4:5], mine_ref),
        (partner_hot_ref, info_ref[5:6, 0:side_pad], other_ref),
        (far_hot_ref, arrival_ref[0:1, 256:512], target_ref),
    ):
        got = dot(stack, hot_ref[...])
        out_ref[...] = fields_case(table, got[:h] + got[h:], case.astype(i32), nf)


def scatter(x, hot, nf):
    high, low = two(x)
    got = dot_t(jnp.concatenate([high, low], axis=0), hot)
    return got[: 32 * nf] + got[32 * nf :]


def side_flux(nf, mine, outer, coefs, case, weight_ref, interp_ref, hot):
    jump, jump_out, area, area_out = coefs
    weight = weight_ref[0:16, 0:1]
    flux = []
    for k in range(nf):
        value, slope = mine[32 * k : 32 * k + 16], mine[32 * k + 16 : 32 * k + 32]
        other, other_slope = outer[32 * k : 32 * k + 16], outer[32 * k + 16 : 32 * k + 32]
        flux.append(
            weight * (jump * value - jump_out * other - area * slope + area_out * other_slope)
        )
        flux.append(weight * (area_out * other - area * value))
    flux = fields_case(interp_ref[...], jnp.concatenate(flux, axis=0), case.astype(i32), nf)
    high, low = two(flux)
    got = dot_t(jnp.concatenate([high, low], axis=0), hot)
    return got[: 32 * nf] + got[32 * nf :]


def halo_coefs(coef, size, other_coef, other_size):
    least = jnp.minimum(size, other_size)
    return 16.0 * (coef + other_coef) * least, 0.5 * least * least


def flux_kernel(
    nf, w_ref, v_ref, u_ref, x_ref, mine_ref, other_ref, info_ref, arrival_ref, weight_ref, interp_ref,
    own_hot_ref, *rest,
):
    h = 32 * nf
    lane = lax.broadcasted_iota(i32, (1, lanes), 1)
    main, after, mixed = received(nf, w_ref, v_ref, u_ref, x_ref)
    got = jnp.concatenate(
        [
            jnp.where(lane < 96, main, pltpu.roll(mixed, 96, 1)),
            jnp.where(lane < 96, after, pltpu.roll(mixed, 72, 1)),
        ],
        axis=1,
    )
    if got.shape[0] > h:
        sum_ref, halo_ref = rest
        halo = halo_coefs(
            arrival_ref[1:2, 0:256], arrival_ref[2:3, 0:256], got[h : h + 1], got[h + 1 : h + 2]
        )
        halo_ref[...] = rows_of(halo, 8, 256)
    else:
        halo_ref, sum_ref = rest
        halo = halo_ref[0:1], halo_ref[1:2]
    coefs = [
        jnp.concatenate([info_ref[k : k + 1, 0:side_pad], halo[k // 2]], axis=1) for k in range(4)
    ]
    outer = jnp.concatenate([other_ref[...], got[0:h]], axis=1)
    sum_ref[...] = side_flux(
        nf, mine_ref, outer, coefs, info_ref[4:5], weight_ref, interp_ref, own_hot_ref[...]
    )


def solve_blocks(inverse_ref, hold_ref, nf):
    sums = [jnp.zeros((64, lanes), f32) for _ in range(nf)]
    for col in range(64):
        block = inverse_ref[col].astype(f32)
        for k in range(nf):
            sums[k] = sums[k] + block * hold_ref[64 * k + col : 64 * k + col + 1, :]
    return sums


def update_kernel(
    nf, nf_next, residual,
    one_ref, local_ref, target_ref, arrival_ref, far_hot_ref, weight_ref, interp_t_ref, lift_ref,
    field_ref, coef_ref, level_ref, inverse_ref, *rest,
):
    if residual:
        rhs_ref, *rest = rest
    else:
        halo_ref, *rest = rest
    if nf_next:
        trace_ref, interp_ref, hot_ref, case_ref, new_ref, stack_ref, *rest = rest
        messages, rest = rest[:4], rest[4:]
    else:
        new_ref, part_ref, *rest = rest
    hold_ref = rest[-1]
    h = 32 * nf
    if residual:
        halo = halo_coefs(
            arrival_ref[1:2, 256:512], arrival_ref[2:3, 256:512],
            one_ref[h : h + 1], one_ref[h + 1 : h + 2],
        )
        rest[0][...] = rows_of(halo, 8, 256)
    else:
        halo = (halo_ref[0:1], halo_ref[1:2])
    total = local_ref[...] + side_flux(
        nf, target_ref, one_ref, (halo[0], halo[0], halo[1], halo[1]), arrival_ref[0:1, 256:512],
        weight_ref, interp_t_ref, far_hot_ref[...],
    )
    coef, size, volume_scale, normal_scale = element_rows(coef_ref, level_ref)
    row = lax.broadcasted_iota(i32, (32, lanes), 0)
    scale = jnp.where(row < 16, 1.0, jnp.broadcast_to(normal_scale, (32, lanes)))
    operands = []
    for k in range(nf):
        mine = total[32 * k : 32 * k + 32]
        faces = jnp.concatenate(
            [mine[:, lanes * f : lanes * f + lanes] * scale for f in range(6)], axis=0
        )
        high, low = two(faces)
        field_high, field_low = two(field_ref[64 * k : 64 * k + 64] * volume_scale)
        operands.append(
            jnp.concatenate([high, low, high, field_high, field_low, field_high], axis=0)
        )
    image = dot(lift_ref[...], cat(operands, 1))
    for k in range(nf):
        part = image[:, lanes * k : lanes * k + lanes]
        if residual and k == 1:
            part = rhs_ref[...] - part
        hold_ref[64 * k : 64 * k + 64, :] = part
    new = solve_blocks(inverse_ref, hold_ref, nf)
    for k in range(nf):
        new_ref[64 * k : 64 * k + 64, :] = new[k]
    if nf_next:
        stack = face_stack(trace_ref, new[:nf_next], normal_scale, nf_next)
        stack_ref[...] = stack
        sent = gather_message(stack, hot_ref[...], interp_ref[...], case_ref[0:1], nf_next)
        fill_messages(sent, nf_next, *messages)
    else:
        before, after = field_ref[...], new[0]
        before = jnp.sum(jnp.sum(before * before, axis=1, keepdims=True), axis=0, keepdims=True)
        after = jnp.sum(jnp.sum(after * after, axis=1, keepdims=True), axis=0, keepdims=True)
        lane = lax.broadcasted_iota(i32, part_ref.shape, 1)
        part_ref[...] = jnp.where(lane == 0, before, jnp.where(lane == 1, after, 0.0))


def finish_kernel(part_ref, guess_ref, first_ref, second_ref, out_ref, bound_ref):
    total = jnp.sum(part_ref[...], axis=0, keepdims=True)
    bound = jnp.sqrt(total[:, 1:2] / total[:, 0:1])
    upper = 1.2 * bound
    lower = upper / 15.0
    center = 0.5 * (upper + lower)
    half = 0.5 * (upper - lower)
    ratio = center / half
    damping = 1.0 / ratio
    damping_next = 1.0 / (2.0 * ratio - damping)
    first = first_ref[64:128] / center
    second = first_ref[64:128] - second_ref[64:128] / center
    out_ref[...] = (
        guess_ref[...] + first + (damping_next * damping * first + 2.0 * damping_next / half * second)
    )
    bound_ref[...] = jnp.broadcast_to(bound, (1, lanes))


def in_vmem(x):
    return pltpu.with_memory_space_constraint(x, pltpu.VMEM)


def in_hbm(x):
    return pltpu.with_memory_space_constraint(x, pltpu.HBM)


def run(body, outs, ins, name, scratch=(), flops=1 << 24, placed=True, kept=True):
    spec = pl.BlockSpec(memory_space=pltpu.VMEM)
    return pl.pallas_call(
        body,
        out_shape=[(pltpu.VMEM if kept else jax.ShapeDtypeStruct)(shape, dtype) for shape, dtype in outs],
        in_specs=[spec if placed else pl.BlockSpec(memory_space=pltpu.HBM)] * len(ins),
        out_specs=[spec] * len(outs),
        scratch_shapes=list(scratch),
        compiler_params=pltpu.CompilerParams(vmem_limit_bytes=24 << 20),
        cost_estimate=pl.CostEstimate(flops=flops, bytes_accessed=1 << 20, transcendentals=0),
        name=name,
    )(*(in_vmem(x) if placed else in_hbm(x) for x in ins))


def local(
    rhs_field, initial_guess, start_vector, coefficient, refine_level, block_inverse,
    side_elem, side_dir, side_case, side_kind, partner, send_list,
):
    devices = lax.axis_size("dom")
    chips = devices // 2
    trace, interp, interp_t, lift, weight = (jnp.asarray(t) for t in const_tables())
    coef = coefficient.reshape(1, lanes)
    level = refine_level.reshape(1, lanes)

    def swap(x, mask):
        return lax.ppermute(x, "dom", [(i, i ^ mask) for i in range(devices)])

    def swap_chips(x, to):
        return lax.ppermute(
            x, "dom",
            [(2 * c + k, 2 * to.get(c, c) + 1 - k) for c in range(chips) for k in range(2)],
        )

    after_pair = {c: c + 1 if c % 2 else c - 1 for c in range(1, chips - 1)}
    two_away = {c: c + 2 if c % 4 >= 2 else c - 2 for c in range(2, chips - 2)}
    two_away.update({c: c ^ 1 for c in (0, 1, chips - 2, chips - 1)})

    def exchange(messages, nf, work):
        w, v, u, x = messages
        first = (swap_chips(w, after_pair), swap_chips(v, two_away), swap(u, 5), swap(x, 3))
        own, *rest = work()
        (one,) = run(
            functools.partial(relay_kernel, nf), [((own.shape[0], 256), f32)],
            [*first, own, *rest[:1]], "relay",
        )
        return first, swap(one, 1), rest

    def message_shapes(nf, extra=0):
        return [((rows * nf + extra, lanes), f32) for rows in (40, 16, 16, 40)]

    sides = [x.reshape(1, -1) for x in (side_elem, side_dir, side_case, side_kind, partner)]
    first = [*sides, send_list, start_vector, initial_guess, coef, level, trace, interp]
    hot, case, stack, sides, rolled, *rest = run(
        functools.partial(send_setup_kernel, chips),
        [((768, 384), bf16), ((8, 384), i32), ((144, 768), bf16), ((8, side_pad), i32), ((56, lanes), i32),
         *message_shapes(2, 8), *((x.shape, x.dtype) for x in first[8:])],
        first,
        "send_setup",
        scratch=[
            pltpu.VMEM((8, 384), i32),
            *(pltpu.VMEM(x.shape, x.dtype) for x in first[:8]), pltpu.SemaphoreType.DMA((len(first),)),
        ],
        placed=False,
    )
    messages, (coef, level, trace, interp) = rest[:4], rest[4:]
    fields = jnp.concatenate([start_vector, initial_guess], axis=0)
    history = []
    for turn, nf in enumerate((2, 2, 1, 1)):
        h = 32 * nf
        sides_out = [((h, side_pad + 256), f32), ((h, side_pad), f32), ((h, 256), f32)]
        own_out = [((h if turn else h + 8, lanes), f32)]

        def first_work():
            own_slots = run(
                functools.partial(own_setup_kernel, chips),
                [((768, lanes), bf16), ((8, lanes), i32)],
                [sides, rolled],
                "own_setup",
            )
            made = run(
                functools.partial(setup_kernel, chips),
                [((8, side_pad + 256), f32), ((768, side_pad + 256), bf16), ((768, side_pad), bf16),
                 ((768, 256), bf16), ((8, 512), f32)],
                [coef, level, sides],
                "setup",
                scratch=[pltpu.VMEM((512, side_pad), bf16)],
            )
            (own,) = run(
                functools.partial(own_kernel, nf), own_out, [stack, *own_slots, interp], "own"
            )
            return [own, *made, *own_slots]

        def later_work():
            return run(
                functools.partial(own_sides_kernel, nf),
                own_out + sides_out,
                [stack, *own_slots, interp, own_hot, partner_hot, far_hot, info, arrival],
                "own_sides",
            )

        arrivals, one, rest = exchange(messages, nf, later_work if turn else first_work)
        if turn == 0:
            info, own_hot, partner_hot, far_hot, arrival, *own_slots = rest
            mine, others, targets = run(
                functools.partial(sides_kernel, nf),
                sides_out,
                [stack, interp, own_hot, partner_hot, far_hot, info, arrival],
                "sides",
            )
        else:
            mine, others, targets = rest
        halo_out = [((8, 256), f32)] if turn == 0 else []
        sums, *made = run(
            functools.partial(flux_kernel, nf),
            [((h, 768), f32)] + halo_out,
            [*arrivals, mine, others, info, arrival, weight, interp_t, own_hot]
            + ([near_halo] if turn else []),
            "flux",
        )
        if turn == 0:
            near_halo = made[0]
        nf_next = (2, 1, 1, 0)[turn]
        ins = [
            one, sums, targets, arrival, far_hot, weight, interp_t, lift,
            fields, coef, level, block_inverse, far_halo if turn else rhs_field,
        ]
        outs = [((64 * nf, lanes), f32)]
        if nf_next:
            ins += [trace, interp, hot, case]
            outs += [((64 * nf_next, 768), bf16)] + message_shapes(nf_next)
        else:
            outs += [((devices, lanes), f32)]
        made = run(
            functools.partial(update_kernel, nf, nf_next, turn == 0),
            outs + halo_out, ins, "update",
            scratch=[pltpu.VMEM((64 * nf, lanes), f32)],
        )
        if turn == 0:
            far_halo = made[-1]
        if nf_next:
            fields, stack, *messages = made[:6]
            history.append(fields)
            if nf_next < nf:
                fields = fields[:64]
        else:
            fields, parts = made
    parts = lax.all_to_all(parts.reshape(devices, 1, lanes), "dom", 0, 0).reshape(devices, lanes)
    smoothed, bound = run(
        finish_kernel,
        [((64, lanes), f32), ((1, lanes), f32)],
        [parts, initial_guess, history[0], history[1]],
        "finish",
        kept=False,
    )
    return smoothed, bound[0, 0]


def solution(mesh):
    placed = (
        P(None, "dom"), P(None, "dom"), P(None, "dom"), P("dom"), P("dom"), P(None, None, "dom"),
        P("dom"), P("dom"), P("dom"), P("dom"), P("dom"), P("dom", None),
    )
    return jax.shard_map(
        local, mesh=mesh, in_specs=placed, out_specs=(P(None, "dom"), P()), check_vma=False
    )
```

```python
import functools
import math

import jax
import jax.numpy as jnp
import numpy as np
from jax import lax
from jax.experimental import pallas as pl
from jax.experimental.pallas import tpu as pltpu
from jax.sharding import PartitionSpec as P

f32 = jnp.float32
bf16 = jnp.bfloat16
i32 = jnp.int32
peer_offsets = (1, -1, 2, -2, 3, -3, 4, -4)
live_width = {1: 96, 2: 48, 3: 24, 4: 24}
lanes = 128
shifts = (0, 24, 48, 96)
side_pad = 1024


def lagrange_tables():
    root_five = 1.0 / math.sqrt(5.0)
    nodes = np.array([0.0, 0.5 - 0.5 * root_five, 0.5 + 0.5 * root_five, 1.0])
    weights = np.array([1.0, 5.0, 5.0, 1.0]) / 12.0
    factor = np.array(
        [np.prod([nodes[i] - nodes[j] for j in range(4) if j != i]) for i in range(4)]
    )
    derivative = np.zeros((4, 4))
    for i in range(4):
        for j in range(4):
            if i != j:
                derivative[i, j] = factor[i] / (factor[j] * (nodes[i] - nodes[j]))
        derivative[i, i] = -np.sum(derivative[i])
    halves = []
    for half in range(2):
        points = 0.5 * (nodes + half)
        table = np.ones((4, 4))
        for j in range(4):
            for other in range(4):
                if other != j:
                    table[:, j] *= (points - nodes[other]) / (nodes[j] - nodes[other])
        halves.append(table)
    return weights, derivative, halves


def basis_tables():
    weights, derivative, halves = lagrange_tables()
    mass = np.diag(weights)
    line = derivative.T @ mass @ derivative
    stiffness = (
        np.kron(np.kron(line, mass), mass)
        + np.kron(np.kron(mass, line), mass)
        + np.kron(np.kron(mass, mass), line)
    )
    trace = np.zeros((6, 32, 64))
    for dim in range(3):
        others = [d for d in range(3) if d != dim]
        for lower in range(2):
            face = 2 * dim + lower
            fixed = 0 if lower else 3
            sign = -1.0 if lower else 1.0
            for first in range(4):
                for second in range(4):
                    node = first * 4 + second
                    for along in range(4):
                        place = [0, 0, 0]
                        place[others[0]] = first
                        place[others[1]] = second
                        place[dim] = along
                        nodal = place[0] * 16 + place[1] * 4 + place[2]
                        if along == fixed:
                            trace[face, node, nodal] = 1.0
                        trace[face, 16 + node, nodal] = sign * derivative[fixed, along]
    quarter = [np.kron(halves[q // 2], halves[q % 2]) for q in range(4)]
    both = np.eye(2)
    interp = np.concatenate([np.kron(both, q) for q in quarter], axis=0)
    interp_t = np.concatenate([np.kron(both, q.T) for q in quarter], axis=0)
    face_weight = np.kron(weights, weights)
    return stiffness, trace.reshape(192, 64), interp, interp_t, face_weight


def stacked(table):
    table = np.asarray(table, np.float32)
    high = table.astype(jnp.bfloat16)
    low = (table - high.astype(np.float32)).astype(jnp.bfloat16)
    return np.concatenate([high, high, low], axis=1)


def const_tables():
    stiffness, trace, interp, interp_t, face_weight = basis_tables()
    lift = np.concatenate([stacked(trace.T), stacked(stiffness)], axis=1)
    weight = np.broadcast_to(np.concatenate([face_weight, face_weight])[:, None], (32, lanes))
    return (
        stacked(trace),
        stacked(interp),
        stacked(interp_t),
        lift,
        np.asarray(weight, np.float32),
    )


def two(x):
    high = x.astype(bf16)
    return high, (x - high.astype(f32)).astype(bf16)


def three(x):
    high = x.astype(bf16)
    rest = x - high.astype(f32)
    mid = rest.astype(bf16)
    return high, mid, (rest - mid.astype(f32)).astype(bf16)


def dot(a, b):
    return jnp.dot(a, b, preferred_element_type=f32)


def dot_t(a, b):
    return lax.dot_general(a, b, (((1,), (1,)), ((), ())), preferred_element_type=f32)


def cat(parts, axis):
    return parts[0] if len(parts) == 1 else jnp.concatenate(parts, axis=axis)


def table_dot(table, x):
    high, low = two(x)
    return dot(table, jnp.concatenate([high, low, high], axis=0))


def apply_case(table, x, case):
    quarters = table_dot(table, x)
    out = x
    for c in range(4):
        out = jnp.where(case == c, quarters[32 * c : 32 * c + 32], out)
    return out


def fields_case(table, x, case, nf):
    wide = cat([x[32 * k : 32 * k + 32] for k in range(nf)], 1)
    out = apply_case(table, wide, cat([case] * nf, 1))
    n = x.shape[1]
    return cat([out[:, n * k : n * k + n] for k in range(nf)], 0)


def rows_of(rows, count, width):
    place = lax.broadcasted_iota(i32, (count, width), 0)
    table = jnp.zeros((count, width), f32)
    for k, r in enumerate(rows):
        table = jnp.where(place == k, r, table)
    return table


def one_hot(index_row, rows, first=0):
    place = lax.broadcasted_iota(i32, (rows, index_row.shape[1]), 0) + first
    return jnp.where(place == index_row, 1.0, 0.0).astype(bf16)


def element_rows(coef_ref, level_ref):
    coef = coef_ref[...]
    level = level_ref[...]
    size = jnp.where(level == 0, 1.0, jnp.where(level == 1, 0.5, 0.25)).astype(f32)
    inverse = jnp.where(level == 0, 1.0, jnp.where(level == 1, 2.0, 4.0)).astype(f32)
    return coef, size, coef * size, coef * inverse


def face_stack(trace_ref, u, normal_scale, nf):
    faces = table_dot(trace_ref[...], cat(u, 1))
    row = lax.broadcasted_iota(i32, (32, lanes), 0)
    scale = jnp.where(row < 16, 1.0, jnp.broadcast_to(normal_scale, (32, lanes)))
    fields = []
    for k in range(nf):
        part = faces[:, lanes * k : lanes * k + lanes]
        fields.append(
            jnp.concatenate([part[32 * f : 32 * f + 32] * scale for f in range(6)], axis=1)
        )
    high, low = two(cat(fields, 0))
    return jnp.concatenate([high, low], axis=0)


def gather_message(stack, hot, interp, case, nf):
    got = dot(stack, hot)
    h = 32 * nf
    out = fields_case(interp, got[:h] + got[h : 2 * h], case, nf)
    if stack.shape[0] == 2 * h:
        return out
    coef = got[2 * h : 2 * h + 1] + got[2 * h + 1 : 2 * h + 2] + got[2 * h + 2 : 2 * h + 3]
    size = got[2 * h + 3 : 2 * h + 4] * jnp.where((case >= 0) & (case < 4), 0.5, 1.0)
    row = lax.broadcasted_iota(i32, (8, out.shape[1]), 0)
    scalars = jnp.where(row == 0, coef, jnp.where(row == 1, size, 0.0))
    return jnp.concatenate([out, scalars], axis=0)


def where_am_i(chips):
    me = lax.axis_index("dom")
    chip = me // 2
    core = me - 2 * chip
    near = jnp.where(lax.rem(chip, 2) == 1, -1, 1)
    far = jnp.where(lax.rem(chip, 4) < 2, 1, -1)
    end = (chip == 0) | (chip == chips - 1)
    far_there = (chip - 2 * far >= 0) & (chip - 2 * far < chips)
    return core, near, far, end, ~end, far_there


def carried(core, near, far, near_there, far_there):
    first = core == 0
    return (
        jnp.where(first, near, -near), jnp.where(first, far, -far),
        first | near_there, first | far_there,
    )


def row_of(offset):
    size = jnp.abs(offset)
    return 2 * (size - 1) + jnp.where(offset < 0, 1, 0)


def narrow(offset):
    return jnp.abs(offset) == 3


def slot_attributes(side_ref, slots):
    live = lax.broadcasted_iota(i32, (1, side_pad), 1) < 930
    rows = [jnp.where(live, side_ref[k : k + 1], 0).astype(f32) for k in range(3)]
    rows.append(jnp.where(live, 1.0, 0.0))
    found = dot(rows_of(rows, 16, side_pad).astype(bf16), one_hot(slots, side_pad))
    valid = found[3:4] > 0.5
    column = jnp.where(valid, (found[1:2] * 128.0 + found[0:1]).astype(i32), -1)
    return column, jnp.where(valid, found[2:3].astype(i32), -1)


def fill_one_hot(hot_ref, column):
    for f in range(6):
        hot_ref[lanes * f : lanes * f + lanes] = one_hot(column, lanes, lanes * f)


def listed_part(rolled_ref, shift, offset, low, high, valid):
    place = shifts.index(shift)
    lane = lax.broadcasted_iota(i32, (1, lanes), 1)
    values = rolled_ref[pl.ds(8 * place + jnp.minimum(row_of(offset), 7), 1), :]
    return jnp.where((lane >= low) & (lane < high) & valid, values, -1)


def send_setup_kernel(chips, *refs):
    sources, refs = refs[:12], refs[12:]
    hot_ref, case_ref, stack_ref, side_ref, rolled_ref = refs[:5]
    sent_ref, landed = refs[5], (*refs[11:19], *refs[6:10])
    slot_ref, arrived = refs[10], refs[19]
    copies = [
        pltpu.make_async_copy(source, target, arrived.at[k])
        for k, (source, target) in enumerate(zip(sources, landed))
    ]
    for copy in copies:
        copy.start()
    elem_ref, dir_ref, sidecase_ref, kind_ref, partner_ref, list_ref = landed[:6]
    start_ref, guess_ref, coef_ref, level_ref, trace_ref, interp_ref = landed[6:]
    for copy in copies:
        copy.wait()
    side_ref[...] = jnp.full((8, side_pad), -1, i32)
    sides = elem_ref.shape[1]
    for k, ref in enumerate((elem_ref, dir_ref, sidecase_ref, kind_ref, partner_ref)):
        side_ref[k : k + 1, 0:sides] = ref[...]
    core, near, far, end, near_there, far_there = where_am_i(chips)
    listed = jnp.concatenate([list_ref[...], jnp.full((8, 32), -1, i32)], axis=1)
    for place, shift in enumerate(shifts):
        rolled_ref[8 * place : 8 * place + 8] = (
            pltpu.roll(listed, shift, 1) if shift else listed
        )
    part = functools.partial(listed_part, rolled_ref)
    other = 1 - core
    step, step_two, there, there_two = carried(other, near, far, near_there, far_there)
    cross, cross_two = 2 * step + other - core, 4 * step_two + other - core
    first = (
        part(0, cross_two, 0, 24, there_two & narrow(cross_two)),
        part(24, 4 * step_two, 24, 48, there_two),
        part(48, 2 * step, 48, 96, there),
        part(96, cross, 96, 120, there & narrow(cross)),
    )
    slot_ref[0:1, 0:128] = functools.reduce(jnp.maximum, first)
    slot_ref[0:1, 128:256] = part(0, cross, 0, 96, there & ~narrow(cross))
    column, slot_case = slot_attributes(side_ref, slot_ref[0:1, :])
    case_ref[0:1, :] = slot_case
    fill_one_hot(hot_ref, column)

    coef, size, volume_scale, normal_scale = element_rows(coef_ref, level_ref)
    stack = face_stack(trace_ref, [start_ref[...], guess_ref[...]], normal_scale, 2)
    scalars = rows_of([x.astype(f32) for x in three(coef)] + [size], 16, lanes).astype(bf16)
    stack = jnp.concatenate([stack, jnp.concatenate([scalars] * 6, axis=1)], axis=0)
    stack_ref[...] = stack
    sent = gather_message(stack, hot_ref[...], interp_ref[...], slot_case, 2)
    sent_ref[...] = sent


def own_setup_kernel(chips, side_ref, rolled_ref, hot_ref, case_ref, slot_ref):
    core, near, far, end, near_there, far_there = where_am_i(chips)
    part = functools.partial(listed_part, rolled_ref)
    flip = 1 - 2 * core
    step, step_two, there, there_two = carried(core, near, far, near_there, far_there)
    cross, cross_two = 2 * step + flip, 4 * step_two + flip
    slot_ref[0:1, 0:128] = jnp.maximum(
        part(0, 4 * step_two, 0, 24, there_two),
        part(24, cross_two, 24, 48, there_two & narrow(cross_two)),
    )
    slot_ref[0:1, 128:256] = jnp.maximum(
        part(0, 2 * step, 0, 48, there), part(96, cross, 96, 120, there & narrow(cross))
    )
    slot_ref[0:1, 256:384] = part(0, cross, 0, 96, there & ~narrow(cross))
    slot_ref[0:1, 384:512] = part(0, flip, 0, 96, core >= 0)
    column, slot_case = slot_attributes(side_ref, slot_ref[0:1, :])
    case_ref[0:1, :] = slot_case
    fill_one_hot(hot_ref, column)


def own_kernel(nf, stack_ref, hot_ref, case_ref, interp_ref, own_ref):
    own_ref[...] = gather_message(
        stack_ref[...], hot_ref[...], interp_ref[...], case_ref[0:1], nf
    )


def carry_kernel(sent_ref, own_ref, two_ref, one_ref):
    lane = lax.broadcasted_iota(i32, (1, lanes), 1)
    sent = sent_ref[:, 0:128]
    handed = jnp.where((lane >= 48) & (lane < 96), pltpu.roll(sent, 48, 1), 0.0)
    two_ref[...] = own_ref[:, 0:128] + handed
    one_ref[:, 0:128] = own_ref[:, 128:256] + jnp.where(lane >= 48, sent, 0.0)
    one_ref[:, 128:256] = own_ref[:, 256:384] + sent_ref[:, 128:256]


def relay_kernel(chips, one_ref, two_ref, own_ref, *rest):
    out_ref = rest[-1]
    core, near, far, end, near_there, far_there = where_am_i(chips)
    lane = lax.broadcasted_iota(i32, (1, lanes), 1)
    one, two_away = one_ref[:, 0:128], two_ref[...]
    out_ref[:, 0:128] = own_ref[:, 384:512]
    passed = jnp.where(lane < 24, pltpu.roll(two_away, 56, 1), two_away)
    out_ref[:, 128:256] = jnp.where((lane < 48) & ~(end & (core == 1)), passed, one)
    out_ref[:, 256:384] = one_ref[:, 128:256]


def setup_kernel(
    chips, coef_ref, level_ref, side_ref,
    info_ref, own_hot_ref, partner_hot_ref, far_hot_ref, arrival_ref, arrival_hot_ref,
):
    core, near, far, end, near_there, far_there = where_am_i(chips)
    elem, direction, case = side_ref[0:1], side_ref[1:2], side_ref[2:3]
    kind, partner = side_ref[3:4], side_ref[4:5]
    live = lax.broadcasted_iota(i32, (1, side_pad), 1) < 930
    own_column = jnp.where(live, direction * lanes + elem, -1)

    coef, size, volume_scale, normal_scale = element_rows(coef_ref, level_ref)
    scalars = rows_of([x.astype(f32) for x in three(coef)] + [size], 16, lanes)
    mine = dot(scalars.astype(bf16), one_hot(jnp.where(live, elem, -1), lanes))
    hanging = (case >= 0) & (case < 4)
    own_coef = mine[0:1] + mine[1:2] + mine[2:3]
    own_size = mine[3:4] * jnp.where(hanging, 0.5, 1.0)

    rows = [jnp.where(live, r, 0).astype(f32) for r in (elem, direction, case)]
    rows.append(jnp.where(live, 1.0, 0.0))
    rows += [mine[0:1], mine[1:2], mine[2:3], own_size]
    attributes = rows_of(rows, 16, side_pad).astype(bf16)
    other = dot(attributes, one_hot(jnp.where(partner < 930, partner, -1), side_pad))
    valid = other[3:4] > 0.5
    fill_one_hot(
        partner_hot_ref, jnp.where(valid, (other[1:2] * 128.0 + other[0:1]).astype(i32), -1)
    )
    edge = jnp.where(kind == 1, 1.0, 0.0)
    least = jnp.where(valid, jnp.minimum(own_size, other[7:8]), 0.0)
    jump = 16.0 * (own_coef + other[4:5] + other[5:6] + other[6:7]) * least
    area = least * least
    info_ref[:, 0:side_pad] = rows_of(
        [jump, jump * (1.0 - edge), area * (0.5 + 0.5 * edge), area * (0.5 - 0.5 * edge),
         case.astype(f32), other[2:3]],
        8, side_pad,
    )

    sought = jnp.where(live & (kind == 0), partner, -7)
    place = lax.broadcasted_iota(i32, (lanes, side_pad), 0)
    def arrives(carrier):
        last = end & (carrier == 1)
        back = jnp.where((carrier == 0) | end, -near, near)
        back_two = jnp.where(carrier == 0, -far, far)
        turn = 2 * core - 1
        return (
            2 * back, 2 * back + turn, 4 * back_two, 4 * back_two + turn,
            ~(end & (carrier == 0)), ~last, last,
        )

    def span(low, high, valid):
        return low, jnp.where(valid, high, low)

    segments = []
    for mine, carrier in ((True, core), (False, 1 - core)):
        straight, cross, straight_two, cross_two, there, there_two, last = arrives(carrier)
        slim, wide = there & narrow(cross), there & ~narrow(cross)
        at_first = (last & (core != 1)) | (~last & (carrier == core))
        if mine:
            two_parts = ((*span(48, 72, there_two & narrow(cross_two)), cross_two),
                         (*span(72, 96, there_two), straight_two))
        else:
            segments.append(((0, 96, 2 * core - 1),))
            two_parts = ((*span(0, 24, there_two), straight_two),
                         (*span(24, 48, there_two & narrow(cross_two)), cross_two))
        segments.append((
            (*span(0, 48, there & at_first), straight), (*span(48, 96, there & ~at_first), straight),
            (*span(96, 120, slim), cross), *two_parts,
        ))
        segments.append(((*span(0, 96, wide), cross),))
    for tile, parts in enumerate(segments):
        slot = jnp.full((lanes, side_pad), -5, i32)
        for low, high, offset in parts:
            entry = 930 + 96 * row_of(offset) - low
            slot = jnp.where((place >= low) & (place < high), entry + place, slot)
        arrival_hot_ref[lanes * tile : lanes * tile + lanes] = jnp.where(
            slot == sought, 1.0, 0.0
        ).astype(bf16)
    target = dot_t(attributes, arrival_hot_ref[...])
    valid = target[3:4] > 0.5
    target_column = jnp.where(valid, (target[1:2] * 128.0 + target[0:1]).astype(i32), -1)
    fill_one_hot(own_hot_ref, jnp.concatenate([own_column, target_column[:, 0:256]], axis=1))
    fill_one_hot(far_hot_ref, target_column[:, 256:640])
    info_ref[:, side_pad:] = rows_of(
        [jnp.zeros((1, 256), f32)] * 4 + [jnp.where(valid, target[2:3], -1.0)[:, 0:256]], 8, 256
    )
    arrival_ref[...] = rows_of(
        [jnp.where(valid, target[2:3], -1.0), target[4:5] + target[5:6] + target[6:7], target[7:8]],
        8, 640,
    )


def sides_kernel(
    nf, stack_ref, interp_ref, own_hot_ref, partner_hot_ref, far_hot_ref, info_ref, arrival_ref,
    mine_ref, other_ref, target_ref,
):
    h = 32 * nf
    stack = stack_ref[0 : 2 * h]
    table = interp_ref[...]
    for hot_ref, case, out_ref in (
        (own_hot_ref, info_ref[4:5], mine_ref),
        (partner_hot_ref, info_ref[5:6, 0:side_pad], other_ref),
        (far_hot_ref, arrival_ref[0:1, 256:640], target_ref),
    ):
        got = dot(stack, hot_ref[...])
        out_ref[...] = fields_case(table, got[:h] + got[h:], case.astype(i32), nf)


def scatter(x, hot, nf):
    high, low = two(x)
    got = dot_t(jnp.concatenate([high, low], axis=0), hot)
    return got[: 32 * nf] + got[32 * nf :]


def side_flux(nf, mine, outer, coefs, case, weight_ref, interp_ref, hot):
    jump, jump_out, area, area_out = coefs
    weight = weight_ref[0:16, 0:1]
    flux = []
    for k in range(nf):
        value, slope = mine[32 * k : 32 * k + 16], mine[32 * k + 16 : 32 * k + 32]
        other, other_slope = outer[32 * k : 32 * k + 16], outer[32 * k + 16 : 32 * k + 32]
        flux.append(
            weight * (jump * value - jump_out * other - area * slope + area_out * other_slope)
        )
        flux.append(weight * (area_out * other - area * value))
    flux = fields_case(interp_ref[...], jnp.concatenate(flux, axis=0), case.astype(i32), nf)
    high, low = two(flux)
    got = dot_t(jnp.concatenate([high, low], axis=0), hot)
    return got[: 32 * nf] + got[32 * nf :]


def halo_coefs(coef, size, other_coef, other_size):
    least = jnp.minimum(size, other_size)
    return 16.0 * (coef + other_coef) * least, 0.5 * least * least


def flux_kernel(
    nf, chips, one_ref, two_ref, mine_ref, other_ref, info_ref, arrival_ref, weight_ref, interp_ref,
    own_hot_ref, *rest,
):
    h = 32 * nf
    core, near, far, end, near_there, far_there = where_am_i(chips)
    lane = lax.broadcasted_iota(i32, (1, lanes), 1)
    two_away = two_ref[...]
    kept = jnp.where(lane < 72, two_away, pltpu.roll(two_away, 72, 1))
    inside = (lane >= 48) & (lane < 96) & ~(end & (core == 1))
    got = jnp.concatenate(
        [jnp.where(inside, kept, one_ref[:, 0:128]), one_ref[:, 128:256]], axis=1
    )
    if got.shape[0] > h:
        sum_ref, halo_ref = rest
        halo = halo_coefs(
            arrival_ref[1:2, 0:256], arrival_ref[2:3, 0:256], got[h : h + 1], got[h + 1 : h + 2]
        )
        halo_ref[...] = rows_of(halo, 8, 256)
    else:
        halo_ref, sum_ref = rest
        halo = halo_ref[0:1], halo_ref[1:2]
    coefs = [
        jnp.concatenate([info_ref[k : k + 1, 0:side_pad], halo[k // 2]], axis=1) for k in range(4)
    ]
    outer = jnp.concatenate([other_ref[...], got[0:h]], axis=1)
    sum_ref[...] = side_flux(
        nf, mine_ref, outer, coefs, info_ref[4:5], weight_ref, interp_ref, own_hot_ref[...]
    )


def solve_blocks(inverse_ref, hold_ref, nf):
    sums = [jnp.zeros((64, lanes), f32) for _ in range(nf)]
    for col in range(64):
        block = inverse_ref[col].astype(f32)
        for k in range(nf):
            sums[k] = sums[k] + block * hold_ref[64 * k + col : 64 * k + col + 1, :]
    return sums


def update_kernel(
    nf, nf_next, residual,
    one_ref, local_ref, target_ref, arrival_ref, far_hot_ref, weight_ref, interp_t_ref, lift_ref,
    field_ref, coef_ref, level_ref, inverse_ref, *rest,
):
    if residual:
        rhs_ref, *rest = rest
    else:
        halo_ref, *rest = rest
    if nf_next:
        trace_ref, interp_ref, hot_ref, case_ref, new_ref, stack_ref, sent_ref, *rest = rest
    else:
        new_ref, part_ref, *rest = rest
    hold_ref = rest[-1]
    h = 32 * nf
    if residual:
        halo = halo_coefs(
            arrival_ref[1:2, 256:640], arrival_ref[2:3, 256:640],
            one_ref[h : h + 1], one_ref[h + 1 : h + 2],
        )
        rest[0][...] = rows_of(halo, 8, 384)
    else:
        halo = (halo_ref[0:1], halo_ref[1:2])
    total = local_ref[...] + side_flux(
        nf, target_ref, one_ref, (halo[0], halo[0], halo[1], halo[1]), arrival_ref[0:1, 256:640],
        weight_ref, interp_t_ref, far_hot_ref[...],
    )
    coef, size, volume_scale, normal_scale = element_rows(coef_ref, level_ref)
    row = lax.broadcasted_iota(i32, (32, lanes), 0)
    scale = jnp.where(row < 16, 1.0, jnp.broadcast_to(normal_scale, (32, lanes)))
    operands = []
    for k in range(nf):
        mine = total[32 * k : 32 * k + 32]
        faces = jnp.concatenate(
            [mine[:, lanes * f : lanes * f + lanes] * scale for f in range(6)], axis=0
        )
        high, low = two(faces)
        field_high, field_low = two(field_ref[64 * k : 64 * k + 64] * volume_scale)
        operands.append(
            jnp.concatenate([high, low, high, field_high, field_low, field_high], axis=0)
        )
    image = dot(lift_ref[...], cat(operands, 1))
    for k in range(nf):
        part = image[:, lanes * k : lanes * k + lanes]
        if residual and k == 1:
            part = rhs_ref[...] - part
        hold_ref[64 * k : 64 * k + 64, :] = part
    new = solve_blocks(inverse_ref, hold_ref, nf)
    for k in range(nf):
        new_ref[64 * k : 64 * k + 64, :] = new[k]
    if nf_next:
        stack = face_stack(trace_ref, new[:nf_next], normal_scale, nf_next)
        stack_ref[...] = stack
        sent = gather_message(stack, hot_ref[...], interp_ref[...], case_ref[0:1], nf_next)
        sent_ref[...] = sent
    else:
        before, after = field_ref[...], new[0]
        before = jnp.sum(jnp.sum(before * before, axis=1, keepdims=True), axis=0, keepdims=True)
        after = jnp.sum(jnp.sum(after * after, axis=1, keepdims=True), axis=0, keepdims=True)
        lane = lax.broadcasted_iota(i32, part_ref.shape, 1)
        part_ref[...] = jnp.where(lane == 0, before, jnp.where(lane == 1, after, 0.0))


def finish_kernel(part_ref, guess_ref, first_ref, second_ref, out_ref, bound_ref):
    total = jnp.sum(part_ref[...], axis=0, keepdims=True)
    bound = jnp.sqrt(total[:, 1:2] / total[:, 0:1])
    upper = 1.2 * bound
    lower = upper / 15.0
    center = 0.5 * (upper + lower)
    half = 0.5 * (upper - lower)
    ratio = center / half
    damping = 1.0 / ratio
    damping_next = 1.0 / (2.0 * ratio - damping)
    first = first_ref[64:128] / center
    second = first_ref[64:128] - second_ref[64:128] / center
    out_ref[...] = (
        guess_ref[...] + first + (damping_next * damping * first + 2.0 * damping_next / half * second)
    )
    bound_ref[...] = jnp.broadcast_to(bound, (1, lanes))


def in_vmem(x):
    return pltpu.with_memory_space_constraint(x, pltpu.VMEM)


def in_hbm(x):
    return pltpu.with_memory_space_constraint(x, pltpu.HBM)


def run(body, outs, ins, name, scratch=(), flops=1 << 24, placed=True, kept=True):
    spec = pl.BlockSpec(memory_space=pltpu.VMEM)
    return pl.pallas_call(
        body,
        out_shape=[(pltpu.VMEM if kept else jax.ShapeDtypeStruct)(shape, dtype) for shape, dtype in outs],
        in_specs=[spec if placed else pl.BlockSpec(memory_space=pltpu.HBM)] * len(ins),
        out_specs=[spec] * len(outs),
        scratch_shapes=list(scratch),
        compiler_params=pltpu.CompilerParams(vmem_limit_bytes=24 << 20),
        cost_estimate=pl.CostEstimate(flops=flops, bytes_accessed=1 << 20, transcendentals=0),
        name=name,
    )(*(in_vmem(x) if placed else in_hbm(x) for x in ins))


def local(
    rhs_field, initial_guess, start_vector, coefficient, refine_level, block_inverse,
    side_elem, side_dir, side_case, side_kind, partner, send_list,
):
    devices = lax.axis_size("dom")
    chips = devices // 2
    trace, interp, interp_t, lift, weight = (jnp.asarray(t) for t in const_tables())
    coef = coefficient.reshape(1, lanes)
    level = refine_level.reshape(1, lanes)

    def permute(x, to):
        return lax.ppermute(x, "dom", sorted(to.items()))

    swapped = {i: i ^ 1 for i in range(devices)}
    two_away, one_away = {}, {}
    for c in range(chips):
        two_away[2 * c] = 2 * (c ^ 2)
        one_away[2 * c] = 2 * (c ^ 1)
        over = c + 2 if c % 4 >= 2 else c - 2
        two_away[2 * c + 1] = 2 * (over if 0 <= over < chips else c ^ 1) + 1
        if 0 < c < chips - 1:
            one_away[2 * c + 1] = 2 * (c + 1 if c % 2 else c - 1) + 1
    for c in (0, chips - 1):
        one_away[2 * (c ^ 1)] = 2 * c + 1
        one_away[2 * c + 1] = 2 * c

    def exchange(sent, nf, own_work, work):
        rows = sent.shape[0]
        (own,) = own_work()
        two_out, one_out = run(
            carry_kernel, [((rows, lanes), f32), ((rows, 256), f32)], [permute(sent, swapped), own],
            "carry",
        )
        arrivals = permute(one_out, one_away), permute(two_out, two_away)
        made = work()
        (last,) = run(
            functools.partial(relay_kernel, chips), [((rows, 384), f32)],
            [*arrivals, own, *made[:1]], "relay",
        )
        return arrivals, permute(last, swapped), made

    sides = [x.reshape(1, -1) for x in (side_elem, side_dir, side_case, side_kind, partner)]
    first = [*sides, send_list, start_vector, initial_guess, coef, level, trace, interp]
    hot, case, stack, sides, rolled, sent, coef, level, trace, interp = run(
        functools.partial(send_setup_kernel, chips),
        [((768, 256), bf16), ((8, 256), i32), ((144, 768), bf16), ((8, side_pad), i32), ((32, lanes), i32),
         ((72, 256), f32), *((x.shape, x.dtype) for x in first[8:])],
        first,
        "send_setup",
        scratch=[
            pltpu.VMEM((8, 256), i32),
            *(pltpu.VMEM(x.shape, x.dtype) for x in first[:8]), pltpu.SemaphoreType.DMA((len(first),)),
        ],
        placed=False,
    )
    own_slots = run(
        functools.partial(own_setup_kernel, chips),
        [((768, 512), bf16), ((8, 512), i32)],
        [sides, rolled],
        "own_setup",
        scratch=[pltpu.VMEM((8, 512), i32)],
    )
    fields = jnp.concatenate([start_vector, initial_guess], axis=0)
    history = []
    for turn, nf in enumerate((2, 2, 1, 1)):
        h = 32 * nf
        def own_work():
            return run(
                functools.partial(own_kernel, nf),
                [((sent.shape[0], 512), f32)],
                [stack, *own_slots, interp],
                "own",
            )

        def side_work():
            return run(
                functools.partial(sides_kernel, nf),
                [((h, side_pad + 256), f32), ((h, side_pad), f32), ((h, 384), f32)],
                [stack, interp, own_hot, partner_hot, far_hot, info, arrival],
                "sides",
            )

        def first_work():
            return run(
                functools.partial(setup_kernel, chips),
                [((8, side_pad + 256), f32), ((768, side_pad + 256), bf16), ((768, side_pad), bf16),
                 ((768, 384), bf16), ((8, 640), f32)],
                [coef, level, sides],
                "setup",
                scratch=[pltpu.VMEM((640, side_pad), bf16)],
            )

        arrivals, last, made = exchange(sent, nf, own_work, side_work if turn else first_work)
        if turn == 0:
            info, own_hot, partner_hot, far_hot, arrival = made
            made = side_work()
        mine, others, targets = made
        sums, *made = run(
            functools.partial(flux_kernel, nf, chips),
            [((h, 768), f32)] + ([] if turn else [((8, 256), f32)]),
            [*arrivals, mine, others, info, arrival, weight, interp_t, own_hot]
            + ([near_halo] if turn else []),
            "flux",
        )
        if turn == 0:
            near_halo = made[0]
        nf_next = (2, 1, 1, 0)[turn]
        ins = [
            last, sums, targets, arrival, far_hot, weight, interp_t, lift,
            fields, coef, level, block_inverse, far_halo if turn else rhs_field,
        ]
        outs = [((64 * nf, lanes), f32)]
        if nf_next:
            ins += [trace, interp, hot, case]
            outs += [((64 * nf_next, 768), bf16), ((32 * nf_next, 256), f32)]
        else:
            outs += [((devices, lanes), f32)]
        made = run(
            functools.partial(update_kernel, nf, nf_next, turn == 0),
            outs + ([] if turn else [((8, 384), f32)]), ins, "update",
            scratch=[pltpu.VMEM((64 * nf, lanes), f32)],
        )
        if turn == 0:
            far_halo = made[-1]
        if nf_next:
            fields, stack, sent = made[:3]
            history.append(fields)
            if nf_next < nf:
                fields = fields[:64]
        else:
            fields, parts = made
    parts = lax.all_to_all(parts.reshape(devices, 1, lanes), "dom", 0, 0).reshape(devices, lanes)
    smoothed, bound = run(
        finish_kernel,
        [((64, lanes), f32), ((1, lanes), f32)],
        [parts, initial_guess, history[0], history[1]],
        "finish",
        kept=False,
    )
    return smoothed, bound[0, 0]


def solution(mesh):
    placed = (
        P(None, "dom"), P(None, "dom"), P(None, "dom"), P("dom"), P("dom"), P(None, None, "dom"),
        P("dom"), P("dom"), P("dom"), P("dom"), P("dom"), P("dom", None),
    )
    return jax.shard_map(
        local, mesh=mesh, in_specs=placed, out_specs=(P(None, "dom"), P()), check_vma=False
    )
```

```python
import functools
import math

import jax
import jax.numpy as jnp
import numpy as np
from jax import lax
from jax.experimental import pallas as pl
from jax.experimental.pallas import tpu as pltpu
from jax.sharding import PartitionSpec as P

f32 = jnp.float32
bf16 = jnp.bfloat16
i32 = jnp.int32
peer_offsets = (1, -1, 2, -2, 3, -3, 4, -4)
live_width = {1: 96, 2: 48, 3: 24, 4: 24}
lanes = 128
shifts = (0, 24, 48, 96)
side_pad = 1024


def lagrange_tables():
    root_five = 1.0 / math.sqrt(5.0)
    nodes = np.array([0.0, 0.5 - 0.5 * root_five, 0.5 + 0.5 * root_five, 1.0])
    weights = np.array([1.0, 5.0, 5.0, 1.0]) / 12.0
    factor = np.array(
        [np.prod([nodes[i] - nodes[j] for j in range(4) if j != i]) for i in range(4)]
    )
    derivative = np.zeros((4, 4))
    for i in range(4):
        for j in range(4):
            if i != j:
                derivative[i, j] = factor[i] / (factor[j] * (nodes[i] - nodes[j]))
        derivative[i, i] = -np.sum(derivative[i])
    halves = []
    for half in range(2):
        points = 0.5 * (nodes + half)
        table = np.ones((4, 4))
        for j in range(4):
            for other in range(4):
                if other != j:
                    table[:, j] *= (points - nodes[other]) / (nodes[j] - nodes[other])
        halves.append(table)
    return weights, derivative, halves


def basis_tables():
    weights, derivative, halves = lagrange_tables()
    mass = np.diag(weights)
    line = derivative.T @ mass @ derivative
    stiffness = (
        np.kron(np.kron(line, mass), mass)
        + np.kron(np.kron(mass, line), mass)
        + np.kron(np.kron(mass, mass), line)
    )
    trace = np.zeros((6, 32, 64))
    for dim in range(3):
        others = [d for d in range(3) if d != dim]
        for lower in range(2):
            face = 2 * dim + lower
            fixed = 0 if lower else 3
            sign = -1.0 if lower else 1.0
            for first in range(4):
                for second in range(4):
                    node = first * 4 + second
                    for along in range(4):
                        place = [0, 0, 0]
                        place[others[0]] = first
                        place[others[1]] = second
                        place[dim] = along
                        nodal = place[0] * 16 + place[1] * 4 + place[2]
                        if along == fixed:
                            trace[face, node, nodal] = 1.0
                        trace[face, 16 + node, nodal] = sign * derivative[fixed, along]
    quarter = [np.kron(halves[q // 2], halves[q % 2]) for q in range(4)]
    both = np.eye(2)
    interp = np.concatenate([np.kron(both, q) for q in quarter], axis=0)
    interp_t = np.concatenate([np.kron(both, q.T) for q in quarter], axis=0)
    face_weight = np.kron(weights, weights)
    return stiffness, trace.reshape(192, 64), interp, interp_t, face_weight


def stacked(table):
    table = np.asarray(table, np.float32)
    high = table.astype(jnp.bfloat16)
    low = (table - high.astype(np.float32)).astype(jnp.bfloat16)
    return np.concatenate([high, high, low], axis=1)


def const_tables():
    stiffness, trace, interp, interp_t, face_weight = basis_tables()
    lift = np.concatenate([stacked(trace.T), stacked(stiffness)], axis=1)
    weight = np.broadcast_to(np.concatenate([face_weight, face_weight])[:, None], (32, lanes))
    return (
        stacked(trace),
        stacked(interp),
        stacked(interp_t),
        lift,
        np.asarray(weight, np.float32),
    )


def two(x):
    high = x.astype(bf16)
    return high, (x - high.astype(f32)).astype(bf16)


def three(x):
    high = x.astype(bf16)
    rest = x - high.astype(f32)
    mid = rest.astype(bf16)
    return high, mid, (rest - mid.astype(f32)).astype(bf16)


def dot(a, b):
    return jnp.dot(a, b, preferred_element_type=f32)


def dot_t(a, b):
    return lax.dot_general(a, b, (((1,), (1,)), ((), ())), preferred_element_type=f32)


def cat(parts, axis):
    return parts[0] if len(parts) == 1 else jnp.concatenate(parts, axis=axis)


def table_dot(table, x):
    high, low = two(x)
    return dot(table, jnp.concatenate([high, low, high], axis=0))


def apply_case(table, x, case):
    quarters = table_dot(table, x)
    out = x
    for c in range(4):
        out = jnp.where(case == c, quarters[32 * c : 32 * c + 32], out)
    return out


def fields_case(table, x, case, nf):
    wide = cat([x[32 * k : 32 * k + 32] for k in range(nf)], 1)
    out = apply_case(table, wide, cat([case] * nf, 1))
    n = x.shape[1]
    return cat([out[:, n * k : n * k + n] for k in range(nf)], 0)


def rows_of(rows, count, width):
    place = lax.broadcasted_iota(i32, (count, width), 0)
    table = jnp.zeros((count, width), f32)
    for k, r in enumerate(rows):
        table = jnp.where(place == k, r, table)
    return table


def one_hot(index_row, rows, first=0):
    place = lax.broadcasted_iota(i32, (rows, index_row.shape[1]), 0) + first
    return jnp.where(place == index_row, 1.0, 0.0).astype(bf16)


def gather_columns(stack, hot, face, nf):
    h = 32 * nf
    if hot.shape[0] == 768:
        got = dot(stack, hot)
        return got[:h] + got[h:]
    parts = [stack[:, lanes * f : lanes * f + lanes] for f in range(6)]
    got = dot(jnp.concatenate(parts, axis=0), hot)
    out = got[:h] + got[h : 2 * h]
    for f in range(1, 6):
        low = 2 * h * f
        out = jnp.where(face == f, got[low : low + h] + got[low + h : low + 2 * h], out)
    return out


def scatter_columns(x, hot, face, nf):
    h = 32 * nf
    high, low = two(x)
    both = jnp.concatenate([high, low], axis=0)
    if hot.shape[1] == 768:
        got = dot(both, hot)
        return got[:h] + got[h:]
    parts = [both * jnp.where(face == f, 1.0, 0.0).astype(bf16) for f in range(6)]
    got = dot_t(jnp.concatenate(parts, axis=0), hot)
    return jnp.concatenate(
        [got[2 * h * f : 2 * h * f + h] + got[2 * h * f + h : 2 * h * f + 2 * h] for f in range(6)],
        axis=1,
    )


def element_rows(coef_ref, level_ref):
    coef = coef_ref[...]
    level = level_ref[...]
    size = jnp.where(level == 0, 1.0, jnp.where(level == 1, 0.5, 0.25)).astype(f32)
    inverse = jnp.where(level == 0, 1.0, jnp.where(level == 1, 2.0, 4.0)).astype(f32)
    return coef, size, coef * size, coef * inverse


def face_stack(trace_ref, u, normal_scale, nf):
    faces = table_dot(trace_ref[...], cat(u, 1))
    row = lax.broadcasted_iota(i32, (32, lanes), 0)
    scale = jnp.where(row < 16, 1.0, jnp.broadcast_to(normal_scale, (32, lanes)))
    fields = []
    for k in range(nf):
        part = faces[:, lanes * k : lanes * k + lanes]
        fields.append(
            jnp.concatenate([part[32 * f : 32 * f + 32] * scale for f in range(6)], axis=1)
        )
    high, low = two(cat(fields, 0))
    return jnp.concatenate([high, low], axis=0)


def gather_message(stack, hot, interp, case, nf):
    got = dot(stack, hot)
    h = 32 * nf
    out = fields_case(interp, got[:h] + got[h : 2 * h], case, nf)
    if stack.shape[0] == 2 * h:
        return out
    coef = got[2 * h : 2 * h + 1] + got[2 * h + 1 : 2 * h + 2] + got[2 * h + 2 : 2 * h + 3]
    size = got[2 * h + 3 : 2 * h + 4] * jnp.where((case >= 0) & (case < 4), 0.5, 1.0)
    row = lax.broadcasted_iota(i32, (8, out.shape[1]), 0)
    scalars = jnp.where(row == 0, coef, jnp.where(row == 1, size, 0.0))
    return jnp.concatenate([out, scalars], axis=0)


def where_am_i(chips):
    me = lax.axis_index("dom")
    chip = me // 2
    core = me - 2 * chip
    near = jnp.where(lax.rem(chip, 2) == 1, -1, 1)
    far = jnp.where(lax.rem(chip, 4) < 2, 1, -1)
    end = (chip == 0) | (chip == chips - 1)
    far_there = (chip - 2 * far >= 0) & (chip - 2 * far < chips)
    return core, near, far, end, ~end, far_there


def carried(core, near, far, near_there, far_there):
    first = core == 0
    return (
        jnp.where(first, near, -near), jnp.where(first, far, -far),
        first | near_there, first | far_there,
    )


def row_of(offset):
    size = jnp.abs(offset)
    return 2 * (size - 1) + jnp.where(offset < 0, 1, 0)


def narrow(offset):
    return jnp.abs(offset) == 3


def side_attributes(side_ref, more=()):
    live = lax.broadcasted_iota(i32, (1, side_pad), 1) < 930
    rows = [jnp.where(live, side_ref[k : k + 1], 0).astype(f32) for k in range(3)]
    rows.append(jnp.where(live, 1.0, 0.0))
    return rows_of(rows + list(more), 16, side_pad).astype(bf16)


def look_up(attributes, index):
    blocks = jnp.concatenate(
        [attributes[:, lanes * k : lanes * k + lanes] for k in range(side_pad // lanes)], axis=0
    )
    found = dot(blocks, one_hot(index & 127, lanes))
    block = index >> 7
    out = jnp.zeros((8, index.shape[1]), f32)
    for k in range(side_pad // lanes):
        out = jnp.where(block == k, found[16 * k : 16 * k + 8], out)
    return out


def place_of(found):
    valid = found[3:4] > 0.5
    return tuple(jnp.where(valid, found[k : k + 1], -1.0).astype(i32) for k in range(3))


def fill_one_hot(hot_ref, elem, face):
    hot = one_hot(elem, lanes)
    for f in range(6):
        hot_ref[lanes * f : lanes * f + lanes] = hot * jnp.where(face == f, 1.0, 0.0).astype(bf16)


def listed_part(rolled_ref, shift, offset, low, high, valid):
    place = shifts.index(shift)
    lane = lax.broadcasted_iota(i32, (1, lanes), 1)
    values = rolled_ref[pl.ds(8 * place + jnp.minimum(row_of(offset), 7), 1), :]
    return jnp.where((lane >= low) & (lane < high) & valid, values, -1)


def send_setup_kernel(chips, *refs):
    sources, refs = refs[:12], refs[12:]
    hot_ref, case_ref, stack_ref, side_ref, rolled_ref = refs[:5]
    sent_ref, landed = refs[5], (*refs[12:19], *refs[6:11])
    slot_ref, arrived = refs[11], refs[19]
    copies = [
        pltpu.make_async_copy(source, target, arrived.at[k])
        for k, (source, target) in enumerate(zip(sources, landed))
    ]
    for copy in copies:
        copy.start()
    elem_ref, dir_ref, sidecase_ref, kind_ref, partner_ref, list_ref = landed[:6]
    start_ref, coef_ref, level_ref, trace_ref, interp_ref = landed[6:11]
    for copy in copies:
        copy.wait()
    side_ref[...] = jnp.full((8, side_pad), -1, i32)
    sides = elem_ref.shape[1]
    for k, ref in enumerate((elem_ref, dir_ref, sidecase_ref, kind_ref, partner_ref)):
        side_ref[k : k + 1, 0:sides] = ref[...]
    core, near, far, end, near_there, far_there = where_am_i(chips)
    listed = jnp.concatenate([list_ref[...], jnp.full((8, 32), -1, i32)], axis=1)
    for place, shift in enumerate(shifts):
        rolled_ref[8 * place : 8 * place + 8] = (
            pltpu.roll(listed, shift, 1) if shift else listed
        )
    part = functools.partial(listed_part, rolled_ref)
    other = 1 - core
    step, step_two, there, there_two = carried(other, near, far, near_there, far_there)
    cross, cross_two = 2 * step + other - core, 4 * step_two + other - core
    first = (
        part(0, cross_two, 0, 24, there_two & narrow(cross_two)),
        part(24, 4 * step_two, 24, 48, there_two),
        part(48, 2 * step, 48, 96, there),
        part(96, cross, 96, 120, there & narrow(cross)),
    )
    slot_ref[0:1, 0:128] = functools.reduce(jnp.maximum, first)
    slot_ref[0:1, 128:256] = part(0, cross, 0, 96, there & ~narrow(cross))
    elem, face, slot_case = place_of(look_up(side_attributes(side_ref), slot_ref[0:1, :]))
    case_ref[0:1, :] = slot_case
    fill_one_hot(hot_ref, elem, face)

    coef, size, volume_scale, normal_scale = element_rows(coef_ref, level_ref)
    stack = face_stack(trace_ref, [start_ref[...]], normal_scale, 1)
    scalars = rows_of([x.astype(f32) for x in three(coef)] + [size], 16, lanes).astype(bf16)
    stack = jnp.concatenate([stack, jnp.concatenate([scalars] * 6, axis=1)], axis=0)
    stack_ref[...] = stack
    sent = gather_message(stack, hot_ref[...], interp_ref[...], slot_case, 1)
    sent_ref[...] = sent


def own_setup_kernel(chips, side_ref, rolled_ref, hot_ref, case_ref, slot_ref):
    core, near, far, end, near_there, far_there = where_am_i(chips)
    part = functools.partial(listed_part, rolled_ref)
    flip = 1 - 2 * core
    step, step_two, there, there_two = carried(core, near, far, near_there, far_there)
    cross, cross_two = 2 * step + flip, 4 * step_two + flip
    slot_ref[0:1, 0:128] = jnp.maximum(
        part(0, 4 * step_two, 0, 24, there_two),
        part(24, cross_two, 24, 48, there_two & narrow(cross_two)),
    )
    slot_ref[0:1, 128:256] = jnp.maximum(
        part(0, 2 * step, 0, 48, there), part(96, cross, 96, 120, there & narrow(cross))
    )
    slot_ref[0:1, 256:384] = part(0, cross, 0, 96, there & ~narrow(cross))
    slot_ref[0:1, 384:512] = part(0, flip, 0, 96, core >= 0)
    elem, face, slot_case = place_of(look_up(side_attributes(side_ref), slot_ref[0:1, :]))
    case_ref[0:1, :] = slot_case
    fill_one_hot(hot_ref, elem, face)


def own_kernel(nf, stack_ref, hot_ref, case_ref, interp_ref, own_ref):
    own_ref[...] = gather_message(
        stack_ref[...], hot_ref[...], interp_ref[...], case_ref[0:1], nf
    )


def carry_kernel(sent_ref, own_ref, *rest):
    two_ref, one_ref = rest[-2:]
    lane = lax.broadcasted_iota(i32, (1, lanes), 1)
    sent = sent_ref[:, 0:128]
    handed = jnp.where((lane >= 48) & (lane < 96), pltpu.roll(sent, 48, 1), 0.0)
    two_ref[...] = own_ref[:, 0:128] + handed
    one_ref[:, 0:128] = own_ref[:, 128:256] + jnp.where(lane >= 48, sent, 0.0)
    one_ref[:, 128:256] = own_ref[:, 256:384] + sent_ref[:, 128:256]


def relay_kernel(chips, one_ref, two_ref, own_ref, *rest):
    out_ref = rest[-1]
    core, near, far, end, near_there, far_there = where_am_i(chips)
    lane = lax.broadcasted_iota(i32, (1, lanes), 1)
    one, two_away = one_ref[:, 0:128], two_ref[...]
    out_ref[:, 0:128] = own_ref[:, 384:512]
    passed = jnp.where(lane < 24, pltpu.roll(two_away, 56, 1), two_away)
    out_ref[:, 128:256] = jnp.where((lane < 48) & ~(end & (core == 1)), passed, one)
    out_ref[:, 256:384] = one_ref[:, 128:256]


def setup_kernel(
    chips, coef_ref, level_ref, side_ref,
    own_hot_ref, partner_hot_ref, far_hot_ref, place_ref, info_ref, arrival_ref,
):
    core, near, far, end, near_there, far_there = where_am_i(chips)
    elem, direction, case = side_ref[0:1], side_ref[1:2], side_ref[2:3]
    kind, partner = side_ref[3:4], side_ref[4:5]
    live = lax.broadcasted_iota(i32, (1, side_pad), 1) < 930

    coef, size, volume_scale, normal_scale = element_rows(coef_ref, level_ref)
    scalars = rows_of([x.astype(f32) for x in three(coef)] + [size], 16, lanes)
    mine = dot(scalars.astype(bf16), one_hot(elem, lanes))
    hanging = (case >= 0) & (case < 4)
    own_coef = mine[0:1] + mine[1:2] + mine[2:3]
    own_size = mine[3:4] * jnp.where(hanging, 0.5, 1.0)

    attributes = side_attributes(side_ref, (mine[0:1], mine[1:2], mine[2:3], own_size))
    here = live & (partner < 930)
    other = look_up(attributes, jnp.where(here, partner, -1))
    other_elem, other_face = place_of(other)[:2]
    partner_hot_ref[...] = one_hot(other_elem, lanes)
    valid = other[3:4] > 0.5
    edge = jnp.where(kind == 1, 1.0, 0.0)
    least = jnp.where(valid, jnp.minimum(own_size, other[7:8]), 0.0)
    jump = 16.0 * (own_coef + other[4:5] + other[5:6] + other[6:7]) * least
    area = least * least
    info_ref[:, 0:side_pad] = rows_of(
        [jump, jump * (1.0 - edge), area * (0.5 + 0.5 * edge), area * (0.5 - 0.5 * edge),
         case.astype(f32), other[2:3]],
        8, side_pad,
    )

    def arrives(carrier):
        last = end & (carrier == 1)
        back = jnp.where((carrier == 0) | end, -near, near)
        back_two = jnp.where(carrier == 0, -far, far)
        turn = 2 * core - 1
        return (
            2 * back, 2 * back + turn, 4 * back_two, 4 * back_two + turn,
            ~(end & (carrier == 0)), ~last, last,
        )

    def span(low, high, valid):
        return low, jnp.where(valid, high, low)

    segments = []
    for mine, carrier in ((True, core), (False, 1 - core)):
        straight, cross, straight_two, cross_two, there, there_two, last = arrives(carrier)
        slim, wide = there & narrow(cross), there & ~narrow(cross)
        at_first = (last & (core != 1)) | (~last & (carrier == core))
        if mine:
            two_parts = ((*span(48, 72, there_two & narrow(cross_two)), cross_two),
                         (*span(72, 96, there_two), straight_two))
        else:
            segments.append(((0, 96, 2 * core - 1),))
            two_parts = ((*span(0, 24, there_two), straight_two),
                         (*span(24, 48, there_two & narrow(cross_two)), cross_two))
        segments.append((
            (*span(0, 48, there & at_first), straight), (*span(48, 96, there & ~at_first), straight),
            (*span(96, 120, slim), cross), *two_parts,
        ))
        segments.append(((*span(0, 96, wide), cross),))
    entry = partner - 930
    peer = (entry * 683) >> 16
    entry = entry - 96 * peer
    sought = live & (partner >= 930) & (kind == 0)
    column = jnp.full((1, side_pad), -1, i32)
    for tile, parts in enumerate(segments):
        for low, high, offset in parts:
            match = sought & (peer == row_of(offset)) & (entry < high - low)
            column = jnp.where(match, lanes * tile + low + entry, column)
    block = column >> 7
    split = [
        attributes * jnp.where(block == tile, 1.0, 0.0).astype(bf16) for tile in range(len(segments))
    ]
    target = dot_t(jnp.concatenate(split, axis=0), one_hot(column & 127, lanes))
    target = jnp.concatenate(
        [target[16 * tile : 16 * tile + 8] for tile in range(len(segments))], axis=1
    )
    target_elem, target_face, target_case = place_of(target)
    elems = jnp.concatenate([elem, target_elem], axis=1)
    faces = jnp.concatenate([direction, target_face], axis=1)
    near = side_pad + 256
    own_hot_ref[...] = one_hot(elems[:, :near], lanes)
    far_hot_ref[...] = one_hot(elems[:, near:], lanes)
    other_face = jnp.concatenate([other_face, jnp.full((1, 640), -1, i32)], axis=1)
    place_ref[...] = rows_of(
        [elems.astype(f32), faces.astype(f32), other_face.astype(f32)], 16, elems.shape[1]
    )
    info_ref[:, side_pad:] = rows_of(
        [jnp.zeros((1, 256), f32)] * 4 + [target_case[:, 0:256].astype(f32)], 8, 256
    )
    arrival_ref[...] = rows_of(
        [target_case.astype(f32), target[4:5] + target[5:6] + target[6:7], target[7:8]],
        8, 640,
    )


def whole_kernel(own_elem_ref, partner_elem_ref, far_elem_ref, place_ref, own_ref, partner_ref, far_ref):
    near = side_pad + 256
    for source, row, low, high, target in (
        (own_elem_ref, 1, 0, near, own_ref),
        (partner_elem_ref, 2, 0, side_pad, partner_ref),
        (far_elem_ref, 1, near, near + 384, far_ref),
    ):
        hot, face = source[...], place_ref[row : row + 1, low:high]
        for f in range(6):
            target[lanes * f : lanes * f + lanes] = hot * jnp.where(face == f, 1.0, 0.0).astype(bf16)


def turn_kernel(place_ref, own_ref, far_ref):
    row = lax.broadcasted_iota(i32, (16, lanes), 0)
    weight = jnp.where(row == 0, 1.0, jnp.where(row == 1, 128.0, 0.0)).astype(bf16)
    column = lax.dot_general(
        place_ref[...].astype(bf16), weight, (((0,), (0,)), ((), ())), preferred_element_type=f32
    )
    lane = lax.broadcasted_iota(i32, (1, lanes), 1).astype(f32)
    split = own_ref.shape[0]
    for f in range(6):
        part = jnp.where(column == lane + 128.0 * f, 1.0, 0.0).astype(bf16)
        own_ref[:, lanes * f : lanes * f + lanes] = part[:split]
        far_ref[:, lanes * f : lanes * f + lanes] = part[split:]


def sides_kernel(
    nf, stack_ref, interp_ref, own_hot_ref, partner_hot_ref, far_hot_ref, place_ref, info_ref,
    arrival_ref, mine_ref, other_ref, target_ref,
):
    stack = stack_ref[0 : 64 * nf]
    near = side_pad + 256
    for hot_ref, face, case, out_ref in (
        (own_hot_ref, place_ref[1:2, 0:near], info_ref[4:5], mine_ref),
        (partner_hot_ref, place_ref[2:3, 0:side_pad], info_ref[5:6, 0:side_pad], other_ref),
        (far_hot_ref, place_ref[1:2, near:], arrival_ref[0:1, 256:640], target_ref),
    ):
        got = gather_columns(stack, hot_ref[...], face, nf)
        out_ref[...] = fields_case(interp_ref[...], got, case.astype(i32), nf)


def side_flux(nf, mine, outer, coefs, case, face, weight_ref, interp_ref, hot):
    jump, jump_out, area, area_out = coefs
    weight = weight_ref[0:16, 0:1]
    flux = []
    for k in range(nf):
        value, slope = mine[32 * k : 32 * k + 16], mine[32 * k + 16 : 32 * k + 32]
        other, other_slope = outer[32 * k : 32 * k + 16], outer[32 * k + 16 : 32 * k + 32]
        flux.append(
            weight * (jump * value - jump_out * other - area * slope + area_out * other_slope)
        )
        flux.append(weight * (area_out * other - area * value))
    flux = fields_case(interp_ref[...], jnp.concatenate(flux, axis=0), case.astype(i32), nf)
    return scatter_columns(flux, hot, face, nf)


def halo_coefs(coef, size, other_coef, other_size):
    least = jnp.minimum(size, other_size)
    return 16.0 * (coef + other_coef) * least, 0.5 * least * least


def flux_kernel(
    nf, chips, one_ref, two_ref, mine_ref, other_ref, place_ref, info_ref, arrival_ref, weight_ref, interp_ref,
    own_hot_ref, *rest,
):
    h = 32 * nf
    core, near, far, end, near_there, far_there = where_am_i(chips)
    lane = lax.broadcasted_iota(i32, (1, lanes), 1)
    two_away = two_ref[...]
    kept = jnp.where(lane < 72, two_away, pltpu.roll(two_away, 72, 1))
    inside = (lane >= 48) & (lane < 96) & ~(end & (core == 1))
    got = jnp.concatenate(
        [jnp.where(inside, kept, one_ref[:, 0:128]), one_ref[:, 128:256]], axis=1
    )
    if got.shape[0] > h:
        sum_ref, halo_ref = rest
        halo = halo_coefs(
            arrival_ref[1:2, 0:256], arrival_ref[2:3, 0:256], got[h : h + 1], got[h + 1 : h + 2]
        )
        halo_ref[...] = rows_of(halo, 8, 256)
    else:
        halo_ref, sum_ref = rest
        halo = halo_ref[0:1], halo_ref[1:2]
    coefs = [
        jnp.concatenate([info_ref[k : k + 1, 0:side_pad], halo[k // 2]], axis=1) for k in range(4)
    ]
    outer = jnp.concatenate([other_ref[...], got[0:h]], axis=1)
    sum_ref[...] = side_flux(
        nf, mine_ref, outer, coefs, info_ref[4:5], place_ref[1:2, 0 : side_pad + 256], weight_ref,
        interp_ref, own_hot_ref[...],
    )


def solve_blocks(inverse_ref, hold_ref, nf):
    sums = [jnp.zeros((64, lanes), f32) for _ in range(nf)]
    for col in range(64):
        block = inverse_ref[col].astype(f32)
        for k in range(nf):
            sums[k] = sums[k] + block * hold_ref[64 * k + col : 64 * k + col + 1, :]
    return sums


def update_kernel(
    turn, nf, nf_next,
    one_ref, local_ref, target_ref, place_ref, arrival_ref, far_hot_ref, weight_ref, interp_t_ref, lift_ref,
    field_ref, coef_ref, level_ref, inverse_ref, *rest,
):
    if turn == 0:
        guess_ref, *rest = rest
    else:
        halo_ref, *rest = rest
    if turn == 1:
        rhs_ref, *rest = rest
    if nf_next:
        trace_ref, interp_ref, hot_ref, case_ref, new_ref, stack_ref, sent_ref, *rest = rest
    else:
        part_ref, *rest = rest
    hold_ref = rest[-1]
    h = 32 * nf
    if turn == 0:
        halo = halo_coefs(
            arrival_ref[1:2, 256:640], arrival_ref[2:3, 256:640],
            one_ref[h : h + 1], one_ref[h + 1 : h + 2],
        )
        rest[0][...] = rows_of(halo, 8, 384)
    else:
        halo = (halo_ref[0:1], halo_ref[1:2])
    total = local_ref[...] + side_flux(
        nf, target_ref, one_ref, (halo[0], halo[0], halo[1], halo[1]), arrival_ref[0:1, 256:640],
        place_ref[1:2, side_pad + 256 :], weight_ref, interp_t_ref, far_hot_ref[...],
    )
    coef, size, volume_scale, normal_scale = element_rows(coef_ref, level_ref)
    row = lax.broadcasted_iota(i32, (32, lanes), 0)
    scale = jnp.where(row < 16, 1.0, jnp.broadcast_to(normal_scale, (32, lanes)))
    operands = []
    for k in range(nf):
        mine = total[32 * k : 32 * k + 32]
        faces = jnp.concatenate(
            [mine[:, lanes * f : lanes * f + lanes] * scale for f in range(6)], axis=0
        )
        high, low = two(faces)
        field_high, field_low = two(field_ref[64 * k : 64 * k + 64] * volume_scale)
        operands.append(
            jnp.concatenate([high, low, high, field_high, field_low, field_high], axis=0)
        )
    image = dot(lift_ref[...], cat(operands, 1))
    for k in range(nf):
        part = image[:, lanes * k : lanes * k + lanes]
        if turn == 1 and k == 1:
            part = rhs_ref[...] - part
        hold_ref[64 * k : 64 * k + 64, :] = part
    new = solve_blocks(inverse_ref, hold_ref, nf)
    if turn == 0:
        new.append(guess_ref[...])
    if nf_next:
        for k, x in enumerate(new):
            new_ref[64 * k : 64 * k + 64, :] = x
        stack = face_stack(trace_ref, new[:nf_next], normal_scale, nf_next)
        stack_ref[...] = stack
        sent = gather_message(stack, hot_ref[...], interp_ref[...], case_ref[0:1], nf_next)
        sent_ref[...] = sent
    else:
        lane = lax.broadcasted_iota(i32, (1, lanes), 1)
        sums = []
        for x in (field_ref[...], new[0]):
            total = jnp.sum(x * x, axis=0, keepdims=True)
            sums.append(total + pltpu.roll(total, 64, 1))
        part_ref[...] = jnp.broadcast_to(jnp.where(lane < 64, sums[0], sums[1]), part_ref.shape)


def finish_kernel(part_ref, guess_ref, first_ref, second_ref, out_ref, bound_ref):
    total = jnp.sum(part_ref[...], axis=0, keepdims=True)
    lane = lax.broadcasted_iota(i32, (1, lanes), 1)
    before = jnp.sum(jnp.where(lane < 64, total, 0.0), axis=1, keepdims=True)
    after = jnp.sum(jnp.where(lane < 64, 0.0, total), axis=1, keepdims=True)
    bound = jnp.sqrt(after / before)
    upper = 1.2 * bound
    lower = upper / 15.0
    center = 0.5 * (upper + lower)
    half = 0.5 * (upper - lower)
    ratio = center / half
    damping = 1.0 / ratio
    damping_next = 1.0 / (2.0 * ratio - damping)
    first = first_ref[64:128] / center
    second = first_ref[64:128] - second_ref[64:128] / center
    out_ref[...] = (
        guess_ref[...] + first + (damping_next * damping * first + 2.0 * damping_next / half * second)
    )
    bound_ref[...] = jnp.broadcast_to(bound, (1, lanes))


def in_vmem(x):
    return pltpu.with_memory_space_constraint(x, pltpu.VMEM)


def in_hbm(x):
    return pltpu.with_memory_space_constraint(x, pltpu.HBM)


def run(body, outs, ins, name, scratch=(), flops=1 << 24, placed=True, kept=True):
    spec = pl.BlockSpec(memory_space=pltpu.VMEM)
    return pl.pallas_call(
        body,
        out_shape=[(pltpu.VMEM if kept else jax.ShapeDtypeStruct)(shape, dtype) for shape, dtype in outs],
        in_specs=[spec if placed else pl.BlockSpec(memory_space=pltpu.HBM)] * len(ins),
        out_specs=[spec] * len(outs),
        scratch_shapes=list(scratch),
        compiler_params=pltpu.CompilerParams(vmem_limit_bytes=24 << 20),
        cost_estimate=pl.CostEstimate(flops=flops, bytes_accessed=1 << 20, transcendentals=0),
        name=name,
    )(*(in_vmem(x) if placed else in_hbm(x) for x in ins))


def local(
    rhs_field, initial_guess, start_vector, coefficient, refine_level, block_inverse,
    side_elem, side_dir, side_case, side_kind, partner, send_list,
):
    devices = lax.axis_size("dom")
    chips = devices // 2
    trace, interp, interp_t, lift, weight = (jnp.asarray(t) for t in const_tables())
    coef = coefficient.reshape(1, lanes)
    level = refine_level.reshape(1, lanes)

    def permute(x, to):
        return lax.ppermute(x, "dom", sorted(to.items()))

    swapped = {i: i ^ 1 for i in range(devices)}
    two_away, one_away = {}, {}
    for c in range(chips):
        two_away[2 * c] = 2 * (c ^ 2)
        one_away[2 * c] = 2 * (c ^ 1)
        over = c + 2 if c % 4 >= 2 else c - 2
        two_away[2 * c + 1] = 2 * (over if 0 <= over < chips else c ^ 1) + 1
        if 0 < c < chips - 1:
            one_away[2 * c + 1] = 2 * (c + 1 if c % 2 else c - 1) + 1
    for c in (0, chips - 1):
        one_away[2 * (c ^ 1)] = 2 * c + 1
        one_away[2 * c + 1] = 2 * c

    def exchange(sent, nf, own_work, work, *beside):
        rows = sent.shape[0]
        (own,) = own_work()
        two_out, one_out = run(
            carry_kernel, [((rows, lanes), f32), ((rows, 256), f32)],
            [permute(sent, swapped), own, *beside[:1]], "carry",
        )
        arrivals = permute(one_out, one_away), permute(two_out, two_away)
        made = work()
        (last,) = run(
            functools.partial(relay_kernel, chips), [((rows, 384), f32)],
            [*arrivals, own, made[2], *beside[1:]], "relay",
        )
        return arrivals, permute(last, swapped), made

    sides = [x.reshape(1, -1) for x in (side_elem, side_dir, side_case, side_kind, partner)]
    first = [*sides, send_list, start_vector, coef, level, trace, interp, initial_guess]
    hot, case, stack, sides, rolled, sent, coef, level, trace, interp, guess = run(
        functools.partial(send_setup_kernel, chips),
        [((768, 256), bf16), ((8, 256), i32), ((80, 768), bf16), ((8, side_pad), i32), ((32, lanes), i32),
         ((40, 256), f32), *((x.shape, x.dtype) for x in first[7:])],
        first,
        "send_setup",
        scratch=[
            pltpu.VMEM((8, 256), i32),
            *(pltpu.VMEM(x.shape, x.dtype) for x in first[:7]), pltpu.SemaphoreType.DMA((len(first),)),
        ],
        placed=False,
    )
    own_slots = run(
        functools.partial(own_setup_kernel, chips),
        [((768, 512), bf16), ((8, 512), i32)],
        [sides, rolled],
        "own_setup",
        scratch=[pltpu.VMEM((8, 512), i32)],
    )
    fields = start_vector
    history = []
    for turn, (nf, nf_next) in enumerate(((1, 2), (2, 2), (2, 1), (1, 0))):
        h = 32 * nf
        def own_work():
            return run(
                functools.partial(own_kernel, nf),
                [((sent.shape[0], 512), f32)],
                [stack, *own_slots, interp],
                "own",
            )

        def side_work(hots):
            return run(
                functools.partial(sides_kernel, nf),
                [((h, side_pad + 256), f32), ((h, side_pad), f32), ((h, 384), f32)],
                [stack, interp, *hots, *places],
                "sides",
            )

        if turn == 0:
            *hots, place, info, arrival = run(
                functools.partial(setup_kernel, chips),
                [((lanes, side_pad + 256), bf16), ((lanes, side_pad), bf16), ((lanes, 384), bf16),
                 ((16, side_pad + 640), f32), ((8, side_pad + 256), f32), ((8, 640), f32)],
                [coef, level, sides],
                "setup",
            )
            places = [place, info, arrival]
            own_scatter, _, far_scatter = hots
        elif turn == 1:
            hots = run(
                whole_kernel,
                [((768, side_pad + 256), bf16), ((768, side_pad), bf16), ((768, 384), bf16)],
                [*hots, place],
                "whole",
            )
            own_scatter, far_scatter = run(
                turn_kernel,
                [((side_pad + 256, 768), bf16), ((384, 768), bf16)],
                [place],
                "turn",
            )
        arrivals, last, made = exchange(
            sent, nf, own_work, functools.partial(side_work, hots),
            *((hots[0], own_scatter) if turn == 1 else ()),
        )
        mine, others, targets = made
        sums, *made = run(
            functools.partial(flux_kernel, nf, chips),
            [((h, 768), f32)] + ([] if turn else [((8, 256), f32)]),
            [*arrivals, mine, others, *places, weight, interp_t, own_scatter]
            + ([near_halo] if turn else []),
            "flux",
        )
        if turn == 0:
            near_halo = made[0]
        ins = [
            last, sums, targets, place, arrival, far_scatter, weight, interp_t, lift,
            fields, coef, level, block_inverse,
        ]
        ins += [far_halo] if turn else [guess]
        ins += [rhs_field] if turn == 1 else []
        if nf_next:
            ins += [trace, interp, hot, case]
            outs = [
                ((64 * max(nf, nf_next), lanes), f32), ((64 * nf_next, 768), bf16), ((32 * nf_next, 256), f32)
            ]
        else:
            outs = [((devices, lanes), f32)]
        made = run(
            functools.partial(update_kernel, turn, nf, nf_next),
            outs + ([] if turn else [((8, 384), f32)]), ins, "update",
            scratch=[pltpu.VMEM((64 * nf, lanes), f32)],
        )
        if turn == 0:
            far_halo = made[-1]
        if nf_next:
            fields, stack, sent = made[:3]
            history.append(fields)
            if nf_next < nf:
                fields = fields[:64]
        else:
            (parts,) = made
    parts = lax.all_to_all(parts.reshape(devices, 1, lanes), "dom", 0, 0).reshape(devices, lanes)
    smoothed, bound = run(
        finish_kernel,
        [((64, lanes), f32), ((1, lanes), f32)],
        [parts, guess, history[1], history[2]],
        "finish",
        kept=False,
    )
    return smoothed, bound[0, 0]


def solution(mesh):
    placed = (
        P(None, "dom"), P(None, "dom"), P(None, "dom"), P("dom"), P("dom"), P(None, None, "dom"),
        P("dom"), P("dom"), P("dom"), P("dom"), P("dom"), P("dom", None),
    )
    return jax.shard_map(
        local, mesh=mesh, in_specs=placed, out_specs=(P(None, "dom"), P()), check_vma=False
    )
```

```python
import functools
import math

import jax
import jax.numpy as jnp
import numpy as np
from jax import lax
from jax.experimental import pallas as pl
from jax.experimental.pallas import tpu as pltpu
from jax.sharding import PartitionSpec as P

f32 = jnp.float32
bf16 = jnp.bfloat16
i32 = jnp.int32
peer_offsets = (1, -1, 2, -2, 3, -3, 4, -4)
live_width = {1: 96, 2: 48, 3: 24, 4: 24}
lanes = 128
shifts = (0, 24, 48, 96)
side_pad = 1024


def lagrange_tables():
    root_five = 1.0 / math.sqrt(5.0)
    nodes = np.array([0.0, 0.5 - 0.5 * root_five, 0.5 + 0.5 * root_five, 1.0])
    weights = np.array([1.0, 5.0, 5.0, 1.0]) / 12.0
    factor = np.array(
        [np.prod([nodes[i] - nodes[j] for j in range(4) if j != i]) for i in range(4)]
    )
    derivative = np.zeros((4, 4))
    for i in range(4):
        for j in range(4):
            if i != j:
                derivative[i, j] = factor[i] / (factor[j] * (nodes[i] - nodes[j]))
        derivative[i, i] = -np.sum(derivative[i])
    halves = []
    for half in range(2):
        points = 0.5 * (nodes + half)
        table = np.ones((4, 4))
        for j in range(4):
            for other in range(4):
                if other != j:
                    table[:, j] *= (points - nodes[other]) / (nodes[j] - nodes[other])
        halves.append(table)
    return weights, derivative, halves


def basis_tables():
    weights, derivative, halves = lagrange_tables()
    mass = np.diag(weights)
    line = derivative.T @ mass @ derivative
    stiffness = (
        np.kron(np.kron(line, mass), mass)
        + np.kron(np.kron(mass, line), mass)
        + np.kron(np.kron(mass, mass), line)
    )
    trace = np.zeros((6, 32, 64))
    for dim in range(3):
        others = [d for d in range(3) if d != dim]
        for lower in range(2):
            face = 2 * dim + lower
            fixed = 0 if lower else 3
            sign = -1.0 if lower else 1.0
            for first in range(4):
                for second in range(4):
                    node = first * 4 + second
                    for along in range(4):
                        place = [0, 0, 0]
                        place[others[0]] = first
                        place[others[1]] = second
                        place[dim] = along
                        nodal = place[0] * 16 + place[1] * 4 + place[2]
                        if along == fixed:
                            trace[face, node, nodal] = 1.0
                        trace[face, 16 + node, nodal] = sign * derivative[fixed, along]
    face_weight = np.kron(weights, weights)
    order = [16 * part + 4 * first + second for first in range(4) for part in range(2) for second in range(4)]
    weight = np.concatenate([face_weight, face_weight])[order]
    return stiffness, trace[:, order].reshape(192, 64), weight


def stacked(table):
    table = np.asarray(table, np.float32)
    high = table.astype(jnp.bfloat16)
    low = (table - high.astype(np.float32)).astype(jnp.bfloat16)
    return np.concatenate([high, high, low], axis=1)


def const_tables():
    stiffness, trace, face_weight = basis_tables()
    lift = np.concatenate([stacked(trace.T), stacked(stiffness)], axis=1)
    weight = np.broadcast_to(face_weight[:, None], (32, lanes))
    return stacked(trace), lift, np.asarray(weight, np.float32)


def two(x):
    high = x.astype(bf16)
    return high, (x - high.astype(f32)).astype(bf16)


def three(x):
    high = x.astype(bf16)
    rest = x - high.astype(f32)
    mid = rest.astype(bf16)
    return high, mid, (rest - mid.astype(f32)).astype(bf16)


def dot(a, b):
    return jnp.dot(a, b, preferred_element_type=f32)


def dot_t(a, b):
    return lax.dot_general(a, b, (((1,), (1,)), ((), ())), preferred_element_type=f32)


def cat(parts, axis):
    return parts[0] if len(parts) == 1 else jnp.concatenate(parts, axis=axis)


def table_dot(table, x):
    high, low = two(x)
    return dot(table, jnp.concatenate([high, low, high], axis=0))


def interpolate(x, case, nf, transposed=False):
    halves = [h.T if transposed else h for h in lagrange_tables()[2]]
    n = x.shape[1]
    case = jnp.broadcast_to(case, (8, n))
    hanging = (case >= 0) & (case < 4)
    place = lax.broadcasted_iota(i32, (8, n), 0) & 3

    def pick(second, low, high, whole):
        return jnp.where(hanging, jnp.where(second, high, low), whole)

    def along(half, step):
        tile = jnp.zeros((8, n), f32)
        for j in range(4):
            if 0 <= j + step < 4:
                tile = jnp.where(place == j, float(half[j, j + step]), tile)
        return tile

    first, second = case >= 2, (case & 1) == 1
    across = [
        [pick(first, float(halves[0][i, j]), float(halves[1][i, j]), float(i == j)) for j in range(4)]
        for i in range(4)
    ]
    within = {
        step: pick(second, along(halves[0], step), along(halves[1], step), float(step == 0))
        for step in range(-3, 4)
    }
    out = []
    for k in range(nf):
        part = [x[32 * k + 8 * i : 32 * k + 8 * i + 8] for i in range(4)]
        for i in range(4):
            mixed = sum(across[i][j] * part[j] for j in range(4))
            out.append(
                sum(
                    within[step] * (pltpu.roll(mixed, -step % 8, 0) if step else mixed)
                    for step in range(-3, 4)
                )
            )
    return jnp.concatenate(out, axis=0)


def other_part(x):
    return jnp.concatenate(
        [pltpu.roll(x[8 * g : 8 * g + 8], 4, 0) for g in range(x.shape[0] // 8)], axis=0
    )


def slope_rows(shape):
    return (lax.broadcasted_iota(i32, shape, 0) & 4) == 4


def rows_of(rows, count, width):
    place = lax.broadcasted_iota(i32, (count, width), 0)
    table = jnp.zeros((count, width), f32)
    for k, r in enumerate(rows):
        table = jnp.where(place == k, r, table)
    return table


def one_hot(index_row, rows, first=0):
    place = lax.broadcasted_iota(i32, (rows, index_row.shape[1]), 0) + first
    return jnp.where(place == index_row, 1.0, 0.0).astype(bf16)


def gather_columns(stack, hot, face, nf):
    h = 32 * nf
    if hot.shape[0] == 768:
        got = dot(stack, hot)
        return got[:h] + got[h:]
    parts = [stack[:, lanes * f : lanes * f + lanes] for f in range(6)]
    got = dot(jnp.concatenate(parts, axis=0), hot)
    out = got[:h] + got[h : 2 * h]
    for f in range(1, 6):
        low = 2 * h * f
        out = jnp.where(face == f, got[low : low + h] + got[low + h : low + 2 * h], out)
    return out


def scatter_columns(x, hot, face, nf):
    h = 32 * nf
    high, low = two(x)
    both = jnp.concatenate([high, low], axis=0)
    if hot.shape[1] == 768:
        got = dot(both, hot)
        return got[:h] + got[h:]
    parts = [both * jnp.where(face == f, 1.0, 0.0).astype(bf16) for f in range(6)]
    got = dot_t(jnp.concatenate(parts, axis=0), hot)
    return jnp.concatenate(
        [got[2 * h * f : 2 * h * f + h] + got[2 * h * f + h : 2 * h * f + 2 * h] for f in range(6)],
        axis=1,
    )


def element_rows(coef_ref, level_ref):
    coef = coef_ref[...]
    level = level_ref[...]
    size = jnp.where(level == 0, 1.0, jnp.where(level == 1, 0.5, 0.25)).astype(f32)
    inverse = jnp.where(level == 0, 1.0, jnp.where(level == 1, 2.0, 4.0)).astype(f32)
    return coef, size, coef * size, coef * inverse


def face_stack(trace_ref, u, normal_scale, nf):
    faces = table_dot(trace_ref[...], cat(u, 1))
    scale = jnp.where(slope_rows((32, lanes)), jnp.broadcast_to(normal_scale, (32, lanes)), 1.0)
    fields = []
    for k in range(nf):
        part = faces[:, lanes * k : lanes * k + lanes]
        fields.append(
            jnp.concatenate([part[32 * f : 32 * f + 32] * scale for f in range(6)], axis=1)
        )
    high, low = two(cat(fields, 0))
    return jnp.concatenate([high, low], axis=0)


def gather_message(stack, hot, case, nf):
    got = dot(stack, hot)
    h = 32 * nf
    out = interpolate(got[:h] + got[h : 2 * h], case, nf)
    if stack.shape[0] == 2 * h:
        return out
    coef = got[2 * h : 2 * h + 1] + got[2 * h + 1 : 2 * h + 2] + got[2 * h + 2 : 2 * h + 3]
    size = got[2 * h + 3 : 2 * h + 4] * jnp.where((case >= 0) & (case < 4), 0.5, 1.0)
    row = lax.broadcasted_iota(i32, (8, out.shape[1]), 0)
    scalars = jnp.where(row == 0, coef, jnp.where(row == 1, size, 0.0))
    return jnp.concatenate([out, scalars], axis=0)


def where_am_i(chips):
    me = lax.axis_index("dom")
    chip = me // 2
    core = me - 2 * chip
    near = jnp.where(lax.rem(chip, 2) == 1, -1, 1)
    far = jnp.where(lax.rem(chip, 4) < 2, 1, -1)
    end = (chip == 0) | (chip == chips - 1)
    far_there = (chip - 2 * far >= 0) & (chip - 2 * far < chips)
    return core, near, far, end, ~end, far_there


def carried(core, near, far, near_there, far_there):
    first = core == 0
    return (
        jnp.where(first, near, -near), jnp.where(first, far, -far),
        first | near_there, first | far_there,
    )


def row_of(offset):
    size = jnp.abs(offset)
    return 2 * (size - 1) + jnp.where(offset < 0, 1, 0)


def narrow(offset):
    return jnp.abs(offset) == 3


def side_attributes(side_ref, more=()):
    live = lax.broadcasted_iota(i32, (1, side_pad), 1) < 930
    rows = [jnp.where(live, side_ref[k : k + 1], 0).astype(f32) for k in range(3)]
    rows.append(jnp.where(live, 1.0, 0.0))
    return rows_of(rows + list(more), 16, side_pad).astype(bf16)


def look_up(attributes, index):
    blocks = jnp.concatenate(
        [attributes[:, lanes * k : lanes * k + lanes] for k in range(side_pad // lanes)], axis=0
    )
    found = dot(blocks, one_hot(index & 127, lanes))
    block = index >> 7
    out = jnp.zeros((8, index.shape[1]), f32)
    for k in range(side_pad // lanes):
        out = jnp.where(block == k, found[16 * k : 16 * k + 8], out)
    return out


def place_of(found):
    valid = found[3:4] > 0.5
    return tuple(jnp.where(valid, found[k : k + 1], -1.0).astype(i32) for k in range(3))


def fill_one_hot(hot_ref, elem, face):
    hot = one_hot(elem, lanes)
    for f in range(6):
        hot_ref[lanes * f : lanes * f + lanes] = hot * jnp.where(face == f, 1.0, 0.0).astype(bf16)


def listed_part(rolled_ref, shift, offset, low, high, valid):
    place = shifts.index(shift)
    lane = lax.broadcasted_iota(i32, (1, lanes), 1)
    values = rolled_ref[pl.ds(8 * place + jnp.minimum(row_of(offset), 7), 1), :]
    return jnp.where((lane >= low) & (lane < high) & valid, values, -1)


def send_setup_kernel(chips, *refs):
    sources, refs = refs[:11], refs[11:]
    hot_ref, case_ref, stack_ref, side_ref, rolled_ref = refs[:5]
    sent_ref, landed = refs[5], (*refs[11:18], *refs[6:10])
    slot_ref, arrived = refs[10], refs[18]
    copies = [
        pltpu.make_async_copy(source, target, arrived.at[k])
        for k, (source, target) in enumerate(zip(sources, landed))
    ]
    for copy in copies:
        copy.start()
    elem_ref, dir_ref, sidecase_ref, kind_ref, partner_ref, list_ref = landed[:6]
    start_ref, coef_ref, level_ref, trace_ref = landed[6:10]
    for copy in copies:
        copy.wait()
    side_ref[...] = jnp.full((8, side_pad), -1, i32)
    sides = elem_ref.shape[1]
    for k, ref in enumerate((elem_ref, dir_ref, sidecase_ref, kind_ref, partner_ref)):
        side_ref[k : k + 1, 0:sides] = ref[...]
    core, near, far, end, near_there, far_there = where_am_i(chips)
    listed = jnp.concatenate([list_ref[...], jnp.full((8, 32), -1, i32)], axis=1)
    for place, shift in enumerate(shifts):
        rolled_ref[8 * place : 8 * place + 8] = (
            pltpu.roll(listed, shift, 1) if shift else listed
        )
    part = functools.partial(listed_part, rolled_ref)
    other = 1 - core
    step, step_two, there, there_two = carried(other, near, far, near_there, far_there)
    cross, cross_two = 2 * step + other - core, 4 * step_two + other - core
    first = (
        part(0, cross_two, 0, 24, there_two & narrow(cross_two)),
        part(24, 4 * step_two, 24, 48, there_two),
        part(48, 2 * step, 48, 96, there),
        part(96, cross, 96, 120, there & narrow(cross)),
    )
    slot_ref[0:1, 0:128] = functools.reduce(jnp.maximum, first)
    slot_ref[0:1, 128:256] = part(0, cross, 0, 96, there & ~narrow(cross))
    elem, face, slot_case = place_of(look_up(side_attributes(side_ref), slot_ref[0:1, :]))
    case_ref[0:1, :] = slot_case
    fill_one_hot(hot_ref, elem, face)

    coef, size, volume_scale, normal_scale = element_rows(coef_ref, level_ref)
    stack = face_stack(trace_ref, [start_ref[...]], normal_scale, 1)
    scalars = rows_of([x.astype(f32) for x in three(coef)] + [size], 16, lanes).astype(bf16)
    stack = jnp.concatenate([stack, jnp.concatenate([scalars] * 6, axis=1)], axis=0)
    stack_ref[...] = stack
    sent = gather_message(stack, hot_ref[...], slot_case, 1)
    sent_ref[...] = sent


def own_setup_kernel(chips, side_ref, rolled_ref, hot_ref, case_ref, slot_ref):
    core, near, far, end, near_there, far_there = where_am_i(chips)
    part = functools.partial(listed_part, rolled_ref)
    flip = 1 - 2 * core
    step, step_two, there, there_two = carried(core, near, far, near_there, far_there)
    cross, cross_two = 2 * step + flip, 4 * step_two + flip
    slot_ref[0:1, 0:128] = jnp.maximum(
        part(0, 4 * step_two, 0, 24, there_two),
        part(24, cross_two, 24, 48, there_two & narrow(cross_two)),
    )
    slot_ref[0:1, 128:256] = jnp.maximum(
        part(0, 2 * step, 0, 48, there), part(96, cross, 96, 120, there & narrow(cross))
    )
    slot_ref[0:1, 256:384] = part(0, cross, 0, 96, there & ~narrow(cross))
    slot_ref[0:1, 384:512] = part(0, flip, 0, 96, core >= 0)
    elem, face, slot_case = place_of(look_up(side_attributes(side_ref), slot_ref[0:1, :]))
    case_ref[0:1, :] = slot_case
    fill_one_hot(hot_ref, elem, face)


def own_kernel(nf, stack_ref, hot_ref, case_ref, own_ref):
    own_ref[...] = gather_message(
        stack_ref[...], hot_ref[...], case_ref[0:1], nf
    )


def carry_kernel(sent_ref, own_ref, *rest):
    two_ref, one_ref = rest[-2:]
    lane = lax.broadcasted_iota(i32, (1, lanes), 1)
    sent = sent_ref[:, 0:128]
    handed = jnp.where((lane >= 48) & (lane < 96), pltpu.roll(sent, 48, 1), 0.0)
    two_ref[...] = own_ref[:, 0:128] + handed
    one_ref[:, 0:128] = own_ref[:, 128:256] + jnp.where(lane >= 48, sent, 0.0)
    one_ref[:, 128:256] = own_ref[:, 256:384] + sent_ref[:, 128:256]


def relay_kernel(chips, one_ref, two_ref, own_ref, *rest):
    out_ref = rest[-1]
    core, near, far, end, near_there, far_there = where_am_i(chips)
    lane = lax.broadcasted_iota(i32, (1, lanes), 1)
    one, two_away = one_ref[:, 0:128], two_ref[...]
    out_ref[:, 0:128] = own_ref[:, 384:512]
    passed = jnp.where(lane < 24, pltpu.roll(two_away, 56, 1), two_away)
    out_ref[:, 128:256] = jnp.where((lane < 48) & ~(end & (core == 1)), passed, one)
    out_ref[:, 256:384] = one_ref[:, 128:256]


def setup_kernel(
    chips, coef_ref, level_ref, side_ref,
    own_hot_ref, partner_hot_ref, far_hot_ref, place_ref, info_ref, arrival_ref,
):
    core, near, far, end, near_there, far_there = where_am_i(chips)
    elem, direction, case = side_ref[0:1], side_ref[1:2], side_ref[2:3]
    kind, partner = side_ref[3:4], side_ref[4:5]
    live = lax.broadcasted_iota(i32, (1, side_pad), 1) < 930

    coef, size, volume_scale, normal_scale = element_rows(coef_ref, level_ref)
    scalars = rows_of([x.astype(f32) for x in three(coef)] + [size], 16, lanes)
    mine = dot(scalars.astype(bf16), one_hot(elem, lanes))
    hanging = (case >= 0) & (case < 4)
    own_coef = mine[0:1] + mine[1:2] + mine[2:3]
    own_size = mine[3:4] * jnp.where(hanging, 0.5, 1.0)

    attributes = side_attributes(side_ref, (mine[0:1], mine[1:2], mine[2:3], own_size))
    here = live & (partner < 930)
    other = look_up(attributes, jnp.where(here, partner, -1))
    other_elem, other_face = place_of(other)[:2]
    partner_hot_ref[...] = one_hot(other_elem, lanes)
    valid = other[3:4] > 0.5
    edge = jnp.where(kind == 1, 1.0, 0.0)
    least = jnp.where(valid, jnp.minimum(own_size, other[7:8]), 0.0)
    jump = 16.0 * (own_coef + other[4:5] + other[5:6] + other[6:7]) * least
    area = least * least
    info_ref[:, 0:side_pad] = rows_of(
        [jump, jump * (1.0 - edge), area * (0.5 + 0.5 * edge), area * (0.5 - 0.5 * edge),
         case.astype(f32), other[2:3]],
        8, side_pad,
    )

    def arrives(carrier):
        last = end & (carrier == 1)
        back = jnp.where((carrier == 0) | end, -near, near)
        back_two = jnp.where(carrier == 0, -far, far)
        turn = 2 * core - 1
        return (
            2 * back, 2 * back + turn, 4 * back_two, 4 * back_two + turn,
            ~(end & (carrier == 0)), ~last, last,
        )

    def span(low, high, valid):
        return low, jnp.where(valid, high, low)

    segments = []
    for mine, carrier in ((True, core), (False, 1 - core)):
        straight, cross, straight_two, cross_two, there, there_two, last = arrives(carrier)
        slim, wide = there & narrow(cross), there & ~narrow(cross)
        at_first = (last & (core != 1)) | (~last & (carrier == core))
        if mine:
            two_parts = ((*span(48, 72, there_two & narrow(cross_two)), cross_two),
                         (*span(72, 96, there_two), straight_two))
        else:
            segments.append(((0, 96, 2 * core - 1),))
            two_parts = ((*span(0, 24, there_two), straight_two),
                         (*span(24, 48, there_two & narrow(cross_two)), cross_two))
        segments.append((
            (*span(0, 48, there & at_first), straight), (*span(48, 96, there & ~at_first), straight),
            (*span(96, 120, slim), cross), *two_parts,
        ))
        segments.append(((*span(0, 96, wide), cross),))
    entry = partner - 930
    peer = (entry * 683) >> 16
    entry = entry - 96 * peer
    sought = live & (partner >= 930) & (kind == 0)
    column = jnp.full((1, side_pad), -1, i32)
    for tile, parts in enumerate(segments):
        for low, high, offset in parts:
            match = sought & (peer == row_of(offset)) & (entry < high - low)
            column = jnp.where(match, lanes * tile + low + entry, column)
    block = column >> 7
    split = [
        attributes * jnp.where(block == tile, 1.0, 0.0).astype(bf16) for tile in range(len(segments))
    ]
    target = dot_t(jnp.concatenate(split, axis=0), one_hot(column & 127, lanes))
    target = jnp.concatenate(
        [target[16 * tile : 16 * tile + 8] for tile in range(len(segments))], axis=1
    )
    target_elem, target_face, target_case = place_of(target)
    elems = jnp.concatenate([elem, target_elem], axis=1)
    faces = jnp.concatenate([direction, target_face], axis=1)
    near = side_pad + 256
    own_hot_ref[...] = one_hot(elems[:, :near], lanes)
    far_hot_ref[...] = one_hot(elems[:, near:], lanes)
    other_face = jnp.concatenate([other_face, jnp.full((1, 640), -1, i32)], axis=1)
    place_ref[...] = rows_of(
        [elems.astype(f32), faces.astype(f32), other_face.astype(f32)], 16, elems.shape[1]
    )
    info_ref[:, side_pad:] = rows_of(
        [jnp.zeros((1, 256), f32)] * 4 + [target_case[:, 0:256].astype(f32)], 8, 256
    )
    arrival_ref[...] = rows_of(
        [target_case.astype(f32), target[4:5] + target[5:6] + target[6:7], target[7:8]],
        8, 640,
    )


def whole_kernel(own_elem_ref, partner_elem_ref, far_elem_ref, place_ref, own_ref, partner_ref, far_ref):
    near = side_pad + 256
    for source, row, low, high, target in (
        (own_elem_ref, 1, 0, near, own_ref),
        (partner_elem_ref, 2, 0, side_pad, partner_ref),
        (far_elem_ref, 1, near, near + 384, far_ref),
    ):
        hot, face = source[...], place_ref[row : row + 1, low:high]
        for f in range(6):
            target[lanes * f : lanes * f + lanes] = hot * jnp.where(face == f, 1.0, 0.0).astype(bf16)


def turn_kernel(place_ref, own_ref, far_ref):
    row = lax.broadcasted_iota(i32, (16, lanes), 0)
    weight = jnp.where(row == 0, 1.0, jnp.where(row == 1, 128.0, 0.0)).astype(bf16)
    column = lax.dot_general(
        place_ref[...].astype(bf16), weight, (((0,), (0,)), ((), ())), preferred_element_type=f32
    )
    lane = lax.broadcasted_iota(i32, (1, lanes), 1).astype(f32)
    split = own_ref.shape[0]
    for f in range(6):
        part = jnp.where(column == lane + 128.0 * f, 1.0, 0.0).astype(bf16)
        own_ref[:, lanes * f : lanes * f + lanes] = part[:split]
        far_ref[:, lanes * f : lanes * f + lanes] = part[split:]


def sides_kernel(
    nf, stack_ref, own_hot_ref, partner_hot_ref, far_hot_ref, place_ref, info_ref,
    arrival_ref, mine_ref, other_ref, target_ref,
):
    stack = stack_ref[0 : 64 * nf]
    near = side_pad + 256
    for hot_ref, face, case, out_ref in (
        (own_hot_ref, place_ref[1:2, 0:near], info_ref[4:5], mine_ref),
        (partner_hot_ref, place_ref[2:3, 0:side_pad], info_ref[5:6, 0:side_pad], other_ref),
        (far_hot_ref, place_ref[1:2, near:], arrival_ref[0:1, 256:640], target_ref),
    ):
        got = gather_columns(stack, hot_ref[...], face, nf)
        out_ref[...] = interpolate(got, case.astype(i32), nf)


def side_flux(nf, mine, outer, coefs, case, face, weight_ref, hot):
    jump, jump_out, area, area_out = coefs
    weight = weight_ref[:, 0:1]
    flux = []
    for k in range(nf):
        inner, other = mine[32 * k : 32 * k + 32], outer[32 * k : 32 * k + 32]
        jumps = jnp.where(slope_rows(inner.shape), 0.0, jump * inner - jump_out * other)
        flux.append(weight * (jumps - other_part(area * inner - area_out * other)))
    flux = interpolate(cat(flux, 0), case.astype(i32), nf, transposed=True)
    return scatter_columns(flux, hot, face, nf)


def halo_coefs(coef, size, other_coef, other_size):
    least = jnp.minimum(size, other_size)
    return 16.0 * (coef + other_coef) * least, 0.5 * least * least


def flux_kernel(
    nf, chips, one_ref, two_ref, mine_ref, other_ref, place_ref, info_ref, arrival_ref, weight_ref,
    own_hot_ref, *rest,
):
    h = 32 * nf
    core, near, far, end, near_there, far_there = where_am_i(chips)
    lane = lax.broadcasted_iota(i32, (1, lanes), 1)
    two_away = two_ref[...]
    kept = jnp.where(lane < 72, two_away, pltpu.roll(two_away, 72, 1))
    inside = (lane >= 48) & (lane < 96) & ~(end & (core == 1))
    got = jnp.concatenate(
        [jnp.where(inside, kept, one_ref[:, 0:128]), one_ref[:, 128:256]], axis=1
    )
    if got.shape[0] > h:
        sum_ref, halo_ref = rest
        halo = halo_coefs(
            arrival_ref[1:2, 0:256], arrival_ref[2:3, 0:256], got[h : h + 1], got[h + 1 : h + 2]
        )
        halo_ref[...] = rows_of(halo, 8, 256)
    else:
        halo_ref, sum_ref = rest
        halo = halo_ref[0:1], halo_ref[1:2]
    coefs = [
        jnp.concatenate([info_ref[k : k + 1, 0:side_pad], halo[k // 2]], axis=1) for k in range(4)
    ]
    outer = jnp.concatenate([other_ref[...], got[0:h]], axis=1)
    sum_ref[...] = side_flux(
        nf, mine_ref, outer, coefs, info_ref[4:5], place_ref[1:2, 0 : side_pad + 256], weight_ref,
        own_hot_ref[...],
    )


def solve_blocks(inverse_ref, hold_ref, nf):
    sums = [jnp.zeros((64, lanes), f32) for _ in range(nf)]
    for col in range(64):
        block = inverse_ref[col].astype(f32)
        for k in range(nf):
            sums[k] = sums[k] + block * hold_ref[64 * k + col : 64 * k + col + 1, :]
    return sums


def update_kernel(
    turn, nf, nf_next,
    one_ref, local_ref, target_ref, place_ref, arrival_ref, far_hot_ref, weight_ref, lift_ref,
    field_ref, coef_ref, level_ref, inverse_ref, *rest,
):
    if turn == 0:
        guess_ref, *rest = rest
    else:
        halo_ref, *rest = rest
    if turn == 1:
        rhs_ref, *rest = rest
    if nf_next:
        trace_ref, hot_ref, case_ref, new_ref, stack_ref, sent_ref, *rest = rest
    else:
        part_ref, *rest = rest
    hold_ref = rest[-1]
    h = 32 * nf
    if turn == 0:
        halo = halo_coefs(
            arrival_ref[1:2, 256:640], arrival_ref[2:3, 256:640],
            one_ref[h : h + 1], one_ref[h + 1 : h + 2],
        )
        rest[0][...] = rows_of(halo, 8, 384)
    else:
        halo = (halo_ref[0:1], halo_ref[1:2])
    total = local_ref[...] + side_flux(
        nf, target_ref, one_ref, (halo[0], halo[0], halo[1], halo[1]), arrival_ref[0:1, 256:640],
        place_ref[1:2, side_pad + 256 :], weight_ref, far_hot_ref[...],
    )
    coef, size, volume_scale, normal_scale = element_rows(coef_ref, level_ref)
    scale = jnp.where(slope_rows((32, lanes)), jnp.broadcast_to(normal_scale, (32, lanes)), 1.0)
    operands = []
    for k in range(nf):
        mine = total[32 * k : 32 * k + 32]
        faces = jnp.concatenate(
            [mine[:, lanes * f : lanes * f + lanes] * scale for f in range(6)], axis=0
        )
        high, low = two(faces)
        field_high, field_low = two(field_ref[64 * k : 64 * k + 64] * volume_scale)
        operands.append(
            jnp.concatenate([high, low, high, field_high, field_low, field_high], axis=0)
        )
    image = dot(lift_ref[...], cat(operands, 1))
    for k in range(nf):
        part = image[:, lanes * k : lanes * k + lanes]
        if turn == 1 and k == 1:
            part = rhs_ref[...] - part
        hold_ref[64 * k : 64 * k + 64, :] = part
    new = solve_blocks(inverse_ref, hold_ref, nf)
    if turn == 0:
        new.append(guess_ref[...])
    if nf_next:
        for k, x in enumerate(new):
            new_ref[64 * k : 64 * k + 64, :] = x
        stack = face_stack(trace_ref, new[:nf_next], normal_scale, nf_next)
        stack_ref[...] = stack
        sent = gather_message(stack, hot_ref[...], case_ref[0:1], nf_next)
        sent_ref[...] = sent
    else:
        lane = lax.broadcasted_iota(i32, (1, lanes), 1)
        sums = []
        for x in (field_ref[...], new[0]):
            total = jnp.sum(x * x, axis=0, keepdims=True)
            sums.append(total + pltpu.roll(total, 64, 1))
        part_ref[...] = jnp.broadcast_to(jnp.where(lane < 64, sums[0], sums[1]), part_ref.shape)


def finish_kernel(part_ref, guess_ref, first_ref, second_ref, out_ref, bound_ref):
    total = jnp.sum(part_ref[...], axis=0, keepdims=True)
    lane = lax.broadcasted_iota(i32, (1, lanes), 1)
    before = jnp.sum(jnp.where(lane < 64, total, 0.0), axis=1, keepdims=True)
    after = jnp.sum(jnp.where(lane < 64, 0.0, total), axis=1, keepdims=True)
    bound = jnp.sqrt(after / before)
    upper = 1.2 * bound
    lower = upper / 15.0
    center = 0.5 * (upper + lower)
    half = 0.5 * (upper - lower)
    ratio = center / half
    damping = 1.0 / ratio
    damping_next = 1.0 / (2.0 * ratio - damping)
    first = first_ref[64:128] / center
    second = first_ref[64:128] - second_ref[64:128] / center
    out_ref[...] = (
        guess_ref[...] + first + (damping_next * damping * first + 2.0 * damping_next / half * second)
    )
    bound_ref[...] = jnp.broadcast_to(bound, (1, lanes))


def in_vmem(x):
    return pltpu.with_memory_space_constraint(x, pltpu.VMEM)


def in_hbm(x):
    return pltpu.with_memory_space_constraint(x, pltpu.HBM)


def run(body, outs, ins, name, scratch=(), flops=1 << 24, placed=True, kept=True):
    spec = pl.BlockSpec(memory_space=pltpu.VMEM)
    return pl.pallas_call(
        body,
        out_shape=[(pltpu.VMEM if kept else jax.ShapeDtypeStruct)(shape, dtype) for shape, dtype in outs],
        in_specs=[spec if placed else pl.BlockSpec(memory_space=pltpu.HBM)] * len(ins),
        out_specs=[spec] * len(outs),
        scratch_shapes=list(scratch),
        compiler_params=pltpu.CompilerParams(vmem_limit_bytes=24 << 20),
        cost_estimate=pl.CostEstimate(flops=flops, bytes_accessed=1 << 20, transcendentals=0),
        name=name,
    )(*(in_vmem(x) if placed else in_hbm(x) for x in ins))


def local(
    rhs_field, initial_guess, start_vector, coefficient, refine_level, block_inverse,
    side_elem, side_dir, side_case, side_kind, partner, send_list,
):
    devices = lax.axis_size("dom")
    chips = devices // 2
    trace, lift, weight = (jnp.asarray(t) for t in const_tables())
    coef = coefficient.reshape(1, lanes)
    level = refine_level.reshape(1, lanes)

    def permute(x, to):
        return lax.ppermute(x, "dom", sorted(to.items()))

    swapped = {i: i ^ 1 for i in range(devices)}
    two_away, one_away = {}, {}
    for c in range(chips):
        two_away[2 * c] = 2 * (c ^ 2)
        one_away[2 * c] = 2 * (c ^ 1)
        over = c + 2 if c % 4 >= 2 else c - 2
        two_away[2 * c + 1] = 2 * (over if 0 <= over < chips else c ^ 1) + 1
        if 0 < c < chips - 1:
            one_away[2 * c + 1] = 2 * (c + 1 if c % 2 else c - 1) + 1
    for c in (0, chips - 1):
        one_away[2 * (c ^ 1)] = 2 * c + 1
        one_away[2 * c + 1] = 2 * c

    def exchange(sent, nf, own_work, work, *beside):
        rows = sent.shape[0]
        (own,) = own_work()
        two_out, one_out = run(
            carry_kernel, [((rows, lanes), f32), ((rows, 256), f32)],
            [permute(sent, swapped), own, *beside[:1]], "carry",
        )
        arrivals = permute(one_out, one_away), permute(two_out, two_away)
        made = work()
        (last,) = run(
            functools.partial(relay_kernel, chips), [((rows, 384), f32)],
            [*arrivals, own, made[2], *beside[1:]], "relay",
        )
        return arrivals, permute(last, swapped), made

    sides = [x.reshape(1, -1) for x in (side_elem, side_dir, side_case, side_kind, partner)]
    first = [*sides, send_list, start_vector, coef, level, trace, initial_guess]
    hot, case, stack, sides, rolled, sent, coef, level, trace, guess = run(
        functools.partial(send_setup_kernel, chips),
        [((768, 256), bf16), ((8, 256), i32), ((80, 768), bf16), ((8, side_pad), i32), ((32, lanes), i32),
         ((40, 256), f32), *((x.shape, x.dtype) for x in first[7:])],
        first,
        "send_setup",
        scratch=[
            pltpu.VMEM((8, 256), i32),
            *(pltpu.VMEM(x.shape, x.dtype) for x in first[:7]), pltpu.SemaphoreType.DMA((len(first),)),
        ],
        placed=False,
    )
    own_slots = run(
        functools.partial(own_setup_kernel, chips),
        [((768, 512), bf16), ((8, 512), i32)],
        [sides, rolled],
        "own_setup",
        scratch=[pltpu.VMEM((8, 512), i32)],
    )
    fields = start_vector
    history = []
    for turn, (nf, nf_next) in enumerate(((1, 2), (2, 2), (2, 1), (1, 0))):
        h = 32 * nf
        def own_work():
            return run(
                functools.partial(own_kernel, nf),
                [((sent.shape[0], 512), f32)],
                [stack, *own_slots],
                "own",
            )

        def side_work(hots):
            return run(
                functools.partial(sides_kernel, nf),
                [((h, side_pad + 256), f32), ((h, side_pad), f32), ((h, 384), f32)],
                [stack, *hots, *places],
                "sides",
            )

        if turn == 0:
            *hots, place, info, arrival = run(
                functools.partial(setup_kernel, chips),
                [((lanes, side_pad + 256), bf16), ((lanes, side_pad), bf16), ((lanes, 384), bf16),
                 ((16, side_pad + 640), f32), ((8, side_pad + 256), f32), ((8, 640), f32)],
                [coef, level, sides],
                "setup",
            )
            places = [place, info, arrival]
            own_scatter, _, far_scatter = hots
        elif turn == 1:
            hots = run(
                whole_kernel,
                [((768, side_pad + 256), bf16), ((768, side_pad), bf16), ((768, 384), bf16)],
                [*hots, place],
                "whole",
            )
            own_scatter, far_scatter = run(
                turn_kernel,
                [((side_pad + 256, 768), bf16), ((384, 768), bf16)],
                [place],
                "turn",
            )
        arrivals, last, made = exchange(
            sent, nf, own_work, functools.partial(side_work, hots),
            *((hots[0], own_scatter) if turn == 1 else ()),
        )
        mine, others, targets = made
        sums, *made = run(
            functools.partial(flux_kernel, nf, chips),
            [((h, 768), f32)] + ([] if turn else [((8, 256), f32)]),
            [*arrivals, mine, others, *places, weight, own_scatter]
            + ([near_halo] if turn else []),
            "flux",
        )
        if turn == 0:
            near_halo = made[0]
        ins = [
            last, sums, targets, place, arrival, far_scatter, weight, lift,
            fields, coef, level, block_inverse,
        ]
        ins += [far_halo] if turn else [guess]
        ins += [rhs_field] if turn == 1 else []
        if nf_next:
            ins += [trace, hot, case]
            outs = [
                ((64 * max(nf, nf_next), lanes), f32), ((64 * nf_next, 768), bf16), ((32 * nf_next, 256), f32)
            ]
        else:
            outs = [((devices, lanes), f32)]
        made = run(
            functools.partial(update_kernel, turn, nf, nf_next),
            outs + ([] if turn else [((8, 384), f32)]), ins, "update",
            scratch=[pltpu.VMEM((64 * nf, lanes), f32)],
        )
        if turn == 0:
            far_halo = made[-1]
        if nf_next:
            fields, stack, sent = made[:3]
            history.append(fields)
            if nf_next < nf:
                fields = fields[:64]
        else:
            (parts,) = made
    parts = lax.all_to_all(parts.reshape(devices, 1, lanes), "dom", 0, 0).reshape(devices, lanes)
    smoothed, bound = run(
        finish_kernel,
        [((64, lanes), f32), ((1, lanes), f32)],
        [parts, guess, history[1], history[2]],
        "finish",
        kept=False,
    )
    return smoothed, bound[0, 0]


def solution(mesh):
    placed = (
        P(None, "dom"), P(None, "dom"), P(None, "dom"), P("dom"), P("dom"), P(None, None, "dom"),
        P("dom"), P("dom"), P("dom"), P("dom"), P("dom"), P("dom", None),
    )
    return jax.shard_map(
        local, mesh=mesh, in_specs=placed, out_specs=(P(None, "dom"), P()), check_vma=False
    )
```

```python
import functools
import math

import jax
import jax.numpy as jnp
import numpy as np
from jax import lax
from jax.experimental import pallas as pl
from jax.experimental.pallas import tpu as pltpu
from jax.sharding import PartitionSpec as P

f32 = jnp.float32
bf16 = jnp.bfloat16
i32 = jnp.int32
peer_offsets = (1, -1, 2, -2, 3, -3, 4, -4)
live_width = {1: 96, 2: 48, 3: 24, 4: 24}
lanes = 128
shifts = (0, 24, 48, 96)
side_pad = 1024


def lagrange_tables():
    root_five = 1.0 / math.sqrt(5.0)
    nodes = np.array([0.0, 0.5 - 0.5 * root_five, 0.5 + 0.5 * root_five, 1.0])
    weights = np.array([1.0, 5.0, 5.0, 1.0]) / 12.0
    factor = np.array(
        [np.prod([nodes[i] - nodes[j] for j in range(4) if j != i]) for i in range(4)]
    )
    derivative = np.zeros((4, 4))
    for i in range(4):
        for j in range(4):
            if i != j:
                derivative[i, j] = factor[i] / (factor[j] * (nodes[i] - nodes[j]))
        derivative[i, i] = -np.sum(derivative[i])
    halves = []
    for half in range(2):
        points = 0.5 * (nodes + half)
        table = np.ones((4, 4))
        for j in range(4):
            for other in range(4):
                if other != j:
                    table[:, j] *= (points - nodes[other]) / (nodes[j] - nodes[other])
        halves.append(table)
    return weights, derivative, halves


def stiffness_table():
    weights, derivative, halves = lagrange_tables()
    mass = np.diag(weights)
    line = derivative.T @ mass @ derivative
    return (
        np.kron(np.kron(line, mass), mass)
        + np.kron(np.kron(mass, line), mass)
        + np.kron(np.kron(mass, mass), line)
    )


def weight_table():
    weights = lagrange_tables()[0]
    rows = [weights[first] * weights[second] for first in range(4) for part in range(2) for second in range(4)]
    return np.broadcast_to(np.array(rows, np.float32)[:, None], (32, lanes))


def stacked(table):
    table = np.asarray(table, np.float32)
    high = table.astype(jnp.bfloat16)
    low = (table - high.astype(np.float32)).astype(jnp.bfloat16)
    return np.concatenate([high, high, low], axis=1)


def const_tables():
    return stacked(stiffness_table()), np.ascontiguousarray(weight_table())


def two(x):
    high = x.astype(bf16)
    return high, (x - high.astype(f32)).astype(bf16)


def three(x):
    high = x.astype(bf16)
    rest = x - high.astype(f32)
    mid = rest.astype(bf16)
    return high, mid, (rest - mid.astype(f32)).astype(bf16)


def dot(a, b):
    return jnp.dot(a, b, preferred_element_type=f32)


def dot_t(a, b):
    return lax.dot_general(a, b, (((1,), (1,)), ((), ())), preferred_element_type=f32)


def cat(parts, axis):
    return parts[0] if len(parts) == 1 else jnp.concatenate(parts, axis=axis)


def table_dot(table, x):
    high, low = two(x)
    return dot(table, jnp.concatenate([high, low, high], axis=0))


def interpolate(x, case, nf, transposed=False):
    halves = [h.T if transposed else h for h in lagrange_tables()[2]]
    n = x.shape[1]
    case = jnp.broadcast_to(case, (8, n))
    hanging = (case >= 0) & (case < 4)
    place = lax.broadcasted_iota(i32, (8, n), 0) & 3

    def pick(second, low, high, whole):
        return jnp.where(hanging, jnp.where(second, high, low), whole)

    def along(half, step):
        tile = jnp.zeros((8, n), f32)
        for j in range(4):
            if 0 <= j + step < 4:
                tile = jnp.where(place == j, float(half[j, j + step]), tile)
        return tile

    first, second = case >= 2, (case & 1) == 1
    across = [
        [pick(first, float(halves[0][i, j]), float(halves[1][i, j]), float(i == j)) for j in range(4)]
        for i in range(4)
    ]
    within = {
        step: pick(second, along(halves[0], step), along(halves[1], step), float(step == 0))
        for step in range(-3, 4)
    }
    out = []
    for k in range(nf):
        part = [x[32 * k + 8 * i : 32 * k + 8 * i + 8] for i in range(4)]
        for i in range(4):
            mixed = sum(across[i][j] * part[j] for j in range(4))
            out.append(
                sum(
                    within[step] * (pltpu.roll(mixed, -step % 8, 0) if step else mixed)
                    for step in range(-3, 4)
                )
            )
    return jnp.concatenate(out, axis=0)


def other_part(x):
    return jnp.concatenate(
        [pltpu.roll(x[8 * g : 8 * g + 8], 4, 0) for g in range(x.shape[0] // 8)], axis=0
    )


def slope_rows(shape):
    return (lax.broadcasted_iota(i32, shape, 0) & 4) == 4


def rows_of(rows, count, width):
    place = lax.broadcasted_iota(i32, (count, width), 0)
    table = jnp.zeros((count, width), f32)
    for k, r in enumerate(rows):
        table = jnp.where(place == k, r, table)
    return table


def one_hot(index_row, rows, first=0):
    place = lax.broadcasted_iota(i32, (rows, index_row.shape[1]), 0) + first
    return jnp.where(place == index_row, 1.0, 0.0).astype(bf16)


def gather_columns(stack, hot, face, nf):
    h = 32 * nf
    if hot.shape[0] == 768:
        got = dot(stack, hot)
        return got[:h] + got[h:]
    parts = [stack[:, lanes * f : lanes * f + lanes] for f in range(6)]
    got = dot(jnp.concatenate(parts, axis=0), hot)
    out = got[:h] + got[h : 2 * h]
    for f in range(1, 6):
        low = 2 * h * f
        out = jnp.where(face == f, got[low : low + h] + got[low + h : low + 2 * h], out)
    return out


def scatter_columns(x, hot, face, nf):
    h = 32 * nf
    high, low = two(x)
    both = jnp.concatenate([high, low], axis=0)
    if hot.shape[1] == 768:
        got = dot(both, hot)
        return got[:h] + got[h:]
    parts = [both * jnp.where(face == f, 1.0, 0.0).astype(bf16) for f in range(6)]
    got = dot_t(jnp.concatenate(parts, axis=0), hot)
    return jnp.concatenate(
        [got[2 * h * f : 2 * h * f + h] + got[2 * h * f + h : 2 * h * f + 2 * h] for f in range(6)],
        axis=1,
    )


def element_rows(coef_ref, level_ref):
    coef = coef_ref[...]
    level = level_ref[...]
    size = jnp.where(level == 0, 1.0, jnp.where(level == 1, 0.5, 0.25)).astype(f32)
    inverse = jnp.where(level == 0, 1.0, jnp.where(level == 1, 2.0, 4.0)).astype(f32)
    return coef, size, coef * size, coef * inverse


def by_place(values):
    place = lax.broadcasted_iota(i32, (8, lanes), 0) & (len(values) - 1)
    tile = jnp.full((8, lanes), float(values[0]), f32)
    for p in range(1, len(values)):
        tile = jnp.where(place == p, float(values[p]), tile)
    return tile


def face_ends():
    derivative = lagrange_tables()[1]
    for dim in range(3):
        for lower in range(2):
            node = 0 if lower else 3
            yield dim, 2 * dim + lower, node, (-1.0 if lower else 1.0) * derivative[node]


def face_traces(u):
    sub = lax.broadcasted_iota(i32, (8, lanes), 0)
    low = sub < 4
    v = [[u[16 * i + 8 * m : 16 * i + 8 * m + 8] for m in range(2)] for i in range(4)]
    out = {}
    for dim, face, node, slope in face_ends():
        rows = []
        if dim == 0:
            for m in range(2):
                normal = sum(float(slope[i]) * v[i][m] for i in range(4))
                rows.append(jnp.where(low, v[node][m], pltpu.roll(normal, 4, 0)))
                rows.append(jnp.where(low, pltpu.roll(v[node][m], 4, 0), normal))
        elif dim == 1:
            scale = [by_place([slope[2 * m]] * 4 + [slope[2 * m + 1]] * 4) for m in range(2)]
            for i in range(4):
                normal = scale[0] * v[i][0] + scale[1] * v[i][1]
                normal = normal + pltpu.roll(normal, 4, 0)
                rows.append(jnp.where(low, pltpu.roll(v[i][1], 4, 0) if node else v[i][0], normal))
        else:
            scale = by_place(slope)
            for i in range(4):
                row = None
                for m in range(2):
                    normal = scale * v[i][m]
                    normal = normal + pltpu.roll(normal, 7, 0)
                    normal = normal + pltpu.roll(normal, 6, 0)
                    for half in range(2):
                        to = 2 * m + half
                        value = pltpu.roll(v[i][m], (to - 4 * half - node) % 8, 0)
                        shift = (to + 4 - 4 * half) % 8
                        moved = pltpu.roll(normal, shift, 0) if shift else normal
                        row = value if row is None else jnp.where(sub == to, value, row)
                        row = jnp.where(sub == to + 4, moved, row)
                rows.append(row)
        out[face] = jnp.concatenate(rows, axis=0)
    return [out[f] for f in range(6)]


def lift_traces(total, faces):
    sub = lax.broadcasted_iota(i32, (8, lanes), 0)
    low = sub < 4
    r = [[total[16 * i + 8 * m : 16 * i + 8 * m + 8] for m in range(2)] for i in range(4)]
    for dim, face, node, slope in face_ends():
        b = [faces[face][8 * i : 8 * i + 8] for i in range(4)]
        if dim == 0:
            for m in range(2):
                even, odd = b[2 * m], b[2 * m + 1]
                normal = jnp.where(low, pltpu.roll(even, 4, 0), odd)
                for i in range(4):
                    r[i][m] = r[i][m] + float(slope[i]) * normal
                r[node][m] = r[node][m] + jnp.where(low, even, pltpu.roll(odd, 4, 0))
        elif dim == 1:
            scale = [by_place([slope[2 * m]] * 4 + [slope[2 * m + 1]] * 4) for m in range(2)]
            for i in range(4):
                turned = pltpu.roll(b[i], 4, 0)
                normal = jnp.where(low, turned, b[i])
                for m in range(2):
                    r[i][m] = r[i][m] + scale[m] * normal
                value = jnp.where(low, 0.0, turned) if node else jnp.where(low, b[i], 0.0)
                r[i][node // 2] = r[i][node // 2] + value
        else:
            scale = by_place(slope)
            here = by_place([1.0 if p == node else 0.0 for p in range(4)])
            for i in range(4):
                for m in range(2):
                    spread = [
                        jnp.where(
                            low,
                            jnp.broadcast_to(b[i][at : at + 1], (8, lanes)),
                            jnp.broadcast_to(b[i][at + 1 : at + 2], (8, lanes)),
                        )
                        for at in (2 * m, 4 + 2 * m)
                    ]
                    r[i][m] = r[i][m] + (here * spread[0] + scale * spread[1])
    return jnp.concatenate([r[i][m] for i in range(4) for m in range(2)], axis=0)


def face_stack(u, normal_scale):
    scale = jnp.where(slope_rows((32, lanes)), jnp.broadcast_to(normal_scale, (32, lanes)), 1.0)
    fields = [jnp.concatenate([part * scale for part in face_traces(x)], axis=1) for x in u]
    high, low = two(cat(fields, 0))
    return jnp.concatenate([high, low], axis=0)


def gather_message(stack, hot, case, nf):
    got = dot(stack, hot)
    h = 32 * nf
    out = interpolate(got[:h] + got[h : 2 * h], case, nf)
    if stack.shape[0] == 2 * h:
        return out
    coef = got[2 * h : 2 * h + 1] + got[2 * h + 1 : 2 * h + 2] + got[2 * h + 2 : 2 * h + 3]
    size = got[2 * h + 3 : 2 * h + 4] * jnp.where((case >= 0) & (case < 4), 0.5, 1.0)
    row = lax.broadcasted_iota(i32, (8, out.shape[1]), 0)
    scalars = jnp.where(row == 0, coef, jnp.where(row == 1, size, 0.0))
    return jnp.concatenate([out, scalars], axis=0)


def where_am_i(chips):
    me = lax.axis_index("dom")
    chip = me // 2
    core = me - 2 * chip
    near = jnp.where(lax.rem(chip, 2) == 1, -1, 1)
    far = jnp.where(lax.rem(chip, 4) < 2, 1, -1)
    end = (chip == 0) | (chip == chips - 1)
    far_there = (chip - 2 * far >= 0) & (chip - 2 * far < chips)
    return core, near, far, end, ~end, far_there


def carried(core, near, far, near_there, far_there):
    first = core == 0
    return (
        jnp.where(first, near, -near), jnp.where(first, far, -far),
        first | near_there, first | far_there,
    )


def row_of(offset):
    size = jnp.abs(offset)
    return 2 * (size - 1) + jnp.where(offset < 0, 1, 0)


def narrow(offset):
    return jnp.abs(offset) == 3


def side_attributes(side_ref, more=()):
    live = lax.broadcasted_iota(i32, (1, side_pad), 1) < 930
    rows = [jnp.where(live, side_ref[k : k + 1], 0).astype(f32) for k in range(3)]
    rows.append(jnp.where(live, 1.0, 0.0))
    return rows_of(rows + list(more), 16, side_pad).astype(bf16)


def look_up(attributes, index):
    blocks = jnp.concatenate(
        [attributes[:, lanes * k : lanes * k + lanes] for k in range(side_pad // lanes)], axis=0
    )
    found = dot(blocks, one_hot(index & 127, lanes))
    block = index >> 7
    out = jnp.zeros((8, index.shape[1]), f32)
    for k in range(side_pad // lanes):
        out = jnp.where(block == k, found[16 * k : 16 * k + 8], out)
    return out


def place_of(found):
    valid = found[3:4] > 0.5
    return tuple(jnp.where(valid, found[k : k + 1], -1.0).astype(i32) for k in range(3))


def fill_one_hot(hot_ref, elem, face):
    hot = one_hot(elem, lanes)
    for f in range(6):
        hot_ref[lanes * f : lanes * f + lanes] = hot * jnp.where(face == f, 1.0, 0.0).astype(bf16)


def listed_part(rolled_ref, shift, offset, low, high, valid):
    place = shifts.index(shift)
    lane = lax.broadcasted_iota(i32, (1, lanes), 1)
    values = rolled_ref[pl.ds(8 * place + jnp.minimum(row_of(offset), 7), 1), :]
    return jnp.where((lane >= low) & (lane < high) & valid, values, -1)


def send_setup_kernel(chips, *refs):
    sources, refs = refs[:10], refs[10:]
    hot_ref, case_ref, stack_ref, side_ref, rolled_ref = refs[:5]
    sent_ref, landed = refs[5], (*refs[10:17], *refs[6:9])
    slot_ref, arrived = refs[9], refs[17]
    copies = [
        pltpu.make_async_copy(source, target, arrived.at[k])
        for k, (source, target) in enumerate(zip(sources, landed))
    ]
    for copy in copies:
        copy.start()
    elem_ref, dir_ref, sidecase_ref, kind_ref, partner_ref, list_ref = landed[:6]
    start_ref, coef_ref, level_ref = landed[6:9]
    for copy in copies:
        copy.wait()
    side_ref[...] = jnp.full((8, side_pad), -1, i32)
    sides = elem_ref.shape[1]
    for k, ref in enumerate((elem_ref, dir_ref, sidecase_ref, kind_ref, partner_ref)):
        side_ref[k : k + 1, 0:sides] = ref[...]
    core, near, far, end, near_there, far_there = where_am_i(chips)
    listed = jnp.concatenate([list_ref[...], jnp.full((8, 32), -1, i32)], axis=1)
    for place, shift in enumerate(shifts):
        rolled_ref[8 * place : 8 * place + 8] = (
            pltpu.roll(listed, shift, 1) if shift else listed
        )
    part = functools.partial(listed_part, rolled_ref)
    other = 1 - core
    step, step_two, there, there_two = carried(other, near, far, near_there, far_there)
    cross, cross_two = 2 * step + other - core, 4 * step_two + other - core
    first = (
        part(0, cross_two, 0, 24, there_two & narrow(cross_two)),
        part(24, 4 * step_two, 24, 48, there_two),
        part(48, 2 * step, 48, 96, there),
        part(96, cross, 96, 120, there & narrow(cross)),
    )
    slot_ref[0:1, 0:128] = functools.reduce(jnp.maximum, first)
    slot_ref[0:1, 128:256] = part(0, cross, 0, 96, there & ~narrow(cross))
    elem, face, slot_case = place_of(look_up(side_attributes(side_ref), slot_ref[0:1, :]))
    case_ref[0:1, :] = slot_case
    fill_one_hot(hot_ref, elem, face)

    coef, size, volume_scale, normal_scale = element_rows(coef_ref, level_ref)
    stack = face_stack([start_ref[...]], normal_scale)
    scalars = rows_of([x.astype(f32) for x in three(coef)] + [size], 16, lanes).astype(bf16)
    stack = jnp.concatenate([stack, jnp.concatenate([scalars] * 6, axis=1)], axis=0)
    stack_ref[...] = stack
    sent = gather_message(stack, hot_ref[...], slot_case, 1)
    sent_ref[...] = sent


def own_setup_kernel(chips, side_ref, rolled_ref, hot_ref, case_ref, slot_ref):
    core, near, far, end, near_there, far_there = where_am_i(chips)
    part = functools.partial(listed_part, rolled_ref)
    flip = 1 - 2 * core
    step, step_two, there, there_two = carried(core, near, far, near_there, far_there)
    cross, cross_two = 2 * step + flip, 4 * step_two + flip
    slot_ref[0:1, 0:128] = jnp.maximum(
        part(0, 4 * step_two, 0, 24, there_two),
        part(24, cross_two, 24, 48, there_two & narrow(cross_two)),
    )
    slot_ref[0:1, 128:256] = jnp.maximum(
        part(0, 2 * step, 0, 48, there), part(96, cross, 96, 120, there & narrow(cross))
    )
    slot_ref[0:1, 256:384] = part(0, cross, 0, 96, there & ~narrow(cross))
    slot_ref[0:1, 384:512] = part(0, flip, 0, 96, core >= 0)
    elem, face, slot_case = place_of(look_up(side_attributes(side_ref), slot_ref[0:1, :]))
    case_ref[0:1, :] = slot_case
    fill_one_hot(hot_ref, elem, face)


def own_kernel(nf, stack_ref, hot_ref, case_ref, own_ref):
    own_ref[...] = gather_message(
        stack_ref[...], hot_ref[...], case_ref[0:1], nf
    )


def carry_kernel(sent_ref, own_ref, *rest):
    two_ref, one_ref = rest[-2:]
    lane = lax.broadcasted_iota(i32, (1, lanes), 1)
    sent = sent_ref[:, 0:128]
    handed = jnp.where((lane >= 48) & (lane < 96), pltpu.roll(sent, 48, 1), 0.0)
    two_ref[...] = own_ref[:, 0:128] + handed
    one_ref[:, 0:128] = own_ref[:, 128:256] + jnp.where(lane >= 48, sent, 0.0)
    one_ref[:, 128:256] = own_ref[:, 256:384] + sent_ref[:, 128:256]


def relay_kernel(chips, one_ref, two_ref, own_ref, *rest):
    out_ref = rest[-1]
    core, near, far, end, near_there, far_there = where_am_i(chips)
    lane = lax.broadcasted_iota(i32, (1, lanes), 1)
    one, two_away = one_ref[:, 0:128], two_ref[...]
    out_ref[:, 0:128] = own_ref[:, 384:512]
    passed = jnp.where(lane < 24, pltpu.roll(two_away, 56, 1), two_away)
    out_ref[:, 128:256] = jnp.where((lane < 48) & ~(end & (core == 1)), passed, one)
    out_ref[:, 256:384] = one_ref[:, 128:256]


def setup_kernel(
    chips, coef_ref, level_ref, side_ref,
    own_hot_ref, partner_hot_ref, far_hot_ref, place_ref, info_ref, arrival_ref,
):
    core, near, far, end, near_there, far_there = where_am_i(chips)
    elem, direction, case = side_ref[0:1], side_ref[1:2], side_ref[2:3]
    kind, partner = side_ref[3:4], side_ref[4:5]
    live = lax.broadcasted_iota(i32, (1, side_pad), 1) < 930

    coef, size, volume_scale, normal_scale = element_rows(coef_ref, level_ref)
    scalars = rows_of([x.astype(f32) for x in three(coef)] + [size], 16, lanes)
    mine = dot(scalars.astype(bf16), one_hot(elem, lanes))
    hanging = (case >= 0) & (case < 4)
    own_coef = mine[0:1] + mine[1:2] + mine[2:3]
    own_size = mine[3:4] * jnp.where(hanging, 0.5, 1.0)

    attributes = side_attributes(side_ref, (mine[0:1], mine[1:2], mine[2:3], own_size))
    here = live & (partner < 930)
    other = look_up(attributes, jnp.where(here, partner, -1))
    other_elem, other_face = place_of(other)[:2]
    partner_hot_ref[...] = one_hot(other_elem, lanes)
    valid = other[3:4] > 0.5
    edge = jnp.where(kind == 1, 1.0, 0.0)
    least = jnp.where(valid, jnp.minimum(own_size, other[7:8]), 0.0)
    jump = 16.0 * (own_coef + other[4:5] + other[5:6] + other[6:7]) * least
    area = least * least
    info_ref[:, 0:side_pad] = rows_of(
        [jump, jump * (1.0 - edge), area * (0.5 + 0.5 * edge), area * (0.5 - 0.5 * edge),
         case.astype(f32), other[2:3]],
        8, side_pad,
    )

    def arrives(carrier):
        last = end & (carrier == 1)
        back = jnp.where((carrier == 0) | end, -near, near)
        back_two = jnp.where(carrier == 0, -far, far)
        turn = 2 * core - 1
        return (
            2 * back, 2 * back + turn, 4 * back_two, 4 * back_two + turn,
            ~(end & (carrier == 0)), ~last, last,
        )

    def span(low, high, valid):
        return low, jnp.where(valid, high, low)

    segments = []
    for mine, carrier in ((True, core), (False, 1 - core)):
        straight, cross, straight_two, cross_two, there, there_two, last = arrives(carrier)
        slim, wide = there & narrow(cross), there & ~narrow(cross)
        at_first = (last & (core != 1)) | (~last & (carrier == core))
        if mine:
            two_parts = ((*span(48, 72, there_two & narrow(cross_two)), cross_two),
                         (*span(72, 96, there_two), straight_two))
        else:
            segments.append(((0, 96, 2 * core - 1),))
            two_parts = ((*span(0, 24, there_two), straight_two),
                         (*span(24, 48, there_two & narrow(cross_two)), cross_two))
        segments.append((
            (*span(0, 48, there & at_first), straight), (*span(48, 96, there & ~at_first), straight),
            (*span(96, 120, slim), cross), *two_parts,
        ))
        segments.append(((*span(0, 96, wide), cross),))
    entry = partner - 930
    peer = (entry * 683) >> 16
    entry = entry - 96 * peer
    sought = live & (partner >= 930) & (kind == 0)
    column = jnp.full((1, side_pad), -1, i32)
    for tile, parts in enumerate(segments):
        for low, high, offset in parts:
            match = sought & (peer == row_of(offset)) & (entry < high - low)
            column = jnp.where(match, lanes * tile + low + entry, column)
    block = column >> 7
    split = [
        attributes * jnp.where(block == tile, 1.0, 0.0).astype(bf16) for tile in range(len(segments))
    ]
    target = dot_t(jnp.concatenate(split, axis=0), one_hot(column & 127, lanes))
    target = jnp.concatenate(
        [target[16 * tile : 16 * tile + 8] for tile in range(len(segments))], axis=1
    )
    target_elem, target_face, target_case = place_of(target)
    elems = jnp.concatenate([elem, target_elem], axis=1)
    faces = jnp.concatenate([direction, target_face], axis=1)
    near = side_pad + 256
    own_hot_ref[...] = one_hot(elems[:, :near], lanes)
    far_hot_ref[...] = one_hot(elems[:, near:], lanes)
    other_face = jnp.concatenate([other_face, jnp.full((1, 640), -1, i32)], axis=1)
    place_ref[...] = rows_of(
        [elems.astype(f32), faces.astype(f32), other_face.astype(f32)], 16, elems.shape[1]
    )
    info_ref[:, side_pad:] = rows_of(
        [jnp.zeros((1, 256), f32)] * 4 + [target_case[:, 0:256].astype(f32)], 8, 256
    )
    arrival_ref[...] = rows_of(
        [target_case.astype(f32), target[4:5] + target[5:6] + target[6:7], target[7:8]],
        8, 640,
    )


def whole_kernel(own_elem_ref, partner_elem_ref, far_elem_ref, place_ref, own_ref, partner_ref, far_ref):
    near = side_pad + 256
    for source, row, low, high, target in (
        (own_elem_ref, 1, 0, near, own_ref),
        (partner_elem_ref, 2, 0, side_pad, partner_ref),
        (far_elem_ref, 1, near, near + 384, far_ref),
    ):
        hot, face = source[...], place_ref[row : row + 1, low:high]
        for f in range(6):
            target[lanes * f : lanes * f + lanes] = hot * jnp.where(face == f, 1.0, 0.0).astype(bf16)


def turn_kernel(place_ref, own_ref, far_ref):
    row = lax.broadcasted_iota(i32, (16, lanes), 0)
    weight = jnp.where(row == 0, 1.0, jnp.where(row == 1, 128.0, 0.0)).astype(bf16)
    column = lax.dot_general(
        place_ref[...].astype(bf16), weight, (((0,), (0,)), ((), ())), preferred_element_type=f32
    )
    lane = lax.broadcasted_iota(i32, (1, lanes), 1).astype(f32)
    split = own_ref.shape[0]
    for f in range(6):
        part = jnp.where(column == lane + 128.0 * f, 1.0, 0.0).astype(bf16)
        own_ref[:, lanes * f : lanes * f + lanes] = part[:split]
        far_ref[:, lanes * f : lanes * f + lanes] = part[split:]


def sides_kernel(
    nf, stack_ref, own_hot_ref, partner_hot_ref, far_hot_ref, place_ref, info_ref,
    arrival_ref, mine_ref, other_ref, target_ref,
):
    stack = stack_ref[0 : 64 * nf]
    near = side_pad + 256
    for hot_ref, face, case, out_ref in (
        (own_hot_ref, place_ref[1:2, 0:near], info_ref[4:5], mine_ref),
        (partner_hot_ref, place_ref[2:3, 0:side_pad], info_ref[5:6, 0:side_pad], other_ref),
        (far_hot_ref, place_ref[1:2, near:], arrival_ref[0:1, 256:640], target_ref),
    ):
        got = gather_columns(stack, hot_ref[...], face, nf)
        out_ref[...] = interpolate(got, case.astype(i32), nf)


def side_flux(nf, mine, outer, coefs, case, face, weight_ref, hot):
    jump, jump_out, area, area_out = coefs
    weight = weight_ref[:, 0:1]
    flux = []
    for k in range(nf):
        inner, other = mine[32 * k : 32 * k + 32], outer[32 * k : 32 * k + 32]
        jumps = jnp.where(slope_rows(inner.shape), 0.0, jump * inner - jump_out * other)
        flux.append(weight * (jumps - other_part(area * inner - area_out * other)))
    flux = interpolate(cat(flux, 0), case.astype(i32), nf, transposed=True)
    return scatter_columns(flux, hot, face, nf)


def halo_coefs(coef, size, other_coef, other_size):
    least = jnp.minimum(size, other_size)
    return 16.0 * (coef + other_coef) * least, 0.5 * least * least


def flux_kernel(
    nf, chips, one_ref, two_ref, mine_ref, other_ref, place_ref, info_ref, arrival_ref, weight_ref,
    own_hot_ref, field_ref, coef_ref, level_ref, stiffness_ref, *rest,
):
    h = 32 * nf
    core, near, far, end, near_there, far_there = where_am_i(chips)
    lane = lax.broadcasted_iota(i32, (1, lanes), 1)
    two_away = two_ref[...]
    kept = jnp.where(lane < 72, two_away, pltpu.roll(two_away, 72, 1))
    inside = (lane >= 48) & (lane < 96) & ~(end & (core == 1))
    got = jnp.concatenate(
        [jnp.where(inside, kept, one_ref[:, 0:128]), one_ref[:, 128:256]], axis=1
    )
    if got.shape[0] > h:
        sum_ref, volume_ref, halo_ref = rest
        halo = halo_coefs(
            arrival_ref[1:2, 0:256], arrival_ref[2:3, 0:256], got[h : h + 1], got[h + 1 : h + 2]
        )
        halo_ref[...] = rows_of(halo, 8, 256)
    else:
        halo_ref, sum_ref, volume_ref = rest
        halo = halo_ref[0:1], halo_ref[1:2]
    coefs = [
        jnp.concatenate([info_ref[k : k + 1, 0:side_pad], halo[k // 2]], axis=1) for k in range(4)
    ]
    outer = jnp.concatenate([other_ref[...], got[0:h]], axis=1)
    sum_ref[...] = side_flux(
        nf, mine_ref, outer, coefs, info_ref[4:5], place_ref[1:2, 0 : side_pad + 256], weight_ref,
        own_hot_ref[...],
    )
    volume_scale = element_rows(coef_ref, level_ref)[2]
    fields = [field_ref[64 * k : 64 * k + 64] * volume_scale for k in range(nf)]
    volume = table_dot(stiffness_ref[...], cat(fields, 1))
    for k in range(nf):
        volume_ref[64 * k : 64 * k + 64, :] = volume[:, lanes * k : lanes * k + lanes]


def solve_blocks(inverse_ref, hold_ref, nf):
    sums = [jnp.zeros((64, lanes), f32) for _ in range(nf)]
    for col in range(64):
        block = inverse_ref[col].astype(f32)
        for k in range(nf):
            sums[k] = sums[k] + block * hold_ref[64 * k + col : 64 * k + col + 1, :]
    return sums


def update_kernel(
    turn, nf, nf_next,
    one_ref, local_ref, volume_ref, target_ref, place_ref, arrival_ref, far_hot_ref, weight_ref,
    field_ref, coef_ref, level_ref, inverse_ref, *rest,
):
    if turn == 0:
        guess_ref, *rest = rest
    else:
        halo_ref, *rest = rest
    if turn == 1:
        rhs_ref, *rest = rest
    if nf_next:
        hot_ref, case_ref, new_ref, stack_ref, sent_ref, *rest = rest
    else:
        part_ref, *rest = rest
    hold_ref = rest[-1]
    h = 32 * nf
    if turn == 0:
        halo = halo_coefs(
            arrival_ref[1:2, 256:640], arrival_ref[2:3, 256:640],
            one_ref[h : h + 1], one_ref[h + 1 : h + 2],
        )
        rest[0][...] = rows_of(halo, 8, 384)
    else:
        halo = (halo_ref[0:1], halo_ref[1:2])
    total = local_ref[...] + side_flux(
        nf, target_ref, one_ref, (halo[0], halo[0], halo[1], halo[1]), arrival_ref[0:1, 256:640],
        place_ref[1:2, side_pad + 256 :], weight_ref, far_hot_ref[...],
    )
    coef, size, volume_scale, normal_scale = element_rows(coef_ref, level_ref)
    scale = jnp.where(slope_rows((32, lanes)), jnp.broadcast_to(normal_scale, (32, lanes)), 1.0)
    for k in range(nf):
        mine = total[32 * k : 32 * k + 32]
        faces = [mine[:, lanes * f : lanes * f + lanes] * scale for f in range(6)]
        part = lift_traces(volume_ref[64 * k : 64 * k + 64], faces)
        if turn == 1 and k == 1:
            part = rhs_ref[...] - part
        hold_ref[64 * k : 64 * k + 64, :] = part
    new = solve_blocks(inverse_ref, hold_ref, nf)
    if turn == 0:
        new.append(guess_ref[...])
    if nf_next:
        for k, x in enumerate(new):
            new_ref[64 * k : 64 * k + 64, :] = x
        stack = face_stack(new[:nf_next], normal_scale)
        stack_ref[...] = stack
        sent = gather_message(stack, hot_ref[...], case_ref[0:1], nf_next)
        sent_ref[...] = sent
    else:
        lane = lax.broadcasted_iota(i32, (1, lanes), 1)
        sums = []
        for x in (field_ref[...], new[0]):
            total = jnp.sum(x * x, axis=0, keepdims=True)
            sums.append(total + pltpu.roll(total, 64, 1))
        part_ref[...] = jnp.broadcast_to(jnp.where(lane < 64, sums[0], sums[1]), part_ref.shape)


def finish_kernel(part_ref, guess_ref, first_ref, second_ref, out_ref, bound_ref):
    total = jnp.sum(part_ref[...], axis=0, keepdims=True)
    lane = lax.broadcasted_iota(i32, (1, lanes), 1)
    before = jnp.sum(jnp.where(lane < 64, total, 0.0), axis=1, keepdims=True)
    after = jnp.sum(jnp.where(lane < 64, 0.0, total), axis=1, keepdims=True)
    bound = jnp.sqrt(after / before)
    upper = 1.2 * bound
    lower = upper / 15.0
    center = 0.5 * (upper + lower)
    half = 0.5 * (upper - lower)
    ratio = center / half
    damping = 1.0 / ratio
    damping_next = 1.0 / (2.0 * ratio - damping)
    first = first_ref[64:128] / center
    second = first_ref[64:128] - second_ref[64:128] / center
    out_ref[...] = (
        guess_ref[...] + first + (damping_next * damping * first + 2.0 * damping_next / half * second)
    )
    bound_ref[...] = jnp.broadcast_to(bound, (1, lanes))


def in_vmem(x):
    return pltpu.with_memory_space_constraint(x, pltpu.VMEM)


def in_hbm(x):
    return pltpu.with_memory_space_constraint(x, pltpu.HBM)


def run(body, outs, ins, name, scratch=(), flops=1 << 24, placed=True, kept=True):
    spec = pl.BlockSpec(memory_space=pltpu.VMEM)
    return pl.pallas_call(
        body,
        out_shape=[(pltpu.VMEM if kept else jax.ShapeDtypeStruct)(shape, dtype) for shape, dtype in outs],
        in_specs=[spec if placed else pl.BlockSpec(memory_space=pltpu.HBM)] * len(ins),
        out_specs=[spec] * len(outs),
        scratch_shapes=list(scratch),
        compiler_params=pltpu.CompilerParams(vmem_limit_bytes=24 << 20),
        cost_estimate=pl.CostEstimate(flops=flops, bytes_accessed=1 << 20, transcendentals=0),
        name=name,
    )(*(in_vmem(x) if placed else in_hbm(x) for x in ins))


def local(
    rhs_field, initial_guess, start_vector, coefficient, refine_level, block_inverse,
    side_elem, side_dir, side_case, side_kind, partner, send_list,
):
    devices = lax.axis_size("dom")
    chips = devices // 2
    stiffness, weight = (jnp.asarray(t) for t in const_tables())
    coef = coefficient.reshape(1, lanes)
    level = refine_level.reshape(1, lanes)

    def permute(x, to):
        return lax.ppermute(x, "dom", sorted(to.items()))

    swapped = {i: i ^ 1 for i in range(devices)}
    two_away, one_away = {}, {}
    for c in range(chips):
        two_away[2 * c] = 2 * (c ^ 2)
        one_away[2 * c] = 2 * (c ^ 1)
        over = c + 2 if c % 4 >= 2 else c - 2
        two_away[2 * c + 1] = 2 * (over if 0 <= over < chips else c ^ 1) + 1
        if 0 < c < chips - 1:
            one_away[2 * c + 1] = 2 * (c + 1 if c % 2 else c - 1) + 1
    for c in (0, chips - 1):
        one_away[2 * (c ^ 1)] = 2 * c + 1
        one_away[2 * c + 1] = 2 * c

    def exchange(sent, nf, own_work, work, *beside):
        rows = sent.shape[0]
        (own,) = own_work()
        two_out, one_out = run(
            carry_kernel, [((rows, lanes), f32), ((rows, 256), f32)],
            [permute(sent, swapped), own, *beside[:1]], "carry",
        )
        arrivals = permute(one_out, one_away), permute(two_out, two_away)
        made = work()
        (last,) = run(
            functools.partial(relay_kernel, chips), [((rows, 384), f32)],
            [*arrivals, own, made[2], *beside[1:]], "relay",
        )
        return arrivals, permute(last, swapped), made

    sides = [x.reshape(1, -1) for x in (side_elem, side_dir, side_case, side_kind, partner)]
    first = [*sides, send_list, start_vector, coef, level, initial_guess]
    hot, case, stack, sides, rolled, sent, coef, level, guess = run(
        functools.partial(send_setup_kernel, chips),
        [((768, 256), bf16), ((8, 256), i32), ((80, 768), bf16), ((8, side_pad), i32), ((32, lanes), i32),
         ((40, 256), f32), *((x.shape, x.dtype) for x in first[7:])],
        first,
        "send_setup",
        scratch=[
            pltpu.VMEM((8, 256), i32),
            *(pltpu.VMEM(x.shape, x.dtype) for x in first[:7]), pltpu.SemaphoreType.DMA((len(first),)),
        ],
        placed=False,
    )
    own_slots = run(
        functools.partial(own_setup_kernel, chips),
        [((768, 512), bf16), ((8, 512), i32)],
        [sides, rolled],
        "own_setup",
        scratch=[pltpu.VMEM((8, 512), i32)],
    )
    fields = start_vector
    history = []
    for turn, (nf, nf_next) in enumerate(((1, 2), (2, 2), (2, 1), (1, 0))):
        h = 32 * nf
        def own_work():
            return run(
                functools.partial(own_kernel, nf),
                [((sent.shape[0], 512), f32)],
                [stack, *own_slots],
                "own",
            )

        def side_work(hots):
            return run(
                functools.partial(sides_kernel, nf),
                [((h, side_pad + 256), f32), ((h, side_pad), f32), ((h, 384), f32)],
                [stack, *hots, *places],
                "sides",
            )

        if turn == 0:
            *hots, place, info, arrival = run(
                functools.partial(setup_kernel, chips),
                [((lanes, side_pad + 256), bf16), ((lanes, side_pad), bf16), ((lanes, 384), bf16),
                 ((16, side_pad + 640), f32), ((8, side_pad + 256), f32), ((8, 640), f32)],
                [coef, level, sides],
                "setup",
            )
            places = [place, info, arrival]
            own_scatter, _, far_scatter = hots
        elif turn == 1:
            hots = run(
                whole_kernel,
                [((768, side_pad + 256), bf16), ((768, side_pad), bf16), ((768, 384), bf16)],
                [*hots, place],
                "whole",
            )
            own_scatter, far_scatter = run(
                turn_kernel,
                [((side_pad + 256, 768), bf16), ((384, 768), bf16)],
                [place],
                "turn",
            )
        arrivals, last, made = exchange(
            sent, nf, own_work, functools.partial(side_work, hots),
            *((hots[0], own_scatter) if turn == 1 else ()),
        )
        mine, others, targets = made
        sums, volume, *made = run(
            functools.partial(flux_kernel, nf, chips),
            [((h, 768), f32), ((64 * nf, lanes), f32)] + ([] if turn else [((8, 256), f32)]),
            [*arrivals, mine, others, *places, weight, own_scatter, fields, coef, level, stiffness]
            + ([near_halo] if turn else []),
            "flux",
        )
        if turn == 0:
            near_halo = made[0]
        ins = [
            last, sums, volume, targets, place, arrival, far_scatter, weight,
            fields, coef, level, block_inverse,
        ]
        ins += [far_halo] if turn else [guess]
        ins += [rhs_field] if turn == 1 else []
        if nf_next:
            ins += [hot, case]
            outs = [
                ((64 * max(nf, nf_next), lanes), f32), ((64 * nf_next, 768), bf16), ((32 * nf_next, 256), f32)
            ]
        else:
            outs = [((devices, lanes), f32)]
        made = run(
            functools.partial(update_kernel, turn, nf, nf_next),
            outs + ([] if turn else [((8, 384), f32)]), ins, "update",
            scratch=[pltpu.VMEM((64 * nf, lanes), f32)],
        )
        if turn == 0:
            far_halo = made[-1]
        if nf_next:
            fields, stack, sent = made[:3]
            history.append(fields)
            if nf_next < nf:
                fields = fields[:64]
        else:
            (parts,) = made
    parts = lax.all_to_all(parts.reshape(devices, 1, lanes), "dom", 0, 0).reshape(devices, lanes)
    smoothed, bound = run(
        finish_kernel,
        [((64, lanes), f32), ((1, lanes), f32)],
        [parts, guess, history[1], history[2]],
        "finish",
        kept=False,
    )
    return smoothed, bound[0, 0]


def solution(mesh):
    placed = (
        P(None, "dom"), P(None, "dom"), P(None, "dom"), P("dom"), P("dom"), P(None, None, "dom"),
        P("dom"), P("dom"), P("dom"), P("dom"), P("dom"), P("dom", None),
    )
    return jax.shard_map(
        local, mesh=mesh, in_specs=placed, out_specs=(P(None, "dom"), P()), check_vma=False
    )
```

```python
import functools
import math

import jax
import jax.numpy as jnp
import numpy as np
from jax import lax
from jax.experimental import pallas as pl
from jax.experimental.pallas import tpu as pltpu
from jax.sharding import PartitionSpec as P

f32 = jnp.float32
bf16 = jnp.bfloat16
i32 = jnp.int32
peer_offsets = (1, -1, 2, -2, 3, -3, 4, -4)
live_width = {1: 96, 2: 48, 3: 24, 4: 24}
lanes = 128
shifts = (0, 24, 48, 96)
side_pad = 1024


def lagrange_tables():
    root_five = 1.0 / math.sqrt(5.0)
    nodes = np.array([0.0, 0.5 - 0.5 * root_five, 0.5 + 0.5 * root_five, 1.0])
    weights = np.array([1.0, 5.0, 5.0, 1.0]) / 12.0
    factor = np.array(
        [np.prod([nodes[i] - nodes[j] for j in range(4) if j != i]) for i in range(4)]
    )
    derivative = np.zeros((4, 4))
    for i in range(4):
        for j in range(4):
            if i != j:
                derivative[i, j] = factor[i] / (factor[j] * (nodes[i] - nodes[j]))
        derivative[i, i] = -np.sum(derivative[i])
    halves = []
    for half in range(2):
        points = 0.5 * (nodes + half)
        table = np.ones((4, 4))
        for j in range(4):
            for other in range(4):
                if other != j:
                    table[:, j] *= (points - nodes[other]) / (nodes[j] - nodes[other])
        halves.append(table)
    return weights, derivative, halves


def stiffness_table():
    weights, derivative, halves = lagrange_tables()
    mass = np.diag(weights)
    line = derivative.T @ mass @ derivative
    return (
        np.kron(np.kron(line, mass), mass)
        + np.kron(np.kron(mass, line), mass)
        + np.kron(np.kron(mass, mass), line)
    )


def weight_table():
    weights = lagrange_tables()[0]
    rows = [weights[first] * weights[second] for first in range(4) for part in range(2) for second in range(4)]
    return np.broadcast_to(np.array(rows, np.float32)[:, None], (32, lanes))


def stacked(table):
    table = np.asarray(table, np.float32)
    high = table.astype(jnp.bfloat16)
    low = (table - high.astype(np.float32)).astype(jnp.bfloat16)
    return np.concatenate([high, high, low], axis=1)


def const_tables():
    return stacked(stiffness_table()), np.ascontiguousarray(weight_table())


def two(x):
    high = x.astype(bf16)
    return high, (x - high.astype(f32)).astype(bf16)


def three(x):
    high = x.astype(bf16)
    rest = x - high.astype(f32)
    mid = rest.astype(bf16)
    return high, mid, (rest - mid.astype(f32)).astype(bf16)


def dot(a, b):
    return jnp.dot(a, b, preferred_element_type=f32)


def dot_t(a, b):
    return lax.dot_general(a, b, (((1,), (1,)), ((), ())), preferred_element_type=f32)


def cat(parts, axis):
    return parts[0] if len(parts) == 1 else jnp.concatenate(parts, axis=axis)


def table_dot(table, x):
    high, low = two(x)
    return dot(table, jnp.concatenate([high, low, high], axis=0))


def interpolate(x, case, nf, transposed=False):
    halves = [h.T if transposed else h for h in lagrange_tables()[2]]
    n = x.shape[1]
    case = jnp.broadcast_to(case, (8, n))
    hanging = (case >= 0) & (case < 4)
    place = lax.broadcasted_iota(i32, (8, n), 0) & 3

    def pick(second, low, high, whole):
        return jnp.where(hanging, jnp.where(second, high, low), whole)

    def along(half, step):
        tile = jnp.zeros((8, n), f32)
        for j in range(4):
            if 0 <= j + step < 4:
                tile = jnp.where(place == j, float(half[j, j + step]), tile)
        return tile

    first, second = case >= 2, (case & 1) == 1
    across = [
        [pick(first, float(halves[0][i, j]), float(halves[1][i, j]), float(i == j)) for j in range(4)]
        for i in range(4)
    ]
    within = {
        step: pick(second, along(halves[0], step), along(halves[1], step), float(step == 0))
        for step in range(-3, 4)
    }
    out = []
    for k in range(nf):
        part = [x[32 * k + 8 * i : 32 * k + 8 * i + 8] for i in range(4)]
        for i in range(4):
            mixed = sum(across[i][j] * part[j] for j in range(4))
            out.append(
                sum(
                    within[step] * (pltpu.roll(mixed, -step % 8, 0) if step else mixed)
                    for step in range(-3, 4)
                )
            )
    return jnp.concatenate(out, axis=0)


def other_part(x):
    return jnp.concatenate(
        [pltpu.roll(x[8 * g : 8 * g + 8], 4, 0) for g in range(x.shape[0] // 8)], axis=0
    )


def slope_rows(shape):
    return (lax.broadcasted_iota(i32, shape, 0) & 4) == 4


def rows_of(rows, count, width):
    place = lax.broadcasted_iota(i32, (count, width), 0)
    table = jnp.zeros((count, width), f32)
    for k, r in enumerate(rows):
        table = jnp.where(place == k, r, table)
    return table


def one_hot(index_row, rows, first=0):
    place = lax.broadcasted_iota(i32, (rows, index_row.shape[1]), 0) + first
    return jnp.where(place == index_row, 1.0, 0.0).astype(bf16)


def gather_columns(stack, hot, face, nf):
    h = 32 * nf
    if hot.shape[0] == 768:
        got = dot(stack, hot)
        return got[:h] + got[h:]
    parts = [stack[:, lanes * f : lanes * f + lanes] for f in range(6)]
    got = dot(jnp.concatenate(parts, axis=0), hot)
    out = got[:h] + got[h : 2 * h]
    for f in range(1, 6):
        low = 2 * h * f
        out = jnp.where(face == f, got[low : low + h] + got[low + h : low + 2 * h], out)
    return out


def scatter_columns(x, hot, face, nf):
    h = 32 * nf
    high, low = two(x)
    both = jnp.concatenate([high, low], axis=0)
    if hot.shape[1] == 768:
        got = dot(both, hot)
        return got[:h] + got[h:]
    parts = [both * jnp.where(face == f, 1.0, 0.0).astype(bf16) for f in range(6)]
    got = dot_t(jnp.concatenate(parts, axis=0), hot)
    return jnp.concatenate(
        [got[2 * h * f : 2 * h * f + h] + got[2 * h * f + h : 2 * h * f + 2 * h] for f in range(6)],
        axis=1,
    )


def element_rows(coef_ref, level_ref):
    coef = coef_ref[...]
    level = level_ref[...]
    size = jnp.where(level == 0, 1.0, jnp.where(level == 1, 0.5, 0.25)).astype(f32)
    inverse = jnp.where(level == 0, 1.0, jnp.where(level == 1, 2.0, 4.0)).astype(f32)
    return coef, size, coef * size, coef * inverse


def by_place(values):
    place = lax.broadcasted_iota(i32, (8, lanes), 0) & (len(values) - 1)
    tile = jnp.full((8, lanes), float(values[0]), f32)
    for p in range(1, len(values)):
        tile = jnp.where(place == p, float(values[p]), tile)
    return tile


def face_ends():
    derivative = lagrange_tables()[1]
    for dim in range(3):
        for lower in range(2):
            node = 0 if lower else 3
            yield dim, 2 * dim + lower, node, (-1.0 if lower else 1.0) * derivative[node]


def face_traces(u):
    sub = lax.broadcasted_iota(i32, (8, lanes), 0)
    low = sub < 4
    v = [[u[16 * i + 8 * m : 16 * i + 8 * m + 8] for m in range(2)] for i in range(4)]
    out = {}
    for dim, face, node, slope in face_ends():
        rows = []
        if dim == 0:
            for m in range(2):
                normal = sum(float(slope[i]) * v[i][m] for i in range(4))
                rows.append(jnp.where(low, v[node][m], pltpu.roll(normal, 4, 0)))
                rows.append(jnp.where(low, pltpu.roll(v[node][m], 4, 0), normal))
        elif dim == 1:
            scale = [by_place([slope[2 * m]] * 4 + [slope[2 * m + 1]] * 4) for m in range(2)]
            for i in range(4):
                normal = scale[0] * v[i][0] + scale[1] * v[i][1]
                normal = normal + pltpu.roll(normal, 4, 0)
                rows.append(jnp.where(low, pltpu.roll(v[i][1], 4, 0) if node else v[i][0], normal))
        else:
            scale = by_place(slope)
            for i in range(4):
                row = None
                for m in range(2):
                    normal = scale * v[i][m]
                    normal = normal + pltpu.roll(normal, 7, 0)
                    normal = normal + pltpu.roll(normal, 6, 0)
                    for half in range(2):
                        to = 2 * m + half
                        value = pltpu.roll(v[i][m], (to - 4 * half - node) % 8, 0)
                        shift = (to + 4 - 4 * half) % 8
                        moved = pltpu.roll(normal, shift, 0) if shift else normal
                        row = value if row is None else jnp.where(sub == to, value, row)
                        row = jnp.where(sub == to + 4, moved, row)
                rows.append(row)
        out[face] = jnp.concatenate(rows, axis=0)
    return [out[f] for f in range(6)]


def lift_traces(total, faces):
    sub = lax.broadcasted_iota(i32, (8, lanes), 0)
    low = sub < 4
    r = [[total[16 * i + 8 * m : 16 * i + 8 * m + 8] for m in range(2)] for i in range(4)]
    for dim, face, node, slope in face_ends():
        b = [faces[face][8 * i : 8 * i + 8] for i in range(4)]
        if dim == 0:
            for m in range(2):
                even, odd = b[2 * m], b[2 * m + 1]
                normal = jnp.where(low, pltpu.roll(even, 4, 0), odd)
                for i in range(4):
                    r[i][m] = r[i][m] + float(slope[i]) * normal
                r[node][m] = r[node][m] + jnp.where(low, even, pltpu.roll(odd, 4, 0))
        elif dim == 1:
            scale = [by_place([slope[2 * m]] * 4 + [slope[2 * m + 1]] * 4) for m in range(2)]
            for i in range(4):
                turned = pltpu.roll(b[i], 4, 0)
                normal = jnp.where(low, turned, b[i])
                for m in range(2):
                    r[i][m] = r[i][m] + scale[m] * normal
                value = jnp.where(low, 0.0, turned) if node else jnp.where(low, b[i], 0.0)
                r[i][node // 2] = r[i][node // 2] + value
        else:
            scale = by_place(slope)
            here = by_place([1.0 if p == node else 0.0 for p in range(4)])
            for i in range(4):
                for m in range(2):
                    spread = [
                        jnp.where(
                            low,
                            jnp.broadcast_to(b[i][at : at + 1], (8, lanes)),
                            jnp.broadcast_to(b[i][at + 1 : at + 2], (8, lanes)),
                        )
                        for at in (2 * m, 4 + 2 * m)
                    ]
                    r[i][m] = r[i][m] + (here * spread[0] + scale * spread[1])
    return jnp.concatenate([r[i][m] for i in range(4) for m in range(2)], axis=0)


def face_stack(u, normal_scale):
    scale = jnp.where(slope_rows((32, lanes)), jnp.broadcast_to(normal_scale, (32, lanes)), 1.0)
    fields = [jnp.concatenate([part * scale for part in face_traces(x)], axis=1) for x in u]
    high, low = two(cat(fields, 0))
    return jnp.concatenate([high, low], axis=0)


def gather_message(stack, hot, case, nf):
    got = dot(stack, hot)
    h = 32 * nf
    out = interpolate(got[:h] + got[h : 2 * h], case, nf)
    if stack.shape[0] == 2 * h:
        return out
    coef = got[2 * h : 2 * h + 1] + got[2 * h + 1 : 2 * h + 2] + got[2 * h + 2 : 2 * h + 3]
    size = got[2 * h + 3 : 2 * h + 4] * jnp.where((case >= 0) & (case < 4), 0.5, 1.0)
    row = lax.broadcasted_iota(i32, (8, out.shape[1]), 0)
    scalars = jnp.where(row == 0, coef, jnp.where(row == 1, size, 0.0))
    return jnp.concatenate([out, scalars], axis=0)


def where_am_i(chips):
    me = lax.axis_index("dom")
    chip = me // 2
    core = me - 2 * chip
    near = jnp.where(lax.rem(chip, 2) == 1, -1, 1)
    far = jnp.where(lax.rem(chip, 4) < 2, 1, -1)
    end = (chip == 0) | (chip == chips - 1)
    far_there = (chip - 2 * far >= 0) & (chip - 2 * far < chips)
    return core, near, far, end, ~end, far_there


def carried(core, near, far, near_there, far_there):
    first = core == 0
    return (
        jnp.where(first, near, -near), jnp.where(first, far, -far),
        first | near_there, first | far_there,
    )


def row_of(offset):
    size = jnp.abs(offset)
    return 2 * (size - 1) + jnp.where(offset < 0, 1, 0)


def narrow(offset):
    return jnp.abs(offset) == 3


def side_attributes(side_ref, more=()):
    live = lax.broadcasted_iota(i32, (1, side_pad), 1) < 930
    rows = [jnp.where(live, side_ref[k : k + 1], 0).astype(f32) for k in range(3)]
    rows.append(jnp.where(live, 1.0, 0.0))
    return rows_of(rows + list(more), 16, side_pad).astype(bf16)


def look_up(attributes, index):
    blocks = jnp.concatenate(
        [attributes[:, lanes * k : lanes * k + lanes] for k in range(side_pad // lanes)], axis=0
    )
    found = dot(blocks, one_hot(index & 127, lanes))
    block = index >> 7
    out = jnp.zeros((8, index.shape[1]), f32)
    for k in range(side_pad // lanes):
        out = jnp.where(block == k, found[16 * k : 16 * k + 8], out)
    return out


def place_of(found):
    valid = found[3:4] > 0.5
    return tuple(jnp.where(valid, found[k : k + 1], -1.0).astype(i32) for k in range(3))


def fill_one_hot(hot_ref, elem, face):
    hot = one_hot(elem, lanes)
    for f in range(6):
        hot_ref[lanes * f : lanes * f + lanes] = hot * jnp.where(face == f, 1.0, 0.0).astype(bf16)


def listed_part(rolled_ref, shift, offset, low, high, valid):
    place = shifts.index(shift)
    lane = lax.broadcasted_iota(i32, (1, lanes), 1)
    values = rolled_ref[pl.ds(8 * place + jnp.minimum(row_of(offset), 7), 1), :]
    return jnp.where((lane >= low) & (lane < high) & valid, values, -1)


def send_setup_kernel(chips, *refs):
    sources, refs = refs[:10], refs[10:]
    hot_ref, case_ref, stack_ref, side_ref, rolled_ref = refs[:5]
    sent_ref, landed = refs[5], (*refs[10:17], *refs[6:9])
    slot_ref, arrived = refs[9], refs[17]
    copies = [
        pltpu.make_async_copy(source, target, arrived.at[k])
        for k, (source, target) in enumerate(zip(sources, landed))
    ]
    for copy in copies:
        copy.start()
    elem_ref, dir_ref, sidecase_ref, kind_ref, partner_ref, list_ref = landed[:6]
    start_ref, coef_ref, level_ref = landed[6:9]
    for copy in copies:
        copy.wait()
    side_ref[...] = jnp.full((8, side_pad), -1, i32)
    sides = elem_ref.shape[1]
    for k, ref in enumerate((elem_ref, dir_ref, sidecase_ref, kind_ref, partner_ref)):
        side_ref[k : k + 1, 0:sides] = ref[...]
    core, near, far, end, near_there, far_there = where_am_i(chips)
    listed = jnp.concatenate([list_ref[...], jnp.full((8, 32), -1, i32)], axis=1)
    for place, shift in enumerate(shifts):
        rolled_ref[8 * place : 8 * place + 8] = (
            pltpu.roll(listed, shift, 1) if shift else listed
        )
    part = functools.partial(listed_part, rolled_ref)
    other = 1 - core
    step, step_two, there, there_two = carried(other, near, far, near_there, far_there)
    cross, cross_two = 2 * step + other - core, 4 * step_two + other - core
    first = (
        part(0, cross_two, 0, 24, there_two & narrow(cross_two)),
        part(24, 4 * step_two, 24, 48, there_two),
        part(48, 2 * step, 48, 96, there),
        part(96, cross, 96, 120, there & narrow(cross)),
    )
    slot_ref[0:1, 0:128] = functools.reduce(jnp.maximum, first)
    slot_ref[0:1, 128:256] = part(0, cross, 0, 96, there & ~narrow(cross))
    elem, face, slot_case = place_of(look_up(side_attributes(side_ref), slot_ref[0:1, :]))
    case_ref[0:1, :] = slot_case
    fill_one_hot(hot_ref, elem, face)

    coef, size, volume_scale, normal_scale = element_rows(coef_ref, level_ref)
    stack = face_stack([start_ref[...]], normal_scale)
    scalars = rows_of([x.astype(f32) for x in three(coef)] + [size], 16, lanes).astype(bf16)
    stack = jnp.concatenate([stack, jnp.concatenate([scalars] * 6, axis=1)], axis=0)
    stack_ref[...] = stack
    sent = gather_message(stack, hot_ref[...], slot_case, 1)
    sent_ref[...] = sent


def own_setup_kernel(chips, side_ref, rolled_ref, hot_ref, case_ref, slot_ref):
    core, near, far, end, near_there, far_there = where_am_i(chips)
    part = functools.partial(listed_part, rolled_ref)
    flip = 1 - 2 * core
    step, step_two, there, there_two = carried(core, near, far, near_there, far_there)
    cross, cross_two = 2 * step + flip, 4 * step_two + flip
    slot_ref[0:1, 0:128] = jnp.maximum(
        part(0, 4 * step_two, 0, 24, there_two),
        part(24, cross_two, 24, 48, there_two & narrow(cross_two)),
    )
    slot_ref[0:1, 128:256] = jnp.maximum(
        part(0, 2 * step, 0, 48, there), part(96, cross, 96, 120, there & narrow(cross))
    )
    slot_ref[0:1, 256:384] = part(0, cross, 0, 96, there & ~narrow(cross))
    slot_ref[0:1, 384:512] = part(0, flip, 0, 96, core >= 0)
    elem, face, slot_case = place_of(look_up(side_attributes(side_ref), slot_ref[0:1, :]))
    case_ref[0:1, :] = slot_case
    fill_one_hot(hot_ref, elem, face)


def own_kernel(nf, stack_ref, hot_ref, case_ref, own_ref):
    own_ref[...] = gather_message(
        stack_ref[...], hot_ref[...], case_ref[0:1], nf
    )


def carry_kernel(sent_ref, own_ref, *rest):
    two_ref, one_ref = rest[-2:]
    lane = lax.broadcasted_iota(i32, (1, lanes), 1)
    sent = sent_ref[:, 0:128]
    handed = jnp.where((lane >= 48) & (lane < 96), pltpu.roll(sent, 48, 1), 0.0)
    two_ref[...] = own_ref[:, 0:128] + handed
    one_ref[:, 0:128] = own_ref[:, 128:256] + jnp.where(lane >= 48, sent, 0.0)
    one_ref[:, 128:256] = own_ref[:, 256:384] + sent_ref[:, 128:256]


def relay_kernel(chips, one_ref, two_ref, own_ref, *rest):
    out_ref = rest[-1]
    core, near, far, end, near_there, far_there = where_am_i(chips)
    lane = lax.broadcasted_iota(i32, (1, lanes), 1)
    one, two_away = one_ref[:, 0:128], two_ref[...]
    out_ref[:, 0:128] = own_ref[:, 384:512]
    passed = jnp.where(lane < 24, pltpu.roll(two_away, 56, 1), two_away)
    out_ref[:, 128:256] = jnp.where((lane < 48) & ~(end & (core == 1)), passed, one)
    out_ref[:, 256:384] = one_ref[:, 128:256]


def setup_kernel(
    chips, coef_ref, level_ref, side_ref,
    own_hot_ref, partner_hot_ref, far_hot_ref, place_ref, info_ref, arrival_ref,
):
    core, near, far, end, near_there, far_there = where_am_i(chips)
    elem, direction, case = side_ref[0:1], side_ref[1:2], side_ref[2:3]
    kind, partner = side_ref[3:4], side_ref[4:5]
    live = lax.broadcasted_iota(i32, (1, side_pad), 1) < 930

    coef, size, volume_scale, normal_scale = element_rows(coef_ref, level_ref)
    scalars = rows_of([x.astype(f32) for x in three(coef)] + [size], 16, lanes)
    mine = dot(scalars.astype(bf16), one_hot(elem, lanes))
    hanging = (case >= 0) & (case < 4)
    own_coef = mine[0:1] + mine[1:2] + mine[2:3]
    own_size = mine[3:4] * jnp.where(hanging, 0.5, 1.0)

    attributes = side_attributes(side_ref, (mine[0:1], mine[1:2], mine[2:3], own_size))
    here = live & (partner < 930)
    other = look_up(attributes, jnp.where(here, partner, -1))
    other_elem, other_face = place_of(other)[:2]
    partner_hot_ref[...] = one_hot(other_elem, lanes)
    valid = other[3:4] > 0.5
    edge = jnp.where(kind == 1, 1.0, 0.0)
    least = jnp.where(valid, jnp.minimum(own_size, other[7:8]), 0.0)
    jump = 16.0 * (own_coef + other[4:5] + other[5:6] + other[6:7]) * least
    area = least * least
    info_ref[:, 0:side_pad] = rows_of(
        [jump, jump * (1.0 - edge), area * (0.5 + 0.5 * edge), area * (0.5 - 0.5 * edge),
         case.astype(f32), other[2:3]],
        8, side_pad,
    )

    def arrives(carrier):
        last = end & (carrier == 1)
        back = jnp.where((carrier == 0) | end, -near, near)
        back_two = jnp.where(carrier == 0, -far, far)
        turn = 2 * core - 1
        return (
            2 * back, 2 * back + turn, 4 * back_two, 4 * back_two + turn,
            ~(end & (carrier == 0)), ~last, last,
        )

    def span(low, high, valid):
        return low, jnp.where(valid, high, low)

    segments = []
    for mine, carrier in ((True, core), (False, 1 - core)):
        straight, cross, straight_two, cross_two, there, there_two, last = arrives(carrier)
        slim, wide = there & narrow(cross), there & ~narrow(cross)
        at_first = (last & (core != 1)) | (~last & (carrier == core))
        if mine:
            two_parts = ((*span(48, 72, there_two & narrow(cross_two)), cross_two),
                         (*span(72, 96, there_two), straight_two))
        else:
            segments.append(((0, 96, 2 * core - 1),))
            two_parts = ((*span(0, 24, there_two), straight_two),
                         (*span(24, 48, there_two & narrow(cross_two)), cross_two))
        segments.append((
            (*span(0, 48, there & at_first), straight), (*span(48, 96, there & ~at_first), straight),
            (*span(96, 120, slim), cross), *two_parts,
        ))
        segments.append(((*span(0, 96, wide), cross),))
    entry = partner - 930
    peer = (entry * 683) >> 16
    entry = entry - 96 * peer
    sought = live & (partner >= 930) & (kind == 0)
    column = jnp.full((1, side_pad), -1, i32)
    for tile, parts in enumerate(segments):
        for low, high, offset in parts:
            match = sought & (peer == row_of(offset)) & (entry < high - low)
            column = jnp.where(match, lanes * tile + low + entry, column)
    block = column >> 7
    split = [
        attributes * jnp.where(block == tile, 1.0, 0.0).astype(bf16) for tile in range(len(segments))
    ]
    target = dot_t(jnp.concatenate(split, axis=0), one_hot(column & 127, lanes))
    target = jnp.concatenate(
        [target[16 * tile : 16 * tile + 8] for tile in range(len(segments))], axis=1
    )
    target_elem, target_face, target_case = place_of(target)
    elems = jnp.concatenate([elem, target_elem], axis=1)
    faces = jnp.concatenate([direction, target_face], axis=1)
    near = side_pad + 256
    own_hot_ref[...] = one_hot(elems[:, :near], lanes)
    far_hot_ref[...] = one_hot(elems[:, near:], lanes)
    other_face = jnp.concatenate([other_face, jnp.full((1, 640), -1, i32)], axis=1)
    place_ref[...] = rows_of(
        [elems.astype(f32), faces.astype(f32), other_face.astype(f32)], 16, elems.shape[1]
    )
    info_ref[:, side_pad:] = rows_of(
        [jnp.zeros((1, 256), f32)] * 4 + [target_case[:, 0:256].astype(f32)], 8, 256
    )
    arrival_ref[...] = rows_of(
        [target_case.astype(f32), target[4:5] + target[5:6] + target[6:7], target[7:8]],
        8, 640,
    )


def whole_kernel(own_elem_ref, partner_elem_ref, far_elem_ref, place_ref, own_ref, partner_ref, far_ref):
    near = side_pad + 256
    for source, row, low, high, target in (
        (own_elem_ref, 1, 0, near, own_ref),
        (partner_elem_ref, 2, 0, side_pad, partner_ref),
        (far_elem_ref, 1, near, near + 384, far_ref),
    ):
        hot, face = source[...], place_ref[row : row + 1, low:high]
        for f in range(6):
            target[lanes * f : lanes * f + lanes] = hot * jnp.where(face == f, 1.0, 0.0).astype(bf16)


def turn_kernel(place_ref, own_ref, far_ref):
    row = lax.broadcasted_iota(i32, (16, lanes), 0)
    weight = jnp.where(row == 0, 1.0, jnp.where(row == 1, 128.0, 0.0)).astype(bf16)
    column = lax.dot_general(
        place_ref[...].astype(bf16), weight, (((0,), (0,)), ((), ())), preferred_element_type=f32
    )
    lane = lax.broadcasted_iota(i32, (1, lanes), 1).astype(f32)
    split = own_ref.shape[0]
    for f in range(6):
        part = jnp.where(column == lane + 128.0 * f, 1.0, 0.0).astype(bf16)
        own_ref[:, lanes * f : lanes * f + lanes] = part[:split]
        far_ref[:, lanes * f : lanes * f + lanes] = part[split:]


def sides_kernel(
    nf, stack_ref, own_hot_ref, partner_hot_ref, far_hot_ref, place_ref, info_ref,
    arrival_ref, mine_ref, other_ref, target_ref,
):
    stack = stack_ref[0 : 64 * nf]
    near = side_pad + 256
    for hot_ref, face, case, out_ref in (
        (own_hot_ref, place_ref[1:2, 0:near], info_ref[4:5], mine_ref),
        (partner_hot_ref, place_ref[2:3, 0:side_pad], info_ref[5:6, 0:side_pad], other_ref),
        (far_hot_ref, place_ref[1:2, near:], arrival_ref[0:1, 256:640], target_ref),
    ):
        got = gather_columns(stack, hot_ref[...], face, nf)
        out_ref[...] = interpolate(got, case.astype(i32), nf)


def side_flux(nf, mine, outer, coefs, case, face, weight_ref, hot):
    jump, jump_out, area, area_out = coefs
    weight = weight_ref[:, 0:1]
    flux = []
    for k in range(nf):
        inner, other = mine[32 * k : 32 * k + 32], outer[32 * k : 32 * k + 32]
        jumps = jnp.where(slope_rows(inner.shape), 0.0, jump * inner - jump_out * other)
        flux.append(weight * (jumps - other_part(area * inner - area_out * other)))
    flux = interpolate(cat(flux, 0), case.astype(i32), nf, transposed=True)
    return scatter_columns(flux, hot, face, nf)


def halo_coefs(coef, size, other_coef, other_size):
    least = jnp.minimum(size, other_size)
    return 16.0 * (coef + other_coef) * least, 0.5 * least * least


def flux_kernel(
    turn, nf, skip, chips, one_ref, two_ref, mine_ref, other_ref, place_ref, info_ref, arrival_ref, weight_ref,
    own_hot_ref, field_ref, coef_ref, level_ref, stiffness_ref, *rest,
):
    h = 32 * nf
    rows = slice(32 * skip, 32 * skip + h)
    core, near, far, end, near_there, far_there = where_am_i(chips)
    lane = lax.broadcasted_iota(i32, (1, lanes), 1)
    two_away = two_ref[...]
    kept = jnp.where(lane < 72, two_away, pltpu.roll(two_away, 72, 1))
    inside = (lane >= 48) & (lane < 96) & ~(end & (core == 1))
    got = jnp.concatenate(
        [jnp.where(inside, kept, one_ref[:, 0:128]), one_ref[:, 128:256]], axis=1
    )
    if turn == 0:
        sum_ref, volume_ref, halo_ref = rest
        halo = halo_coefs(
            arrival_ref[1:2, 0:256], arrival_ref[2:3, 0:256], got[h : h + 1], got[h + 1 : h + 2]
        )
        halo_ref[...] = rows_of(halo, 8, 256)
    else:
        halo_ref, sum_ref, volume_ref = rest
        halo = halo_ref[0:1], halo_ref[1:2]
    coefs = [
        jnp.concatenate([info_ref[k : k + 1, 0:side_pad], halo[k // 2]], axis=1) for k in range(4)
    ]
    outer = jnp.concatenate([other_ref[rows], got[rows]], axis=1)
    sum_ref[...] = side_flux(
        nf, mine_ref[rows], outer, coefs, info_ref[4:5], place_ref[1:2, 0 : side_pad + 256], weight_ref,
        own_hot_ref[...],
    )
    volume_scale = element_rows(coef_ref, level_ref)[2]
    low = 64 * skip
    fields = [field_ref[low + 64 * k : low + 64 * k + 64] * volume_scale for k in range(nf)]
    volume = table_dot(stiffness_ref[...], cat(fields, 1))
    for k in range(nf):
        volume_ref[64 * k : 64 * k + 64, :] = volume[:, lanes * k : lanes * k + lanes]


def solve_blocks(inverse_ref, hold_ref, nf):
    sums = [jnp.zeros((64, lanes), f32) for _ in range(nf)]
    for col in range(64):
        block = inverse_ref[col].astype(f32)
        for k in range(nf):
            sums[k] = sums[k] + block * hold_ref[64 * k + col : 64 * k + col + 1, :]
    return sums


def update_kernel(
    turn, nf, skip, nf_next,
    one_ref, local_ref, volume_ref, target_ref, place_ref, arrival_ref, far_hot_ref, weight_ref,
    field_ref, coef_ref, level_ref, inverse_ref, *rest,
):
    if turn == 0:
        guess_ref, *rest = rest
    else:
        halo_ref, *rest = rest
    if turn == 1:
        rhs_ref, *rest = rest
    if nf_next:
        hot_ref, case_ref, new_ref, stack_ref, sent_ref, *rest = rest
    elif turn == 3:
        part_ref, *rest = rest
    else:
        new_ref, *rest = rest
    hold_ref = rest[-1]
    h = 32 * nf
    rows = slice(32 * skip, 32 * skip + h)
    if turn == 0:
        halo = halo_coefs(
            arrival_ref[1:2, 256:640], arrival_ref[2:3, 256:640],
            one_ref[h : h + 1], one_ref[h + 1 : h + 2],
        )
        rest[0][...] = rows_of(halo, 8, 384)
    else:
        halo = (halo_ref[0:1], halo_ref[1:2])
    total = local_ref[...] + side_flux(
        nf, target_ref[rows], one_ref[rows], (halo[0], halo[0], halo[1], halo[1]), arrival_ref[0:1, 256:640],
        place_ref[1:2, side_pad + 256 :], weight_ref, far_hot_ref[...],
    )
    coef, size, volume_scale, normal_scale = element_rows(coef_ref, level_ref)
    scale = jnp.where(slope_rows((32, lanes)), jnp.broadcast_to(normal_scale, (32, lanes)), 1.0)
    for k in range(nf):
        mine = total[32 * k : 32 * k + 32]
        faces = [mine[:, lanes * f : lanes * f + lanes] * scale for f in range(6)]
        part = lift_traces(volume_ref[64 * k : 64 * k + 64], faces)
        if turn == 1 and k == 1:
            part = rhs_ref[...] - part
        hold_ref[64 * k : 64 * k + 64, :] = part
    new = solve_blocks(inverse_ref, hold_ref, nf)
    if turn == 0:
        new.append(guess_ref[...])
    if turn < 3:
        for k, x in enumerate(new):
            new_ref[64 * k : 64 * k + 64, :] = x
    if nf_next:
        stack = face_stack(new[:nf_next], normal_scale)
        stack_ref[...] = stack
        sent = gather_message(stack, hot_ref[...], case_ref[0:1], nf_next)
        sent_ref[...] = sent
    if turn == 3:
        lane = lax.broadcasted_iota(i32, (1, lanes), 1)
        sums = []
        for x in (field_ref[...], new[0]):
            total = jnp.sum(x * x, axis=0, keepdims=True)
            sums.append(total + pltpu.roll(total, 64, 1))
        part_ref[...] = jnp.broadcast_to(jnp.where(lane < 64, sums[0], sums[1]), part_ref.shape)


def finish_kernel(part_ref, guess_ref, first_ref, second_ref, out_ref, bound_ref):
    total = jnp.sum(part_ref[...], axis=0, keepdims=True)
    lane = lax.broadcasted_iota(i32, (1, lanes), 1)
    before = jnp.sum(jnp.where(lane < 64, total, 0.0), axis=1, keepdims=True)
    after = jnp.sum(jnp.where(lane < 64, 0.0, total), axis=1, keepdims=True)
    bound = jnp.sqrt(after / before)
    upper = 1.2 * bound
    lower = upper / 15.0
    center = 0.5 * (upper + lower)
    half = 0.5 * (upper - lower)
    ratio = center / half
    damping = 1.0 / ratio
    damping_next = 1.0 / (2.0 * ratio - damping)
    first = first_ref[64:128] / center
    second = first_ref[64:128] - second_ref[...] / center
    out_ref[...] = (
        guess_ref[...] + first + (damping_next * damping * first + 2.0 * damping_next / half * second)
    )
    bound_ref[...] = jnp.broadcast_to(bound, (1, lanes))


def in_vmem(x):
    return pltpu.with_memory_space_constraint(x, pltpu.VMEM)


def in_hbm(x):
    return pltpu.with_memory_space_constraint(x, pltpu.HBM)


def run(body, outs, ins, name, scratch=(), flops=1 << 24, placed=True, kept=True):
    spec = pl.BlockSpec(memory_space=pltpu.VMEM)
    return pl.pallas_call(
        body,
        out_shape=[(pltpu.VMEM if kept else jax.ShapeDtypeStruct)(shape, dtype) for shape, dtype in outs],
        in_specs=[spec if placed else pl.BlockSpec(memory_space=pltpu.HBM)] * len(ins),
        out_specs=[spec] * len(outs),
        scratch_shapes=list(scratch),
        compiler_params=pltpu.CompilerParams(vmem_limit_bytes=24 << 20),
        cost_estimate=pl.CostEstimate(flops=flops, bytes_accessed=1 << 20, transcendentals=0),
        name=name,
    )(*(in_vmem(x) if placed else in_hbm(x) for x in ins))


def local(
    rhs_field, initial_guess, start_vector, coefficient, refine_level, block_inverse,
    side_elem, side_dir, side_case, side_kind, partner, send_list,
):
    devices = lax.axis_size("dom")
    chips = devices // 2
    stiffness, weight = (jnp.asarray(t) for t in const_tables())
    coef = coefficient.reshape(1, lanes)
    level = refine_level.reshape(1, lanes)

    def permute(x, to):
        return lax.ppermute(x, "dom", sorted(to.items()))

    swapped = {i: i ^ 1 for i in range(devices)}
    two_away, one_away = {}, {}
    for c in range(chips):
        two_away[2 * c] = 2 * (c ^ 2)
        one_away[2 * c] = 2 * (c ^ 1)
        over = c + 2 if c % 4 >= 2 else c - 2
        two_away[2 * c + 1] = 2 * (over if 0 <= over < chips else c ^ 1) + 1
        if 0 < c < chips - 1:
            one_away[2 * c + 1] = 2 * (c + 1 if c % 2 else c - 1) + 1
    for c in (0, chips - 1):
        one_away[2 * (c ^ 1)] = 2 * c + 1
        one_away[2 * c + 1] = 2 * c

    def exchange(sent, nf, own_work, work, *beside):
        rows = sent.shape[0]
        (own,) = own_work()
        two_out, one_out = run(
            carry_kernel, [((rows, lanes), f32), ((rows, 256), f32)],
            [permute(sent, swapped), own, *beside[:1]], "carry",
        )
        arrivals = permute(one_out, one_away), permute(two_out, two_away)
        made = work()
        (last,) = run(
            functools.partial(relay_kernel, chips), [((rows, 384), f32)],
            [*arrivals, own, made[2], *beside[1:]], "relay",
        )
        return arrivals, permute(last, swapped), made

    sides = [x.reshape(1, -1) for x in (side_elem, side_dir, side_case, side_kind, partner)]
    first = [*sides, send_list, start_vector, coef, level, initial_guess]
    hot, case, stack, sides, rolled, sent, coef, level, guess = run(
        functools.partial(send_setup_kernel, chips),
        [((768, 256), bf16), ((8, 256), i32), ((80, 768), bf16), ((8, side_pad), i32), ((32, lanes), i32),
         ((40, 256), f32), *((x.shape, x.dtype) for x in first[7:])],
        first,
        "send_setup",
        scratch=[
            pltpu.VMEM((8, 256), i32),
            *(pltpu.VMEM(x.shape, x.dtype) for x in first[:7]), pltpu.SemaphoreType.DMA((len(first),)),
        ],
        placed=False,
    )
    own_slots = run(
        functools.partial(own_setup_kernel, chips),
        [((768, 512), bf16), ((8, 512), i32)],
        [sides, rolled],
        "own_setup",
        scratch=[pltpu.VMEM((8, 512), i32)],
    )
    fields, halo, late = start_vector, [], []
    for turn, (nf, nf_next) in enumerate(((1, 2), (2, 2), (2, 1), (1, 0))):
        h = 32 * nf
        def own_work():
            return run(
                functools.partial(own_kernel, nf),
                [((sent.shape[0], 512), f32)],
                [stack, *own_slots],
                "own",
            )

        def side_work(hots):
            return run(
                functools.partial(sides_kernel, nf),
                [((h, side_pad + 256), f32), ((h, side_pad), f32), ((h, 384), f32)],
                [stack, *hots, *places],
                "sides",
            )

        if turn == 0:
            *hots, place, info, arrival = run(
                functools.partial(setup_kernel, chips),
                [((lanes, side_pad + 256), bf16), ((lanes, side_pad), bf16), ((lanes, 384), bf16),
                 ((16, side_pad + 640), f32), ((8, side_pad + 256), f32), ((8, 640), f32)],
                [coef, level, sides],
                "setup",
            )
            places = [place, info, arrival]
            own_scatter, _, far_scatter = hots
        elif turn == 1:
            hots = run(
                whole_kernel,
                [((768, side_pad + 256), bf16), ((768, side_pad), bf16), ((768, 384), bf16)],
                [*hots, place],
                "whole",
            )
            own_scatter, far_scatter = run(
                turn_kernel,
                [((side_pad + 256, 768), bf16), ((384, 768), bf16)],
                [place],
                "turn",
            )
        beside = (hots[0], own_scatter) if turn == 1 else late if turn == 3 else ()
        arrivals, last, made = exchange(
            sent, nf, own_work, functools.partial(side_work, hots), *beside
        )
        mine, others, targets = made

        def apply(count, skip, count_next):
            rows = 32 * count
            sums, volume, *near = run(
                functools.partial(flux_kernel, turn, count, skip, chips),
                [((rows, 768), f32), ((64 * count, lanes), f32)] + ([] if turn else [((8, 256), f32)]),
                [*arrivals, mine, others, *places, weight, own_scatter, fields, coef, level, stiffness]
                + halo[:1],
                "flux",
            )
            ins = [
                last, sums, volume, targets, place, arrival, far_scatter, weight, fields, coef, level,
                block_inverse, *(halo[1:] if turn else [guess]), *([rhs_field] if turn == 1 else []),
            ]
            outs = [((devices, lanes) if turn == 3 else (64 * max(count, count_next), lanes), f32)]
            if count_next:
                ins += [hot, case]
                outs += [((64 * count_next, 768), bf16), ((32 * count_next, 256), f32)]
            outs += [] if turn else [((8, 384), f32)]
            late.append(sums)
            made = run(
                functools.partial(update_kernel, turn, count, skip, count_next),
                outs, ins, "update",
                scratch=[pltpu.VMEM((64 * count, lanes), f32)],
            )
            return [*made, *near]

        if turn == 0:
            new, stack, sent, far_halo, near_halo = apply(nf, 0, nf_next)
            halo = [near_halo, far_halo]
        elif turn == 1:
            new, stack, sent = apply(nf, 0, nf_next)
            first = new
        elif turn == 2:
            new, stack, sent = apply(1, 0, 1)
            late.clear()
            late += apply(1, 1, 0)
            second = late[1]
        else:
            (parts,) = apply(1, 0, 0)
        fields = new
    parts = lax.all_to_all(parts.reshape(devices, 1, lanes), "dom", 0, 0).reshape(devices, lanes)
    smoothed, bound = run(
        finish_kernel,
        [((64, lanes), f32), ((1, lanes), f32)],
        [parts, guess, first, second],
        "finish",
        kept=False,
    )
    return smoothed, bound[0, 0]


def solution(mesh):
    placed = (
        P(None, "dom"), P(None, "dom"), P(None, "dom"), P("dom"), P("dom"), P(None, None, "dom"),
        P("dom"), P("dom"), P("dom"), P("dom"), P("dom"), P("dom", None),
    )
    return jax.shard_map(
        local, mesh=mesh, in_specs=placed, out_specs=(P(None, "dom"), P()), check_vma=False
    )
```

```python
import functools
import math

import jax
import jax.numpy as jnp
import numpy as np
from jax import lax
from jax.experimental import pallas as pl
from jax.experimental.pallas import tpu as pltpu
from jax.sharding import PartitionSpec as P

f32 = jnp.float32
bf16 = jnp.bfloat16
i32 = jnp.int32
peer_offsets = (1, -1, 2, -2, 3, -3, 4, -4)
live_width = {1: 96, 2: 48, 3: 24, 4: 24}
lanes = 128
shifts = (0, 24, 48, 96)
side_pad = 1024
terms = 2


def lagrange_tables():
    root_five = 1.0 / math.sqrt(5.0)
    nodes = np.array([0.0, 0.5 - 0.5 * root_five, 0.5 + 0.5 * root_five, 1.0])
    weights = np.array([1.0, 5.0, 5.0, 1.0]) / 12.0
    factor = np.array(
        [np.prod([nodes[i] - nodes[j] for j in range(4) if j != i]) for i in range(4)]
    )
    derivative = np.zeros((4, 4))
    for i in range(4):
        for j in range(4):
            if i != j:
                derivative[i, j] = factor[i] / (factor[j] * (nodes[i] - nodes[j]))
        derivative[i, i] = -np.sum(derivative[i])
    halves = []
    for half in range(2):
        points = 0.5 * (nodes + half)
        table = np.ones((4, 4))
        for j in range(4):
            for other in range(4):
                if other != j:
                    table[:, j] *= (points - nodes[other]) / (nodes[j] - nodes[other])
        halves.append(table)
    return weights, derivative, halves


def stiffness_table():
    weights, derivative, halves = lagrange_tables()
    mass = np.diag(weights)
    line = derivative.T @ mass @ derivative
    return (
        np.kron(np.kron(line, mass), mass)
        + np.kron(np.kron(mass, line), mass)
        + np.kron(np.kron(mass, mass), line)
    )


def weight_table():
    weights = lagrange_tables()[0]
    rows = [weights[first] * weights[second] for first in range(4) for part in range(2) for second in range(4)]
    return np.broadcast_to(np.array(rows, np.float32)[:, None], (32, lanes))


def stacked(table):
    rest = np.asarray(table, np.float32)
    parts = []
    for _ in range(3):
        parts.append(rest.astype(jnp.bfloat16))
        rest = rest - parts[-1].astype(np.float32)
    high, mid, low = parts
    return np.concatenate([high, high, mid, mid, high, low], axis=1)


def const_tables():
    return stacked(stiffness_table()), np.ascontiguousarray(weight_table())


def three(x):
    high = x.astype(bf16)
    rest = x - high.astype(f32)
    mid = rest.astype(bf16)
    return high, mid, (rest - mid.astype(f32)).astype(bf16)


def added(got, first, rows):
    return sum(got[first + rows * t : first + rows * t + rows] for t in range(1, terms)) + got[
        first : first + rows
    ]


def dot(a, b):
    return jnp.dot(a, b, preferred_element_type=f32)


def dot_t(a, b):
    return lax.dot_general(a, b, (((1,), (1,)), ((), ())), preferred_element_type=f32)


def cat(parts, axis):
    return parts[0] if len(parts) == 1 else jnp.concatenate(parts, axis=axis)


def table_dot(table, x):
    high, mid, low = three(x)
    return dot(table, jnp.concatenate([high, mid, high, mid, low, high], axis=0))


def interpolate(x, case, nf, transposed=False):
    halves = [h.T if transposed else h for h in lagrange_tables()[2]]
    n = x.shape[1]
    case = jnp.broadcast_to(case, (8, n))
    hanging = (case >= 0) & (case < 4)
    place = lax.broadcasted_iota(i32, (8, n), 0) & 3

    def pick(second, low, high, whole):
        return jnp.where(hanging, jnp.where(second, high, low), whole)

    def along(half, step):
        tile = jnp.zeros((8, n), f32)
        for j in range(4):
            if 0 <= j + step < 4:
                tile = jnp.where(place == j, float(half[j, j + step]), tile)
        return tile

    first, second = case >= 2, (case & 1) == 1
    across = [
        [pick(first, float(halves[0][i, j]), float(halves[1][i, j]), float(i == j)) for j in range(4)]
        for i in range(4)
    ]
    within = {
        step: pick(second, along(halves[0], step), along(halves[1], step), float(step == 0))
        for step in range(-3, 4)
    }
    out = []
    for k in range(nf):
        part = [x[32 * k + 8 * i : 32 * k + 8 * i + 8] for i in range(4)]
        for i in range(4):
            mixed = sum(across[i][j] * part[j] for j in range(4))
            out.append(
                sum(
                    within[step] * (pltpu.roll(mixed, -step % 8, 0) if step else mixed)
                    for step in range(-3, 4)
                )
            )
    return jnp.concatenate(out, axis=0)


def other_part(x):
    return jnp.concatenate(
        [pltpu.roll(x[8 * g : 8 * g + 8], 4, 0) for g in range(x.shape[0] // 8)], axis=0
    )


def slope_rows(shape):
    return (lax.broadcasted_iota(i32, shape, 0) & 4) == 4


def rows_of(rows, count, width):
    place = lax.broadcasted_iota(i32, (count, width), 0)
    table = jnp.zeros((count, width), f32)
    for k, r in enumerate(rows):
        table = jnp.where(place == k, r, table)
    return table


def one_hot(index_row, rows, first=0):
    place = lax.broadcasted_iota(i32, (rows, index_row.shape[1]), 0) + first
    return jnp.where(place == index_row, 1.0, 0.0).astype(bf16)


def gather_columns(stack, hot, face, nf):
    h = 32 * nf
    if hot.shape[0] == 768:
        return added(dot(stack, hot), 0, h)
    parts = [stack[:, lanes * f : lanes * f + lanes] for f in range(6)]
    got = dot(jnp.concatenate(parts, axis=0), hot)
    out = added(got, 0, h)
    for f in range(1, 6):
        out = jnp.where(face == f, added(got, terms * h * f, h), out)
    return out


def scatter_columns(x, hot, face, nf):
    h = 32 * nf
    stack = jnp.concatenate(three(x)[:terms], axis=0)
    if hot.shape[1] == 768:
        return added(dot(stack, hot), 0, h)
    parts = [stack * jnp.where(face == f, 1.0, 0.0).astype(bf16) for f in range(6)]
    got = dot_t(jnp.concatenate(parts, axis=0), hot)
    return jnp.concatenate([added(got, terms * h * f, h) for f in range(6)], axis=1)


def element_rows(coef_ref, level_ref):
    coef = coef_ref[...]
    level = level_ref[...]
    size = jnp.where(level == 0, 1.0, jnp.where(level == 1, 0.5, 0.25)).astype(f32)
    inverse = jnp.where(level == 0, 1.0, jnp.where(level == 1, 2.0, 4.0)).astype(f32)
    return coef, size, coef * size, coef * inverse


def by_place(values):
    place = lax.broadcasted_iota(i32, (8, lanes), 0) & (len(values) - 1)
    tile = jnp.full((8, lanes), float(values[0]), f32)
    for p in range(1, len(values)):
        tile = jnp.where(place == p, float(values[p]), tile)
    return tile


def face_ends():
    derivative = lagrange_tables()[1]
    for dim in range(3):
        for lower in range(2):
            node = 0 if lower else 3
            yield dim, 2 * dim + lower, node, (-1.0 if lower else 1.0) * derivative[node]


def face_traces(u):
    sub = lax.broadcasted_iota(i32, (8, lanes), 0)
    low = sub < 4
    v = [[u[16 * i + 8 * m : 16 * i + 8 * m + 8] for m in range(2)] for i in range(4)]
    out = {}
    for dim, face, node, slope in face_ends():
        rows = []
        if dim == 0:
            for m in range(2):
                normal = sum(float(slope[i]) * v[i][m] for i in range(4))
                rows.append(jnp.where(low, v[node][m], pltpu.roll(normal, 4, 0)))
                rows.append(jnp.where(low, pltpu.roll(v[node][m], 4, 0), normal))
        elif dim == 1:
            scale = [by_place([slope[2 * m]] * 4 + [slope[2 * m + 1]] * 4) for m in range(2)]
            for i in range(4):
                normal = scale[0] * v[i][0] + scale[1] * v[i][1]
                normal = normal + pltpu.roll(normal, 4, 0)
                rows.append(jnp.where(low, pltpu.roll(v[i][1], 4, 0) if node else v[i][0], normal))
        else:
            scale = by_place(slope)
            for i in range(4):
                row = None
                for m in range(2):
                    normal = scale * v[i][m]
                    normal = normal + pltpu.roll(normal, 7, 0)
                    normal = normal + pltpu.roll(normal, 6, 0)
                    for half in range(2):
                        to = 2 * m + half
                        value = pltpu.roll(v[i][m], (to - 4 * half - node) % 8, 0)
                        shift = (to + 4 - 4 * half) % 8
                        moved = pltpu.roll(normal, shift, 0) if shift else normal
                        row = value if row is None else jnp.where(sub == to, value, row)
                        row = jnp.where(sub == to + 4, moved, row)
                rows.append(row)
        out[face] = jnp.concatenate(rows, axis=0)
    return [out[f] for f in range(6)]


def lift_traces(total, faces):
    sub = lax.broadcasted_iota(i32, (8, lanes), 0)
    low = sub < 4
    r = [[total[16 * i + 8 * m : 16 * i + 8 * m + 8] for m in range(2)] for i in range(4)]
    for dim, face, node, slope in face_ends():
        b = [faces[face][8 * i : 8 * i + 8] for i in range(4)]
        if dim == 0:
            for m in range(2):
                even, odd = b[2 * m], b[2 * m + 1]
                normal = jnp.where(low, pltpu.roll(even, 4, 0), odd)
                for i in range(4):
                    r[i][m] = r[i][m] + float(slope[i]) * normal
                r[node][m] = r[node][m] + jnp.where(low, even, pltpu.roll(odd, 4, 0))
        elif dim == 1:
            scale = [by_place([slope[2 * m]] * 4 + [slope[2 * m + 1]] * 4) for m in range(2)]
            for i in range(4):
                turned = pltpu.roll(b[i], 4, 0)
                normal = jnp.where(low, turned, b[i])
                for m in range(2):
                    r[i][m] = r[i][m] + scale[m] * normal
                value = jnp.where(low, 0.0, turned) if node else jnp.where(low, b[i], 0.0)
                r[i][node // 2] = r[i][node // 2] + value
        else:
            scale = by_place(slope)
            here = by_place([1.0 if p == node else 0.0 for p in range(4)])
            for i in range(4):
                for m in range(2):
                    spread = [
                        jnp.where(
                            low,
                            jnp.broadcast_to(b[i][at : at + 1], (8, lanes)),
                            jnp.broadcast_to(b[i][at + 1 : at + 2], (8, lanes)),
                        )
                        for at in (2 * m, 4 + 2 * m)
                    ]
                    r[i][m] = r[i][m] + (here * spread[0] + scale * spread[1])
    return jnp.concatenate([r[i][m] for i in range(4) for m in range(2)], axis=0)


def face_stack(u, normal_scale):
    scale = jnp.where(slope_rows((32, lanes)), jnp.broadcast_to(normal_scale, (32, lanes)), 1.0)
    fields = [jnp.concatenate([part * scale for part in face_traces(x)], axis=1) for x in u]
    return jnp.concatenate(three(cat(fields, 0))[:terms], axis=0)


def gather_message(stack, hot, case, nf):
    got = dot(stack, hot)
    h = 32 * nf
    out = interpolate(added(got, 0, h), case, nf)
    low = terms * h
    if stack.shape[0] == low:
        return out
    coef = got[low : low + 1] + got[low + 1 : low + 2] + got[low + 2 : low + 3]
    size = got[low + 3 : low + 4] * jnp.where((case >= 0) & (case < 4), 0.5, 1.0)
    row = lax.broadcasted_iota(i32, (8, out.shape[1]), 0)
    scalars = jnp.where(row == 0, coef, jnp.where(row == 1, size, 0.0))
    return jnp.concatenate([out, scalars], axis=0)


def where_am_i(chips):
    me = lax.axis_index("dom")
    chip = me // 2
    core = me - 2 * chip
    near = jnp.where(lax.rem(chip, 2) == 1, -1, 1)
    far = jnp.where(lax.rem(chip, 4) < 2, 1, -1)
    end = (chip == 0) | (chip == chips - 1)
    far_there = (chip - 2 * far >= 0) & (chip - 2 * far < chips)
    return core, near, far, end, ~end, far_there


def carried(core, near, far, near_there, far_there):
    first = core == 0
    return (
        jnp.where(first, near, -near), jnp.where(first, far, -far),
        first | near_there, first | far_there,
    )


def row_of(offset):
    size = jnp.abs(offset)
    return 2 * (size - 1) + jnp.where(offset < 0, 1, 0)


def narrow(offset):
    return jnp.abs(offset) == 3


def side_attributes(side_ref, more=()):
    live = lax.broadcasted_iota(i32, (1, side_pad), 1) < 930
    rows = [jnp.where(live, side_ref[k : k + 1], 0).astype(f32) for k in range(3)]
    rows.append(jnp.where(live, 1.0, 0.0))
    return rows_of(rows + list(more), 16, side_pad).astype(bf16)


def look_up(attributes, index):
    blocks = jnp.concatenate(
        [attributes[:, lanes * k : lanes * k + lanes] for k in range(side_pad // lanes)], axis=0
    )
    found = dot(blocks, one_hot(index & 127, lanes))
    block = index >> 7
    out = jnp.zeros((8, index.shape[1]), f32)
    for k in range(side_pad // lanes):
        out = jnp.where(block == k, found[16 * k : 16 * k + 8], out)
    return out


def place_of(found):
    valid = found[3:4] > 0.5
    return tuple(jnp.where(valid, found[k : k + 1], -1.0).astype(i32) for k in range(3))


def fill_one_hot(hot_ref, elem, face):
    hot = one_hot(elem, lanes)
    for f in range(6):
        hot_ref[lanes * f : lanes * f + lanes] = hot * jnp.where(face == f, 1.0, 0.0).astype(bf16)


def listed_part(rolled_ref, shift, offset, low, high, valid):
    place = shifts.index(shift)
    lane = lax.broadcasted_iota(i32, (1, lanes), 1)
    values = rolled_ref[pl.ds(8 * place + jnp.minimum(row_of(offset), 7), 1), :]
    return jnp.where((lane >= low) & (lane < high) & valid, values, -1)


def send_setup_kernel(chips, *refs):
    sources, refs = refs[:10], refs[10:]
    hot_ref, case_ref, stack_ref, side_ref, rolled_ref = refs[:5]
    sent_ref, landed = refs[5], (*refs[10:17], *refs[6:9])
    slot_ref, arrived = refs[9], refs[17]
    copies = [
        pltpu.make_async_copy(source, target, arrived.at[k])
        for k, (source, target) in enumerate(zip(sources, landed))
    ]
    for k in (5, 0, 1, 2, 6, 7, 8, 3, 4, 9):
        copies[k].start()
    list_ref = landed[5]
    start_ref, coef_ref, level_ref = landed[6:9]
    side_ref[...] = jnp.full((8, side_pad), -1, i32)
    sides = landed[0].shape[1]
    copies[5].wait()
    core, near, far, end, near_there, far_there = where_am_i(chips)
    listed = jnp.concatenate([list_ref[...], jnp.full((8, 32), -1, i32)], axis=1)
    for place, shift in enumerate(shifts):
        rolled_ref[8 * place : 8 * place + 8] = (
            pltpu.roll(listed, shift, 1) if shift else listed
        )
    part = functools.partial(listed_part, rolled_ref)
    other = 1 - core
    step, step_two, there, there_two = carried(other, near, far, near_there, far_there)
    cross, cross_two = 2 * step + other - core, 4 * step_two + other - core
    first = (
        part(0, cross_two, 0, 24, there_two & narrow(cross_two)),
        part(24, 4 * step_two, 24, 48, there_two),
        part(48, 2 * step, 48, 96, there),
        part(96, cross, 96, 120, there & narrow(cross)),
    )
    slot_ref[0:1, 0:128] = functools.reduce(jnp.maximum, first)
    slot_ref[0:1, 128:256] = part(0, cross, 0, 96, there & ~narrow(cross))
    for k in range(3):
        copies[k].wait()
        side_ref[k : k + 1, 0:sides] = landed[k][...]
    elem, face, slot_case = place_of(look_up(side_attributes(side_ref), slot_ref[0:1, :]))
    case_ref[0:1, :] = slot_case
    fill_one_hot(hot_ref, elem, face)

    for k in (6, 7, 8):
        copies[k].wait()
    coef, size, volume_scale, normal_scale = element_rows(coef_ref, level_ref)
    stack = face_stack([start_ref[...]], normal_scale)
    scalars = rows_of([x.astype(f32) for x in three(coef)] + [size], 16, lanes).astype(bf16)
    stack = jnp.concatenate([stack, jnp.concatenate([scalars] * 6, axis=1)], axis=0)
    stack_ref[...] = stack
    sent = gather_message(stack, hot_ref[...], slot_case, 1)
    sent_ref[...] = sent
    for k in (3, 4):
        copies[k].wait()
        side_ref[k : k + 1, 0:sides] = landed[k][...]
    copies[9].wait()


def own_setup_kernel(chips, side_ref, rolled_ref, hot_ref, case_ref, slot_ref):
    core, near, far, end, near_there, far_there = where_am_i(chips)
    part = functools.partial(listed_part, rolled_ref)
    flip = 1 - 2 * core
    step, step_two, there, there_two = carried(core, near, far, near_there, far_there)
    cross, cross_two = 2 * step + flip, 4 * step_two + flip
    slot_ref[0:1, 0:128] = jnp.maximum(
        part(0, 4 * step_two, 0, 24, there_two),
        part(24, cross_two, 24, 48, there_two & narrow(cross_two)),
    )
    slot_ref[0:1, 128:256] = jnp.maximum(
        part(0, 2 * step, 0, 48, there), part(96, cross, 96, 120, there & narrow(cross))
    )
    slot_ref[0:1, 256:384] = part(0, cross, 0, 96, there & ~narrow(cross))
    slot_ref[0:1, 384:512] = part(0, flip, 0, 96, core >= 0)
    elem, face, slot_case = place_of(look_up(side_attributes(side_ref), slot_ref[0:1, :]))
    case_ref[0:1, :] = slot_case
    fill_one_hot(hot_ref, elem, face)


def own_kernel(nf, stack_ref, hot_ref, case_ref, own_ref):
    own_ref[...] = gather_message(
        stack_ref[...], hot_ref[...], case_ref[0:1], nf
    )


def pack(x, nf):
    lane = lax.broadcasted_iota(i32, (1, lanes), 1)
    out = []
    for k in range(nf):
        last = x[32 * k + 24 : 32 * k + 32]
        for g in range(3):
            part = x[32 * k + 8 * g : 32 * k + 8 * g + 8]
            out.append(jnp.where(lane < 96, part, pltpu.roll(last, 96 - 32 * g, 1)))
    return jnp.concatenate(out, axis=0)


def unpack(x, nf):
    lane = lax.broadcasted_iota(i32, (1, lanes), 1)
    out = []
    for k in range(nf):
        part = [x[24 * k + 8 * g : 24 * k + 8 * g + 8] for g in range(3)]
        moved = [pltpu.roll(p, 32 * g + 32, 1) for g, p in enumerate(part)]
        out += part
        out.append(jnp.where(lane < 32, moved[0], jnp.where(lane < 64, moved[1], moved[2])))
    return jnp.concatenate(out, axis=0)


def carry_kernel(nf, sent_ref, own_ref, *rest):
    two_ref, one_ref = rest[-2:]
    h = 32 * nf
    lane = lax.broadcasted_iota(i32, (1, lanes), 1)
    sent = sent_ref[:, 0:128]
    handed = jnp.where((lane >= 48) & (lane < 96), pltpu.roll(sent, 48, 1), 0.0)
    two_away = own_ref[:, 0:128] + handed
    first = own_ref[:, 128:256] + jnp.where(lane >= 48, sent, 0.0)
    second = own_ref[:, 256:384] + sent_ref[:, 128:256]
    if nf == 1:
        two_ref[...] = two_away
        one_ref[:, 0:128] = first
        one_ref[:, 128:256] = second
    else:
        two_ref[...] = pack(two_away, nf)
        one_ref[0:h] = first
        one_ref[h:] = pack(second, nf)


def received(nf, one_ref, two_ref):
    if nf == 1:
        return two_ref[...], one_ref[:, 0:128], one_ref[:, 128:256]
    h = 32 * nf
    return unpack(two_ref[...], nf), one_ref[0:h], unpack(one_ref[h:], nf)


def relay_kernel(nf, chips, one_ref, two_ref, own_ref, *rest):
    out_ref = rest[-1]
    core, near, far, end, near_there, far_there = where_am_i(chips)
    lane = lax.broadcasted_iota(i32, (1, lanes), 1)
    two_away, one, second = received(nf, one_ref, two_ref)
    out_ref[:, 0:128] = own_ref[:, 384:512]
    passed = jnp.where(lane < 24, pltpu.roll(two_away, 56, 1), two_away)
    out_ref[:, 128:256] = jnp.where((lane < 48) & ~(end & (core == 1)), passed, one)
    out_ref[:, 256:384] = second


def setup_kernel(
    chips, coef_ref, level_ref, side_ref,
    own_hot_ref, partner_hot_ref, far_hot_ref, place_ref, info_ref, arrival_ref,
):
    core, near, far, end, near_there, far_there = where_am_i(chips)
    elem, direction, case = side_ref[0:1], side_ref[1:2], side_ref[2:3]
    kind, partner = side_ref[3:4], side_ref[4:5]
    live = lax.broadcasted_iota(i32, (1, side_pad), 1) < 930

    coef, size, volume_scale, normal_scale = element_rows(coef_ref, level_ref)
    scalars = rows_of([x.astype(f32) for x in three(coef)] + [size], 16, lanes)
    mine = dot(scalars.astype(bf16), one_hot(elem, lanes))
    hanging = (case >= 0) & (case < 4)
    own_coef = mine[0:1] + mine[1:2] + mine[2:3]
    own_size = mine[3:4] * jnp.where(hanging, 0.5, 1.0)

    attributes = side_attributes(side_ref, (mine[0:1], mine[1:2], mine[2:3], own_size))
    here = live & (partner < 930)
    other = look_up(attributes, jnp.where(here, partner, -1))
    other_elem, other_face = place_of(other)[:2]
    partner_hot_ref[...] = one_hot(other_elem, lanes)
    valid = other[3:4] > 0.5
    edge = jnp.where(kind == 1, 1.0, 0.0)
    least = jnp.where(valid, jnp.minimum(own_size, other[7:8]), 0.0)
    jump = 16.0 * (own_coef + other[4:5] + other[5:6] + other[6:7]) * least
    area = least * least
    info_ref[:, 0:side_pad] = rows_of(
        [jump, jump * (1.0 - edge), area * (0.5 + 0.5 * edge), area * (0.5 - 0.5 * edge),
         case.astype(f32), other[2:3]],
        8, side_pad,
    )

    def arrives(carrier):
        last = end & (carrier == 1)
        back = jnp.where((carrier == 0) | end, -near, near)
        back_two = jnp.where(carrier == 0, -far, far)
        turn = 2 * core - 1
        return (
            2 * back, 2 * back + turn, 4 * back_two, 4 * back_two + turn,
            ~(end & (carrier == 0)), ~last, last,
        )

    def span(low, high, valid):
        return low, jnp.where(valid, high, low)

    segments = []
    for mine, carrier in ((True, core), (False, 1 - core)):
        straight, cross, straight_two, cross_two, there, there_two, last = arrives(carrier)
        slim, wide = there & narrow(cross), there & ~narrow(cross)
        at_first = (last & (core != 1)) | (~last & (carrier == core))
        if mine:
            two_parts = ((*span(48, 72, there_two & narrow(cross_two)), cross_two),
                         (*span(72, 96, there_two), straight_two))
        else:
            segments.append(((0, 96, 2 * core - 1),))
            two_parts = ((*span(0, 24, there_two), straight_two),
                         (*span(24, 48, there_two & narrow(cross_two)), cross_two))
        segments.append((
            (*span(0, 48, there & at_first), straight), (*span(48, 96, there & ~at_first), straight),
            (*span(96, 120, slim), cross), *two_parts,
        ))
        segments.append(((*span(0, 96, wide), cross),))
    entry = partner - 930
    peer = (entry * 683) >> 16
    entry = entry - 96 * peer
    sought = live & (partner >= 930) & (kind == 0)
    column = jnp.full((1, side_pad), -1, i32)
    for tile, parts in enumerate(segments):
        for low, high, offset in parts:
            match = sought & (peer == row_of(offset)) & (entry < high - low)
            column = jnp.where(match, lanes * tile + low + entry, column)
    block = column >> 7
    split = [
        attributes * jnp.where(block == tile, 1.0, 0.0).astype(bf16) for tile in range(len(segments))
    ]
    target = dot_t(jnp.concatenate(split, axis=0), one_hot(column & 127, lanes))
    target = jnp.concatenate(
        [target[16 * tile : 16 * tile + 8] for tile in range(len(segments))], axis=1
    )
    target_elem, target_face, target_case = place_of(target)
    elems = jnp.concatenate([elem, target_elem], axis=1)
    faces = jnp.concatenate([direction, target_face], axis=1)
    near = side_pad + 256
    own_hot_ref[...] = one_hot(elems[:, :near], lanes)
    far_hot_ref[...] = one_hot(elems[:, near:], lanes)
    other_face = jnp.concatenate([other_face, jnp.full((1, 640), -1, i32)], axis=1)
    place_ref[...] = rows_of(
        [elems.astype(f32), faces.astype(f32), other_face.astype(f32)], 16, elems.shape[1]
    )
    info_ref[:, side_pad:] = rows_of(
        [jnp.zeros((1, 256), f32)] * 4 + [target_case[:, 0:256].astype(f32)], 8, 256
    )
    arrival_ref[...] = rows_of(
        [target_case.astype(f32), target[4:5] + target[5:6] + target[6:7], target[7:8]],
        8, 640,
    )


def whole_kernel(own_elem_ref, partner_elem_ref, far_elem_ref, place_ref, own_ref, partner_ref, far_ref):
    near = side_pad + 256
    for source, row, low, high, target in (
        (own_elem_ref, 1, 0, near, own_ref),
        (partner_elem_ref, 2, 0, side_pad, partner_ref),
        (far_elem_ref, 1, near, near + 384, far_ref),
    ):
        hot, face = source[...], place_ref[row : row + 1, low:high]
        for f in range(6):
            target[lanes * f : lanes * f + lanes] = hot * jnp.where(face == f, 1.0, 0.0).astype(bf16)


def turn_kernel(place_ref, own_ref, far_ref):
    row = lax.broadcasted_iota(i32, (16, lanes), 0)
    weight = jnp.where(row == 0, 1.0, jnp.where(row == 1, 128.0, 0.0)).astype(bf16)
    column = lax.dot_general(
        place_ref[...].astype(bf16), weight, (((0,), (0,)), ((), ())), preferred_element_type=f32
    )
    lane = lax.broadcasted_iota(i32, (1, lanes), 1).astype(f32)
    split = own_ref.shape[0]
    for f in range(6):
        part = jnp.where(column == lane + 128.0 * f, 1.0, 0.0).astype(bf16)
        own_ref[:, lanes * f : lanes * f + lanes] = part[:split]
        far_ref[:, lanes * f : lanes * f + lanes] = part[split:]


def sides_kernel(
    nf, stack_ref, own_hot_ref, partner_hot_ref, far_hot_ref, place_ref, info_ref,
    arrival_ref, mine_ref, other_ref, target_ref,
):
    stack = stack_ref[0 : 32 * terms * nf]
    near = side_pad + 256
    for hot_ref, face, case, out_ref in (
        (own_hot_ref, place_ref[1:2, 0:near], info_ref[4:5], mine_ref),
        (partner_hot_ref, place_ref[2:3, 0:side_pad], info_ref[5:6, 0:side_pad], other_ref),
        (far_hot_ref, place_ref[1:2, near:], arrival_ref[0:1, 256:640], target_ref),
    ):
        got = gather_columns(stack, hot_ref[...], face, nf)
        out_ref[...] = interpolate(got, case.astype(i32), nf)


def side_flux(nf, mine, outer, coefs, case, face, weight_ref, hot):
    jump, jump_out, area, area_out = coefs
    weight = weight_ref[:, 0:1]
    flux = []
    for k in range(nf):
        inner, other = mine[32 * k : 32 * k + 32], outer[32 * k : 32 * k + 32]
        jumps = jnp.where(slope_rows(inner.shape), 0.0, jump * inner - jump_out * other)
        flux.append(weight * (jumps - other_part(area * inner - area_out * other)))
    flux = interpolate(cat(flux, 0), case.astype(i32), nf, transposed=True)
    return scatter_columns(flux, hot, face, nf)


def halo_coefs(coef, size, other_coef, other_size):
    least = jnp.minimum(size, other_size)
    return 16.0 * (coef + other_coef) * least, 0.5 * least * least


def flux_kernel(
    turn, nf, skip, both, chips, one_ref, two_ref, mine_ref, other_ref, place_ref, info_ref, arrival_ref, weight_ref,
    own_hot_ref, field_ref, coef_ref, level_ref, stiffness_ref, *rest,
):
    h = 32 * nf
    rows = slice(32 * skip, 32 * skip + h)
    core, near, far, end, near_there, far_there = where_am_i(chips)
    lane = lax.broadcasted_iota(i32, (1, lanes), 1)
    two_away, first, second = received(both, one_ref, two_ref)
    kept = jnp.where(lane < 72, two_away, pltpu.roll(two_away, 72, 1))
    inside = (lane >= 48) & (lane < 96) & ~(end & (core == 1))
    got = jnp.concatenate(
        [jnp.where(inside, kept, first), second], axis=1
    )
    if turn == 0:
        sum_ref, volume_ref, halo_ref = rest
        halo = halo_coefs(
            arrival_ref[1:2, 0:256], arrival_ref[2:3, 0:256], got[h : h + 1], got[h + 1 : h + 2]
        )
        halo_ref[...] = rows_of(halo, 8, 256)
    else:
        halo_ref, sum_ref, volume_ref = rest
        halo = halo_ref[0:1], halo_ref[1:2]
    coefs = [
        jnp.concatenate([info_ref[k : k + 1, 0:side_pad], halo[k // 2]], axis=1) for k in range(4)
    ]
    outer = jnp.concatenate([other_ref[rows], got[rows]], axis=1)
    sum_ref[...] = side_flux(
        nf, mine_ref[rows], outer, coefs, info_ref[4:5], place_ref[1:2, 0 : side_pad + 256], weight_ref,
        own_hot_ref[...],
    )
    volume_scale = element_rows(coef_ref, level_ref)[2]
    low = 64 * skip
    fields = [field_ref[low + 64 * k : low + 64 * k + 64] * volume_scale for k in range(nf)]
    volume = table_dot(stiffness_ref[...], cat(fields, 1))
    for k in range(nf):
        volume_ref[64 * k : 64 * k + 64, :] = volume[:, lanes * k : lanes * k + lanes]


def solve_blocks(inverse_ref, hold_ref, nf):
    sums = [jnp.zeros((64, lanes), f32) for _ in range(nf)]
    for col in range(64):
        block = inverse_ref[col].astype(f32)
        for k in range(nf):
            sums[k] = sums[k] + block * hold_ref[64 * k + col : 64 * k + col + 1, :]
    return sums


def update_kernel(
    turn, nf, skip, nf_next,
    one_ref, local_ref, volume_ref, target_ref, place_ref, arrival_ref, far_hot_ref, weight_ref,
    field_ref, coef_ref, level_ref, inverse_ref, *rest,
):
    if turn == 0:
        guess_ref, *rest = rest
    else:
        halo_ref, *rest = rest
    if turn == 1:
        rhs_ref, *rest = rest
    if nf_next:
        hot_ref, case_ref, new_ref, stack_ref, sent_ref, *rest = rest
    elif turn == 3:
        part_ref, *rest = rest
    else:
        new_ref, *rest = rest
    hold_ref = rest[-1]
    h = 32 * nf
    rows = slice(32 * skip, 32 * skip + h)
    if turn == 0:
        halo = halo_coefs(
            arrival_ref[1:2, 256:640], arrival_ref[2:3, 256:640],
            one_ref[h : h + 1], one_ref[h + 1 : h + 2],
        )
        rest[0][...] = rows_of(halo, 8, 384)
    else:
        halo = (halo_ref[0:1], halo_ref[1:2])
    total = local_ref[...] + side_flux(
        nf, target_ref[rows], one_ref[rows], (halo[0], halo[0], halo[1], halo[1]), arrival_ref[0:1, 256:640],
        place_ref[1:2, side_pad + 256 :], weight_ref, far_hot_ref[...],
    )
    coef, size, volume_scale, normal_scale = element_rows(coef_ref, level_ref)
    scale = jnp.where(slope_rows((32, lanes)), jnp.broadcast_to(normal_scale, (32, lanes)), 1.0)
    for k in range(nf):
        mine = total[32 * k : 32 * k + 32]
        faces = [mine[:, lanes * f : lanes * f + lanes] * scale for f in range(6)]
        part = lift_traces(volume_ref[64 * k : 64 * k + 64], faces)
        if turn == 1 and k == 1:
            part = rhs_ref[...] - part
        hold_ref[64 * k : 64 * k + 64, :] = part
    new = solve_blocks(inverse_ref, hold_ref, nf)
    if turn == 0:
        new.append(guess_ref[...])
    if turn < 3:
        for k, x in enumerate(new):
            new_ref[64 * k : 64 * k + 64, :] = x
    if nf_next:
        stack = face_stack(new[:nf_next], normal_scale)
        stack_ref[...] = stack
        sent = gather_message(stack, hot_ref[...], case_ref[0:1], nf_next)
        sent_ref[...] = sent
    if turn == 3:
        lane = lax.broadcasted_iota(i32, (1, lanes), 1)
        sums = []
        for x in (field_ref[...], new[0]):
            total = jnp.sum(x * x, axis=0, keepdims=True)
            sums.append(total + pltpu.roll(total, 64, 1))
        part_ref[...] = jnp.broadcast_to(jnp.where(lane < 64, sums[0], sums[1]), part_ref.shape)


def finish_kernel(part_ref, guess_ref, first_ref, second_ref, out_ref, bound_ref):
    total = jnp.sum(part_ref[...], axis=0, keepdims=True)
    lane = lax.broadcasted_iota(i32, (1, lanes), 1)
    before = jnp.sum(jnp.where(lane < 64, total, 0.0), axis=1, keepdims=True)
    after = jnp.sum(jnp.where(lane < 64, 0.0, total), axis=1, keepdims=True)
    bound = jnp.sqrt(after / before)
    upper = 1.2 * bound
    lower = upper / 15.0
    center = 0.5 * (upper + lower)
    half = 0.5 * (upper - lower)
    ratio = center / half
    damping = 1.0 / ratio
    damping_next = 1.0 / (2.0 * ratio - damping)
    first = first_ref[64:128] / center
    second = first_ref[64:128] - second_ref[...] / center
    out_ref[...] = (
        guess_ref[...] + first + (damping_next * damping * first + 2.0 * damping_next / half * second)
    )
    bound_ref[...] = jnp.broadcast_to(bound, (1, lanes))


def in_vmem(x):
    return pltpu.with_memory_space_constraint(x, pltpu.VMEM)


def in_hbm(x):
    return pltpu.with_memory_space_constraint(x, pltpu.HBM)


def run(body, outs, ins, name, scratch=(), flops=1 << 24, placed=True, kept=True):
    spec = pl.BlockSpec(memory_space=pltpu.VMEM)
    return pl.pallas_call(
        body,
        out_shape=[(pltpu.VMEM if kept else jax.ShapeDtypeStruct)(shape, dtype) for shape, dtype in outs],
        in_specs=[spec if placed else pl.BlockSpec(memory_space=pltpu.HBM)] * len(ins),
        out_specs=[spec] * len(outs),
        scratch_shapes=list(scratch),
        compiler_params=pltpu.CompilerParams(vmem_limit_bytes=24 << 20),
        cost_estimate=pl.CostEstimate(flops=flops, bytes_accessed=1 << 20, transcendentals=0),
        name=name,
    )(*(in_vmem(x) if placed else in_hbm(x) for x in ins))


def local(
    rhs_field, initial_guess, start_vector, coefficient, refine_level, block_inverse,
    side_elem, side_dir, side_case, side_kind, partner, send_list,
):
    devices = lax.axis_size("dom")
    chips = devices // 2
    stiffness, weight = (jnp.asarray(t) for t in const_tables())
    coef = coefficient.reshape(1, lanes)
    level = refine_level.reshape(1, lanes)

    def permute(x, to):
        return lax.ppermute(x, "dom", sorted(to.items()))

    swapped = {i: i ^ 1 for i in range(devices)}
    two_away, one_away = {}, {}
    for c in range(chips):
        two_away[2 * c] = 2 * (c ^ 2)
        one_away[2 * c] = 2 * (c ^ 1)
        over = c + 2 if c % 4 >= 2 else c - 2
        two_away[2 * c + 1] = 2 * (over if 0 <= over < chips else c ^ 1) + 1
        if 0 < c < chips - 1:
            one_away[2 * c + 1] = 2 * (c + 1 if c % 2 else c - 1) + 1
    for c in (0, chips - 1):
        one_away[2 * (c ^ 1)] = 2 * c + 1
        one_away[2 * c + 1] = 2 * c

    def exchange(sent, nf, own_work, work, *beside):
        rows = sent.shape[0]
        (own,) = own_work()
        two_out, one_out = run(
            functools.partial(carry_kernel, nf),
            [((rows, lanes), f32), ((rows, 256), f32)] if nf == 1
            else [((24 * nf, lanes), f32), ((56 * nf, lanes), f32)],
            [permute(sent, swapped), own, *beside[:1]], "carry",
        )
        arrivals = permute(one_out, one_away), permute(two_out, two_away)
        made = work()
        (last,) = run(
            functools.partial(relay_kernel, nf, chips), [((rows, 384), f32)],
            [*arrivals, own, made[2], *beside[1:]], "relay",
        )
        return arrivals, permute(last, swapped), made

    sides = [x.reshape(1, -1) for x in (side_elem, side_dir, side_case, side_kind, partner)]
    first = [*sides, send_list, start_vector, coef, level, initial_guess]
    hot, case, stack, sides, rolled, sent, coef, level, guess = run(
        functools.partial(send_setup_kernel, chips),
        [((768, 256), bf16), ((8, 256), i32), ((32 * terms + 16, 768), bf16), ((8, side_pad), i32), ((32, lanes), i32),
         ((40, 256), f32), *((x.shape, x.dtype) for x in first[7:])],
        first,
        "send_setup",
        scratch=[
            pltpu.VMEM((8, 256), i32),
            *(pltpu.VMEM(x.shape, x.dtype) for x in first[:7]), pltpu.SemaphoreType.DMA((len(first),)),
        ],
        placed=False,
    )
    own_slots = run(
        functools.partial(own_setup_kernel, chips),
        [((768, 512), bf16), ((8, 512), i32)],
        [sides, rolled],
        "own_setup",
        scratch=[pltpu.VMEM((8, 512), i32)],
    )
    fields, halo, late = start_vector, [], []
    for turn, (nf, nf_next) in enumerate(((1, 2), (2, 2), (2, 1), (1, 0))):
        h = 32 * nf
        def own_work():
            return run(
                functools.partial(own_kernel, nf),
                [((sent.shape[0], 512), f32)],
                [stack, *own_slots],
                "own",
            )

        def side_work(hots):
            return run(
                functools.partial(sides_kernel, nf),
                [((h, side_pad + 256), f32), ((h, side_pad), f32), ((h, 384), f32)],
                [stack, *hots, *places],
                "sides",
            )

        if turn == 0:
            *hots, place, info, arrival = run(
                functools.partial(setup_kernel, chips),
                [((lanes, side_pad + 256), bf16), ((lanes, side_pad), bf16), ((lanes, 384), bf16),
                 ((16, side_pad + 640), f32), ((8, side_pad + 256), f32), ((8, 640), f32)],
                [coef, level, sides],
                "setup",
            )
            places = [place, info, arrival]
            own_scatter, _, far_scatter = hots
        elif turn == 1:
            hots = run(
                whole_kernel,
                [((768, side_pad + 256), bf16), ((768, side_pad), bf16), ((768, 384), bf16)],
                [*hots, place],
                "whole",
            )
            own_scatter, far_scatter = run(
                turn_kernel,
                [((side_pad + 256, 768), bf16), ((384, 768), bf16)],
                [place],
                "turn",
            )
        beside = (hots[0], own_scatter) if turn == 1 else late if turn == 3 else ()
        arrivals, last, made = exchange(
            sent, nf, own_work, functools.partial(side_work, hots), *beside
        )
        mine, others, targets = made

        def apply(count, skip, count_next):
            rows = 32 * count
            sums, volume, *near = run(
                functools.partial(flux_kernel, turn, count, skip, nf, chips),
                [((rows, 768), f32), ((64 * count, lanes), f32)] + ([] if turn else [((8, 256), f32)]),
                [*arrivals, mine, others, *places, weight, own_scatter, fields, coef, level, stiffness]
                + halo[:1],
                "flux",
            )
            ins = [
                last, sums, volume, targets, place, arrival, far_scatter, weight, fields, coef, level,
                block_inverse, *(halo[1:] if turn else [guess]), *([rhs_field] if turn == 1 else []),
            ]
            outs = [((devices, lanes) if turn == 3 else (64 * max(count, count_next), lanes), f32)]
            if count_next:
                ins += [hot, case]
                outs += [((32 * terms * count_next, 768), bf16), ((32 * count_next, 256), f32)]
            outs += [] if turn else [((8, 384), f32)]
            late.append(sums)
            made = run(
                functools.partial(update_kernel, turn, count, skip, count_next),
                outs, ins, "update",
                scratch=[pltpu.VMEM((64 * count, lanes), f32)],
            )
            return [*made, *near]

        if turn == 0:
            new, stack, sent, far_halo, near_halo = apply(nf, 0, nf_next)
            halo = [near_halo, far_halo]
        elif turn == 1:
            new, stack, sent = apply(nf, 0, nf_next)
            first = new
        elif turn == 2:
            new, stack, sent = apply(1, 0, 1)
            late.clear()
            late += apply(1, 1, 0)
            second = late[1]
        else:
            (parts,) = apply(1, 0, 0)
        fields = new
    parts = lax.all_to_all(parts.reshape(devices, 1, lanes), "dom", 0, 0).reshape(devices, lanes)
    smoothed, bound = run(
        finish_kernel,
        [((64, lanes), f32), ((1, lanes), f32)],
        [parts, guess, first, second],
        "finish",
        kept=False,
    )
    return smoothed, bound[0, 0]


def solution(mesh):
    placed = (
        P(None, "dom"), P(None, "dom"), P(None, "dom"), P("dom"), P("dom"), P(None, None, "dom"),
        P("dom"), P("dom"), P("dom"), P("dom"), P("dom"), P("dom", None),
    )
    return jax.shard_map(
        local, mesh=mesh, in_specs=placed, out_specs=(P(None, "dom"), P()), check_vma=False
    )
```

```python
import functools
import math

import jax
import jax.numpy as jnp
import numpy as np
from jax import lax
from jax.experimental import pallas as pl
from jax.experimental.pallas import tpu as pltpu
from jax.sharding import PartitionSpec as P

f32 = jnp.float32
bf16 = jnp.bfloat16
i32 = jnp.int32
peer_offsets = (1, -1, 2, -2, 3, -3, 4, -4)
live_width = {1: 96, 2: 48, 3: 24, 4: 24}
lanes = 128
shifts = (0, 24, 48, 96)
side_pad = 1024
near_lanes, far_lanes = 384, 256
terms = 2


def lagrange_tables():
    root_five = 1.0 / math.sqrt(5.0)
    nodes = np.array([0.0, 0.5 - 0.5 * root_five, 0.5 + 0.5 * root_five, 1.0])
    weights = np.array([1.0, 5.0, 5.0, 1.0]) / 12.0
    factor = np.array(
        [np.prod([nodes[i] - nodes[j] for j in range(4) if j != i]) for i in range(4)]
    )
    derivative = np.zeros((4, 4))
    for i in range(4):
        for j in range(4):
            if i != j:
                derivative[i, j] = factor[i] / (factor[j] * (nodes[i] - nodes[j]))
        derivative[i, i] = -np.sum(derivative[i])
    halves = []
    for half in range(2):
        points = 0.5 * (nodes + half)
        table = np.ones((4, 4))
        for j in range(4):
            for other in range(4):
                if other != j:
                    table[:, j] *= (points - nodes[other]) / (nodes[j] - nodes[other])
        halves.append(table)
    return weights, derivative, halves


def stiffness_table():
    weights, derivative, halves = lagrange_tables()
    mass = np.diag(weights)
    line = derivative.T @ mass @ derivative
    return (
        np.kron(np.kron(line, mass), mass)
        + np.kron(np.kron(mass, line), mass)
        + np.kron(np.kron(mass, mass), line)
    )


def weight_table():
    weights = lagrange_tables()[0]
    rows = [weights[first] * weights[second] for first in range(4) for part in range(2) for second in range(4)]
    return np.broadcast_to(np.array(rows, np.float32)[:, None], (32, lanes))


def stacked(table):
    rest = np.asarray(table, np.float32)
    parts = []
    for _ in range(3):
        parts.append(rest.astype(jnp.bfloat16))
        rest = rest - parts[-1].astype(np.float32)
    high, mid, low = parts
    return np.concatenate([high, high, mid, mid, high, low], axis=1)


def const_tables():
    return stacked(stiffness_table()), np.ascontiguousarray(weight_table())


def three(x):
    high = x.astype(bf16)
    rest = x - high.astype(f32)
    mid = rest.astype(bf16)
    return high, mid, (rest - mid.astype(f32)).astype(bf16)


def added(got, first, rows):
    return sum(got[first + rows * t : first + rows * t + rows] for t in range(1, terms)) + got[
        first : first + rows
    ]


def dot(a, b):
    return jnp.dot(a, b, preferred_element_type=f32)


def dot_t(a, b):
    return lax.dot_general(a, b, (((1,), (1,)), ((), ())), preferred_element_type=f32)


def cat(parts, axis):
    return parts[0] if len(parts) == 1 else jnp.concatenate(parts, axis=axis)


def table_dot(table, x):
    high, mid, low = three(x)
    return dot(table, jnp.concatenate([high, mid, high, mid, low, high], axis=0))


def interpolate(x, case, nf, transposed=False):
    halves = [h.T if transposed else h for h in lagrange_tables()[2]]
    n = x.shape[1]
    case = jnp.broadcast_to(case, (8, n))
    hanging = (case >= 0) & (case < 4)
    place = lax.broadcasted_iota(i32, (8, n), 0) & 3

    def pick(second, low, high, whole):
        return jnp.where(hanging, jnp.where(second, high, low), whole)

    def along(half, step):
        tile = jnp.zeros((8, n), f32)
        for j in range(4):
            if 0 <= j + step < 4:
                tile = jnp.where(place == j, float(half[j, j + step]), tile)
        return tile

    first, second = case >= 2, (case & 1) == 1
    across = [
        [pick(first, float(halves[0][i, j]), float(halves[1][i, j]), float(i == j)) for j in range(4)]
        for i in range(4)
    ]
    within = {
        step: pick(second, along(halves[0], step), along(halves[1], step), float(step == 0))
        for step in range(-3, 4)
    }
    out = []
    for k in range(nf):
        part = [x[32 * k + 8 * i : 32 * k + 8 * i + 8] for i in range(4)]
        for i in range(4):
            mixed = sum(across[i][j] * part[j] for j in range(4))
            out.append(
                sum(
                    within[step] * (pltpu.roll(mixed, -step % 8, 0) if step else mixed)
                    for step in range(-3, 4)
                )
            )
    return jnp.concatenate(out, axis=0)


def other_part(x):
    return jnp.concatenate(
        [pltpu.roll(x[8 * g : 8 * g + 8], 4, 0) for g in range(x.shape[0] // 8)], axis=0
    )


def slope_rows(shape):
    return (lax.broadcasted_iota(i32, shape, 0) & 4) == 4


def rows_of(rows, count, width):
    place = lax.broadcasted_iota(i32, (count, width), 0)
    table = jnp.zeros((count, width), f32)
    for k, r in enumerate(rows):
        table = jnp.where(place == k, r, table)
    return table


def one_hot(index_row, rows, first=0):
    place = lax.broadcasted_iota(i32, (rows, index_row.shape[1]), 0) + first
    return jnp.where(place == index_row, 1.0, 0.0).astype(bf16)


def gather_columns(stack, hot, face, nf):
    h = 32 * nf
    if hot.shape[0] == 768:
        return added(dot(stack, hot), 0, h)
    parts = [stack[:, lanes * f : lanes * f + lanes] for f in range(6)]
    got = dot(jnp.concatenate(parts, axis=0), hot)
    out = added(got, 0, h)
    for f in range(1, 6):
        out = jnp.where(face == f, added(got, terms * h * f, h), out)
    return out


def scatter_columns(x, hot, face, nf):
    h = 32 * nf
    stack = jnp.concatenate(three(x)[:terms], axis=0)
    if hot.shape[1] == 768:
        return added(dot(stack, hot), 0, h)
    parts = [stack * jnp.where(face == f, 1.0, 0.0).astype(bf16) for f in range(6)]
    got = dot_t(jnp.concatenate(parts, axis=0), hot)
    return jnp.concatenate([added(got, terms * h * f, h) for f in range(6)], axis=1)


def element_rows(coef_ref, level_ref):
    coef = coef_ref[...]
    level = level_ref[...]
    size = jnp.where(level == 0, 1.0, jnp.where(level == 1, 0.5, 0.25)).astype(f32)
    inverse = jnp.where(level == 0, 1.0, jnp.where(level == 1, 2.0, 4.0)).astype(f32)
    return coef, size, coef * size, coef * inverse


def by_place(values):
    place = lax.broadcasted_iota(i32, (8, lanes), 0) & (len(values) - 1)
    tile = jnp.full((8, lanes), float(values[0]), f32)
    for p in range(1, len(values)):
        tile = jnp.where(place == p, float(values[p]), tile)
    return tile


def face_ends():
    derivative = lagrange_tables()[1]
    for dim in range(3):
        for lower in range(2):
            node = 0 if lower else 3
            yield dim, 2 * dim + lower, node, (-1.0 if lower else 1.0) * derivative[node]


def face_traces(u):
    sub = lax.broadcasted_iota(i32, (8, lanes), 0)
    low = sub < 4
    v = [[u[16 * i + 8 * m : 16 * i + 8 * m + 8] for m in range(2)] for i in range(4)]
    out = {}
    for dim, face, node, slope in face_ends():
        rows = []
        if dim == 0:
            for m in range(2):
                normal = sum(float(slope[i]) * v[i][m] for i in range(4))
                rows.append(jnp.where(low, v[node][m], pltpu.roll(normal, 4, 0)))
                rows.append(jnp.where(low, pltpu.roll(v[node][m], 4, 0), normal))
        elif dim == 1:
            scale = [by_place([slope[2 * m]] * 4 + [slope[2 * m + 1]] * 4) for m in range(2)]
            for i in range(4):
                normal = scale[0] * v[i][0] + scale[1] * v[i][1]
                normal = normal + pltpu.roll(normal, 4, 0)
                rows.append(jnp.where(low, pltpu.roll(v[i][1], 4, 0) if node else v[i][0], normal))
        else:
            scale = by_place(slope)
            for i in range(4):
                row = None
                for m in range(2):
                    normal = scale * v[i][m]
                    normal = normal + pltpu.roll(normal, 7, 0)
                    normal = normal + pltpu.roll(normal, 6, 0)
                    for half in range(2):
                        to = 2 * m + half
                        value = pltpu.roll(v[i][m], (to - 4 * half - node) % 8, 0)
                        shift = (to + 4 - 4 * half) % 8
                        moved = pltpu.roll(normal, shift, 0) if shift else normal
                        row = value if row is None else jnp.where(sub == to, value, row)
                        row = jnp.where(sub == to + 4, moved, row)
                rows.append(row)
        out[face] = jnp.concatenate(rows, axis=0)
    return [out[f] for f in range(6)]


def lift_traces(total, faces):
    sub = lax.broadcasted_iota(i32, (8, lanes), 0)
    low = sub < 4
    r = [[total[16 * i + 8 * m : 16 * i + 8 * m + 8] for m in range(2)] for i in range(4)]
    for dim, face, node, slope in face_ends():
        b = [faces[face][8 * i : 8 * i + 8] for i in range(4)]
        if dim == 0:
            for m in range(2):
                even, odd = b[2 * m], b[2 * m + 1]
                normal = jnp.where(low, pltpu.roll(even, 4, 0), odd)
                for i in range(4):
                    r[i][m] = r[i][m] + float(slope[i]) * normal
                r[node][m] = r[node][m] + jnp.where(low, even, pltpu.roll(odd, 4, 0))
        elif dim == 1:
            scale = [by_place([slope[2 * m]] * 4 + [slope[2 * m + 1]] * 4) for m in range(2)]
            for i in range(4):
                turned = pltpu.roll(b[i], 4, 0)
                normal = jnp.where(low, turned, b[i])
                for m in range(2):
                    r[i][m] = r[i][m] + scale[m] * normal
                value = jnp.where(low, 0.0, turned) if node else jnp.where(low, b[i], 0.0)
                r[i][node // 2] = r[i][node // 2] + value
        else:
            scale = by_place(slope)
            here = by_place([1.0 if p == node else 0.0 for p in range(4)])
            for i in range(4):
                for m in range(2):
                    spread = [
                        jnp.where(
                            low,
                            jnp.broadcast_to(b[i][at : at + 1], (8, lanes)),
                            jnp.broadcast_to(b[i][at + 1 : at + 2], (8, lanes)),
                        )
                        for at in (2 * m, 4 + 2 * m)
                    ]
                    r[i][m] = r[i][m] + (here * spread[0] + scale * spread[1])
    return jnp.concatenate([r[i][m] for i in range(4) for m in range(2)], axis=0)


def face_stack(u, normal_scale):
    scale = jnp.where(slope_rows((32, lanes)), jnp.broadcast_to(normal_scale, (32, lanes)), 1.0)
    fields = [jnp.concatenate([part * scale for part in face_traces(x)], axis=1) for x in u]
    return jnp.concatenate(three(cat(fields, 0))[:terms], axis=0)


def gather_message(stack, hot, case, nf):
    got = dot(stack, hot)
    h = 32 * nf
    out = interpolate(added(got, 0, h), case, nf)
    low = terms * h
    if stack.shape[0] == low:
        return out
    coef = got[low : low + 1] + got[low + 1 : low + 2] + got[low + 2 : low + 3]
    size = got[low + 3 : low + 4] * jnp.where((case >= 0) & (case < 4), 0.5, 1.0)
    row = lax.broadcasted_iota(i32, (8, out.shape[1]), 0)
    scalars = jnp.where(row == 0, coef, jnp.where(row == 1, size, 0.0))
    return jnp.concatenate([out, scalars], axis=0)


def where_am_i(chips):
    me = lax.axis_index("dom")
    chip = me // 2
    core = me - 2 * chip
    near = jnp.where(lax.rem(chip, 2) == 1, -1, 1)
    far = jnp.where(lax.rem(chip, 4) < 2, 1, -1)
    end = (chip == 0) | (chip == chips - 1)
    far_there = (chip - 2 * far >= 0) & (chip - 2 * far < chips)
    return core, near, far, end, ~end, far_there


def carried(core, near, far, near_there, far_there):
    first = core == 0
    return (
        jnp.where(first, near, -near), jnp.where(first, far, -far),
        first | near_there, first | far_there,
    )


def row_of(offset):
    size = jnp.abs(offset)
    return 2 * (size - 1) + jnp.where(offset < 0, 1, 0)


def narrow(offset):
    return jnp.abs(offset) == 3


def side_attributes(side_ref, more=()):
    live = lax.broadcasted_iota(i32, (1, side_pad), 1) < 930
    rows = [jnp.where(live, side_ref[k : k + 1], 0).astype(f32) for k in range(3)]
    rows.append(jnp.where(live, 1.0, 0.0))
    return rows_of(rows + list(more), 16, side_pad).astype(bf16)


def look_up(attributes, index):
    blocks = jnp.concatenate(
        [attributes[:, lanes * k : lanes * k + lanes] for k in range(side_pad // lanes)], axis=0
    )
    found = dot(blocks, one_hot(index & 127, lanes))
    block = index >> 7
    out = jnp.zeros((8, index.shape[1]), f32)
    for k in range(side_pad // lanes):
        out = jnp.where(block == k, found[16 * k : 16 * k + 8], out)
    return out


def place_of(found):
    valid = found[3:4] > 0.5
    return tuple(jnp.where(valid, found[k : k + 1], -1.0).astype(i32) for k in range(3))


def fill_one_hot(hot_ref, elem, face):
    hot = one_hot(elem, lanes)
    for f in range(6):
        hot_ref[lanes * f : lanes * f + lanes] = hot * jnp.where(face == f, 1.0, 0.0).astype(bf16)


def listed_part(rolled_ref, shift, offset, low, high, valid):
    place = shifts.index(shift)
    lane = lax.broadcasted_iota(i32, (1, lanes), 1)
    values = rolled_ref[pl.ds(8 * place + jnp.minimum(row_of(offset), 7), 1), :]
    return jnp.where((lane >= low) & (lane < high) & valid, values, -1)


def send_setup_kernel(chips, *refs):
    sources, refs = refs[:10], refs[10:]
    hot_ref, case_ref, stack_ref, side_ref, rolled_ref = refs[:5]
    sent_ref, landed = refs[5], (*refs[10:17], *refs[6:9])
    slot_ref, arrived = refs[9], refs[17]
    copies = [
        pltpu.make_async_copy(source, target, arrived.at[k])
        for k, (source, target) in enumerate(zip(sources, landed))
    ]
    for k in (5, 0, 1, 2, 6, 7, 8, 3, 4, 9):
        copies[k].start()
    list_ref = landed[5]
    start_ref, coef_ref, level_ref = landed[6:9]
    side_ref[...] = jnp.full((8, side_pad), -1, i32)
    sides = landed[0].shape[1]
    copies[5].wait()
    core, near, far, end, near_there, far_there = where_am_i(chips)
    listed = jnp.concatenate([list_ref[...], jnp.full((8, 32), -1, i32)], axis=1)
    for place, shift in enumerate(shifts):
        rolled_ref[8 * place : 8 * place + 8] = (
            pltpu.roll(listed, shift, 1) if shift else listed
        )
    part = functools.partial(listed_part, rolled_ref)
    other = 1 - core
    step, step_two, there, there_two = carried(other, near, far, near_there, far_there)
    cross, cross_two = 2 * step + other - core, 4 * step_two + other - core
    first = (
        part(0, cross_two, 0, 24, there_two & narrow(cross_two)),
        part(24, 4 * step_two, 24, 48, there_two),
        part(48, 2 * step, 48, 96, there),
        part(96, cross, 96, 120, there & narrow(cross)),
    )
    slot_ref[0:1, 0:128] = functools.reduce(jnp.maximum, first)
    slot_ref[0:1, 128:256] = part(0, cross, 0, 96, there & ~narrow(cross))
    slot_ref[0:1, 256:384] = part(0, 1 - 2 * core, 0, 96, core >= 0)
    for k in range(3):
        copies[k].wait()
        side_ref[k : k + 1, 0:sides] = landed[k][...]
    elem, face, slot_case = place_of(look_up(side_attributes(side_ref), slot_ref[0:1, :]))
    case_ref[0:1, :] = slot_case
    fill_one_hot(hot_ref, elem, face)

    for k in (6, 7, 8):
        copies[k].wait()
    coef, size, volume_scale, normal_scale = element_rows(coef_ref, level_ref)
    stack = face_stack([start_ref[...]], normal_scale)
    scalars = rows_of([x.astype(f32) for x in three(coef)] + [size], 16, lanes).astype(bf16)
    stack = jnp.concatenate([stack, jnp.concatenate([scalars] * 6, axis=1)], axis=0)
    stack_ref[...] = stack
    sent = gather_message(stack, hot_ref[...], slot_case, 1)
    sent_ref[...] = sent
    for k in (3, 4):
        copies[k].wait()
        side_ref[k : k + 1, 0:sides] = landed[k][...]
    copies[9].wait()


def own_setup_kernel(chips, side_ref, rolled_ref, hot_ref, case_ref, slot_ref):
    core, near, far, end, near_there, far_there = where_am_i(chips)
    part = functools.partial(listed_part, rolled_ref)
    flip = 1 - 2 * core
    step, step_two, there, there_two = carried(core, near, far, near_there, far_there)
    cross, cross_two = 2 * step + flip, 4 * step_two + flip
    slot_ref[0:1, 0:128] = jnp.maximum(
        part(0, 4 * step_two, 0, 24, there_two),
        part(24, cross_two, 24, 48, there_two & narrow(cross_two)),
    )
    slot_ref[0:1, 128:256] = jnp.maximum(
        part(0, 2 * step, 0, 48, there), part(96, cross, 96, 120, there & narrow(cross))
    )
    slot_ref[0:1, 256:384] = part(0, cross, 0, 96, there & ~narrow(cross))
    elem, face, slot_case = place_of(look_up(side_attributes(side_ref), slot_ref[0:1, :]))
    case_ref[0:1, :] = slot_case
    fill_one_hot(hot_ref, elem, face)


def own_kernel(nf, stack_ref, hot_ref, case_ref, own_ref):
    own_ref[...] = gather_message(stack_ref[...], hot_ref[...], case_ref[0:1], nf)


def pack(x, nf):
    lane = lax.broadcasted_iota(i32, (1, lanes), 1)
    out = []
    for k in range(nf):
        last = x[32 * k + 24 : 32 * k + 32]
        for g in range(3):
            part = x[32 * k + 8 * g : 32 * k + 8 * g + 8]
            out.append(jnp.where(lane < 96, part, pltpu.roll(last, 96 - 32 * g, 1)))
    return jnp.concatenate(out, axis=0)


def unpack(x, nf):
    lane = lax.broadcasted_iota(i32, (1, lanes), 1)
    out = []
    for k in range(nf):
        part = [x[24 * k + 8 * g : 24 * k + 8 * g + 8] for g in range(3)]
        moved = [pltpu.roll(p, 32 * g + 32, 1) for g, p in enumerate(part)]
        out += part
        out.append(jnp.where(lane < 32, moved[0], jnp.where(lane < 64, moved[1], moved[2])))
    return jnp.concatenate(out, axis=0)


def carry_kernel(nf, sent_ref, own_ref, *rest):
    two_ref, one_ref = rest[-2:]
    h = 32 * nf
    lane = lax.broadcasted_iota(i32, (1, lanes), 1)
    sent = sent_ref[:, 0:128]
    handed = jnp.where((lane >= 48) & (lane < 96), pltpu.roll(sent, 48, 1), 0.0)
    two_away = own_ref[:, 0:128] + handed
    first = own_ref[:, 128:256] + jnp.where(lane >= 48, sent, 0.0)
    second = own_ref[:, 256:384] + sent_ref[:, 128:256]
    if nf == 1:
        two_ref[...] = two_away
        one_ref[:, 0:128] = first
        one_ref[:, 128:256] = second
    else:
        two_ref[...] = pack(two_away, nf)
        one_ref[0:h] = first
        one_ref[h:] = pack(second, nf)


def received(nf, one_ref, two_ref):
    if nf == 1:
        return two_ref[...], one_ref[:, 0:128], one_ref[:, 128:256]
    h = 32 * nf
    return unpack(two_ref[...], nf), one_ref[0:h], unpack(one_ref[h:], nf)


def relay_kernel(nf, chips, one_ref, two_ref, *rest):
    out_ref = rest[-1]
    core, near, far, end, near_there, far_there = where_am_i(chips)
    lane = lax.broadcasted_iota(i32, (1, lanes), 1)
    two_away, one, second = received(nf, one_ref, two_ref)
    passed = jnp.where(lane < 24, pltpu.roll(two_away, 56, 1), two_away)
    out_ref[:, 0:128] = jnp.where((lane < 48) & ~(end & (core == 1)), passed, one)
    out_ref[:, 128:256] = second


def setup_kernel(
    chips, coef_ref, level_ref, side_ref,
    own_hot_ref, partner_hot_ref, far_hot_ref, place_ref, info_ref, arrival_ref,
):
    core, near, far, end, near_there, far_there = where_am_i(chips)
    elem, direction, case = side_ref[0:1], side_ref[1:2], side_ref[2:3]
    kind, partner = side_ref[3:4], side_ref[4:5]
    live = lax.broadcasted_iota(i32, (1, side_pad), 1) < 930

    coef, size, volume_scale, normal_scale = element_rows(coef_ref, level_ref)
    scalars = rows_of([x.astype(f32) for x in three(coef)] + [size], 16, lanes)
    mine = dot(scalars.astype(bf16), one_hot(elem, lanes))
    hanging = (case >= 0) & (case < 4)
    own_coef = mine[0:1] + mine[1:2] + mine[2:3]
    own_size = mine[3:4] * jnp.where(hanging, 0.5, 1.0)

    attributes = side_attributes(side_ref, (mine[0:1], mine[1:2], mine[2:3], own_size))
    here = live & (partner < 930)
    other = look_up(attributes, jnp.where(here, partner, -1))
    other_elem, other_face = place_of(other)[:2]
    partner_hot_ref[...] = one_hot(other_elem, lanes)
    valid = other[3:4] > 0.5
    edge = jnp.where(kind == 1, 1.0, 0.0)
    least = jnp.where(valid, jnp.minimum(own_size, other[7:8]), 0.0)
    jump = 16.0 * (own_coef + other[4:5] + other[5:6] + other[6:7]) * least
    area = least * least
    info_ref[:, 0:side_pad] = rows_of(
        [jump, jump * (1.0 - edge), area * (0.5 + 0.5 * edge), area * (0.5 - 0.5 * edge),
         case.astype(f32), other[2:3]],
        8, side_pad,
    )

    def arrives(carrier):
        last = end & (carrier == 1)
        back = jnp.where((carrier == 0) | end, -near, near)
        back_two = jnp.where(carrier == 0, -far, far)
        turn = 2 * core - 1
        return (
            2 * back, 2 * back + turn, 4 * back_two, 4 * back_two + turn,
            ~(end & (carrier == 0)), ~last, last,
        )

    def span(low, high, valid):
        return low, jnp.where(valid, high, low)

    segments = []
    for mine, carrier in ((True, core), (False, 1 - core)):
        straight, cross, straight_two, cross_two, there, there_two, last = arrives(carrier)
        slim, wide = there & narrow(cross), there & ~narrow(cross)
        at_first = (last & (core != 1)) | (~last & (carrier == core))
        if mine:
            two_parts = ((*span(48, 72, there_two & narrow(cross_two)), cross_two),
                         (*span(72, 96, there_two), straight_two))
        else:
            two_parts = ((*span(0, 24, there_two), straight_two),
                         (*span(24, 48, there_two & narrow(cross_two)), cross_two))
        segments.append((
            (*span(0, 48, there & at_first), straight), (*span(48, 96, there & ~at_first), straight),
            (*span(96, 120, slim), cross), *two_parts,
        ))
        segments.append(((*span(0, 96, wide), cross),))
        if mine:
            segments.append(((0, 96, 2 * core - 1),))
    entry = partner - 930
    peer = (entry * 683) >> 16
    entry = entry - 96 * peer
    sought = live & (partner >= 930) & (kind == 0)
    column = jnp.full((1, side_pad), -1, i32)
    for tile, parts in enumerate(segments):
        for low, high, offset in parts:
            match = sought & (peer == row_of(offset)) & (entry < high - low)
            column = jnp.where(match, lanes * tile + low + entry, column)
    block = column >> 7
    split = [
        attributes * jnp.where(block == tile, 1.0, 0.0).astype(bf16) for tile in range(len(segments))
    ]
    target = dot_t(jnp.concatenate(split, axis=0), one_hot(column & 127, lanes))
    target = jnp.concatenate(
        [target[16 * tile : 16 * tile + 8] for tile in range(len(segments))], axis=1
    )
    target_elem, target_face, target_case = place_of(target)
    elems = jnp.concatenate([elem, target_elem], axis=1)
    faces = jnp.concatenate([direction, target_face], axis=1)
    near = side_pad + near_lanes
    own_hot_ref[...] = one_hot(elems[:, :near], lanes)
    far_hot_ref[...] = one_hot(elems[:, near:], lanes)
    other_face = jnp.concatenate([other_face, jnp.full((1, 640), -1, i32)], axis=1)
    place_ref[...] = rows_of(
        [elems.astype(f32), faces.astype(f32), other_face.astype(f32)], 16, elems.shape[1]
    )
    info_ref[:, side_pad:] = rows_of(
        [jnp.zeros((1, near_lanes), f32)] * 4 + [target_case[:, 0:near_lanes].astype(f32)], 8, near_lanes
    )
    arrival_ref[...] = rows_of(
        [target_case.astype(f32), target[4:5] + target[5:6] + target[6:7], target[7:8]],
        8, 640,
    )


def whole_kernel(own_elem_ref, partner_elem_ref, far_elem_ref, place_ref, own_ref, partner_ref, far_ref):
    near = side_pad + near_lanes
    for source, row, low, high, target in (
        (own_elem_ref, 1, 0, near, own_ref),
        (partner_elem_ref, 2, 0, side_pad, partner_ref),
        (far_elem_ref, 1, near, near + far_lanes, far_ref),
    ):
        hot, face = source[...], place_ref[row : row + 1, low:high]
        for f in range(6):
            target[lanes * f : lanes * f + lanes] = hot * jnp.where(face == f, 1.0, 0.0).astype(bf16)


def turn_kernel(place_ref, own_ref, far_ref):
    row = lax.broadcasted_iota(i32, (16, lanes), 0)
    weight = jnp.where(row == 0, 1.0, jnp.where(row == 1, 128.0, 0.0)).astype(bf16)
    column = lax.dot_general(
        place_ref[...].astype(bf16), weight, (((0,), (0,)), ((), ())), preferred_element_type=f32
    )
    lane = lax.broadcasted_iota(i32, (1, lanes), 1).astype(f32)
    split = own_ref.shape[0]
    for f in range(6):
        part = jnp.where(column == lane + 128.0 * f, 1.0, 0.0).astype(bf16)
        own_ref[:, lanes * f : lanes * f + lanes] = part[:split]
        far_ref[:, lanes * f : lanes * f + lanes] = part[split:]


def sides_kernel(
    nf, stack_ref, own_hot_ref, partner_hot_ref, far_hot_ref, place_ref, info_ref,
    arrival_ref, mine_ref, other_ref, target_ref,
):
    stack = stack_ref[0 : 32 * terms * nf]
    near = side_pad + near_lanes
    for hot_ref, face, case, out_ref in (
        (own_hot_ref, place_ref[1:2, 0:near], info_ref[4:5], mine_ref),
        (partner_hot_ref, place_ref[2:3, 0:side_pad], info_ref[5:6, 0:side_pad], other_ref),
        (far_hot_ref, place_ref[1:2, near:], arrival_ref[0:1, near_lanes:640], target_ref),
    ):
        got = gather_columns(stack, hot_ref[...], face, nf)
        out_ref[...] = interpolate(got, case.astype(i32), nf)


def side_flux(nf, mine, outer, coefs, case, face, weight_ref, hot):
    jump, jump_out, area, area_out = coefs
    weight = weight_ref[:, 0:1]
    flux = []
    for k in range(nf):
        inner, other = mine[32 * k : 32 * k + 32], outer[32 * k : 32 * k + 32]
        jumps = jnp.where(slope_rows(inner.shape), 0.0, jump * inner - jump_out * other)
        flux.append(weight * (jumps - other_part(area * inner - area_out * other)))
    flux = interpolate(cat(flux, 0), case.astype(i32), nf, transposed=True)
    return scatter_columns(flux, hot, face, nf)


def halo_coefs(coef, size, other_coef, other_size):
    least = jnp.minimum(size, other_size)
    return 16.0 * (coef + other_coef) * least, 0.5 * least * least


def flux_kernel(
    turn, nf, skip, both, chips, handed_ref, one_ref, two_ref, mine_ref, other_ref, place_ref,
    info_ref, arrival_ref, weight_ref, own_hot_ref, field_ref, coef_ref, level_ref, stiffness_ref, *rest,
):
    h = 32 * nf
    rows = slice(32 * skip, 32 * skip + h)
    core, near, far, end, near_there, far_there = where_am_i(chips)
    lane = lax.broadcasted_iota(i32, (1, lanes), 1)
    two_away, first, second = received(both, one_ref, two_ref)
    kept = jnp.where(lane < 72, two_away, pltpu.roll(two_away, 72, 1))
    inside = (lane >= 48) & (lane < 96) & ~(end & (core == 1))
    got = jnp.concatenate(
        [jnp.where(inside, kept, first), second, handed_ref[:, 256:384]], axis=1
    )
    if turn == 0:
        sum_ref, volume_ref, halo_ref = rest
        halo = halo_coefs(
            arrival_ref[1:2, 0:near_lanes], arrival_ref[2:3, 0:near_lanes],
            got[h : h + 1], got[h + 1 : h + 2],
        )
        halo_ref[...] = rows_of(halo, 8, near_lanes)
    else:
        halo_ref, sum_ref, volume_ref = rest
        halo = halo_ref[0:1], halo_ref[1:2]
    coefs = [
        jnp.concatenate([info_ref[k : k + 1, 0:side_pad], halo[k // 2]], axis=1) for k in range(4)
    ]
    outer = jnp.concatenate([other_ref[rows], got[rows]], axis=1)
    sum_ref[...] = side_flux(
        nf, mine_ref[rows], outer, coefs, info_ref[4:5], place_ref[1:2, 0 : side_pad + near_lanes], weight_ref,
        own_hot_ref[...],
    )
    volume_scale = element_rows(coef_ref, level_ref)[2]
    low = 64 * skip
    fields = [field_ref[low + 64 * k : low + 64 * k + 64] * volume_scale for k in range(nf)]
    volume = table_dot(stiffness_ref[...], cat(fields, 1))
    for k in range(nf):
        volume_ref[64 * k : 64 * k + 64, :] = volume[:, lanes * k : lanes * k + lanes]


def solve_blocks(inverse_ref, hold_ref, nf):
    sums = [jnp.zeros((64, lanes), f32) for _ in range(nf)]
    for col in range(64):
        block = inverse_ref[col].astype(f32)
        for k in range(nf):
            sums[k] = sums[k] + block * hold_ref[64 * k + col : 64 * k + col + 1, :]
    return sums


def update_kernel(
    turn, nf, skip, nf_next,
    one_ref, local_ref, volume_ref, target_ref, place_ref, arrival_ref, far_hot_ref, weight_ref,
    field_ref, coef_ref, level_ref, inverse_ref, *rest,
):
    if turn == 0:
        guess_ref, *rest = rest
    else:
        halo_ref, *rest = rest
    if turn == 1:
        rhs_ref, *rest = rest
    if nf_next:
        hot_ref, case_ref, new_ref, stack_ref, sent_ref, *rest = rest
    elif turn == 3:
        part_ref, *rest = rest
    else:
        new_ref, *rest = rest
    hold_ref = rest[-1]
    h = 32 * nf
    rows = slice(32 * skip, 32 * skip + h)
    if turn == 0:
        halo = halo_coefs(
            arrival_ref[1:2, near_lanes:640], arrival_ref[2:3, near_lanes:640],
            one_ref[h : h + 1], one_ref[h + 1 : h + 2],
        )
        rest[0][...] = rows_of(halo, 8, far_lanes)
    else:
        halo = (halo_ref[0:1], halo_ref[1:2])
    total = local_ref[...] + side_flux(
        nf, target_ref[rows], one_ref[rows], (halo[0], halo[0], halo[1], halo[1]), arrival_ref[0:1, near_lanes:640],
        place_ref[1:2, side_pad + near_lanes :], weight_ref, far_hot_ref[...],
    )
    coef, size, volume_scale, normal_scale = element_rows(coef_ref, level_ref)
    scale = jnp.where(slope_rows((32, lanes)), jnp.broadcast_to(normal_scale, (32, lanes)), 1.0)
    for k in range(nf):
        mine = total[32 * k : 32 * k + 32]
        faces = [mine[:, lanes * f : lanes * f + lanes] * scale for f in range(6)]
        part = lift_traces(volume_ref[64 * k : 64 * k + 64], faces)
        if turn == 1 and k == 1:
            part = rhs_ref[...] - part
        hold_ref[64 * k : 64 * k + 64, :] = part
    new = solve_blocks(inverse_ref, hold_ref, nf)
    if turn == 0:
        new.append(guess_ref[...])
    if turn < 3:
        for k, x in enumerate(new):
            new_ref[64 * k : 64 * k + 64, :] = x
    if nf_next:
        stack = face_stack(new[:nf_next], normal_scale)
        stack_ref[...] = stack
        sent = gather_message(stack, hot_ref[...], case_ref[0:1], nf_next)
        sent_ref[...] = sent
    if turn == 3:
        lane = lax.broadcasted_iota(i32, (1, lanes), 1)
        sums = []
        for x in (field_ref[...], new[0]):
            total = jnp.sum(x * x, axis=0, keepdims=True)
            sums.append(total + pltpu.roll(total, 64, 1))
        part_ref[...] = jnp.broadcast_to(jnp.where(lane < 64, sums[0], sums[1]), part_ref.shape)


def finish_kernel(part_ref, guess_ref, first_ref, second_ref, out_ref, bound_ref):
    total = jnp.sum(part_ref[...], axis=0, keepdims=True)
    lane = lax.broadcasted_iota(i32, (1, lanes), 1)
    before = jnp.sum(jnp.where(lane < 64, total, 0.0), axis=1, keepdims=True)
    after = jnp.sum(jnp.where(lane < 64, 0.0, total), axis=1, keepdims=True)
    bound = jnp.sqrt(after / before)
    upper = 1.2 * bound
    lower = upper / 15.0
    center = 0.5 * (upper + lower)
    half = 0.5 * (upper - lower)
    ratio = center / half
    damping = 1.0 / ratio
    damping_next = 1.0 / (2.0 * ratio - damping)
    first = first_ref[64:128] / center
    second = first_ref[64:128] - second_ref[...] / center
    out_ref[...] = (
        guess_ref[...] + first + (damping_next * damping * first + 2.0 * damping_next / half * second)
    )
    bound_ref[...] = jnp.broadcast_to(bound, (1, lanes))


def in_vmem(x):
    return pltpu.with_memory_space_constraint(x, pltpu.VMEM)


def in_hbm(x):
    return pltpu.with_memory_space_constraint(x, pltpu.HBM)


def run(body, outs, ins, name, scratch=(), flops=1 << 24, placed=True, kept=True):
    spec = pl.BlockSpec(memory_space=pltpu.VMEM)
    return pl.pallas_call(
        body,
        out_shape=[(pltpu.VMEM if kept else jax.ShapeDtypeStruct)(shape, dtype) for shape, dtype in outs],
        in_specs=[spec if placed else pl.BlockSpec(memory_space=pltpu.HBM)] * len(ins),
        out_specs=[spec] * len(outs),
        scratch_shapes=list(scratch),
        compiler_params=pltpu.CompilerParams(vmem_limit_bytes=24 << 20),
        cost_estimate=pl.CostEstimate(flops=flops, bytes_accessed=1 << 20, transcendentals=0),
        name=name,
    )(*(in_vmem(x) if placed else in_hbm(x) for x in ins))


def local(
    rhs_field, initial_guess, start_vector, coefficient, refine_level, block_inverse,
    side_elem, side_dir, side_case, side_kind, partner, send_list,
):
    devices = lax.axis_size("dom")
    chips = devices // 2
    stiffness, weight = (jnp.asarray(t) for t in const_tables())
    coef = coefficient.reshape(1, lanes)
    level = refine_level.reshape(1, lanes)

    def permute(x, to):
        return lax.ppermute(x, "dom", sorted(to.items()))

    swapped = {i: i ^ 1 for i in range(devices)}
    two_away, one_away = {}, {}
    for c in range(chips):
        two_away[2 * c] = 2 * (c ^ 2)
        one_away[2 * c] = 2 * (c ^ 1)
        over = c + 2 if c % 4 >= 2 else c - 2
        two_away[2 * c + 1] = 2 * (over if 0 <= over < chips else c ^ 1) + 1
        if 0 < c < chips - 1:
            one_away[2 * c + 1] = 2 * (c + 1 if c % 2 else c - 1) + 1
    for c in (0, chips - 1):
        one_away[2 * (c ^ 1)] = 2 * c + 1
        one_away[2 * c + 1] = 2 * c

    def exchange(sent, nf, own_work, work, *beside):
        rows = sent.shape[0]
        (own,) = own_work()
        handed = permute(sent, swapped)
        two_out, one_out = run(
            functools.partial(carry_kernel, nf),
            [((rows, lanes), f32), ((rows, 256), f32)] if nf == 1
            else [((24 * nf, lanes), f32), ((56 * nf, lanes), f32)],
            [handed, own, *beside[:1]], "carry",
        )
        arrivals = permute(one_out, one_away), permute(two_out, two_away)
        made = work()
        (last,) = run(
            functools.partial(relay_kernel, nf, chips), [((rows, 256), f32)],
            [*arrivals, made[2], *beside[1:]], "relay",
        )
        return (handed, *arrivals), permute(last, swapped), made

    sides = [x.reshape(1, -1) for x in (side_elem, side_dir, side_case, side_kind, partner)]
    first = [*sides, send_list, start_vector, coef, level, initial_guess]
    hot, case, stack, sides, rolled, sent, coef, level, guess = run(
        functools.partial(send_setup_kernel, chips),
        [((768, 384), bf16), ((8, 384), i32), ((32 * terms + 16, 768), bf16), ((8, side_pad), i32), ((32, lanes), i32),
         ((40, 384), f32), *((x.shape, x.dtype) for x in first[7:])],
        first,
        "send_setup",
        scratch=[
            pltpu.VMEM((8, 384), i32),
            *(pltpu.VMEM(x.shape, x.dtype) for x in first[:7]), pltpu.SemaphoreType.DMA((len(first),)),
        ],
        placed=False,
    )
    own_slots = run(
        functools.partial(own_setup_kernel, chips),
        [((768, 384), bf16), ((8, 384), i32)],
        [sides, rolled],
        "own_setup",
        scratch=[pltpu.VMEM((8, 384), i32)],
    )
    fields, halo, late = start_vector, [], []
    for turn, (nf, nf_next) in enumerate(((1, 2), (2, 2), (2, 1), (1, 0))):
        h = 32 * nf
        def own_work():
            return run(
                functools.partial(own_kernel, nf),
                [((sent.shape[0], 384), f32)],
                [stack, *own_slots],
                "own",
            )

        def side_work(hots):
            return run(
                functools.partial(sides_kernel, nf),
                [((h, side_pad + near_lanes), f32), ((h, side_pad), f32), ((h, far_lanes), f32)],
                [stack, *hots, *places],
                "sides",
            )

        if turn == 0:
            *hots, place, info, arrival = run(
                functools.partial(setup_kernel, chips),
                [((lanes, side_pad + near_lanes), bf16), ((lanes, side_pad), bf16), ((lanes, far_lanes), bf16),
                 ((16, side_pad + 640), f32), ((8, side_pad + near_lanes), f32), ((8, 640), f32)],
                [coef, level, sides],
                "setup",
            )
            places = [place, info, arrival]
            own_scatter, _, far_scatter = hots
        elif turn == 1:
            hots = run(
                whole_kernel,
                [((768, side_pad + near_lanes), bf16), ((768, side_pad), bf16), ((768, far_lanes), bf16)],
                [*hots, place],
                "whole",
            )
            own_scatter, far_scatter = run(
                turn_kernel,
                [((side_pad + near_lanes, 768), bf16), ((far_lanes, 768), bf16)],
                [place],
                "turn",
            )
        beside = (hots[0], own_scatter) if turn == 1 else late if turn == 3 else ()
        arrivals, last, made = exchange(
            sent, nf, own_work, functools.partial(side_work, hots), *beside
        )
        mine, others, targets = made

        def apply(count, skip, count_next):
            rows = 32 * count
            sums, volume, *near = run(
                functools.partial(flux_kernel, turn, count, skip, nf, chips),
                [((rows, 768), f32), ((64 * count, lanes), f32)] + ([] if turn else [((8, near_lanes), f32)]),
                [*arrivals, mine, others, *places, weight, own_scatter, fields, coef, level, stiffness]
                + halo[:1],
                "flux",
            )
            ins = [
                last, sums, volume, targets, place, arrival, far_scatter, weight, fields, coef, level,
                block_inverse, *(halo[1:] if turn else [guess]), *([rhs_field] if turn == 1 else []),
            ]
            outs = [((devices, lanes) if turn == 3 else (64 * max(count, count_next), lanes), f32)]
            if count_next:
                ins += [hot, case]
                outs += [((32 * terms * count_next, 768), bf16), ((32 * count_next, 384), f32)]
            outs += [] if turn else [((8, far_lanes), f32)]
            late.append(sums)
            made = run(
                functools.partial(update_kernel, turn, count, skip, count_next),
                outs, ins, "update",
                scratch=[pltpu.VMEM((64 * count, lanes), f32)],
            )
            return [*made, *near]

        if turn == 0:
            new, stack, sent, far_halo, near_halo = apply(nf, 0, nf_next)
            halo = [near_halo, far_halo]
        elif turn == 1:
            new, stack, sent = apply(nf, 0, nf_next)
            first = new
        elif turn == 2:
            new, stack, sent = apply(1, 0, 1)
            late.clear()
            late += apply(1, 1, 0)
            second = late[1]
        else:
            (parts,) = apply(1, 0, 0)
        fields = new
    parts = lax.all_to_all(parts.reshape(devices, 1, lanes), "dom", 0, 0).reshape(devices, lanes)
    smoothed, bound = run(
        finish_kernel,
        [((64, lanes), f32), ((1, lanes), f32)],
        [parts, guess, first, second],
        "finish",
        kept=False,
    )
    return smoothed, bound[0, 0]


def solution(mesh):
    placed = (
        P(None, "dom"), P(None, "dom"), P(None, "dom"), P("dom"), P("dom"), P(None, None, "dom"),
        P("dom"), P("dom"), P("dom"), P("dom"), P("dom"), P("dom", None),
    )
    return jax.shard_map(
        local, mesh=mesh, in_specs=placed, out_specs=(P(None, "dom"), P()), check_vma=False
    )
```

```python
import functools
import math

import jax
import jax.numpy as jnp
import numpy as np
from jax import lax
from jax.experimental import pallas as pl
from jax.experimental.pallas import tpu as pltpu
from jax.sharding import PartitionSpec as P

f32 = jnp.float32
bf16 = jnp.bfloat16
i32 = jnp.int32
peer_offsets = (1, -1, 2, -2, 3, -3, 4, -4)
live_width = {1: 96, 2: 48, 3: 24, 4: 24}
lanes = 128
shifts = (0, 24, 48, 96)
side_pad = 1024
near_lanes, far_lanes = 384, 256
terms = 2


def lagrange_tables():
    root_five = 1.0 / math.sqrt(5.0)
    nodes = np.array([0.0, 0.5 - 0.5 * root_five, 0.5 + 0.5 * root_five, 1.0])
    weights = np.array([1.0, 5.0, 5.0, 1.0]) / 12.0
    factor = np.array(
        [np.prod([nodes[i] - nodes[j] for j in range(4) if j != i]) for i in range(4)]
    )
    derivative = np.zeros((4, 4))
    for i in range(4):
        for j in range(4):
            if i != j:
                derivative[i, j] = factor[i] / (factor[j] * (nodes[i] - nodes[j]))
        derivative[i, i] = -np.sum(derivative[i])
    halves = []
    for half in range(2):
        points = 0.5 * (nodes + half)
        table = np.ones((4, 4))
        for j in range(4):
            for other in range(4):
                if other != j:
                    table[:, j] *= (points - nodes[other]) / (nodes[j] - nodes[other])
        halves.append(table)
    return weights, derivative, halves


def stiffness_table():
    weights, derivative, halves = lagrange_tables()
    mass = np.diag(weights)
    line = derivative.T @ mass @ derivative
    return (
        np.kron(np.kron(line, mass), mass)
        + np.kron(np.kron(mass, line), mass)
        + np.kron(np.kron(mass, mass), line)
    )


def weight_table():
    weights = lagrange_tables()[0]
    rows = [weights[first] * weights[second] for first in range(4) for part in range(2) for second in range(4)]
    return np.broadcast_to(np.array(rows, np.float32)[:, None], (32, lanes))


def stacked(table):
    rest = np.asarray(table, np.float32)
    parts = []
    for _ in range(3):
        parts.append(rest.astype(jnp.bfloat16))
        rest = rest - parts[-1].astype(np.float32)
    high, mid, low = parts
    return np.concatenate([high, high, mid, mid, high, low], axis=1)


def const_tables():
    return stacked(stiffness_table()), np.ascontiguousarray(weight_table())


def three(x):
    high = x.astype(bf16)
    rest = x - high.astype(f32)
    mid = rest.astype(bf16)
    return high, mid, (rest - mid.astype(f32)).astype(bf16)


def added(got, first, rows):
    return sum(got[first + rows * t : first + rows * t + rows] for t in range(1, terms)) + got[
        first : first + rows
    ]


def dot(a, b):
    return jnp.dot(a, b, preferred_element_type=f32)


def dot_t(a, b):
    return lax.dot_general(a, b, (((1,), (1,)), ((), ())), preferred_element_type=f32)


def cat(parts, axis):
    return parts[0] if len(parts) == 1 else jnp.concatenate(parts, axis=axis)


def table_dot(table, x):
    high, mid, low = three(x)
    return dot(table, jnp.concatenate([high, mid, high, mid, low, high], axis=0))


def interpolate(x, case, nf, transposed=False):
    halves = [h.T if transposed else h for h in lagrange_tables()[2]]
    n = x.shape[1]
    case = jnp.broadcast_to(case, (8, n))
    hanging = (case >= 0) & (case < 4)
    place = lax.broadcasted_iota(i32, (8, n), 0) & 3

    def pick(second, low, high, whole):
        return jnp.where(hanging, jnp.where(second, high, low), whole)

    def along(half, step):
        tile = jnp.zeros((8, n), f32)
        for j in range(4):
            if 0 <= j + step < 4:
                tile = jnp.where(place == j, float(half[j, j + step]), tile)
        return tile

    first, second = case >= 2, (case & 1) == 1
    across = [
        [pick(first, float(halves[0][i, j]), float(halves[1][i, j]), float(i == j)) for j in range(4)]
        for i in range(4)
    ]
    within = {
        step: pick(second, along(halves[0], step), along(halves[1], step), float(step == 0))
        for step in range(-3, 4)
    }
    out = []
    for k in range(nf):
        part = [x[32 * k + 8 * i : 32 * k + 8 * i + 8] for i in range(4)]
        for i in range(4):
            mixed = sum(across[i][j] * part[j] for j in range(4))
            out.append(
                sum(
                    within[step] * (pltpu.roll(mixed, -step % 8, 0) if step else mixed)
                    for step in range(-3, 4)
                )
            )
    return jnp.concatenate(out, axis=0)


def other_part(x):
    return jnp.concatenate(
        [pltpu.roll(x[8 * g : 8 * g + 8], 4, 0) for g in range(x.shape[0] // 8)], axis=0
    )


def slope_rows(shape):
    return (lax.broadcasted_iota(i32, shape, 0) & 4) == 4


def rows_of(rows, count, width):
    place = lax.broadcasted_iota(i32, (count, width), 0)
    table = jnp.zeros((count, width), f32)
    for k, r in enumerate(rows):
        table = jnp.where(place == k, r, table)
    return table


def one_hot(index_row, rows, first=0):
    place = lax.broadcasted_iota(i32, (rows, index_row.shape[1]), 0) + first
    return jnp.where(place == index_row, 1.0, 0.0).astype(bf16)


def gather_columns(stack, hot, face, nf):
    h = 32 * nf
    if hot.shape[0] == 768:
        return added(dot(stack, hot), 0, h)
    parts = [stack[:, lanes * f : lanes * f + lanes] for f in range(6)]
    got = dot(jnp.concatenate(parts, axis=0), hot)
    out = added(got, 0, h)
    for f in range(1, 6):
        out = jnp.where(face == f, added(got, terms * h * f, h), out)
    return out


def scatter_columns(x, hot, face, nf):
    h = 32 * nf
    stack = jnp.concatenate(three(x)[:terms], axis=0)
    if hot.shape[1] == 768:
        return added(dot(stack, hot), 0, h)
    parts = [stack * jnp.where(face == f, 1.0, 0.0).astype(bf16) for f in range(6)]
    got = dot_t(jnp.concatenate(parts, axis=0), hot)
    return jnp.concatenate([added(got, terms * h * f, h) for f in range(6)], axis=1)


def element_rows(coef_ref, level_ref):
    coef = coef_ref[...]
    level = level_ref[...]
    size = jnp.where(level == 0, 1.0, jnp.where(level == 1, 0.5, 0.25)).astype(f32)
    inverse = jnp.where(level == 0, 1.0, jnp.where(level == 1, 2.0, 4.0)).astype(f32)
    return coef, size, coef * size, coef * inverse


def by_place(values):
    place = lax.broadcasted_iota(i32, (8, lanes), 0) & (len(values) - 1)
    tile = jnp.full((8, lanes), float(values[0]), f32)
    for p in range(1, len(values)):
        tile = jnp.where(place == p, float(values[p]), tile)
    return tile


def face_ends():
    derivative = lagrange_tables()[1]
    for dim in range(3):
        for lower in range(2):
            node = 0 if lower else 3
            yield dim, 2 * dim + lower, node, (-1.0 if lower else 1.0) * derivative[node]


def face_traces(u):
    sub = lax.broadcasted_iota(i32, (8, lanes), 0)
    low = sub < 4
    v = [[u[16 * i + 8 * m : 16 * i + 8 * m + 8] for m in range(2)] for i in range(4)]
    out = {}
    for dim, face, node, slope in face_ends():
        rows = []
        if dim == 0:
            for m in range(2):
                normal = sum(float(slope[i]) * v[i][m] for i in range(4))
                rows.append(jnp.where(low, v[node][m], pltpu.roll(normal, 4, 0)))
                rows.append(jnp.where(low, pltpu.roll(v[node][m], 4, 0), normal))
        elif dim == 1:
            scale = [by_place([slope[2 * m]] * 4 + [slope[2 * m + 1]] * 4) for m in range(2)]
            for i in range(4):
                normal = scale[0] * v[i][0] + scale[1] * v[i][1]
                normal = normal + pltpu.roll(normal, 4, 0)
                rows.append(jnp.where(low, pltpu.roll(v[i][1], 4, 0) if node else v[i][0], normal))
        else:
            scale = by_place(slope)
            for i in range(4):
                row = None
                for m in range(2):
                    normal = scale * v[i][m]
                    normal = normal + pltpu.roll(normal, 7, 0)
                    normal = normal + pltpu.roll(normal, 6, 0)
                    for half in range(2):
                        to = 2 * m + half
                        value = pltpu.roll(v[i][m], (to - 4 * half - node) % 8, 0)
                        shift = (to + 4 - 4 * half) % 8
                        moved = pltpu.roll(normal, shift, 0) if shift else normal
                        row = value if row is None else jnp.where(sub == to, value, row)
                        row = jnp.where(sub == to + 4, moved, row)
                rows.append(row)
        out[face] = jnp.concatenate(rows, axis=0)
    return [out[f] for f in range(6)]


def lift_traces(total, faces):
    sub = lax.broadcasted_iota(i32, (8, lanes), 0)
    low = sub < 4
    r = [[total[16 * i + 8 * m : 16 * i + 8 * m + 8] for m in range(2)] for i in range(4)]
    for dim, face, node, slope in face_ends():
        b = [faces[face][8 * i : 8 * i + 8] for i in range(4)]
        if dim == 0:
            for m in range(2):
                even, odd = b[2 * m], b[2 * m + 1]
                normal = jnp.where(low, pltpu.roll(even, 4, 0), odd)
                for i in range(4):
                    r[i][m] = r[i][m] + float(slope[i]) * normal
                r[node][m] = r[node][m] + jnp.where(low, even, pltpu.roll(odd, 4, 0))
        elif dim == 1:
            scale = [by_place([slope[2 * m]] * 4 + [slope[2 * m + 1]] * 4) for m in range(2)]
            for i in range(4):
                turned = pltpu.roll(b[i], 4, 0)
                normal = jnp.where(low, turned, b[i])
                for m in range(2):
                    r[i][m] = r[i][m] + scale[m] * normal
                value = jnp.where(low, 0.0, turned) if node else jnp.where(low, b[i], 0.0)
                r[i][node // 2] = r[i][node // 2] + value
        else:
            scale = by_place(slope)
            here = by_place([1.0 if p == node else 0.0 for p in range(4)])
            for i in range(4):
                for m in range(2):
                    spread = [
                        jnp.where(
                            low,
                            jnp.broadcast_to(b[i][at : at + 1], (8, lanes)),
                            jnp.broadcast_to(b[i][at + 1 : at + 2], (8, lanes)),
                        )
                        for at in (2 * m, 4 + 2 * m)
                    ]
                    r[i][m] = r[i][m] + (here * spread[0] + scale * spread[1])
    return jnp.concatenate([r[i][m] for i in range(4) for m in range(2)], axis=0)


def face_stack(u, normal_scale):
    scale = jnp.where(slope_rows((32, lanes)), jnp.broadcast_to(normal_scale, (32, lanes)), 1.0)
    fields = [jnp.concatenate([part * scale for part in face_traces(x)], axis=1) for x in u]
    return jnp.concatenate(three(cat(fields, 0))[:terms], axis=0)


def gather_message(stack, hot, case, nf):
    got = dot(stack, hot)
    h = 32 * nf
    out = interpolate(added(got, 0, h), case, nf)
    low = terms * h
    if stack.shape[0] == low:
        return out
    coef = got[low : low + 1] + got[low + 1 : low + 2] + got[low + 2 : low + 3]
    size = got[low + 3 : low + 4] * jnp.where((case >= 0) & (case < 4), 0.5, 1.0)
    row = lax.broadcasted_iota(i32, (8, out.shape[1]), 0)
    scalars = jnp.where(row == 0, coef, jnp.where(row == 1, size, 0.0))
    return jnp.concatenate([out, scalars], axis=0)


def where_am_i(chips):
    me = lax.axis_index("dom")
    chip = me // 2
    core = me - 2 * chip
    near = jnp.where(lax.rem(chip, 2) == 1, -1, 1)
    far = jnp.where(lax.rem(chip, 4) < 2, 1, -1)
    end = (chip == 0) | (chip == chips - 1)
    far_there = (chip - 2 * far >= 0) & (chip - 2 * far < chips)
    return core, near, far, end, ~end, far_there


def carried(core, near, far, near_there, far_there):
    first = core == 0
    return (
        jnp.where(first, near, -near), jnp.where(first, far, -far),
        first | near_there, first | far_there,
    )


def row_of(offset):
    size = jnp.abs(offset)
    return 2 * (size - 1) + jnp.where(offset < 0, 1, 0)


def narrow(offset):
    return jnp.abs(offset) == 3


def side_attributes(side_ref, more=()):
    live = lax.broadcasted_iota(i32, (1, side_pad), 1) < 930
    rows = [jnp.where(live, side_ref[k : k + 1], 0).astype(f32) for k in range(3)]
    rows.append(jnp.where(live, 1.0, 0.0))
    return rows_of(rows + list(more), 16, side_pad).astype(bf16)


def look_up(attributes, index):
    blocks = jnp.concatenate(
        [attributes[:, lanes * k : lanes * k + lanes] for k in range(side_pad // lanes)], axis=0
    )
    found = dot(blocks, one_hot(index & 127, lanes))
    block = index >> 7
    out = jnp.zeros((8, index.shape[1]), f32)
    for k in range(side_pad // lanes):
        out = jnp.where(block == k, found[16 * k : 16 * k + 8], out)
    return out


def place_of(found):
    valid = found[3:4] > 0.5
    return tuple(jnp.where(valid, found[k : k + 1], -1.0).astype(i32) for k in range(3))


def fill_one_hot(hot_ref, elem, face):
    hot = one_hot(elem, lanes)
    for f in range(6):
        hot_ref[lanes * f : lanes * f + lanes] = hot * jnp.where(face == f, 1.0, 0.0).astype(bf16)


def listed_part(rolled_ref, shift, offset, low, high, valid):
    place = shifts.index(shift)
    lane = lax.broadcasted_iota(i32, (1, lanes), 1)
    values = rolled_ref[pl.ds(8 * place + jnp.minimum(row_of(offset), 7), 1), :]
    return jnp.where((lane >= low) & (lane < high) & valid, values, -1)


def send_setup_kernel(chips, *refs):
    sources, refs = refs[:10], refs[10:]
    hot_ref, case_ref, stack_ref, side_ref, rolled_ref = refs[:5]
    sent_ref, landed = refs[5], (*refs[10:17], *refs[6:9])
    slot_ref, arrived = refs[9], refs[17]
    copies = [
        pltpu.make_async_copy(source, target, arrived.at[k])
        for k, (source, target) in enumerate(zip(sources, landed))
    ]
    for k in (5, 0, 1, 2, 6, 7, 8, 3, 4, 9):
        copies[k].start()
    list_ref = landed[5]
    start_ref, coef_ref, level_ref = landed[6:9]
    side_ref[...] = jnp.full((8, side_pad), -1, i32)
    sides = landed[0].shape[1]
    copies[5].wait()
    core, near, far, end, near_there, far_there = where_am_i(chips)
    listed = jnp.concatenate([list_ref[...], jnp.full((8, 32), -1, i32)], axis=1)
    for place, shift in enumerate(shifts):
        rolled_ref[8 * place : 8 * place + 8] = (
            pltpu.roll(listed, shift, 1) if shift else listed
        )
    part = functools.partial(listed_part, rolled_ref)
    other = 1 - core
    step, step_two, there, there_two = carried(other, near, far, near_there, far_there)
    cross, cross_two = 2 * step + other - core, 4 * step_two + other - core
    first = (
        part(0, cross_two, 0, 24, there_two & narrow(cross_two)),
        part(24, 4 * step_two, 24, 48, there_two),
        part(48, 2 * step, 48, 96, there),
        part(96, cross, 96, 120, there & narrow(cross)),
    )
    slot_ref[0:1, 0:128] = functools.reduce(jnp.maximum, first)
    slot_ref[0:1, 128:256] = part(0, cross, 0, 96, there & ~narrow(cross))
    slot_ref[0:1, 256:384] = part(0, 1 - 2 * core, 0, 96, core >= 0)
    for k in range(3):
        copies[k].wait()
        side_ref[k : k + 1, 0:sides] = landed[k][...]
    elem, face, slot_case = place_of(look_up(side_attributes(side_ref), slot_ref[0:1, :]))
    case_ref[0:1, :] = slot_case
    fill_one_hot(hot_ref, elem, face)

    for k in (6, 7, 8):
        copies[k].wait()
    coef, size, volume_scale, normal_scale = element_rows(coef_ref, level_ref)
    stack = face_stack([start_ref[...]], normal_scale)
    scalars = rows_of([x.astype(f32) for x in three(coef)] + [size], 16, lanes).astype(bf16)
    stack = jnp.concatenate([stack, jnp.concatenate([scalars] * 6, axis=1)], axis=0)
    stack_ref[...] = stack
    sent = gather_message(stack, hot_ref[...], slot_case, 1)
    sent_ref[...] = sent
    for k in (3, 4):
        copies[k].wait()
        side_ref[k : k + 1, 0:sides] = landed[k][...]
    copies[9].wait()


def own_setup_kernel(chips, side_ref, rolled_ref, hot_ref, case_ref, slot_ref):
    core, near, far, end, near_there, far_there = where_am_i(chips)
    part = functools.partial(listed_part, rolled_ref)
    flip = 1 - 2 * core
    step, step_two, there, there_two = carried(core, near, far, near_there, far_there)
    cross, cross_two = 2 * step + flip, 4 * step_two + flip
    slot_ref[0:1, 0:128] = jnp.maximum(
        part(0, 4 * step_two, 0, 24, there_two),
        part(24, cross_two, 24, 48, there_two & narrow(cross_two)),
    )
    slot_ref[0:1, 128:256] = jnp.maximum(
        part(0, 2 * step, 0, 48, there), part(96, cross, 96, 120, there & narrow(cross))
    )
    slot_ref[0:1, 256:384] = part(0, cross, 0, 96, there & ~narrow(cross))
    elem, face, slot_case = place_of(look_up(side_attributes(side_ref), slot_ref[0:1, :]))
    case_ref[0:1, :] = slot_case
    fill_one_hot(hot_ref, elem, face)


def own_kernel(nf, stack_ref, hot_ref, case_ref, own_ref):
    own_ref[...] = gather_message(stack_ref[...], hot_ref[...], case_ref[0:1], nf)


def pack(x, nf):
    lane = lax.broadcasted_iota(i32, (1, lanes), 1)
    out = []
    for k in range(nf):
        last = x[32 * k + 24 : 32 * k + 32]
        for g in range(3):
            part = x[32 * k + 8 * g : 32 * k + 8 * g + 8]
            out.append(jnp.where(lane < 96, part, pltpu.roll(last, 96 - 32 * g, 1)))
    return jnp.concatenate(out, axis=0)


def unpack(x, nf):
    lane = lax.broadcasted_iota(i32, (1, lanes), 1)
    out = []
    for k in range(nf):
        part = [x[24 * k + 8 * g : 24 * k + 8 * g + 8] for g in range(3)]
        moved = [pltpu.roll(p, 32 * g + 32, 1) for g, p in enumerate(part)]
        out += part
        out.append(jnp.where(lane < 32, moved[0], jnp.where(lane < 64, moved[1], moved[2])))
    return jnp.concatenate(out, axis=0)


def carry_kernel(nf, sent_ref, own_ref, *rest):
    two_ref, one_ref = rest[-2:]
    h = 32 * nf
    lane = lax.broadcasted_iota(i32, (1, lanes), 1)
    sent = sent_ref[:, 0:128]
    handed = jnp.where((lane >= 48) & (lane < 96), pltpu.roll(sent, 48, 1), 0.0)
    two_away = own_ref[:, 0:128] + handed
    first = own_ref[:, 128:256] + jnp.where(lane >= 48, sent, 0.0)
    second = own_ref[:, 256:384] + sent_ref[:, 128:256]
    if nf == 1:
        two_ref[...] = two_away
        one_ref[:, 0:128] = first
        one_ref[:, 128:256] = second
    else:
        two_ref[...] = pack(two_away, nf)
        one_ref[0:h] = first
        one_ref[h:] = pack(second, nf)


def received(nf, one_ref, two_ref):
    if nf == 1:
        return two_ref[...], one_ref[:, 0:128], one_ref[:, 128:256]
    h = 32 * nf
    return unpack(two_ref[...], nf), one_ref[0:h], unpack(one_ref[h:], nf)


def relay_kernel(nf, chips, one_ref, two_ref, *rest):
    out_ref = rest[-1]
    core, near, far, end, near_there, far_there = where_am_i(chips)
    lane = lax.broadcasted_iota(i32, (1, lanes), 1)
    two_away, one, second = received(nf, one_ref, two_ref)
    passed = jnp.where(lane < 24, pltpu.roll(two_away, 56, 1), two_away)
    out_ref[:, 0:128] = jnp.where((lane < 48) & ~(end & (core == 1)), passed, one)
    out_ref[:, 128:256] = second


def setup_kernel(
    chips, coef_ref, level_ref, side_ref,
    own_hot_ref, partner_hot_ref, far_hot_ref, place_ref, info_ref, arrival_ref,
):
    core, near, far, end, near_there, far_there = where_am_i(chips)
    elem, direction, case = side_ref[0:1], side_ref[1:2], side_ref[2:3]
    kind, partner = side_ref[3:4], side_ref[4:5]
    live = lax.broadcasted_iota(i32, (1, side_pad), 1) < 930

    coef, size, volume_scale, normal_scale = element_rows(coef_ref, level_ref)
    scalars = rows_of([x.astype(f32) for x in three(coef)] + [size], 16, lanes)
    mine = dot(scalars.astype(bf16), one_hot(elem, lanes))
    hanging = (case >= 0) & (case < 4)
    own_coef = mine[0:1] + mine[1:2] + mine[2:3]
    own_size = mine[3:4] * jnp.where(hanging, 0.5, 1.0)

    attributes = side_attributes(side_ref, (mine[0:1], mine[1:2], mine[2:3], own_size))
    here = live & (partner < 930)
    other = look_up(attributes, jnp.where(here, partner, -1))
    other_elem, other_face = place_of(other)[:2]
    partner_hot_ref[...] = one_hot(other_elem, lanes)
    valid = other[3:4] > 0.5
    edge = jnp.where(kind == 1, 1.0, 0.0)
    least = jnp.where(valid, jnp.minimum(own_size, other[7:8]), 0.0)
    jump = 16.0 * (own_coef + other[4:5] + other[5:6] + other[6:7]) * least
    area = least * least
    info_ref[:, 0:side_pad] = rows_of(
        [jump, jump * (1.0 - edge), area * (0.5 + 0.5 * edge), area * (0.5 - 0.5 * edge),
         case.astype(f32), other[2:3]],
        8, side_pad,
    )

    def arrives(carrier):
        last = end & (carrier == 1)
        back = jnp.where((carrier == 0) | end, -near, near)
        back_two = jnp.where(carrier == 0, -far, far)
        turn = 2 * core - 1
        return (
            2 * back, 2 * back + turn, 4 * back_two, 4 * back_two + turn,
            ~(end & (carrier == 0)), ~last, last,
        )

    def span(low, high, valid):
        return low, jnp.where(valid, high, low)

    segments = []
    for mine, carrier in ((True, core), (False, 1 - core)):
        straight, cross, straight_two, cross_two, there, there_two, last = arrives(carrier)
        slim, wide = there & narrow(cross), there & ~narrow(cross)
        at_first = (last & (core != 1)) | (~last & (carrier == core))
        if mine:
            two_parts = ((*span(48, 72, there_two & narrow(cross_two)), cross_two),
                         (*span(72, 96, there_two), straight_two))
        else:
            two_parts = ((*span(0, 24, there_two), straight_two),
                         (*span(24, 48, there_two & narrow(cross_two)), cross_two))
        segments.append((
            (*span(0, 48, there & at_first), straight), (*span(48, 96, there & ~at_first), straight),
            (*span(96, 120, slim), cross), *two_parts,
        ))
        segments.append(((*span(0, 96, wide), cross),))
        if mine:
            segments.append(((0, 96, 2 * core - 1),))
    entry = partner - 930
    peer = (entry * 683) >> 16
    entry = entry - 96 * peer
    sought = live & (partner >= 930) & (kind == 0)
    column = jnp.full((1, side_pad), -1, i32)
    for tile, parts in enumerate(segments):
        for low, high, offset in parts:
            match = sought & (peer == row_of(offset)) & (entry < high - low)
            column = jnp.where(match, lanes * tile + low + entry, column)
    block = column >> 7
    split = [
        attributes * jnp.where(block == tile, 1.0, 0.0).astype(bf16) for tile in range(len(segments))
    ]
    target = dot_t(jnp.concatenate(split, axis=0), one_hot(column & 127, lanes))
    target = jnp.concatenate(
        [target[16 * tile : 16 * tile + 8] for tile in range(len(segments))], axis=1
    )
    target_elem, target_face, target_case = place_of(target)
    elems = jnp.concatenate([elem, target_elem], axis=1)
    faces = jnp.concatenate([direction, target_face], axis=1)
    near = side_pad + near_lanes
    own_hot_ref[...] = one_hot(elems[:, :near], lanes)
    far_hot_ref[...] = one_hot(elems[:, near:], lanes)
    other_face = jnp.concatenate([other_face, jnp.full((1, 640), -1, i32)], axis=1)
    place_ref[...] = rows_of(
        [elems.astype(f32), faces.astype(f32), other_face.astype(f32)], 16, elems.shape[1]
    )
    info_ref[:, side_pad:] = rows_of(
        [jnp.zeros((1, near_lanes), f32)] * 4 + [target_case[:, 0:near_lanes].astype(f32)], 8, near_lanes
    )
    arrival_ref[...] = rows_of(
        [target_case.astype(f32), target[4:5] + target[5:6] + target[6:7], target[7:8]],
        8, 640,
    )


def whole_kernel(own_elem_ref, partner_elem_ref, far_elem_ref, place_ref, own_ref, partner_ref, far_ref):
    near = side_pad + near_lanes
    for source, row, low, high, target in (
        (own_elem_ref, 1, 0, near, own_ref),
        (partner_elem_ref, 2, 0, side_pad, partner_ref),
        (far_elem_ref, 1, near, near + far_lanes, far_ref),
    ):
        hot, face = source[...], place_ref[row : row + 1, low:high]
        for f in range(6):
            target[lanes * f : lanes * f + lanes] = hot * jnp.where(face == f, 1.0, 0.0).astype(bf16)


def turn_kernel(place_ref, own_ref, far_ref):
    row = lax.broadcasted_iota(i32, (16, lanes), 0)
    weight = jnp.where(row == 0, 1.0, jnp.where(row == 1, 128.0, 0.0)).astype(bf16)
    column = lax.dot_general(
        place_ref[...].astype(bf16), weight, (((0,), (0,)), ((), ())), preferred_element_type=f32
    )
    lane = lax.broadcasted_iota(i32, (1, lanes), 1).astype(f32)
    split = own_ref.shape[0]
    for f in range(6):
        part = jnp.where(column == lane + 128.0 * f, 1.0, 0.0).astype(bf16)
        own_ref[:, lanes * f : lanes * f + lanes] = part[:split]
        far_ref[:, lanes * f : lanes * f + lanes] = part[split:]


def sides_kernel(
    nf, stack_ref, own_hot_ref, partner_hot_ref, far_hot_ref, place_ref, info_ref,
    arrival_ref, mine_ref, other_ref, target_ref,
):
    stack = stack_ref[0 : 32 * terms * nf]
    near = side_pad + near_lanes
    for hot_ref, face, case, out_ref in (
        (own_hot_ref, place_ref[1:2, 0:near], info_ref[4:5], mine_ref),
        (partner_hot_ref, place_ref[2:3, 0:side_pad], info_ref[5:6, 0:side_pad], other_ref),
        (far_hot_ref, place_ref[1:2, near:], arrival_ref[0:1, near_lanes:640], target_ref),
    ):
        got = gather_columns(stack, hot_ref[...], face, nf)
        out_ref[...] = interpolate(got, case.astype(i32), nf)


def side_flux(nf, mine, outer, coefs, case, face, weight_ref, hot):
    jump, jump_out, area, area_out = coefs
    weight = weight_ref[:, 0:1]
    flux = []
    for k in range(nf):
        inner, other = mine[32 * k : 32 * k + 32], outer[32 * k : 32 * k + 32]
        jumps = jnp.where(slope_rows(inner.shape), 0.0, jump * inner - jump_out * other)
        flux.append(weight * (jumps - other_part(area * inner - area_out * other)))
    flux = interpolate(cat(flux, 0), case.astype(i32), nf, transposed=True)
    return scatter_columns(flux, hot, face, nf)


def halo_coefs(coef, size, other_coef, other_size):
    least = jnp.minimum(size, other_size)
    return 16.0 * (coef + other_coef) * least, 0.5 * least * least


def flux_kernel(
    turn, nf, skip, both, chips, handed_ref, one_ref, two_ref, mine_ref, other_ref, place_ref,
    info_ref, arrival_ref, weight_ref, own_hot_ref, field_ref, coef_ref, level_ref, stiffness_ref, *rest,
):
    h = 32 * nf
    rows = slice(32 * skip, 32 * skip + h)
    core, near, far, end, near_there, far_there = where_am_i(chips)
    lane = lax.broadcasted_iota(i32, (1, lanes), 1)
    two_away, first, second = received(both, one_ref, two_ref)
    kept = jnp.where(lane < 72, two_away, pltpu.roll(two_away, 72, 1))
    inside = (lane >= 48) & (lane < 96) & ~(end & (core == 1))
    got = jnp.concatenate(
        [jnp.where(inside, kept, first), second, handed_ref[:, 256:384]], axis=1
    )
    if turn == 0:
        sum_ref, volume_ref, halo_ref = rest
        halo = halo_coefs(
            arrival_ref[1:2, 0:near_lanes], arrival_ref[2:3, 0:near_lanes],
            got[h : h + 1], got[h + 1 : h + 2],
        )
        halo_ref[...] = rows_of(halo, 8, near_lanes)
    else:
        halo_ref, sum_ref, volume_ref = rest
        halo = halo_ref[0:1], halo_ref[1:2]
    coefs = [
        jnp.concatenate([info_ref[k : k + 1, 0:side_pad], halo[k // 2]], axis=1) for k in range(4)
    ]
    outer = jnp.concatenate([other_ref[rows], got[rows]], axis=1)
    sum_ref[...] = side_flux(
        nf, mine_ref[rows], outer, coefs, info_ref[4:5], place_ref[1:2, 0 : side_pad + near_lanes], weight_ref,
        own_hot_ref[...],
    )
    volume_scale = element_rows(coef_ref, level_ref)[2]
    low = 64 * skip
    fields = [field_ref[low + 64 * k : low + 64 * k + 64] * volume_scale for k in range(nf)]
    volume = table_dot(stiffness_ref[...], cat(fields, 1))
    for k in range(nf):
        volume_ref[64 * k : 64 * k + 64, :] = volume[:, lanes * k : lanes * k + lanes]


def widen_kernel(inverse_ref, wide_ref):
    for col in range(64):
        wide_ref[col] = inverse_ref[col].astype(f32)


def solve_blocks(inverse_ref, hold_ref, nf):
    sums = [jnp.zeros((64, lanes), f32) for _ in range(nf)]
    for col in range(64):
        block = inverse_ref[col].astype(f32)
        for k in range(nf):
            sums[k] = sums[k] + block * hold_ref[64 * k + col : 64 * k + col + 1, :]
    return sums


def update_kernel(
    turn, nf, skip, nf_next,
    one_ref, local_ref, volume_ref, target_ref, place_ref, arrival_ref, far_hot_ref, weight_ref,
    field_ref, coef_ref, level_ref, inverse_ref, *rest,
):
    if turn == 0:
        guess_ref, *rest = rest
    else:
        halo_ref, *rest = rest
    if turn == 1:
        rhs_ref, *rest = rest
    if nf_next:
        hot_ref, case_ref, new_ref, stack_ref, sent_ref, *rest = rest
    elif turn == 3:
        part_ref, *rest = rest
    else:
        new_ref, *rest = rest
    hold_ref = rest[-1]
    h = 32 * nf
    rows = slice(32 * skip, 32 * skip + h)
    if turn == 0:
        halo = halo_coefs(
            arrival_ref[1:2, near_lanes:640], arrival_ref[2:3, near_lanes:640],
            one_ref[h : h + 1], one_ref[h + 1 : h + 2],
        )
        rest[0][...] = rows_of(halo, 8, far_lanes)
    else:
        halo = (halo_ref[0:1], halo_ref[1:2])
    total = local_ref[...] + side_flux(
        nf, target_ref[rows], one_ref[rows], (halo[0], halo[0], halo[1], halo[1]), arrival_ref[0:1, near_lanes:640],
        place_ref[1:2, side_pad + near_lanes :], weight_ref, far_hot_ref[...],
    )
    coef, size, volume_scale, normal_scale = element_rows(coef_ref, level_ref)
    scale = jnp.where(slope_rows((32, lanes)), jnp.broadcast_to(normal_scale, (32, lanes)), 1.0)
    for k in range(nf):
        mine = total[32 * k : 32 * k + 32]
        faces = [mine[:, lanes * f : lanes * f + lanes] * scale for f in range(6)]
        part = lift_traces(volume_ref[64 * k : 64 * k + 64], faces)
        if turn == 1 and k == 1:
            part = rhs_ref[...] - part
        hold_ref[64 * k : 64 * k + 64, :] = part
    new = solve_blocks(inverse_ref, hold_ref, nf)
    if turn == 0:
        new.append(guess_ref[...])
    if turn < 3:
        for k, x in enumerate(new):
            new_ref[64 * k : 64 * k + 64, :] = x
    if nf_next:
        stack = face_stack(new[:nf_next], normal_scale)
        stack_ref[...] = stack
        sent = gather_message(stack, hot_ref[...], case_ref[0:1], nf_next)
        sent_ref[...] = sent
    if turn == 3:
        lane = lax.broadcasted_iota(i32, (1, lanes), 1)
        sums = []
        for x in (field_ref[...], new[0]):
            total = jnp.sum(x * x, axis=0, keepdims=True)
            sums.append(total + pltpu.roll(total, 64, 1))
        part_ref[...] = jnp.broadcast_to(jnp.where(lane < 64, sums[0], sums[1]), part_ref.shape)


def finish_kernel(part_ref, guess_ref, first_ref, second_ref, out_ref, bound_ref):
    total = jnp.sum(part_ref[...], axis=0, keepdims=True)
    lane = lax.broadcasted_iota(i32, (1, lanes), 1)
    before = jnp.sum(jnp.where(lane < 64, total, 0.0), axis=1, keepdims=True)
    after = jnp.sum(jnp.where(lane < 64, 0.0, total), axis=1, keepdims=True)
    bound = jnp.sqrt(after / before)
    upper = 1.2 * bound
    lower = upper / 15.0
    center = 0.5 * (upper + lower)
    half = 0.5 * (upper - lower)
    ratio = center / half
    damping = 1.0 / ratio
    damping_next = 1.0 / (2.0 * ratio - damping)
    first = first_ref[64:128] / center
    second = first_ref[64:128] - second_ref[...] / center
    out_ref[...] = (
        guess_ref[...] + first + (damping_next * damping * first + 2.0 * damping_next / half * second)
    )
    bound_ref[...] = jnp.broadcast_to(bound, (1, lanes))


def in_vmem(x):
    return pltpu.with_memory_space_constraint(x, pltpu.VMEM)


def in_hbm(x):
    return pltpu.with_memory_space_constraint(x, pltpu.HBM)


def run(body, outs, ins, name, scratch=(), flops=1 << 24, placed=True, kept=True):
    spec = pl.BlockSpec(memory_space=pltpu.VMEM)
    return pl.pallas_call(
        body,
        out_shape=[(pltpu.VMEM if kept else jax.ShapeDtypeStruct)(shape, dtype) for shape, dtype in outs],
        in_specs=[spec if placed else pl.BlockSpec(memory_space=pltpu.HBM)] * len(ins),
        out_specs=[spec] * len(outs),
        scratch_shapes=list(scratch),
        compiler_params=pltpu.CompilerParams(vmem_limit_bytes=24 << 20),
        cost_estimate=pl.CostEstimate(flops=flops, bytes_accessed=1 << 20, transcendentals=0),
        name=name,
    )(*(in_vmem(x) if placed else in_hbm(x) for x in ins))


def local(
    rhs_field, initial_guess, start_vector, coefficient, refine_level, block_inverse,
    side_elem, side_dir, side_case, side_kind, partner, send_list,
):
    devices = lax.axis_size("dom")
    chips = devices // 2
    stiffness, weight = (jnp.asarray(t) for t in const_tables())
    coef = coefficient.reshape(1, lanes)
    level = refine_level.reshape(1, lanes)

    def permute(x, to):
        return lax.ppermute(x, "dom", sorted(to.items()))

    swapped = {i: i ^ 1 for i in range(devices)}
    two_away, one_away = {}, {}
    for c in range(chips):
        two_away[2 * c] = 2 * (c ^ 2)
        one_away[2 * c] = 2 * (c ^ 1)
        over = c + 2 if c % 4 >= 2 else c - 2
        two_away[2 * c + 1] = 2 * (over if 0 <= over < chips else c ^ 1) + 1
        if 0 < c < chips - 1:
            one_away[2 * c + 1] = 2 * (c + 1 if c % 2 else c - 1) + 1
    for c in (0, chips - 1):
        one_away[2 * (c ^ 1)] = 2 * c + 1
        one_away[2 * c + 1] = 2 * c

    def exchange(sent, nf, own_work, work, *beside):
        rows = sent.shape[0]
        (own,) = own_work()
        handed = permute(sent, swapped)
        two_out, one_out = run(
            functools.partial(carry_kernel, nf),
            [((rows, lanes), f32), ((rows, 256), f32)] if nf == 1
            else [((24 * nf, lanes), f32), ((56 * nf, lanes), f32)],
            [handed, own, *beside[:1]], "carry",
        )
        arrivals = permute(one_out, one_away), permute(two_out, two_away)
        made = work()
        (last,) = run(
            functools.partial(relay_kernel, nf, chips), [((rows, 256), f32)],
            [*arrivals, made[2], *beside[1:]], "relay",
        )
        return (handed, *arrivals), permute(last, swapped), made

    sides = [x.reshape(1, -1) for x in (side_elem, side_dir, side_case, side_kind, partner)]
    first = [*sides, send_list, start_vector, coef, level, initial_guess]
    hot, case, stack, sides, rolled, sent, coef, level, guess = run(
        functools.partial(send_setup_kernel, chips),
        [((768, 384), bf16), ((8, 384), i32), ((32 * terms + 16, 768), bf16), ((8, side_pad), i32), ((32, lanes), i32),
         ((40, 384), f32), *((x.shape, x.dtype) for x in first[7:])],
        first,
        "send_setup",
        scratch=[
            pltpu.VMEM((8, 384), i32),
            *(pltpu.VMEM(x.shape, x.dtype) for x in first[:7]), pltpu.SemaphoreType.DMA((len(first),)),
        ],
        placed=False,
    )
    own_slots = run(
        functools.partial(own_setup_kernel, chips),
        [((768, 384), bf16), ((8, 384), i32)],
        [sides, rolled],
        "own_setup",
        scratch=[pltpu.VMEM((8, 384), i32)],
    )
    fields, halo, late = start_vector, [], []
    (inverse,) = run(widen_kernel, [(block_inverse.shape, f32)], [block_inverse], "widen")
    for turn, (nf, nf_next) in enumerate(((1, 2), (2, 2), (2, 1), (1, 0))):
        h = 32 * nf
        def own_work():
            return run(
                functools.partial(own_kernel, nf),
                [((sent.shape[0], 384), f32)],
                [stack, *own_slots],
                "own",
            )

        def side_work(hots):
            return run(
                functools.partial(sides_kernel, nf),
                [((h, side_pad + near_lanes), f32), ((h, side_pad), f32), ((h, far_lanes), f32)],
                [stack, *hots, *places],
                "sides",
            )

        if turn == 0:
            *hots, place, info, arrival = run(
                functools.partial(setup_kernel, chips),
                [((lanes, side_pad + near_lanes), bf16), ((lanes, side_pad), bf16), ((lanes, far_lanes), bf16),
                 ((16, side_pad + 640), f32), ((8, side_pad + near_lanes), f32), ((8, 640), f32)],
                [coef, level, sides],
                "setup",
            )
            places = [place, info, arrival]
            own_scatter, _, far_scatter = hots
        elif turn == 1:
            hots = run(
                whole_kernel,
                [((768, side_pad + near_lanes), bf16), ((768, side_pad), bf16), ((768, far_lanes), bf16)],
                [*hots, place],
                "whole",
            )
            own_scatter, far_scatter = run(
                turn_kernel,
                [((side_pad + near_lanes, 768), bf16), ((far_lanes, 768), bf16)],
                [place],
                "turn",
            )
        beside = (hots[0], own_scatter) if turn == 1 else late if turn == 3 else ()
        arrivals, last, made = exchange(
            sent, nf, own_work, functools.partial(side_work, hots), *beside
        )
        mine, others, targets = made

        def apply(count, skip, count_next):
            rows = 32 * count
            sums, volume, *near = run(
                functools.partial(flux_kernel, turn, count, skip, nf, chips),
                [((rows, 768), f32), ((64 * count, lanes), f32)] + ([] if turn else [((8, near_lanes), f32)]),
                [*arrivals, mine, others, *places, weight, own_scatter, fields, coef, level, stiffness]
                + halo[:1],
                "flux",
            )
            ins = [
                last, sums, volume, targets, place, arrival, far_scatter, weight, fields, coef, level,
                inverse, *(halo[1:] if turn else [guess]), *([rhs_field] if turn == 1 else []),
            ]
            outs = [((devices, lanes) if turn == 3 else (64 * max(count, count_next), lanes), f32)]
            if count_next:
                ins += [hot, case]
                outs += [((32 * terms * count_next, 768), bf16), ((32 * count_next, 384), f32)]
            outs += [] if turn else [((8, far_lanes), f32)]
            late.append(sums)
            made = run(
                functools.partial(update_kernel, turn, count, skip, count_next),
                outs, ins, "update",
                scratch=[pltpu.VMEM((64 * count, lanes), f32)],
            )
            return [*made, *near]

        if turn == 0:
            new, stack, sent, far_halo, near_halo = apply(nf, 0, nf_next)
            halo = [near_halo, far_halo]
        elif turn == 1:
            new, stack, sent = apply(nf, 0, nf_next)
            first = new
        elif turn == 2:
            new, stack, sent = apply(1, 0, 1)
            late.clear()
            late += apply(1, 1, 0)
            second = late[1]
        else:
            (parts,) = apply(1, 0, 0)
        fields = new
    parts = lax.all_to_all(parts.reshape(devices, 1, lanes), "dom", 0, 0).reshape(devices, lanes)
    smoothed, bound = run(
        finish_kernel,
        [((64, lanes), f32), ((1, lanes), f32)],
        [parts, guess, first, second],
        "finish",
        kept=False,
    )
    return smoothed, bound[0, 0]


def solution(mesh):
    placed = (
        P(None, "dom"), P(None, "dom"), P(None, "dom"), P("dom"), P("dom"), P(None, None, "dom"),
        P("dom"), P("dom"), P("dom"), P("dom"), P("dom"), P("dom", None),
    )
    return jax.shard_map(
        local, mesh=mesh, in_specs=placed, out_specs=(P(None, "dom"), P()), check_vma=False
    )
```

```python
import functools
import math

import jax
import jax.numpy as jnp
import numpy as np
from jax import lax
from jax.experimental import pallas as pl
from jax.experimental.pallas import tpu as pltpu
from jax.sharding import PartitionSpec as P

f32 = jnp.float32
bf16 = jnp.bfloat16
i32 = jnp.int32
peer_offsets = (1, -1, 2, -2, 3, -3, 4, -4)
live_width = {1: 96, 2: 48, 3: 24, 4: 24}
lanes = 128
shifts = (0, 24, 48, 96)
side_pad = 1024
terms = 2


def lagrange_tables():
    root_five = 1.0 / math.sqrt(5.0)
    nodes = np.array([0.0, 0.5 - 0.5 * root_five, 0.5 + 0.5 * root_five, 1.0])
    weights = np.array([1.0, 5.0, 5.0, 1.0]) / 12.0
    factor = np.array(
        [np.prod([nodes[i] - nodes[j] for j in range(4) if j != i]) for i in range(4)]
    )
    derivative = np.zeros((4, 4))
    for i in range(4):
        for j in range(4):
            if i != j:
                derivative[i, j] = factor[i] / (factor[j] * (nodes[i] - nodes[j]))
        derivative[i, i] = -np.sum(derivative[i])
    halves = []
    for half in range(2):
        points = 0.5 * (nodes + half)
        table = np.ones((4, 4))
        for j in range(4):
            for other in range(4):
                if other != j:
                    table[:, j] *= (points - nodes[other]) / (nodes[j] - nodes[other])
        halves.append(table)
    return weights, derivative, halves


def stiffness_table():
    weights, derivative, halves = lagrange_tables()
    mass = np.diag(weights)
    line = derivative.T @ mass @ derivative
    return (
        np.kron(np.kron(line, mass), mass)
        + np.kron(np.kron(mass, line), mass)
        + np.kron(np.kron(mass, mass), line)
    )


def weight_table():
    weights = lagrange_tables()[0]
    rows = [weights[first] * weights[second] for first in range(4) for part in range(2) for second in range(4)]
    return np.broadcast_to(np.array(rows, np.float32)[:, None], (32, lanes))


def stacked(table):
    rest = np.asarray(table, np.float32)
    parts = []
    for _ in range(3):
        parts.append(rest.astype(jnp.bfloat16))
        rest = rest - parts[-1].astype(np.float32)
    high, mid, low = parts
    return np.concatenate([high, high, mid, mid, high, low], axis=1)


def const_tables():
    return stacked(stiffness_table()), np.ascontiguousarray(weight_table())


def three(x):
    high = x.astype(bf16)
    rest = x - high.astype(f32)
    mid = rest.astype(bf16)
    return high, mid, (rest - mid.astype(f32)).astype(bf16)


def added(got, first, rows):
    return sum(got[first + rows * t : first + rows * t + rows] for t in range(1, terms)) + got[
        first : first + rows
    ]


def dot(a, b):
    return jnp.dot(a, b, preferred_element_type=f32)


def dot_t(a, b):
    return lax.dot_general(a, b, (((1,), (1,)), ((), ())), preferred_element_type=f32)


def cat(parts, axis):
    return parts[0] if len(parts) == 1 else jnp.concatenate(parts, axis=axis)


def table_dot(table, x):
    high, mid, low = three(x)
    return dot(table, jnp.concatenate([high, mid, high, mid, low, high], axis=0))


def interpolate(x, case, nf, transposed=False):
    halves = [h.T if transposed else h for h in lagrange_tables()[2]]
    n = x.shape[1]
    case = jnp.broadcast_to(case, (8, n))
    hanging = (case >= 0) & (case < 4)
    place = lax.broadcasted_iota(i32, (8, n), 0) & 3

    def pick(second, low, high, whole):
        return jnp.where(hanging, jnp.where(second, high, low), whole)

    def along(half, step):
        tile = jnp.zeros((8, n), f32)
        for j in range(4):
            if 0 <= j + step < 4:
                tile = jnp.where(place == j, float(half[j, j + step]), tile)
        return tile

    first, second = case >= 2, (case & 1) == 1
    across = [
        [pick(first, float(halves[0][i, j]), float(halves[1][i, j]), float(i == j)) for j in range(4)]
        for i in range(4)
    ]
    within = {
        step: pick(second, along(halves[0], step), along(halves[1], step), float(step == 0))
        for step in range(-3, 4)
    }
    out = []
    for k in range(nf):
        part = [x[32 * k + 8 * i : 32 * k + 8 * i + 8] for i in range(4)]
        for i in range(4):
            mixed = sum(across[i][j] * part[j] for j in range(4))
            out.append(
                sum(
                    within[step] * (pltpu.roll(mixed, -step % 8, 0) if step else mixed)
                    for step in range(-3, 4)
                )
            )
    return jnp.concatenate(out, axis=0)


def other_part(x):
    return jnp.concatenate(
        [pltpu.roll(x[8 * g : 8 * g + 8], 4, 0) for g in range(x.shape[0] // 8)], axis=0
    )


def slope_rows(shape):
    return (lax.broadcasted_iota(i32, shape, 0) & 4) == 4


def rows_of(rows, count, width):
    place = lax.broadcasted_iota(i32, (count, width), 0)
    table = jnp.zeros((count, width), f32)
    for k, r in enumerate(rows):
        table = jnp.where(place == k, r, table)
    return table


def one_hot(index_row, rows, first=0):
    place = lax.broadcasted_iota(i32, (rows, index_row.shape[1]), 0) + first
    return jnp.where(place == index_row, 1.0, 0.0).astype(bf16)


def gather_columns(stack, hot, face, nf):
    h = 32 * nf
    if hot.shape[0] == 768:
        return added(dot(stack, hot), 0, h)
    parts = [stack[:, lanes * f : lanes * f + lanes] for f in range(6)]
    got = dot(jnp.concatenate(parts, axis=0), hot)
    out = added(got, 0, h)
    for f in range(1, 6):
        out = jnp.where(face == f, added(got, terms * h * f, h), out)
    return out


def scatter_columns(x, hot, face, nf):
    h = 32 * nf
    stack = jnp.concatenate(three(x)[:terms], axis=0)
    if hot.shape[1] == 768:
        return added(dot(stack, hot), 0, h)
    parts = [stack * jnp.where(face == f, 1.0, 0.0).astype(bf16) for f in range(6)]
    got = dot_t(jnp.concatenate(parts, axis=0), hot)
    return jnp.concatenate([added(got, terms * h * f, h) for f in range(6)], axis=1)


def element_rows(coef_ref, level_ref):
    coef = coef_ref[...]
    level = level_ref[...]
    size = jnp.where(level == 0, 1.0, jnp.where(level == 1, 0.5, 0.25)).astype(f32)
    inverse = jnp.where(level == 0, 1.0, jnp.where(level == 1, 2.0, 4.0)).astype(f32)
    return coef, size, coef * size, coef * inverse


def by_place(values):
    place = lax.broadcasted_iota(i32, (8, lanes), 0) & (len(values) - 1)
    tile = jnp.full((8, lanes), float(values[0]), f32)
    for p in range(1, len(values)):
        tile = jnp.where(place == p, float(values[p]), tile)
    return tile


def face_ends():
    derivative = lagrange_tables()[1]
    for dim in range(3):
        for lower in range(2):
            node = 0 if lower else 3
            yield dim, 2 * dim + lower, node, (-1.0 if lower else 1.0) * derivative[node]


def face_traces(u):
    sub = lax.broadcasted_iota(i32, (8, lanes), 0)
    low = sub < 4
    v = [[u[16 * i + 8 * m : 16 * i + 8 * m + 8] for m in range(2)] for i in range(4)]
    out = {}
    for dim, face, node, slope in face_ends():
        rows = []
        if dim == 0:
            for m in range(2):
                normal = sum(float(slope[i]) * v[i][m] for i in range(4))
                rows.append(jnp.where(low, v[node][m], pltpu.roll(normal, 4, 0)))
                rows.append(jnp.where(low, pltpu.roll(v[node][m], 4, 0), normal))
        elif dim == 1:
            scale = [by_place([slope[2 * m]] * 4 + [slope[2 * m + 1]] * 4) for m in range(2)]
            for i in range(4):
                normal = scale[0] * v[i][0] + scale[1] * v[i][1]
                normal = normal + pltpu.roll(normal, 4, 0)
                rows.append(jnp.where(low, pltpu.roll(v[i][1], 4, 0) if node else v[i][0], normal))
        else:
            scale = by_place(slope)
            for i in range(4):
                row = None
                for m in range(2):
                    normal = scale * v[i][m]
                    normal = normal + pltpu.roll(normal, 7, 0)
                    normal = normal + pltpu.roll(normal, 6, 0)
                    for half in range(2):
                        to = 2 * m + half
                        value = pltpu.roll(v[i][m], (to - 4 * half - node) % 8, 0)
                        shift = (to + 4 - 4 * half) % 8
                        moved = pltpu.roll(normal, shift, 0) if shift else normal
                        row = value if row is None else jnp.where(sub == to, value, row)
                        row = jnp.where(sub == to + 4, moved, row)
                rows.append(row)
        out[face] = jnp.concatenate(rows, axis=0)
    return [out[f] for f in range(6)]


def lift_traces(total, faces):
    sub = lax.broadcasted_iota(i32, (8, lanes), 0)
    low = sub < 4
    r = [[total[16 * i + 8 * m : 16 * i + 8 * m + 8] for m in range(2)] for i in range(4)]
    for dim, face, node, slope in face_ends():
        b = [faces[face][8 * i : 8 * i + 8] for i in range(4)]
        if dim == 0:
            for m in range(2):
                even, odd = b[2 * m], b[2 * m + 1]
                normal = jnp.where(low, pltpu.roll(even, 4, 0), odd)
                for i in range(4):
                    r[i][m] = r[i][m] + float(slope[i]) * normal
                r[node][m] = r[node][m] + jnp.where(low, even, pltpu.roll(odd, 4, 0))
        elif dim == 1:
            scale = [by_place([slope[2 * m]] * 4 + [slope[2 * m + 1]] * 4) for m in range(2)]
            for i in range(4):
                turned = pltpu.roll(b[i], 4, 0)
                normal = jnp.where(low, turned, b[i])
                for m in range(2):
                    r[i][m] = r[i][m] + scale[m] * normal
                value = jnp.where(low, 0.0, turned) if node else jnp.where(low, b[i], 0.0)
                r[i][node // 2] = r[i][node // 2] + value
        else:
            scale = by_place(slope)
            here = by_place([1.0 if p == node else 0.0 for p in range(4)])
            for i in range(4):
                for m in range(2):
                    spread = [
                        jnp.where(
                            low,
                            jnp.broadcast_to(b[i][at : at + 1], (8, lanes)),
                            jnp.broadcast_to(b[i][at + 1 : at + 2], (8, lanes)),
                        )
                        for at in (2 * m, 4 + 2 * m)
                    ]
                    r[i][m] = r[i][m] + (here * spread[0] + scale * spread[1])
    return jnp.concatenate([r[i][m] for i in range(4) for m in range(2)], axis=0)


def face_stack(u, normal_scale):
    scale = jnp.where(slope_rows((32, lanes)), jnp.broadcast_to(normal_scale, (32, lanes)), 1.0)
    fields = [jnp.concatenate([part * scale for part in face_traces(x)], axis=1) for x in u]
    return jnp.concatenate(three(cat(fields, 0))[:terms], axis=0)


def gather_message(stack, hot, case, nf):
    got = dot(stack, hot)
    h = 32 * nf
    out = interpolate(added(got, 0, h), case, nf)
    low = terms * h
    if stack.shape[0] == low:
        return out
    coef = got[low : low + 1] + got[low + 1 : low + 2] + got[low + 2 : low + 3]
    size = got[low + 3 : low + 4] * jnp.where((case >= 0) & (case < 4), 0.5, 1.0)
    row = lax.broadcasted_iota(i32, (8, out.shape[1]), 0)
    scalars = jnp.where(row == 0, coef, jnp.where(row == 1, size, 0.0))
    return jnp.concatenate([out, scalars], axis=0)


def where_am_i(chips):
    me = lax.axis_index("dom")
    chip = me // 2
    core = me - 2 * chip
    near = jnp.where(lax.rem(chip, 2) == 1, -1, 1)
    far = jnp.where(lax.rem(chip, 4) < 2, 1, -1)
    end = (chip == 0) | (chip == chips - 1)
    far_there = (chip - 2 * far >= 0) & (chip - 2 * far < chips)
    return core, near, far, end, ~end, far_there


def carried(core, near, far, near_there, far_there):
    first = core == 0
    return (
        jnp.where(first, near, -near), jnp.where(first, far, -far),
        first | near_there, first | far_there,
    )


def row_of(offset):
    size = jnp.abs(offset)
    return 2 * (size - 1) + jnp.where(offset < 0, 1, 0)


def narrow(offset):
    return jnp.abs(offset) == 3


def side_attributes(side_ref, more=()):
    live = lax.broadcasted_iota(i32, (1, side_pad), 1) < 930
    rows = [jnp.where(live, side_ref[k : k + 1], 0).astype(f32) for k in range(3)]
    rows.append(jnp.where(live, 1.0, 0.0))
    return rows_of(rows + list(more), 16, side_pad).astype(bf16)


def look_up(attributes, index):
    blocks = jnp.concatenate(
        [attributes[:, lanes * k : lanes * k + lanes] for k in range(side_pad // lanes)], axis=0
    )
    found = dot(blocks, one_hot(index & 127, lanes))
    block = index >> 7
    out = jnp.zeros((8, index.shape[1]), f32)
    for k in range(side_pad // lanes):
        out = jnp.where(block == k, found[16 * k : 16 * k + 8], out)
    return out


def place_of(found):
    valid = found[3:4] > 0.5
    return tuple(jnp.where(valid, found[k : k + 1], -1.0).astype(i32) for k in range(3))


def fill_one_hot(hot_ref, elem, face):
    hot = one_hot(elem, lanes)
    for f in range(6):
        hot_ref[lanes * f : lanes * f + lanes] = hot * jnp.where(face == f, 1.0, 0.0).astype(bf16)


def listed_part(rolled_ref, shift, offset, low, high, valid):
    place = shifts.index(shift)
    lane = lax.broadcasted_iota(i32, (1, lanes), 1)
    values = rolled_ref[pl.ds(8 * place + jnp.minimum(row_of(offset), 7), 1), :]
    return jnp.where((lane >= low) & (lane < high) & valid, values, -1)


def send_setup_kernel(chips, *refs):
    sources, refs = refs[:10], refs[10:]
    hot_ref, case_ref, stack_ref, side_ref, rolled_ref = refs[:5]
    sent_ref, landed = refs[5], (*refs[10:17], *refs[6:9])
    slot_ref, arrived = refs[9], refs[17]
    copies = [
        pltpu.make_async_copy(source, target, arrived.at[k])
        for k, (source, target) in enumerate(zip(sources, landed))
    ]
    for k in (5, 0, 1, 2, 6, 7, 8, 3, 4, 9):
        copies[k].start()
    list_ref = landed[5]
    start_ref, coef_ref, level_ref = landed[6:9]
    side_ref[...] = jnp.full((8, side_pad), -1, i32)
    sides = landed[0].shape[1]
    copies[5].wait()
    core, near, far, end, near_there, far_there = where_am_i(chips)
    listed = jnp.concatenate([list_ref[...], jnp.full((8, 32), -1, i32)], axis=1)
    for place, shift in enumerate(shifts):
        rolled_ref[8 * place : 8 * place + 8] = (
            pltpu.roll(listed, shift, 1) if shift else listed
        )
    part = functools.partial(listed_part, rolled_ref)
    other = 1 - core
    step, step_two, there, there_two = carried(other, near, far, near_there, far_there)
    cross, cross_two = 2 * step + other - core, 4 * step_two + other - core
    first = (
        part(0, cross_two, 0, 24, there_two & narrow(cross_two)),
        part(24, 4 * step_two, 24, 48, there_two),
        part(48, 2 * step, 48, 96, there),
        part(96, cross, 96, 120, there & narrow(cross)),
    )
    slot_ref[0:1, 0:128] = functools.reduce(jnp.maximum, first)
    slot_ref[0:1, 128:256] = part(0, cross, 0, 96, there & ~narrow(cross))
    for k in range(3):
        copies[k].wait()
        side_ref[k : k + 1, 0:sides] = landed[k][...]
    elem, face, slot_case = place_of(look_up(side_attributes(side_ref), slot_ref[0:1, :]))
    case_ref[0:1, :] = slot_case
    fill_one_hot(hot_ref, elem, face)

    for k in (6, 7, 8):
        copies[k].wait()
    coef, size, volume_scale, normal_scale = element_rows(coef_ref, level_ref)
    stack = face_stack([start_ref[...]], normal_scale)
    scalars = rows_of([x.astype(f32) for x in three(coef)] + [size], 16, lanes).astype(bf16)
    stack = jnp.concatenate([stack, jnp.concatenate([scalars] * 6, axis=1)], axis=0)
    stack_ref[...] = stack
    sent = gather_message(stack, hot_ref[...], slot_case, 1)
    sent_ref[...] = sent
    for k in (3, 4):
        copies[k].wait()
        side_ref[k : k + 1, 0:sides] = landed[k][...]
    copies[9].wait()


def own_setup_kernel(chips, side_ref, rolled_ref, hot_ref, case_ref, slot_ref):
    core, near, far, end, near_there, far_there = where_am_i(chips)
    part = functools.partial(listed_part, rolled_ref)
    flip = 1 - 2 * core
    step, step_two, there, there_two = carried(core, near, far, near_there, far_there)
    cross, cross_two = 2 * step + flip, 4 * step_two + flip
    slot_ref[0:1, 0:128] = jnp.maximum(
        part(0, 4 * step_two, 0, 24, there_two),
        part(24, cross_two, 24, 48, there_two & narrow(cross_two)),
    )
    slot_ref[0:1, 128:256] = jnp.maximum(
        part(0, 2 * step, 0, 48, there), part(96, cross, 96, 120, there & narrow(cross))
    )
    slot_ref[0:1, 256:384] = part(0, cross, 0, 96, there & ~narrow(cross))
    slot_ref[0:1, 384:512] = part(0, flip, 0, 96, core >= 0)
    elem, face, slot_case = place_of(look_up(side_attributes(side_ref), slot_ref[0:1, :]))
    case_ref[0:1, :] = slot_case
    fill_one_hot(hot_ref, elem, face)


def own_kernel(nf, stack_ref, hot_ref, case_ref, own_ref):
    own_ref[...] = gather_message(
        stack_ref[...], hot_ref[...], case_ref[0:1], nf
    )


def pack(x, nf):
    lane = lax.broadcasted_iota(i32, (1, lanes), 1)
    out = []
    for k in range(nf):
        last = x[32 * k + 24 : 32 * k + 32]
        for g in range(3):
            part = x[32 * k + 8 * g : 32 * k + 8 * g + 8]
            out.append(jnp.where(lane < 96, part, pltpu.roll(last, 96 - 32 * g, 1)))
    return jnp.concatenate(out, axis=0)


def unpack(x, nf):
    lane = lax.broadcasted_iota(i32, (1, lanes), 1)
    out = []
    for k in range(nf):
        part = [x[24 * k + 8 * g : 24 * k + 8 * g + 8] for g in range(3)]
        moved = [pltpu.roll(p, 32 * g + 32, 1) for g, p in enumerate(part)]
        out += part
        out.append(jnp.where(lane < 32, moved[0], jnp.where(lane < 64, moved[1], moved[2])))
    return jnp.concatenate(out, axis=0)


def carry_kernel(nf, sent_ref, own_ref, *rest):
    two_ref, one_ref = rest[-2:]
    h = 32 * nf
    lane = lax.broadcasted_iota(i32, (1, lanes), 1)
    sent = sent_ref[:, 0:128]
    handed = jnp.where((lane >= 48) & (lane < 96), pltpu.roll(sent, 48, 1), 0.0)
    two_away = own_ref[:, 0:128] + handed
    first = own_ref[:, 128:256] + jnp.where(lane >= 48, sent, 0.0)
    second = own_ref[:, 256:384] + sent_ref[:, 128:256]
    if nf == 1:
        two_ref[...] = two_away
        one_ref[:, 0:128] = first
        one_ref[:, 128:256] = second
    else:
        two_ref[...] = pack(two_away, nf)
        one_ref[0:h] = first
        one_ref[h:] = pack(second, nf)


def received(nf, one_ref, two_ref):
    if nf == 1:
        return two_ref[...], one_ref[:, 0:128], one_ref[:, 128:256]
    h = 32 * nf
    return unpack(two_ref[...], nf), one_ref[0:h], unpack(one_ref[h:], nf)


def relay_kernel(nf, chips, one_ref, two_ref, own_ref, *rest):
    out_ref = rest[-1]
    core, near, far, end, near_there, far_there = where_am_i(chips)
    lane = lax.broadcasted_iota(i32, (1, lanes), 1)
    two_away, one, second = received(nf, one_ref, two_ref)
    out_ref[:, 0:128] = own_ref[:, 384:512]
    passed = jnp.where(lane < 24, pltpu.roll(two_away, 56, 1), two_away)
    out_ref[:, 128:256] = jnp.where((lane < 48) & ~(end & (core == 1)), passed, one)
    out_ref[:, 256:384] = second


def setup_kernel(
    chips, coef_ref, level_ref, side_ref,
    own_hot_ref, partner_hot_ref, far_hot_ref, place_ref, info_ref, arrival_ref,
):
    core, near, far, end, near_there, far_there = where_am_i(chips)
    elem, direction, case = side_ref[0:1], side_ref[1:2], side_ref[2:3]
    kind, partner = side_ref[3:4], side_ref[4:5]
    live = lax.broadcasted_iota(i32, (1, side_pad), 1) < 930

    coef, size, volume_scale, normal_scale = element_rows(coef_ref, level_ref)
    scalars = rows_of([x.astype(f32) for x in three(coef)] + [size], 16, lanes)
    mine = dot(scalars.astype(bf16), one_hot(elem, lanes))
    hanging = (case >= 0) & (case < 4)
    own_coef = mine[0:1] + mine[1:2] + mine[2:3]
    own_size = mine[3:4] * jnp.where(hanging, 0.5, 1.0)

    attributes = side_attributes(side_ref, (mine[0:1], mine[1:2], mine[2:3], own_size))
    here = live & (partner < 930)
    other = look_up(attributes, jnp.where(here, partner, -1))
    other_elem, other_face = place_of(other)[:2]
    partner_hot_ref[...] = one_hot(other_elem, lanes)
    valid = other[3:4] > 0.5
    edge = jnp.where(kind == 1, 1.0, 0.0)
    least = jnp.where(valid, jnp.minimum(own_size, other[7:8]), 0.0)
    jump = 16.0 * (own_coef + other[4:5] + other[5:6] + other[6:7]) * least
    area = least * least
    info_ref[:, 0:side_pad] = rows_of(
        [jump, jump * (1.0 - edge), area * (0.5 + 0.5 * edge), area * (0.5 - 0.5 * edge),
         case.astype(f32), other[2:3]],
        8, side_pad,
    )

    def arrives(carrier):
        last = end & (carrier == 1)
        back = jnp.where((carrier == 0) | end, -near, near)
        back_two = jnp.where(carrier == 0, -far, far)
        turn = 2 * core - 1
        return (
            2 * back, 2 * back + turn, 4 * back_two, 4 * back_two + turn,
            ~(end & (carrier == 0)), ~last, last,
        )

    def span(low, high, valid):
        return low, jnp.where(valid, high, low)

    segments = []
    for mine, carrier in ((True, core), (False, 1 - core)):
        straight, cross, straight_two, cross_two, there, there_two, last = arrives(carrier)
        slim, wide = there & narrow(cross), there & ~narrow(cross)
        at_first = (last & (core != 1)) | (~last & (carrier == core))
        if mine:
            two_parts = ((*span(48, 72, there_two & narrow(cross_two)), cross_two),
                         (*span(72, 96, there_two), straight_two))
        else:
            segments.append(((0, 96, 2 * core - 1),))
            two_parts = ((*span(0, 24, there_two), straight_two),
                         (*span(24, 48, there_two & narrow(cross_two)), cross_two))
        segments.append((
            (*span(0, 48, there & at_first), straight), (*span(48, 96, there & ~at_first), straight),
            (*span(96, 120, slim), cross), *two_parts,
        ))
        segments.append(((*span(0, 96, wide), cross),))
    entry = partner - 930
    peer = (entry * 683) >> 16
    entry = entry - 96 * peer
    sought = live & (partner >= 930) & (kind == 0)
    column = jnp.full((1, side_pad), -1, i32)
    for tile, parts in enumerate(segments):
        for low, high, offset in parts:
            match = sought & (peer == row_of(offset)) & (entry < high - low)
            column = jnp.where(match, lanes * tile + low + entry, column)
    block = column >> 7
    split = [
        attributes * jnp.where(block == tile, 1.0, 0.0).astype(bf16) for tile in range(len(segments))
    ]
    target = dot_t(jnp.concatenate(split, axis=0), one_hot(column & 127, lanes))
    target = jnp.concatenate(
        [target[16 * tile : 16 * tile + 8] for tile in range(len(segments))], axis=1
    )
    target_elem, target_face, target_case = place_of(target)
    elems = jnp.concatenate([elem, target_elem], axis=1)
    faces = jnp.concatenate([direction, target_face], axis=1)
    near = side_pad + 256
    own_hot_ref[...] = one_hot(elems[:, :near], lanes)
    far_hot_ref[...] = one_hot(elems[:, near:], lanes)
    other_face = jnp.concatenate([other_face, jnp.full((1, 640), -1, i32)], axis=1)
    place_ref[...] = rows_of(
        [elems.astype(f32), faces.astype(f32), other_face.astype(f32)], 16, elems.shape[1]
    )
    info_ref[:, side_pad:] = rows_of(
        [jnp.zeros((1, 256), f32)] * 4 + [target_case[:, 0:256].astype(f32)], 8, 256
    )
    arrival_ref[...] = rows_of(
        [target_case.astype(f32), target[4:5] + target[5:6] + target[6:7], target[7:8]],
        8, 640,
    )


def whole_kernel(own_elem_ref, partner_elem_ref, far_elem_ref, place_ref, own_ref, partner_ref, far_ref):
    near = side_pad + 256
    for source, row, low, high, target in (
        (own_elem_ref, 1, 0, near, own_ref),
        (partner_elem_ref, 2, 0, side_pad, partner_ref),
        (far_elem_ref, 1, near, near + 384, far_ref),
    ):
        hot, face = source[...], place_ref[row : row + 1, low:high]
        for f in range(6):
            target[lanes * f : lanes * f + lanes] = hot * jnp.where(face == f, 1.0, 0.0).astype(bf16)


def turn_kernel(place_ref, own_ref, far_ref):
    row = lax.broadcasted_iota(i32, (16, lanes), 0)
    weight = jnp.where(row == 0, 1.0, jnp.where(row == 1, 128.0, 0.0)).astype(bf16)
    column = lax.dot_general(
        place_ref[...].astype(bf16), weight, (((0,), (0,)), ((), ())), preferred_element_type=f32
    )
    lane = lax.broadcasted_iota(i32, (1, lanes), 1).astype(f32)
    split = own_ref.shape[0]
    for f in range(6):
        part = jnp.where(column == lane + 128.0 * f, 1.0, 0.0).astype(bf16)
        own_ref[:, lanes * f : lanes * f + lanes] = part[:split]
        far_ref[:, lanes * f : lanes * f + lanes] = part[split:]


def sides_kernel(
    nf, stack_ref, own_hot_ref, partner_hot_ref, far_hot_ref, place_ref, info_ref,
    arrival_ref, mine_ref, other_ref, target_ref,
):
    stack = stack_ref[0 : 32 * terms * nf]
    near = side_pad + 256
    for hot_ref, face, case, out_ref in (
        (own_hot_ref, place_ref[1:2, 0:near], info_ref[4:5], mine_ref),
        (partner_hot_ref, place_ref[2:3, 0:side_pad], info_ref[5:6, 0:side_pad], other_ref),
        (far_hot_ref, place_ref[1:2, near:], arrival_ref[0:1, 256:640], target_ref),
    ):
        got = gather_columns(stack, hot_ref[...], face, nf)
        out_ref[...] = interpolate(got, case.astype(i32), nf)


def side_flux(nf, mine, outer, coefs, case, face, weight_ref, hot):
    jump, jump_out, area, area_out = coefs
    weight = weight_ref[:, 0:1]
    flux = []
    for k in range(nf):
        inner, other = mine[32 * k : 32 * k + 32], outer[32 * k : 32 * k + 32]
        jumps = jnp.where(slope_rows(inner.shape), 0.0, jump * inner - jump_out * other)
        flux.append(weight * (jumps - other_part(area * inner - area_out * other)))
    flux = interpolate(cat(flux, 0), case.astype(i32), nf, transposed=True)
    return scatter_columns(flux, hot, face, nf)


def halo_coefs(coef, size, other_coef, other_size):
    least = jnp.minimum(size, other_size)
    return 16.0 * (coef + other_coef) * least, 0.5 * least * least


def flux_kernel(
    turn, nf, skip, both, chips, one_ref, two_ref, mine_ref, other_ref, place_ref, info_ref, arrival_ref, weight_ref,
    own_hot_ref, field_ref, coef_ref, level_ref, stiffness_ref, *rest,
):
    h = 32 * nf
    rows = slice(32 * skip, 32 * skip + h)
    core, near, far, end, near_there, far_there = where_am_i(chips)
    lane = lax.broadcasted_iota(i32, (1, lanes), 1)
    two_away, first, second = received(both, one_ref, two_ref)
    kept = jnp.where(lane < 72, two_away, pltpu.roll(two_away, 72, 1))
    inside = (lane >= 48) & (lane < 96) & ~(end & (core == 1))
    got = jnp.concatenate(
        [jnp.where(inside, kept, first), second], axis=1
    )
    if turn == 0:
        sum_ref, volume_ref, halo_ref = rest
        halo = halo_coefs(
            arrival_ref[1:2, 0:256], arrival_ref[2:3, 0:256], got[h : h + 1], got[h + 1 : h + 2]
        )
        halo_ref[...] = rows_of(halo, 8, 256)
    else:
        halo_ref, sum_ref, volume_ref = rest
        halo = halo_ref[0:1], halo_ref[1:2]
    coefs = [
        jnp.concatenate([info_ref[k : k + 1, 0:side_pad], halo[k // 2]], axis=1) for k in range(4)
    ]
    outer = jnp.concatenate([other_ref[rows], got[rows]], axis=1)
    sum_ref[...] = side_flux(
        nf, mine_ref[rows], outer, coefs, info_ref[4:5], place_ref[1:2, 0 : side_pad + 256], weight_ref,
        own_hot_ref[...],
    )
    volume_scale = element_rows(coef_ref, level_ref)[2]
    low = 64 * skip
    fields = [field_ref[low + 64 * k : low + 64 * k + 64] * volume_scale for k in range(nf)]
    volume = table_dot(stiffness_ref[...], cat(fields, 1))
    for k in range(nf):
        volume_ref[64 * k : 64 * k + 64, :] = volume[:, lanes * k : lanes * k + lanes]


def widen_kernel(inverse_ref, wide_ref):
    for col in range(64):
        wide_ref[col] = inverse_ref[col].astype(f32)


def solve_blocks(inverse_ref, hold_ref, nf):
    sums = [jnp.zeros((64, lanes), f32) for _ in range(nf)]
    for col in range(64):
        block = inverse_ref[col].astype(f32)
        for k in range(nf):
            sums[k] = sums[k] + block * hold_ref[64 * k + col : 64 * k + col + 1, :]
    return sums


def update_kernel(
    turn, nf, skip, nf_next,
    one_ref, local_ref, volume_ref, target_ref, place_ref, arrival_ref, far_hot_ref, weight_ref,
    field_ref, coef_ref, level_ref, inverse_ref, *rest,
):
    if turn == 0:
        guess_ref, *rest = rest
    else:
        halo_ref, *rest = rest
    if turn == 1:
        rhs_ref, *rest = rest
    if nf_next:
        hot_ref, case_ref, new_ref, stack_ref, sent_ref, *rest = rest
    elif turn == 3:
        part_ref, *rest = rest
    else:
        new_ref, *rest = rest
    hold_ref = rest[-1]
    h = 32 * nf
    rows = slice(32 * skip, 32 * skip + h)
    if turn == 0:
        halo = halo_coefs(
            arrival_ref[1:2, 256:640], arrival_ref[2:3, 256:640],
            one_ref[h : h + 1], one_ref[h + 1 : h + 2],
        )
        rest[0][...] = rows_of(halo, 8, 384)
    else:
        halo = (halo_ref[0:1], halo_ref[1:2])
    total = local_ref[...] + side_flux(
        nf, target_ref[rows], one_ref[rows], (halo[0], halo[0], halo[1], halo[1]), arrival_ref[0:1, 256:640],
        place_ref[1:2, side_pad + 256 :], weight_ref, far_hot_ref[...],
    )
    coef, size, volume_scale, normal_scale = element_rows(coef_ref, level_ref)
    scale = jnp.where(slope_rows((32, lanes)), jnp.broadcast_to(normal_scale, (32, lanes)), 1.0)
    for k in range(nf):
        mine = total[32 * k : 32 * k + 32]
        faces = [mine[:, lanes * f : lanes * f + lanes] * scale for f in range(6)]
        part = lift_traces(volume_ref[64 * k : 64 * k + 64], faces)
        if turn == 1 and k == 1:
            part = rhs_ref[...] - part
        hold_ref[64 * k : 64 * k + 64, :] = part
    new = solve_blocks(inverse_ref, hold_ref, nf)
    if turn == 0:
        new.append(guess_ref[...])
    if turn < 3:
        for k, x in enumerate(new):
            new_ref[64 * k : 64 * k + 64, :] = x
    if nf_next:
        stack = face_stack(new[:nf_next], normal_scale)
        stack_ref[...] = stack
        sent = gather_message(stack, hot_ref[...], case_ref[0:1], nf_next)
        sent_ref[...] = sent
    if turn == 3:
        lane = lax.broadcasted_iota(i32, (1, lanes), 1)
        sums = []
        for x in (field_ref[...], new[0]):
            total = jnp.sum(x * x, axis=0, keepdims=True)
            sums.append(total + pltpu.roll(total, 64, 1))
        part_ref[...] = jnp.broadcast_to(jnp.where(lane < 64, sums[0], sums[1]), part_ref.shape)


def finish_kernel(part_ref, guess_ref, first_ref, second_ref, out_ref, bound_ref):
    total = jnp.sum(part_ref[...], axis=0, keepdims=True)
    lane = lax.broadcasted_iota(i32, (1, lanes), 1)
    before = jnp.sum(jnp.where(lane < 64, total, 0.0), axis=1, keepdims=True)
    after = jnp.sum(jnp.where(lane < 64, 0.0, total), axis=1, keepdims=True)
    bound = jnp.sqrt(after / before)
    upper = 1.2 * bound
    lower = upper / 15.0
    center = 0.5 * (upper + lower)
    half = 0.5 * (upper - lower)
    ratio = center / half
    damping = 1.0 / ratio
    damping_next = 1.0 / (2.0 * ratio - damping)
    first = first_ref[64:128] / center
    second = first_ref[64:128] - second_ref[...] / center
    out_ref[...] = (
        guess_ref[...] + first + (damping_next * damping * first + 2.0 * damping_next / half * second)
    )
    bound_ref[...] = jnp.broadcast_to(bound, (1, lanes))


def in_vmem(x):
    return pltpu.with_memory_space_constraint(x, pltpu.VMEM)


def in_hbm(x):
    return pltpu.with_memory_space_constraint(x, pltpu.HBM)


def run(body, outs, ins, name, scratch=(), flops=1 << 24, placed=True, kept=True):
    spec = pl.BlockSpec(memory_space=pltpu.VMEM)
    return pl.pallas_call(
        body,
        out_shape=[(pltpu.VMEM if kept else jax.ShapeDtypeStruct)(shape, dtype) for shape, dtype in outs],
        in_specs=[spec if placed else pl.BlockSpec(memory_space=pltpu.HBM)] * len(ins),
        out_specs=[spec] * len(outs),
        scratch_shapes=list(scratch),
        compiler_params=pltpu.CompilerParams(vmem_limit_bytes=24 << 20),
        cost_estimate=pl.CostEstimate(flops=flops, bytes_accessed=1 << 20, transcendentals=0),
        name=name,
    )(*(in_vmem(x) if placed else in_hbm(x) for x in ins))


def local(
    rhs_field, initial_guess, start_vector, coefficient, refine_level, block_inverse,
    side_elem, side_dir, side_case, side_kind, partner, send_list,
):
    devices = lax.axis_size("dom")
    chips = devices // 2
    stiffness, weight = (jnp.asarray(t) for t in const_tables())
    coef = coefficient.reshape(1, lanes)
    level = refine_level.reshape(1, lanes)

    def permute(x, to):
        return lax.ppermute(x, "dom", sorted(to.items()))

    swapped = {i: i ^ 1 for i in range(devices)}
    two_away, one_away = {}, {}
    for c in range(chips):
        two_away[2 * c] = 2 * (c ^ 2)
        one_away[2 * c] = 2 * (c ^ 1)
        over = c + 2 if c % 4 >= 2 else c - 2
        two_away[2 * c + 1] = 2 * (over if 0 <= over < chips else c ^ 1) + 1
        if 0 < c < chips - 1:
            one_away[2 * c + 1] = 2 * (c + 1 if c % 2 else c - 1) + 1
    for c in (0, chips - 1):
        one_away[2 * (c ^ 1)] = 2 * c + 1
        one_away[2 * c + 1] = 2 * c

    def exchange(sent, nf, own_work, work, *beside):
        rows = sent.shape[0]
        (own,) = own_work()
        two_out, one_out = run(
            functools.partial(carry_kernel, nf),
            [((rows, lanes), f32), ((rows, 256), f32)] if nf == 1
            else [((24 * nf, lanes), f32), ((56 * nf, lanes), f32)],
            [permute(sent, swapped), own, *beside[:1]], "carry",
        )
        arrivals = permute(one_out, one_away), permute(two_out, two_away)
        made = work()
        (last,) = run(
            functools.partial(relay_kernel, nf, chips), [((rows, 384), f32)],
            [*arrivals, own, made[2], *beside[1:]], "relay",
        )
        return arrivals, permute(last, swapped), made

    sides = [x.reshape(1, -1) for x in (side_elem, side_dir, side_case, side_kind, partner)]
    first = [*sides, send_list, start_vector, coef, level, initial_guess]
    hot, case, stack, sides, rolled, sent, coef, level, guess = run(
        functools.partial(send_setup_kernel, chips),
        [((768, 256), bf16), ((8, 256), i32), ((32 * terms + 16, 768), bf16), ((8, side_pad), i32), ((32, lanes), i32),
         ((40, 256), f32), *((x.shape, x.dtype) for x in first[7:])],
        first,
        "send_setup",
        scratch=[
            pltpu.VMEM((8, 256), i32),
            *(pltpu.VMEM(x.shape, x.dtype) for x in first[:7]), pltpu.SemaphoreType.DMA((len(first),)),
        ],
        placed=False,
    )
    own_slots = run(
        functools.partial(own_setup_kernel, chips),
        [((768, 512), bf16), ((8, 512), i32)],
        [sides, rolled],
        "own_setup",
        scratch=[pltpu.VMEM((8, 512), i32)],
    )
    fields, halo, late = start_vector, [], []
    (inverse,) = run(widen_kernel, [(block_inverse.shape, f32)], [block_inverse], "widen")
    for turn, (nf, nf_next) in enumerate(((1, 2), (2, 2), (2, 1), (1, 0))):
        h = 32 * nf
        def own_work():
            return run(
                functools.partial(own_kernel, nf),
                [((sent.shape[0], 512), f32)],
                [stack, *own_slots],
                "own",
            )

        def side_work(hots):
            return run(
                functools.partial(sides_kernel, nf),
                [((h, side_pad + 256), f32), ((h, side_pad), f32), ((h, 384), f32)],
                [stack, *hots, *places],
                "sides",
            )

        if turn == 0:
            *hots, place, info, arrival = run(
                functools.partial(setup_kernel, chips),
                [((lanes, side_pad + 256), bf16), ((lanes, side_pad), bf16), ((lanes, 384), bf16),
                 ((16, side_pad + 640), f32), ((8, side_pad + 256), f32), ((8, 640), f32)],
                [coef, level, sides],
                "setup",
            )
            places = [place, info, arrival]
            own_scatter, _, far_scatter = hots
        elif turn == 1:
            hots = run(
                whole_kernel,
                [((768, side_pad + 256), bf16), ((768, side_pad), bf16), ((768, 384), bf16)],
                [*hots, place],
                "whole",
            )
            own_scatter, far_scatter = run(
                turn_kernel,
                [((side_pad + 256, 768), bf16), ((384, 768), bf16)],
                [place],
                "turn",
            )
        beside = (hots[0], own_scatter) if turn == 1 else late if turn == 3 else ()
        arrivals, last, made = exchange(
            sent, nf, own_work, functools.partial(side_work, hots), *beside
        )
        mine, others, targets = made

        def apply(count, skip, count_next):
            rows = 32 * count
            sums, volume, *near = run(
                functools.partial(flux_kernel, turn, count, skip, nf, chips),
                [((rows, 768), f32), ((64 * count, lanes), f32)] + ([] if turn else [((8, 256), f32)]),
                [*arrivals, mine, others, *places, weight, own_scatter, fields, coef, level, stiffness]
                + halo[:1],
                "flux",
            )
            ins = [
                last, sums, volume, targets, place, arrival, far_scatter, weight, fields, coef, level,
                inverse, *(halo[1:] if turn else [guess]), *([rhs_field] if turn == 1 else []),
            ]
            outs = [((devices, lanes) if turn == 3 else (64 * max(count, count_next), lanes), f32)]
            if count_next:
                ins += [hot, case]
                outs += [((32 * terms * count_next, 768), bf16), ((32 * count_next, 256), f32)]
            outs += [] if turn else [((8, 384), f32)]
            late.append(sums)
            made = run(
                functools.partial(update_kernel, turn, count, skip, count_next),
                outs, ins, "update",
                scratch=[pltpu.VMEM((64 * count, lanes), f32)],
            )
            return [*made, *near]

        if turn == 0:
            new, stack, sent, far_halo, near_halo = apply(nf, 0, nf_next)
            halo = [near_halo, far_halo]
        elif turn == 1:
            new, stack, sent = apply(nf, 0, nf_next)
            first = new
        elif turn == 2:
            new, stack, sent = apply(1, 0, 1)
            late.clear()
            late += apply(1, 1, 0)
            second = late[1]
        else:
            (parts,) = apply(1, 0, 0)
        fields = new
    parts = lax.all_to_all(parts.reshape(devices, 1, lanes), "dom", 0, 0).reshape(devices, lanes)
    smoothed, bound = run(
        finish_kernel,
        [((64, lanes), f32), ((1, lanes), f32)],
        [parts, guess, first, second],
        "finish",
        kept=False,
    )
    return smoothed, bound[0, 0]


def solution(mesh):
    placed = (
        P(None, "dom"), P(None, "dom"), P(None, "dom"), P("dom"), P("dom"), P(None, None, "dom"),
        P("dom"), P("dom"), P("dom"), P("dom"), P("dom"), P("dom", None),
    )
    return jax.shard_map(
        local, mesh=mesh, in_specs=placed, out_specs=(P(None, "dom"), P()), check_vma=False
    )
```
